32 devices in a mesh: ch: 8 (over z, x), seq: 4 (over y, core).
Axes of the slice: x: 2, y: 2, z: 4, core: 2. Of those that a mesh axis runs over, the one named last changes fastest.
Arguments:
- tokens: bfloat16 [4, 2048, 2, 1024], P('seq', 'ch'), may hold values from -6 to 6
- lengths: int32 [4, 2], P('seq'), may hold values from 257 to 2048, as said below
- in_weight: bfloat16 [1024, 3072], P(('ch', 'seq')), may hold values from -0.1875 to 0.1875
- out_weight: bfloat16 [1024, 1024], P(('ch', 'seq')), may hold values from -0.1875 to 0.1875
- up_weight: bfloat16 [1024, 4096], P(('ch', 'seq')), may hold values from -0.1875 to 0.1875
- down_weight: bfloat16 [4096, 1024], P(('ch', 'seq')), may hold values from -0.09375 to 0.09375
- gain_one: bfloat16 [1024], P(('ch', 'seq')), may hold values from 0.5 to 1.5
- gain_two: bfloat16 [1024], P(('ch', 'seq')), may hold values from 0.5 to 1.5
- conv_taps: float32 [3, 3, 1024], P(None, None, 'ch'), may hold values from -3.5 to 3.5
- skip_gain: float32 [1024], P('ch'), may hold values from -4 to 4
- filter_first: float32 [33, 64], replicated, may hold values from -1 to 1
- filter_bias: float32 [64], replicated, may hold values from -1 to 1
- frequency: float32 [64], replicated, may hold values from 0.5 to 2
- filter_second: float32 [64, 1024], P(None, 'ch'), may hold values from -0.046875 to 0.046875
- cotangent: bfloat16 [4, 2048, 2, 1024], P('seq', 'ch'), may hold values from -6 to 6
Outputs:
- output: bfloat16 [4, 2048, 2, 1024], P('seq', 'ch')
- grad_tokens: bfloat16 [4, 2048, 2, 1024], P('seq', 'ch')
- grad_in_weight: float32 [1024, 3072], P(('ch', 'seq'))
- grad_out_weight: float32 [1024, 1024], P(('ch', 'seq'))
- grad_up_weight: float32 [1024, 4096], P(('ch', 'seq'))
- grad_down_weight: float32 [4096, 1024], P(('ch', 'seq'))
- grad_gain_one: float32 [1024], P(('ch', 'seq'))
- grad_gain_two: float32 [1024], P(('ch', 'seq'))
- grad_conv_taps: float32 [3, 3, 1024], P(None, None, 'ch')
- grad_skip_gain: float32 [1024], P('ch')
- grad_filter_first: float32 [33, 64], replicated
- grad_filter_bias: float32 [64], replicated
- grad_frequency: float32 [64], replicated
- grad_filter_second: float32 [64, 1024], P(None, 'ch')
The draws below stay inside these ranges and needn't reach their ends.
Inputs may be any that keep to these rules, and one draw needn't show every extreme that they name: `lengths`: in every group one bucket, which one drawn from the seed, holds a sequence of all 2048 positions.
All inputs are finite; a program needn't handle non-finite values.
Results may differ from the reference program's by a relative error of at most 0.012.
Values may be sent and summed in bfloat16 or wider, within the bound.
A program may use at most 256 MiB of HBM per device.

```python
import math
import jax
import jax.numpy as jnp
from jax import lax

D = 1024
FF = 4096
EMB = 33
FILT = 64
NB = 2
BUCKET = 2048
GROUPS = 4


def draw_lengths(key, part):
    key = jax.random.fold_in(key, 11)
    key_div, key_cut, key_full = jax.random.split(key, 3)
    divisor = jax.random.randint(key_div, (GROUPS, NB), 1, 5)
    trimmed = jax.random.randint(key_cut, (GROUPS, NB), 0, BUCKET // 8)
    shorter = BUCKET // divisor - trimmed
    chosen = jax.random.randint(key_full, (GROUPS,), 0, NB)
    full_slot = jnp.arange(NB)[None, :] == chosen[:, None]
    return jnp.where(full_slot, BUCKET, shorter).astype(jnp.int32)


def shard_levels(own_key, shape, cuts, least, high):
    def one(dim, shards_of):
        heights = jax.random.uniform(jax.random.fold_in(jax.random.fold_in(own_key, 6), dim), (shards_of,), jnp.float32, least / len(cuts), high / len(cuts))
        return jnp.repeat(jnp.exp(heights), shape[dim] // shards_of).reshape((-1,) + (1,) * (len(shape) - dim - 1))

    loudness = one(*cuts[0])
    for cut in cuts[1:]:
        loudness = loudness * one(*cut)
    return loudness


def centred(rng, dims, scale, reach, pieces=(), kind=jnp.bfloat16):
    drawn = jax.random.normal(rng, dims, jnp.float32) * scale
    if len(pieces) > 0:
        drawn = shard_levels(rng, dims, pieces, -0.22, 0.18) * drawn
    return jnp.clip(drawn, min=-reach, max=reach).astype(kind)


def setup_inputs(seed: int = 0) -> dict:
    keys = jax.random.split(jax.random.key(seed), 16)
    return {
        "tokens": centred(keys[0], (GROUPS, BUCKET, NB, D), 1.0, 6.0, ((0, 4), (1, 8))),
        "lengths": draw_lengths(jax.random.fold_in(keys[15], 71), 0),
        "in_weight": centred(keys[2], (D, 3 * D), D ** -0.5, 0.1875, ((0, 32),)),
        "out_weight": centred(keys[3], (D, D), D ** -0.5, 0.1875, ((0, 32),)),
        "up_weight": centred(keys[4], (D, FF), D ** -0.5, 0.1875, ((0, 32),)),
        "down_weight": centred(keys[5], (FF, D), FF ** -0.5, 0.09375, ((0, 32),)),
        "gain_one": jnp.clip(1.0 + 0.1 * jax.random.normal(keys[6], (D,), jnp.float32), 0.5, 1.5).astype(jnp.bfloat16),
        "gain_two": jnp.clip(1.0 + 0.1 * jax.random.normal(keys[7], (D,), jnp.float32), 0.5, 1.5).astype(jnp.bfloat16),
        "conv_taps": centred(keys[8], (3, 3, D), 3 ** -0.5, 3.5, ((2, 8),), jnp.float32),
        "skip_gain": centred(keys[9], (D,), 1.0, 4.0, ((0, 8),), jnp.float32),
        "filter_first": centred(keys[10], (EMB, FILT), EMB ** -0.5, 1.0, (), jnp.float32),
        "filter_bias": jnp.clip(jax.random.uniform(keys[11], (FILT,), jnp.float32, -1.0, 1.0), -1.0, 1.0),
        "frequency": jnp.clip(jax.random.uniform(keys[12], (FILT,), jnp.float32, 0.5, 2.0), 0.5, 2.0),
        "filter_second": centred(keys[13], (FILT, D), (8 * BUCKET) ** -0.5, 0.046875, ((1, 8),), jnp.float32),
        "cotangent": centred(keys[14], (GROUPS, BUCKET, NB, D), 1.0, 6.0, ((0, 4), (1, 8))),
    }


EPS = 1e-05
SLOW_RATE = math.log(100.0) / 1.5
FAST_RATE = math.log(100.0) / 0.3
HIGH = lax.Precision.HIGHEST

@jax.custom_vjp
def low(v):
    return lax.optimization_barrier(v.astype(jnp.bfloat16)).astype(jnp.float32)

@jax.custom_vjp
def low_back(v):
    return v

def low_keep(v):
    return (low(v), None)

def low_pass(kept, grad):
    return (grad,)

def back_keep(v):
    return (v, None)

def back_low(kept, grad):
    return (low(grad),)
low.defvjp(low_keep, low_pass)
low_back.defvjp(back_keep, back_low)

def layer_norm(values, gain):
    centre = values - lax.optimization_barrier(jnp.mean(values, axis=-1, keepdims=True))
    spread = lax.optimization_barrier(jnp.mean(centre * centre, axis=-1, keepdims=True))
    return centre * lax.rsqrt(spread + EPS) * gain

def positions_table(length, features):
    steps = jnp.arange(length).astype(jnp.float32)
    scaled = steps / (length - 1)
    bands = (features - 1) // 2
    freqs = 0.0001 + (bands - 1 - 0.0001) * jnp.arange(bands).astype(jnp.float32) / (bands - 1)
    angles = freqs[None, :] * (2.0 * math.pi * steps / length)[:, None]
    return jnp.concatenate([scaled[:, None], jnp.cos(angles), -jnp.sin(angles)], axis=1)

def decay_table(length, chan_start, count, width):
    scaled = jnp.arange(length).astype(jnp.float32) / (length - 1)
    chans = (chan_start + jnp.arange(count)).astype(jnp.float32)
    rates = SLOW_RATE + (FAST_RATE - SLOW_RATE) * chans / (width - 1)
    return jnp.exp(-scaled[:, None] * rates[None, :])

def filter_hidden(filter_first, filter_bias, frequency, table):
    inner = jnp.dot(table, filter_first, precision=HIGH) + filter_bias
    return jnp.sin(frequency * inner)

def both_low(values):
    return low(low_back(values))

def group_forward(params, x_group, length_group):
    in_weight, out_weight, up_weight, down_weight, gain_one, gain_two, conv_taps, skip_gain, filter_first, filter_bias, frequency, filter_second = params
    length = x_group.shape[0]
    buckets = x_group.shape[1]
    width = x_group.shape[2]
    places = jnp.arange(length, dtype=jnp.int32)
    mask = (places[:, None] < length_group[None, :].astype(jnp.int32)).astype(jnp.float32)
    x_zero = x_group * mask[:, :, None]
    normed = low(layer_norm(x_zero, gain_one))
    streams = both_low(jnp.dot(normed, in_weight, precision=HIGH)).reshape(length, buckets, 3, width)
    padded = jnp.pad(streams, ((2, 0), (0, 0), (0, 0), (0, 0)))
    conv = conv_taps[0] * streams + conv_taps[1] * padded[1:-1] + conv_taps[2] * padded[:-2]
    gate = conv[:, :, 0]
    key_part = conv[:, :, 1]
    value_part = conv[:, :, 2]
    mixed = key_part * value_part
    table = positions_table(length, filter_first.shape[0])
    hidden = filter_hidden(filter_first, filter_bias, frequency, table)
    filt = jnp.dot(hidden, filter_second, precision=HIGH) * decay_table(length, 0, width, width)
    spectrum = jnp.fft.rfft(mixed, n=2 * length, axis=0) * jnp.fft.rfft(filt, n=2 * length, axis=0)[:, None, :]
    long_part = jnp.fft.irfft(spectrum, n=2 * length, axis=0)[:length] + skip_gain * mixed
    mixer = both_low(gate * long_part * mask[:, :, None])
    after_mix = x_zero + low_back(jnp.dot(mixer, out_weight, precision=HIGH))
    normed_two = low(layer_norm(after_mix, gain_two))
    inner = low_back(jnp.dot(normed_two, up_weight, precision=HIGH))
    active = low(jax.nn.gelu(inner))
    return after_mix + jnp.dot(active, down_weight, precision=HIGH)

def whole_layer(params, tokens_all, lengths):
    step = jax.checkpoint(group_forward)

    def one_group(pair):
        return step(params, pair[0], pair[1])
    return lax.map(one_group, (tokens_all, lengths))

def reference(tokens, lengths, in_weight, out_weight, up_weight, down_weight, gain_one, gain_two, conv_taps, skip_gain, filter_first, filter_bias, frequency, filter_second, cotangent):
    params = (in_weight.astype(jnp.float32), out_weight.astype(jnp.float32), up_weight.astype(jnp.float32), down_weight.astype(jnp.float32), gain_one.astype(jnp.float32), gain_two.astype(jnp.float32), conv_taps.astype(jnp.float32), skip_gain.astype(jnp.float32), filter_first.astype(jnp.float32), filter_bias.astype(jnp.float32), frequency.astype(jnp.float32), filter_second.astype(jnp.float32))

    def forward(param_tuple, inputs):
        return whole_layer(param_tuple, inputs, lengths)
    result, pull = jax.vjp(forward, params, tokens.astype(jnp.float32))
    grads, grad_input = pull(cotangent.astype(jnp.float32))
    return (result.astype(jnp.bfloat16), grad_input.astype(jnp.bfloat16), grads[0], grads[1], grads[2], grads[3], grads[4], grads[5], grads[6], grads[7], grads[8], grads[9], grads[10], grads[11])
```

```python
import functools
import math

import jax
import jax.numpy as jnp
import numpy as np
from jax import lax
from jax.experimental import pallas as pl
from jax.experimental.pallas import tpu as pltpu
from jax.sharding import PartitionSpec as P

EPS = 1e-05
SLOW_RATE = math.log(100.0) / 1.5
FAST_RATE = math.log(100.0) / 0.3
HIGH = lax.Precision.HIGHEST
BF = jnp.bfloat16
F32 = jnp.float32
MESH = pl.DeviceIdType.MESH
VMEM_LIMIT = 56 << 20


def layer_norm(values, gain):
    centre = values - jnp.mean(values, axis=-1, keepdims=True)
    spread = jnp.mean(centre * centre, axis=-1, keepdims=True)
    return centre * lax.rsqrt(spread + EPS) * gain


def positions_table(length, features):
    steps = jnp.arange(length).astype(jnp.float32)
    scaled = steps / (length - 1)
    bands = (features - 1) // 2
    freqs = 0.0001 + (bands - 1 - 0.0001) * jnp.arange(bands).astype(jnp.float32) / (bands - 1)
    angles = freqs[None, :] * (2.0 * math.pi * steps / length)[:, None]
    return jnp.concatenate([scaled[:, None], jnp.cos(angles), -jnp.sin(angles)], axis=1)


def decay_table(length, chan_start, count, width):
    scaled = jnp.arange(length).astype(jnp.float32) / (length - 1)
    chans = (chan_start + jnp.arange(count)).astype(jnp.float32)
    rates = SLOW_RATE + (FAST_RATE - SLOW_RATE) * chans / (width - 1)
    return jnp.exp(-scaled[:, None] * rates[None, :])


def filter_hidden(filter_first, filter_bias, frequency, table):
    inner = jnp.dot(table, filter_first, precision=HIGH) + filter_bias
    return jnp.sin(frequency * inner)


def block_tables(size):
    k = np.arange(size)[:, None]
    t = np.arange(size)[None, :]
    angle = 2.0 * np.pi * ((k * t) % (2 * size)) / (2 * size)
    real = np.cos(angle)
    imag = -np.sin(angle)
    imag[0] = np.where(np.arange(size) % 2 == 0, 1.0, -1.0)
    full = np.concatenate([real, imag], axis=0).astype(np.float32)
    high = full.astype(jnp.bfloat16)
    low = (full - high.astype(np.float32)).astype(jnp.bfloat16)
    weight = np.full((size, 1), 1.0 / size, np.float32)
    weight[0] = 0.5 / size
    sign = np.where(np.arange(size) % 2 == 0, 1.0, -1.0).astype(np.float32)[:, None]
    lanes = np.zeros((size, 128), np.float32)
    lanes[:, 0:1] = weight
    lanes[:, 1:2] = sign
    lanes[:, 2] = 1.0
    lanes[0, 2] = 0.0
    return high, low, high.T.copy(), low.T.copy(), lanes


def split_high(values):
    high = values.astype(BF)
    return high, (values - high.astype(F32)).astype(BF)


def mm(a, b):
    return jnp.dot(a, b, preferred_element_type=F32)


def spectra(fh, fl, source, target, blocks, first=0):
    def step(i, carry):
        block = source[i]
        target[i] = mm(fh[...], block) + mm(fl[...], block)
        return carry

    lax.fori_loop(first, blocks, step, 0)


def filter_spectra(fh, fl, lanes, h_ref, abc, blocks, size):
    weight = lanes[:, 0:1]
    sign = lanes[:, 1:2]
    keep = lanes[:, 2:3]

    def step(j, carry):
        prev_re, prev_im = carry
        high, low = split_high(h_ref[j])
        now = mm(fh[...], high) + mm(fl[...], high) + mm(fh[...], low)
        now_re = now[:size]
        now_im = now[size:]
        g_re = (now_re + sign * prev_re) * weight
        g_im = (now_im + sign * prev_im) * weight
        abc[j, 0] = g_re
        abc[j, 1] = g_im * keep
        abc[j, 2] = jnp.where(keep > 0.5, g_re, g_im)
        return now_re, now_im

    zero = jnp.zeros((size, h_ref.shape[2]), F32)
    lax.fori_loop(0, blocks, step, (zero, zero))


def row_chunks(size, cols, body):
    width = min(128, cols)
    for lane in range(0, cols, width):

        def step(i, carry, lane=lane):
            body(pl.multiple_of(i * 8, 8), lane, width)
            return carry

        lax.fori_loop(0, size // 8, step, 0)


def products_forward(xs, abc, out, blocks, size):
    cols = xs.shape[2]

    def body(row, lane, width):
        re = [xs[i, pl.ds(row, 8), lane : lane + width] for i in range(blocks)]
        im = [xs[i, pl.ds(size + row, 8), lane : lane + width] for i in range(blocks)]
        a = [abc[j, 0, pl.ds(row, 8), lane : lane + width] for j in range(blocks)]
        b = [abc[j, 1, pl.ds(row, 8), lane : lane + width] for j in range(blocks)]
        c = [abc[j, 2, pl.ds(row, 8), lane : lane + width] for j in range(blocks)]
        for m in range(blocks):
            sum_re = re[0] * a[m] - im[0] * b[m]
            sum_im = re[0] * b[m] + im[0] * c[m]
            for i in range(1, m + 1):
                sum_re = sum_re + (re[i] * a[m - i] - im[i] * b[m - i])
                sum_im = sum_im + (re[i] * b[m - i] + im[i] * c[m - i])
            out[m, pl.ds(row, 8), lane : lane + width] = sum_re
            out[m, pl.ds(size + row, 8), lane : lane + width] = sum_im

    row_chunks(size, cols, body)


def products_backward(xs, ds, abc, out, lanes, blocks, size):
    cols = xs.shape[2]

    def body(row, lane, width):
        here = pl.ds(row, 8)
        there = pl.ds(size + row, 8)
        piece = slice(lane, lane + width)
        x_re = [xs[i, here, piece] for i in range(blocks)]
        x_im = [xs[i, there, piece] for i in range(blocks)]
        d_re = [ds[i, here, piece] for i in range(blocks)]
        d_im = [ds[i, there, piece] for i in range(blocks)]
        a = [abc[j, 0, here, piece] for j in range(blocks)]
        b = [abc[j, 1, here, piece] for j in range(blocks)]
        c = [abc[j, 2, here, piece] for j in range(blocks)]
        for i in range(blocks):
            sum_re = d_re[i] * a[0] + d_im[i] * b[0]
            sum_im = d_im[i] * c[0] - d_re[i] * b[0]
            for m in range(i + 1, blocks):
                sum_re = sum_re + (d_re[m] * a[m - i] + d_im[m] * b[m - i])
                sum_im = sum_im + (d_im[m] * c[m - i] - d_re[m] * b[m - i])
            out[i, here, piece] = sum_re
            out[i, there, piece] = sum_im
        weight = lanes[here, 0:1]
        sign = lanes[here, 1:2]
        keep = lanes[here, 2:3] > 0.5
        later_re = None
        later_im = None
        for j in range(blocks - 1, -1, -1):
            rr = d_re[j] * x_re[0]
            ii = d_im[j] * x_im[0]
            cross = d_im[j] * x_re[0] - d_re[j] * x_im[0]
            for i in range(1, blocks - j):
                rr = rr + d_re[i + j] * x_re[i]
                ii = ii + d_im[i + j] * x_im[i]
                cross = cross + (d_im[i + j] * x_re[i] - d_re[i + j] * x_im[i])
            g_re = jnp.where(keep, rr + ii, rr) * weight
            g_im = jnp.where(keep, cross, ii) * weight
            abc[j, 0, here, piece] = g_re if later_re is None else g_re + sign * later_re
            abc[j, 1, here, piece] = g_im if later_im is None else g_im + sign * later_im
            later_re, later_im = g_re, g_im

    row_chunks(size, cols, body)


def inverse_of(th, tl, values):
    high, low = split_high(values)
    return mm(th[...], high) + mm(tl[...], high) + mm(th[...], low)


def inverse_blocks(th, tl, source, target, blocks):
    def step(m, carry):
        target[m] = inverse_of(th, tl, source[m]).astype(target.dtype)
        return carry

    lax.fori_loop(0, blocks, step, 0)


def filter_gradient(th, tl, abc, out, blocks, size):
    def step(j, carry):
        re_high, re_low = split_high(abc[j, 0])
        im_high, im_low = split_high(abc[j, 1])
        left, right = th[:, :size], th[:, size:]
        total = mm(left, re_high) + mm(right, im_high) + mm(left, re_low) + mm(right, im_low)
        total = total + mm(tl[:, :size], re_high) + mm(tl[:, size:], im_high)
        out[j] = total
        return carry

    lax.fori_loop(0, blocks, step, 0)


def peers(count):
    me = lax.axis_index("ch")
    return me, [lax.rem(me + d, count) for d in range(1, count)], [lax.rem(me + count - d, count) for d in range(1, count)]


def greet(ids):
    barrier = pltpu.get_barrier_semaphore()
    for one in ids:
        pl.semaphore_signal(barrier, inc=1, device_id=one, device_id_type=MESH)
    pl.semaphore_wait(barrier, len(ids))


def to_channels(rows_ref, blocks_ref, send, recv, local, count, buckets, size, chans):
    me, ahead, behind = peers(count)
    copies = []
    for d in range(count - 1):
        for b in range(buckets):
            copy = pltpu.make_async_remote_copy(
                src_ref=rows_ref.at[pl.ds(b * size, size), pl.ds(pl.multiple_of(ahead[d] * chans, chans), chans)],
                dst_ref=blocks_ref.at[me, :, pl.ds(b * chans, chans)],
                send_sem=send.at[d, b],
                recv_sem=recv.at[d, b],
                device_id={"ch": ahead[d]},
                device_id_type=MESH,
            )
            copy.start()
            copies.append(copy)
    own = []
    for b in range(buckets):
        copy = pltpu.make_async_copy(
            rows_ref.at[pl.ds(b * size, size), pl.ds(pl.multiple_of(me * chans, chans), chans)],
            blocks_ref.at[me, :, pl.ds(b * chans, chans)],
            local.at[b],
        )
        copy.start()
        own.append(copy)
    return own + copies


def to_rows(blocks_ref, rows_ref, send, recv, local, count, buckets, size, chans):
    me, ahead, behind = peers(count)
    copies = []
    lane = pl.multiple_of(me * chans, chans)
    for d in range(count - 1):
        for b in range(buckets):
            copy = pltpu.make_async_remote_copy(
                src_ref=blocks_ref.at[ahead[d], :, pl.ds(b * chans, chans)],
                dst_ref=rows_ref.at[pl.ds(b * size, size), pl.ds(lane, chans)],
                send_sem=send.at[d, b],
                recv_sem=recv.at[d, b],
                device_id={"ch": ahead[d]},
                device_id_type=MESH,
            )
            copy.start()
            copies.append(copy)
    own = []
    for b in range(buckets):
        copy = pltpu.make_async_copy(
            blocks_ref.at[me, :, pl.ds(b * chans, chans)],
            rows_ref.at[pl.ds(b * size, size), pl.ds(lane, chans)],
            local.at[b],
        )
        copy.start()
        own.append(copy)
    return own + copies


def wait_all(copies):
    for copy in copies:
        copy.wait()


def conv_forward_kernel(dims, comm, rows_in, h_ref, fh, fl, th, tl, lanes, rows_out, blocks_out, xs, abc, ss, ys, *sems):
    blocks, size, buckets, chans = dims
    if comm:
        greet([{"ch": one} for one in peers(blocks)[1]])
        arriving = to_channels(rows_in, blocks_out, sems[0], sems[1], sems[2], blocks, buckets, size, chans)
        filter_spectra(fh, fl, lanes, h_ref, abc, blocks, size)
        wait_all(arriving)
    else:
        filter_spectra(fh, fl, lanes, h_ref, abc, blocks, size)
        blocks_out[...] = rows_in[...]
    spectra(fh, fl, blocks_out, xs, blocks)
    products_forward(xs, abc, ss, blocks, size)
    if comm:
        inverse_blocks(th, tl, ss, ys, blocks)
        wait_all(to_rows(ys, rows_out, sems[3], sems[4], sems[5], blocks, buckets, size, chans))
    else:
        inverse_blocks(th, tl, ss, rows_out, blocks)


def conv_backward_kernel(
    dims, comm, rows_in, x_ref, h_ref, fh, fl, th, tl, lanes, rows_out, dh_ref, xs, ds, abc, ss, ys, dblocks, *sems
):
    blocks, size, buckets, chans = dims
    if comm:
        greet([{"ch": one} for one in peers(blocks)[1]])
        arriving = to_channels(rows_in, dblocks, sems[0], sems[1], sems[2], blocks, buckets, size, chans)
        filter_spectra(fh, fl, lanes, h_ref, abc, blocks, size)
        spectra(fh, fl, x_ref, xs, blocks)
        wait_all(arriving)
        source = dblocks
    else:
        filter_spectra(fh, fl, lanes, h_ref, abc, blocks, size)
        spectra(fh, fl, x_ref, xs, blocks)
        source = rows_in
    spectra(fh, fl, source, ds, blocks)
    products_backward(xs, ds, abc, ss, lanes, blocks, size)
    if comm:
        inverse_blocks(th, tl, ss, ys, blocks)
        leaving = to_rows(ys, rows_out, sems[3], sems[4], sems[5], blocks, buckets, size, chans)
        filter_gradient(th, tl, abc, dh_ref, blocks, size)
        wait_all(leaving)
    else:
        inverse_blocks(th, tl, ss, rows_out, blocks)
        filter_gradient(th, tl, abc, dh_ref, blocks, size)


def exchange_sems(blocks, buckets):
    one = [pltpu.SemaphoreType.DMA((blocks - 1, buckets))] * 2 + [pltpu.SemaphoreType.DMA((buckets,))]
    return one + one


def conv_call(kernel, dims, comm, operands, out_shapes, scratch, collective_id):
    blocks, size, buckets, chans = dims
    vmem = pl.BlockSpec(memory_space=pltpu.VMEM)
    params = {"vmem_limit_bytes": VMEM_LIMIT}
    if comm:
        params["collective_id"] = collective_id
        params["has_side_effects"] = True
        scratch = scratch + exchange_sems(blocks, buckets)
    return pl.pallas_call(
        functools.partial(kernel, dims, comm),
        out_shape=out_shapes,
        in_specs=[vmem] * len(operands),
        out_specs=[vmem] * len(out_shapes),
        scratch_shapes=scratch,
        compiler_params=pltpu.CompilerParams(**params),
    )(*operands)


def rows_to_blocks(rows, dims):
    blocks, size, buckets, chans = dims
    moved = lax.all_to_all(rows.reshape(buckets, size, blocks, chans), "ch", split_axis=2, concat_axis=0)
    return jnp.transpose(moved, (0, 2, 1, 3)).reshape(blocks, size, buckets * chans)


def blocks_to_rows(values, dims):
    blocks, size, buckets, chans = dims
    moved = lax.all_to_all(values.reshape(blocks, size, buckets, chans), "ch", split_axis=0, concat_axis=0)
    return jnp.transpose(moved, (2, 1, 0, 3)).reshape(buckets * size, blocks * chans)


def conv_forward(rows, filt, tables, dims, comm):
    blocks, size, buckets, chans = dims
    cols = buckets * chans
    spectrum = pltpu.VMEM((blocks, 2 * size, cols), F32)
    scratch = [spectrum, pltpu.VMEM((blocks, 3, size, cols), F32), spectrum, pltpu.VMEM((blocks, size, cols), BF)]
    held = jax.ShapeDtypeStruct((blocks, size, cols), BF)
    shapes = [jax.ShapeDtypeStruct(rows.shape, BF) if comm else held, held]
    source = rows if comm else rows_to_blocks(rows, dims)
    out, kept = conv_call(conv_forward_kernel, dims, comm, (source, filt) + tables, shapes, scratch, 1)
    return (out if comm else blocks_to_rows(out, dims)), kept


def conv_backward(rows, kept, filt, tables, dims, comm):
    blocks, size, buckets, chans = dims
    cols = buckets * chans
    spectrum = pltpu.VMEM((blocks, 2 * size, cols), F32)
    half = pltpu.VMEM((blocks, size, cols), BF)
    scratch = [spectrum, spectrum, pltpu.VMEM((blocks, 3, size, cols), F32), spectrum, half, half]
    held = jax.ShapeDtypeStruct((blocks, size, cols), BF)
    shapes = [
        jax.ShapeDtypeStruct(rows.shape, BF) if comm else held,
        jax.ShapeDtypeStruct((blocks, size, cols), F32),
    ]
    source = rows if comm else rows_to_blocks(rows, dims)
    out, dfilt = conv_call(conv_backward_kernel, dims, comm, (source, kept, filt) + tables, shapes, scratch, 2)
    return (out if comm else blocks_to_rows(out, dims)), dfilt


def add_rows(target, other):
    return (target.astype(F32) + other.astype(F32)).astype(BF)


def scatter_kernel(count, *refs):
    grads = refs[:count]
    small_vec, small_sec, small_fst = refs[count : count + 3]
    outs = refs[count + 3 : 2 * count + 3]
    small_out = refs[2 * count + 3]
    rest = refs[2 * count + 4 :]
    own = rest[:count]
    acc = rest[count : 2 * count]
    one_a = rest[2 * count : 3 * count]
    one_b = rest[3 * count : 4 * count]
    two_a = rest[4 * count : 5 * count]
    two_b = rest[5 * count : 6 * count]
    three = rest[6 * count : 7 * count]
    gathered, joined, send, recv, local, small_send, small_recv = rest[7 * count :]

    ch = lax.axis_index("ch")
    seq = lax.axis_index("seq")
    z, x = ch // 2, lax.rem(ch, 2)
    y, core = seq // 2, lax.rem(seq, 2)
    sibling = {"seq": y * 2 + (1 - core)}
    along_y = {"seq": (1 - y) * 2 + core}
    along_x = {"ch": z * 2 + (1 - x)}
    others = [lax.rem(z + d, 4) for d in range(1, 4)]
    along_z = [{"ch": one * 2 + x} for one in others]
    ch_count, seq_count = 8, 4
    ch_ahead = [lax.rem(ch + d, ch_count) for d in range(1, ch_count)]
    seq_ahead = [lax.rem(seq + d, seq_count) for d in range(1, seq_count)]

    greet([{"ch": one} for one in ch_ahead] + [{"seq": one} for one in seq_ahead])

    def remote(src, dst, slot, array, device):
        copy = pltpu.make_async_remote_copy(
            src_ref=src,
            dst_ref=dst,
            send_sem=send.at[array, slot],
            recv_sem=recv.at[array, slot],
            device_id=device,
            device_id_type=MESH,
        )
        copy.start()
        return copy

    core_copies, own_copies = [], []
    for i in range(count):
        core_copies.append(remote(grads[i].at[:, :, :, 1 - core], acc[i], 0, i, sibling))
        copy = pltpu.make_async_copy(grads[i].at[:, :, :, core], own[i], local.at[i])
        copy.start()
        own_copies.append(copy)

    vec_rows = small_vec.shape[0]
    fst_rows = small_fst.shape[0]
    sec_rows = small_sec.shape[0]
    small_copies = []
    for d in range(ch_count - 1):
        lane = pl.multiple_of(ch_ahead[d] * 128, 128)
        pairs = (
            (small_vec.at[:, pl.ds(lane, 128)], gathered.at[ch, pl.ds(0, vec_rows)]),
            (small_fst, gathered.at[ch, pl.ds(vec_rows, fst_rows)]),
        )
        for s in range(2):
            copy = pltpu.make_async_remote_copy(
                src_ref=pairs[s][0],
                dst_ref=pairs[s][1],
                send_sem=small_send.at[2 * d + s],
                recv_sem=small_recv.at[2 * d + s],
                device_id={"ch": ch_ahead[d]},
                device_id_type=MESH,
            )
            copy.start()
            small_copies.append(copy)
    gathered[ch, :vec_rows] = small_vec[:, pl.ds(pl.multiple_of(ch * 128, 128), 128)]
    gathered[ch, vec_rows:] = small_fst[...]

    one_copies = [None] * count
    two_copies = [None] * count
    three_copies = [None] * count

    def stage_core(i):
        own_copies[i].wait()
        core_copies[i].wait()

        def step(n, carry):
            zz, xy = n // 4, lax.rem(n, 4)
            xx, yy = xy // 2, lax.rem(xy, 2)
            acc[i][zz, xx, yy] = add_rows(acc[i][zz, xx, yy], own[i][zz, xx, yy])
            return carry

        lax.fori_loop(0, 16, step, 0)
        half = acc[i].shape[3] // 2
        one_copies[i] = (
            remote(acc[i].at[:, :, 1 - y, pl.ds(0, half)], one_a[i], 1, i, along_y),
            remote(acc[i].at[:, 1 - x, :, pl.ds(half, half)], one_b[i], 2, i, along_x),
        )

    def stage_one(i):
        wait_all(one_copies[i])
        half = acc[i].shape[3] // 2

        def step(n, carry):
            zz, w = n // 2, lax.rem(n, 2)
            acc[i][zz, w, y, :half] = add_rows(acc[i][zz, w, y, :half], one_a[i][zz, w])
            acc[i][zz, x, w, half:] = add_rows(acc[i][zz, x, w, half:], one_b[i][zz, w])
            return carry

        lax.fori_loop(0, 8, step, 0)
        two_copies[i] = (
            remote(acc[i].at[:, 1 - x, y, pl.ds(0, half)], two_a[i], 3, i, along_x),
            remote(acc[i].at[:, x, 1 - y, pl.ds(half, half)], two_b[i], 4, i, along_y),
        )

    def stage_two(i):
        wait_all(two_copies[i])
        half = acc[i].shape[3] // 2

        def step(zz, carry):
            acc[i][zz, x, y, :half] = add_rows(acc[i][zz, x, y, :half], two_a[i][zz])
            acc[i][zz, x, y, half:] = add_rows(acc[i][zz, x, y, half:], two_b[i][zz])
            return carry

        lax.fori_loop(0, 4, step, 0)
        three_copies[i] = [
            remote(acc[i].at[others[d], x, y], three[i].at[d], 5 + d, i, along_z[d]) for d in range(3)
        ]

    def stage_three(i):
        wait_all(three_copies[i])
        total = acc[i][z, x, y].astype(F32)
        for d in range(3):
            total = total + three[i][d].astype(F32)
        outs[i][...] = total

    stages = (stage_core, stage_one, stage_two, stage_three)
    for time in range(count + 3):
        for s in range(4):
            if 0 <= time - s < count:
                stages[s](time - s)
        if time == 0:
            wait_all(small_copies)
            total = gathered[0]
            for n in range(1, ch_count):
                total = total + gathered[n]
            joined[seq, : vec_rows + fst_rows] = total
            joined[seq, vec_rows + fst_rows :] = small_sec[...]
            small_copies = []
            for d in range(seq_count - 1):
                copy = pltpu.make_async_remote_copy(
                    src_ref=joined.at[seq],
                    dst_ref=joined.at[seq],
                    send_sem=small_send.at[14 + d],
                    recv_sem=small_recv.at[14 + d],
                    device_id={"seq": seq_ahead[d]},
                    device_id_type=MESH,
                )
                copy.start()
                small_copies.append(copy)
    wait_all(small_copies)
    total = joined[0]
    for n in range(1, seq_count):
        total = total + joined[n]
    small_out[...] = total


def scatter_sums(grads, vec, sec, fst):
    count = len(grads)
    views = []
    outs = []
    bufs = [[] for _ in range(7)]
    for grad in grads:
        rows, cols = grad.shape[0] // 32, grad.shape[1]
        half = rows // 2
        views.append(grad.reshape(4, 2, 2, 2, rows, cols))
        outs.append(jax.ShapeDtypeStruct((rows, cols), F32))
        for place, shape in enumerate(
            (
                (4, 2, 2, rows, cols),
                (4, 2, 2, rows, cols),
                (4, 2, half, cols),
                (4, 2, half, cols),
                (4, half, cols),
                (4, half, cols),
                (3, rows, cols),
            )
        ):
            bufs[place].append(pltpu.VMEM(shape, BF))
    small = vec.shape[0] + fst.shape[0]
    scratch = [one for group in bufs for one in group]
    scratch += [
        pltpu.VMEM((8, small, 128), F32),
        pltpu.VMEM((4, small + sec.shape[0], 128), F32),
        pltpu.SemaphoreType.DMA((count, 8)),
        pltpu.SemaphoreType.DMA((count, 8)),
        pltpu.SemaphoreType.DMA((count,)),
        pltpu.SemaphoreType.DMA((17,)),
        pltpu.SemaphoreType.DMA((17,)),
    ]
    vmem = pl.BlockSpec(memory_space=pltpu.VMEM)
    outs.append(jax.ShapeDtypeStruct((small + sec.shape[0], 128), F32))
    return pl.pallas_call(
        functools.partial(scatter_kernel, count),
        out_shape=outs,
        in_specs=[pl.BlockSpec(memory_space=pl.ANY)] * count + [vmem] * 3,
        out_specs=[vmem] * (count + 1),
        scratch_shapes=scratch,
        compiler_params=pltpu.CompilerParams(
            collective_id=3, has_side_effects=True, vmem_limit_bytes=VMEM_LIMIT
        ),
    )(*views, vec, sec, fst)


def body(
    tokens,
    lengths,
    in_weight,
    out_weight,
    up_weight,
    down_weight,
    gain_one,
    gain_two,
    conv_taps,
    skip_gain,
    filter_first,
    filter_bias,
    frequency,
    filter_second,
    cotangent,
):
    ch_count = lax.axis_size("ch")
    seq_count = lax.axis_size("seq")
    ch_place = lax.axis_index("ch")
    seq_place = lax.axis_index("seq")
    size = tokens.shape[1]
    buckets = tokens.shape[2]
    width = tokens.shape[3]
    chans = skip_gain.shape[0]
    length = size * ch_count
    rows = size * buckets
    dims = (ch_count, size, buckets, chans)
    comm = chans % 128 == 0
    custom = comm and ch_count == 8 and seq_count == 4
    tables = tuple(jnp.asarray(one) for one in block_tables(size))

    def gather(shard):
        return lax.all_gather(shard, ("ch", "seq"), axis=0, tiled=True)

    full_in = gather(in_weight)
    full_gain_one = gather(gain_one).astype(F32)
    full_gain_two = gather(gain_two).astype(F32)
    full_out = gather(out_weight)
    full_up = gather(up_weight)
    full_down = gather(down_weight)

    local = ch_place * size + jnp.arange(size, dtype=jnp.int32)
    mask = (local[None, :] < lengths[0][:, None]).astype(F32).reshape(rows, 1)
    before = ch_place * size - 2 + jnp.arange(2, dtype=jnp.int32)
    mask_before = (before[None, :] < lengths[0][:, None]).astype(F32).reshape(2 * buckets, 1)
    chain = [(i, i + 1) for i in range(ch_count - 1)]
    halo = lax.ppermute(tokens[0, size - 2 :], "ch", chain)
    x_zero = jnp.swapaxes(tokens[0], 0, 1).reshape(rows, width).astype(F32) * mask
    x_before = jnp.swapaxes(halo, 0, 1).reshape(2 * buckets, width).astype(F32) * mask_before

    taps_full = lax.all_gather(conv_taps.reshape(9, chans), "ch", axis=1, tiled=True).reshape(3, 3, width)
    skip_full = lax.all_gather(skip_gain.reshape(1, chans), "ch", axis=1, tiled=True)

    table = positions_table(length, filter_first.shape[0])
    hidden = filter_hidden(filter_first, filter_bias, frequency, table)
    decay = decay_table(length, ch_place * chans, chans, width)
    filt = jnp.dot(hidden, filter_second, precision=HIGH) * decay
    filt_blocks = jnp.tile(filt.reshape(ch_count, size, chans), (1, 1, buckets))

    normed_one = layer_norm(x_zero, full_gain_one).astype(BF)
    normed_before = layer_norm(x_before, full_gain_one).astype(BF)
    streams = jnp.dot(normed_one, full_in, preferred_element_type=F32).astype(BF)
    streams_before = jnp.dot(normed_before, full_in, preferred_element_type=F32).astype(BF)
    lag = jnp.concatenate(
        [streams_before.reshape(buckets, 2, 3, width), streams.reshape(buckets, size, 3, width)], axis=1
    ).astype(F32)
    lag_zero, lag_one, lag_two = lag[:, 2:], lag[:, 1:-1], lag[:, :-2]
    conv = taps_full[0] * lag_zero + taps_full[1] * lag_one + taps_full[2] * lag_two
    gate = conv[:, :, 0].reshape(rows, width)
    key_part = conv[:, :, 1].reshape(rows, width)
    value_part = conv[:, :, 2].reshape(rows, width)
    mixed = key_part * value_part

    convolved, kept = conv_forward(mixed.astype(BF), filt_blocks, tables, dims, comm)
    long_part = convolved.astype(F32) + skip_full * mixed
    mixer = (gate * long_part * mask).astype(BF)
    after_mix = x_zero + jnp.dot(mixer, full_out, preferred_element_type=F32)
    normed_two = layer_norm(after_mix, full_gain_two).astype(BF)
    inner_act = jnp.dot(normed_two, full_up, preferred_element_type=F32)
    active = jax.nn.gelu(inner_act).astype(BF)
    result = (after_mix + jnp.dot(active, full_down, preferred_element_type=F32)).astype(BF)
    result = jnp.swapaxes(result.reshape(buckets, size, width), 0, 1).reshape(1, size, buckets, width)

    grad_result = jnp.swapaxes(cotangent[0], 0, 1).reshape(rows, width)
    grad_active = jnp.dot(grad_result, full_down.T, preferred_element_type=F32)
    _, gelu_pull = jax.vjp(jax.nn.gelu, inner_act)
    grad_inner = gelu_pull(grad_active)[0].astype(BF)
    kind = BF if custom else F32
    grad_down = jnp.dot(active.T, grad_result, preferred_element_type=F32).astype(kind)
    grad_up = jnp.dot(normed_two.T, grad_inner, preferred_element_type=F32).astype(kind)
    grad_normed_two = jnp.dot(grad_inner, full_up.T, preferred_element_type=F32)
    _, norm_two_pull = jax.vjp(layer_norm, after_mix, full_gain_two)
    grad_after_part, grad_gain_two = norm_two_pull(grad_normed_two)
    grad_after = grad_result.astype(F32) + grad_after_part
    grad_mix = grad_after.astype(BF)
    grad_out = jnp.dot(mixer.T, grad_mix, preferred_element_type=F32).astype(kind)
    grad_mixer = jnp.dot(grad_mix, full_out.T, preferred_element_type=F32).astype(BF)
    grad_masked = grad_mixer.astype(F32) * mask
    grad_gate = grad_masked * long_part
    grad_long = grad_masked * gate
    grad_skip = jnp.sum(grad_long * mixed, axis=0)
    grad_convolved, grad_filt = conv_backward(grad_long.astype(BF), kept, filt_blocks, tables, dims, comm)
    grad_mixed = grad_convolved.astype(F32) + skip_full * grad_long
    grad_conv = jnp.stack([grad_gate, grad_mixed * value_part, grad_mixed * key_part], axis=1)
    grad_conv = grad_conv.reshape(buckets, size, 3, width)
    grad_taps = jnp.stack(
        [
            jnp.sum(grad_conv * lag_zero, axis=(0, 1)),
            jnp.sum(grad_conv * lag_one, axis=(0, 1)),
            jnp.sum(grad_conv * lag_two, axis=(0, 1)),
        ],
        axis=0,
    )
    next_rows = lax.ppermute(grad_conv[:, :2], "ch", [(j, i) for i, j in chain])
    ahead = jnp.concatenate([grad_conv, next_rows], axis=1)
    grad_streams = taps_full[0] * ahead[:, :-2] + taps_full[1] * ahead[:, 1:-1] + taps_full[2] * ahead[:, 2:]
    grad_projected = grad_streams.astype(BF).reshape(rows, 3 * width)
    grad_in = jnp.dot(normed_one.T, grad_projected, preferred_element_type=F32).astype(kind)
    grad_normed_one = jnp.dot(grad_projected, full_in.T, preferred_element_type=F32)
    _, norm_one_pull = jax.vjp(layer_norm, x_zero, full_gain_one)
    grad_zero_part, grad_gain_one = norm_one_pull(grad_normed_one)
    grad_input = ((grad_after + grad_zero_part) * mask).astype(BF)
    grad_input = jnp.swapaxes(grad_input.reshape(buckets, size, width), 0, 1).reshape(1, size, buckets, width)

    grad_filt = jnp.sum(grad_filt.reshape(length, buckets, chans), axis=1)
    grad_raw = grad_filt * decay
    grad_second = jnp.dot(hidden.T, grad_raw, precision=HIGH)
    grad_hidden = jnp.dot(grad_raw, filter_second.T, precision=HIGH)

    def hidden_of(first_layer, first_shift, freq_values):
        return filter_hidden(first_layer, first_shift, freq_values, table)

    _, hidden_pull = jax.vjp(hidden_of, filter_first, filter_bias, frequency)
    grad_first, grad_bias, grad_freq = hidden_pull(grad_hidden)

    if custom:
        emb, filt_width = filter_first.shape
        vec = jnp.concatenate(
            [grad_taps.reshape(9, width), grad_skip[None], grad_gain_one[None], grad_gain_two[None], jnp.zeros((4, width), F32)]
        )
        fst = jnp.concatenate([grad_first, grad_bias[None], grad_freq[None]])
        fst = jnp.pad(fst, ((0, -fst.shape[0] % 8), (0, 128 - filt_width)))
        sum_down, sum_up, sum_in, sum_out, small = scatter_sums(
            (grad_down, grad_up, grad_in, grad_out), vec, grad_second, fst
        )
        sum_taps = small[:9].reshape(3, 3, chans)
        sum_skip = small[9]
        part = gain_one.shape[0]
        gains = lax.dynamic_slice_in_dim(small[10:12], seq_place * part, part, 1)
        sum_gain_one, sum_gain_two = gains[0], gains[1]
        sum_first = small[16 : 16 + emb, :filt_width]
        sum_bias = small[16 + emb, :filt_width]
        sum_freq = small[17 + emb, :filt_width]
        sum_second = small[16 + fst.shape[0] :]
    else:
        sum_in, sum_out, sum_up, sum_down, sum_gain_one, sum_gain_two = (
            lax.psum_scatter(one, ("ch", "seq"), scatter_dimension=0, tiled=True)
            for one in (grad_in, grad_out, grad_up, grad_down, grad_gain_one, grad_gain_two)
        )
        sum_second = lax.psum(grad_second, "seq")
        all_taps, all_skip, sum_first, sum_bias, sum_freq = lax.psum(
            (grad_taps, grad_skip, grad_first, grad_bias, grad_freq), ("ch", "seq")
        )
        sum_taps = lax.dynamic_slice_in_dim(all_taps, ch_place * chans, chans, 2)
        sum_skip = lax.dynamic_slice_in_dim(all_skip, ch_place * chans, chans, 0)
    return (
        result,
        grad_input,
        sum_in,
        sum_out,
        sum_up,
        sum_down,
        sum_gain_one,
        sum_gain_two,
        sum_taps,
        sum_skip,
        sum_first,
        sum_bias,
        sum_freq,
        sum_second,
    )


def solution(mesh):
    placed = (
        P("seq", "ch", None, None),
        P("seq", None),
        P(("ch", "seq"), None),
        P(("ch", "seq"), None),
        P(("ch", "seq"), None),
        P(("ch", "seq"), None),
        P(("ch", "seq")),
        P(("ch", "seq")),
        P(None, None, "ch"),
        P("ch"),
        P(),
        P(),
        P(),
        P(None, "ch"),
        P("seq", "ch", None, None),
    )
    return jax.shard_map(
        body,
        mesh=mesh,
        in_specs=placed,
        out_specs=(
            P("seq", "ch", None, None),
            P("seq", "ch", None, None),
            P(("ch", "seq"), None),
            P(("ch", "seq"), None),
            P(("ch", "seq"), None),
            P(("ch", "seq"), None),
            P(("ch", "seq")),
            P(("ch", "seq")),
            P(None, None, "ch"),
            P("ch"),
            P(),
            P(),
            P(),
            P(None, "ch"),
        ),
        check_vma=False,
    )
```

```python
import functools
import math

import jax
import jax.numpy as jnp
import numpy as np
from jax import lax
from jax.experimental import pallas as pl
from jax.experimental.pallas import tpu as pltpu
from jax.sharding import PartitionSpec as P

EPS = 1e-05
SLOW_RATE = math.log(100.0) / 1.5
FAST_RATE = math.log(100.0) / 0.3
HIGH = lax.Precision.HIGHEST
BF = jnp.bfloat16
F32 = jnp.float32
MESH = pl.DeviceIdType.MESH
VMEM_LIMIT = 56 << 20


def layer_norm(values, gain):
    centre = values - jnp.mean(values, axis=-1, keepdims=True)
    spread = jnp.mean(centre * centre, axis=-1, keepdims=True)
    return centre * lax.rsqrt(spread + EPS) * gain


def positions_table(length, features):
    steps = jnp.arange(length).astype(jnp.float32)
    scaled = steps / (length - 1)
    bands = (features - 1) // 2
    freqs = 0.0001 + (bands - 1 - 0.0001) * jnp.arange(bands).astype(jnp.float32) / (bands - 1)
    angles = freqs[None, :] * (2.0 * math.pi * steps / length)[:, None]
    return jnp.concatenate([scaled[:, None], jnp.cos(angles), -jnp.sin(angles)], axis=1)


def decay_table(length, chan_start, count, width):
    scaled = jnp.arange(length).astype(jnp.float32) / (length - 1)
    chans = (chan_start + jnp.arange(count)).astype(jnp.float32)
    rates = SLOW_RATE + (FAST_RATE - SLOW_RATE) * chans / (width - 1)
    return jnp.exp(-scaled[:, None] * rates[None, :])


def filter_hidden(filter_first, filter_bias, frequency, table):
    inner = jnp.dot(table, filter_first, precision=HIGH) + filter_bias
    return jnp.sin(frequency * inner)


def block_tables(size):
    k = np.arange(size)[:, None]
    t = np.arange(size)[None, :]
    angle = 2.0 * np.pi * ((k * t) % (2 * size)) / (2 * size)
    real = np.cos(angle)
    imag = -np.sin(angle)
    imag[0] = np.where(np.arange(size) % 2 == 0, 1.0, -1.0)
    full = np.concatenate([real, imag], axis=0).astype(np.float32)
    high = full.astype(jnp.bfloat16)
    low = (full - high.astype(np.float32)).astype(jnp.bfloat16)
    weight = np.full((size, 1), 1.0 / size, np.float32)
    weight[0] = 0.5 / size
    sign = np.where(np.arange(size) % 2 == 0, 1.0, -1.0).astype(np.float32)[:, None]
    lanes = np.zeros((size, 128), np.float32)
    lanes[:, 0:1] = weight
    lanes[:, 1:2] = sign
    lanes[:, 2] = 1.0
    lanes[0, 2] = 0.0
    return high, low, high.T.copy(), low.T.copy(), lanes


def split_high(values):
    high = values.astype(BF)
    return high, (values - high.astype(F32)).astype(BF)


def mm(a, b):
    return jnp.dot(a, b, preferred_element_type=F32)


def spectra(fh, fl, source, target, blocks, first=0):
    def step(i, carry):
        block = source[i]
        target[i] = mm(fh[...], block) + mm(fl[...], block)
        return carry

    lax.fori_loop(first, blocks, step, 0)


def filter_spectra(fh, fl, lanes, h_ref, abc, blocks, size):
    weight = lanes[:, 0:1]
    sign = lanes[:, 1:2]
    keep = lanes[:, 2:3]

    def step(j, carry):
        prev_re, prev_im = carry
        high, low = split_high(h_ref[j])
        now = mm(fh[...], high) + mm(fl[...], high) + mm(fh[...], low)
        now_re = now[:size]
        now_im = now[size:]
        g_re = (now_re + sign * prev_re) * weight
        g_im = (now_im + sign * prev_im) * weight
        abc[j, 0] = g_re
        abc[j, 1] = g_im * keep
        abc[j, 2] = jnp.where(keep > 0.5, g_re, g_im)
        return now_re, now_im

    zero = jnp.zeros((size, h_ref.shape[2]), F32)
    lax.fori_loop(0, blocks, step, (zero, zero))


def row_chunks(size, cols, body):
    width = min(128, cols)
    for lane in range(0, cols, width):

        def step(i, carry, lane=lane):
            body(pl.multiple_of(i * 8, 8), lane, width)
            return carry

        lax.fori_loop(0, size // 8, step, 0)


def products_forward(xs, abc, out, blocks, size):
    cols = xs.shape[2]

    def body(row, lane, width):
        re = [xs[i, pl.ds(row, 8), lane : lane + width] for i in range(blocks)]
        im = [xs[i, pl.ds(size + row, 8), lane : lane + width] for i in range(blocks)]
        a = [abc[j, 0, pl.ds(row, 8), lane : lane + width] for j in range(blocks)]
        b = [abc[j, 1, pl.ds(row, 8), lane : lane + width] for j in range(blocks)]
        c = [abc[j, 2, pl.ds(row, 8), lane : lane + width] for j in range(blocks)]
        for m in range(blocks):
            sum_re = re[0] * a[m] - im[0] * b[m]
            sum_im = re[0] * b[m] + im[0] * c[m]
            for i in range(1, m + 1):
                sum_re = sum_re + (re[i] * a[m - i] - im[i] * b[m - i])
                sum_im = sum_im + (re[i] * b[m - i] + im[i] * c[m - i])
            out[m, pl.ds(row, 8), lane : lane + width] = sum_re
            out[m, pl.ds(size + row, 8), lane : lane + width] = sum_im

    row_chunks(size, cols, body)


def products_backward(xs, ds, abc, out, lanes, blocks, size):
    cols = xs.shape[2]

    def body(row, lane, width):
        here = pl.ds(row, 8)
        there = pl.ds(size + row, 8)
        piece = slice(lane, lane + width)
        x_re = [xs[i, here, piece] for i in range(blocks)]
        x_im = [xs[i, there, piece] for i in range(blocks)]
        d_re = [ds[i, here, piece] for i in range(blocks)]
        d_im = [ds[i, there, piece] for i in range(blocks)]
        a = [abc[j, 0, here, piece] for j in range(blocks)]
        b = [abc[j, 1, here, piece] for j in range(blocks)]
        c = [abc[j, 2, here, piece] for j in range(blocks)]
        for i in range(blocks):
            sum_re = d_re[i] * a[0] + d_im[i] * b[0]
            sum_im = d_im[i] * c[0] - d_re[i] * b[0]
            for m in range(i + 1, blocks):
                sum_re = sum_re + (d_re[m] * a[m - i] + d_im[m] * b[m - i])
                sum_im = sum_im + (d_im[m] * c[m - i] - d_re[m] * b[m - i])
            out[i, here, piece] = sum_re
            out[i, there, piece] = sum_im
        weight = lanes[here, 0:1]
        sign = lanes[here, 1:2]
        keep = lanes[here, 2:3] > 0.5
        later_re = None
        later_im = None
        for j in range(blocks - 1, -1, -1):
            rr = d_re[j] * x_re[0]
            ii = d_im[j] * x_im[0]
            cross = d_im[j] * x_re[0] - d_re[j] * x_im[0]
            for i in range(1, blocks - j):
                rr = rr + d_re[i + j] * x_re[i]
                ii = ii + d_im[i + j] * x_im[i]
                cross = cross + (d_im[i + j] * x_re[i] - d_re[i + j] * x_im[i])
            g_re = jnp.where(keep, rr + ii, rr) * weight
            g_im = jnp.where(keep, cross, ii) * weight
            abc[j, 0, here, piece] = g_re if later_re is None else g_re + sign * later_re
            abc[j, 1, here, piece] = g_im if later_im is None else g_im + sign * later_im
            later_re, later_im = g_re, g_im

    row_chunks(size, cols, body)


def inverse_of(th, tl, values):
    high, low = split_high(values)
    return mm(th[...], high) + mm(tl[...], high) + mm(th[...], low)


def inverse_blocks(th, tl, source, target, blocks):
    def step(m, carry):
        target[m] = inverse_of(th, tl, source[m]).astype(target.dtype)
        return carry

    lax.fori_loop(0, blocks, step, 0)


def filter_gradient(th, tl, abc, out, blocks, size):
    def step(j, carry):
        re_high, re_low = split_high(abc[j, 0])
        im_high, im_low = split_high(abc[j, 1])
        left, right = th[:, :size], th[:, size:]
        total = mm(left, re_high) + mm(right, im_high) + mm(left, re_low) + mm(right, im_low)
        total = total + mm(tl[:, :size], re_high) + mm(tl[:, size:], im_high)
        out[j] = total
        return carry

    lax.fori_loop(0, blocks, step, 0)


def conv_forward_kernel(dims, x_ref, h_ref, fh, fl, th, tl, lanes, out, xs, abc):
    blocks, size, buckets, chans = dims
    filter_spectra(fh, fl, lanes, h_ref, abc, blocks, size)
    spectra(fh, fl, x_ref, xs, blocks)
    products_forward(xs, abc, xs, blocks, size)
    inverse_blocks(th, tl, xs, out, blocks)


def conv_backward_kernel(dims, d_ref, x_ref, h_ref, fh, fl, th, tl, lanes, out, dh_ref, xs, ds, abc):
    blocks, size, buckets, chans = dims
    filter_spectra(fh, fl, lanes, h_ref, abc, blocks, size)
    spectra(fh, fl, x_ref, xs, blocks)
    spectra(fh, fl, d_ref, ds, blocks)
    products_backward(xs, ds, abc, ds, lanes, blocks, size)
    inverse_blocks(th, tl, ds, out, blocks)
    filter_gradient(th, tl, abc, dh_ref, blocks, size)


VM = pl.BlockSpec(memory_space=pltpu.VMEM)
ANYWHERE = pl.BlockSpec(memory_space=pl.ANY)


def conv_call(kernel, dims, operands, kinds, spectra_count):
    blocks, size, buckets, chans = dims
    cols = buckets * chans
    scratch = [pltpu.VMEM((blocks, 2 * size, cols), F32)] * spectra_count
    return pl.pallas_call(
        functools.partial(kernel, dims),
        out_shape=[jax.ShapeDtypeStruct((blocks, size, cols), kind) for kind in kinds],
        in_specs=[VM] * len(operands),
        out_specs=[VM] * len(kinds),
        scratch_shapes=scratch + [pltpu.VMEM((blocks, 3, size, cols), F32)],
        compiler_params=pltpu.CompilerParams(vmem_limit_bytes=VMEM_LIMIT),
    )(*operands)


def rows_to_blocks(rows, dims):
    blocks, size, buckets, chans = dims
    moved = lax.all_to_all(rows.reshape(buckets, size, blocks, chans), "ch", split_axis=2, concat_axis=0)
    return jnp.transpose(moved, (0, 2, 1, 3)).reshape(blocks, size, buckets * chans)


def blocks_to_rows(values, dims):
    blocks, size, buckets, chans = dims
    moved = lax.all_to_all(values.reshape(blocks, size, buckets, chans), "ch", split_axis=0, concat_axis=0)
    return jnp.transpose(moved, (2, 1, 0, 3)).reshape(buckets * size, blocks * chans)


def conv_forward(rows, filt, tables, dims):
    kept = rows_to_blocks(rows, dims)
    (out,) = conv_call(conv_forward_kernel, dims, (kept, filt) + tables, (BF,), 1)
    return blocks_to_rows(out, dims), kept


def conv_backward(rows, kept, filt, tables, dims):
    moved = rows_to_blocks(rows, dims)
    out, dfilt = conv_call(conv_backward_kernel, dims, (moved, kept, filt) + tables, (BF, F32), 2)
    return blocks_to_rows(out, dims), dfilt


class Place:
    def __init__(self):
        self.ch = lax.axis_index("ch")
        self.seq = lax.axis_index("seq")
        self.z, self.x = self.ch // 2, lax.rem(self.ch, 2)
        self.y, self.core = self.seq // 2, lax.rem(self.seq, 2)
        self.sibling = {"seq": self.y * 2 + (1 - self.core)}
        self.along_y = {"seq": (1 - self.y) * 2 + self.core}
        self.along_x = {"ch": self.z * 2 + (1 - self.x)}
        self.others = [self.z + 1 - 2 * lax.rem(self.z, 2), lax.rem(self.z + 2, 4), 3 - self.z]
        self.along_z = [{"ch": one * 2 + self.x} for one in self.others]
        self.ch_ahead = [lax.rem(self.ch + d, 8) for d in range(1, 8)]
        self.seq_ahead = [lax.rem(self.seq + d, 4) for d in range(1, 4)]


def greet(ids):
    barrier = pltpu.get_barrier_semaphore()
    for one in ids:
        pl.semaphore_signal(barrier, inc=1, device_id=one, device_id_type=MESH)
    pl.semaphore_wait(barrier, len(ids))


def wait_all(copies):
    for copy in copies:
        copy.wait()


def push(src, dst, send, recv, device):
    copy = pltpu.make_async_remote_copy(
        src_ref=src, dst_ref=dst, send_sem=send, recv_sem=recv, device_id=device, device_id_type=MESH
    )
    copy.start()
    return copy


class Gather:
    SLOTS = 36

    def __init__(self, place, shards, fulls, send, recv, local):
        self.p, self.shards, self.fulls = place, shards, fulls
        self.send, self.recv, self.local = send, recv, local
        self.copies = {}

    def go(self, i, name, slot, src, dst, device):
        self.copies[(i, name)] = push(src, dst, self.send.at[i, slot], self.recv.at[i, slot], device)

    def start(self):
        p = self.p
        for i, shard in enumerate(self.shards):
            mine = self.fulls[i].at[p.z, p.x, p.y, p.core]
            for d in range(3):
                self.go(i, ("z", d), d, shard, mine, p.along_z[d])
            self.go(i, ("x", 0), 3, shard, mine, p.along_x)
            self.go(i, ("y", 0), 7, shard, mine, p.along_y)
            self.go(i, ("c", 0), 19, shard, mine, p.sibling)
            copy = pltpu.make_async_copy(shard, mine, self.local.at[i])
            copy.start()
            self.copies[(i, "own")] = copy

    def pass_column(self, d):
        p = self.p
        for i in range(len(self.shards)):
            self.copies[(i, ("z", d))].wait_recv()
            here = self.fulls[i].at[p.others[d], p.x, p.y, p.core]
            self.go(i, ("x", d + 1), 4 + d, here, here, p.along_x)
            self.go(i, ("y", d + 1), 8 + d, here, here, p.along_y)
            self.go(i, ("c", d + 1), 20 + d, here, here, p.sibling)

    def pass_sides(self, n):
        p = self.p
        zz = p.z if n == 0 else p.others[n - 1]
        for i in range(len(self.shards)):
            half = self.shards[i].shape[0] // 2
            full = self.fulls[i]
            self.copies[(i, ("x", n))].wait_recv()
            top = full.at[zz, 1 - p.x, p.y, p.core, pl.ds(0, half)]
            self.go(i, ("top", n), 11 + n, top, top, p.along_y)
            whole = full.at[zz, 1 - p.x, p.y, p.core]
            self.go(i, ("c", 4 + n), 23 + n, whole, whole, p.sibling)
            self.copies[(i, ("y", n))].wait_recv()
            low = full.at[zz, p.x, 1 - p.y, p.core, pl.ds(half, half)]
            self.go(i, ("low", n), 15 + n, low, low, p.along_x)
            whole = full.at[zz, p.x, 1 - p.y, p.core]
            self.go(i, ("c", 8 + n), 27 + n, whole, whole, p.sibling)

    def pass_last(self, n):
        p = self.p
        zz = p.z if n == 0 else p.others[n - 1]
        for i in range(len(self.shards)):
            self.copies[(i, ("top", n))].wait_recv()
            self.copies[(i, ("low", n))].wait_recv()
            whole = self.fulls[i].at[zz, 1 - p.x, 1 - p.y, p.core]
            self.go(i, ("c", 12 + n), 31 + n, whole, whole, p.sibling)

    def finish(self):
        for (i, name), copy in self.copies.items():
            if name == "own":
                copy.wait()
            else:
                copy.wait_send()
                if name[0] == "c":
                    copy.wait_recv()

    def rest(self):
        for d in range(3):
            self.pass_column(d)
            self.pass_sides(d)
        self.pass_sides(3)
        for n in range(4):
            self.pass_last(n)
        self.finish()

    @classmethod
    def scratch(cls, count):
        return [
            pltpu.SemaphoreType.DMA((count, cls.SLOTS)),
            pltpu.SemaphoreType.DMA((count, cls.SLOTS)),
            pltpu.SemaphoreType.DMA((count,)),
        ]


def everyone(p):
    ids = []
    for d in range(8):
        for e in range(4):
            if d or e:
                ids.append({"ch": lax.rem(p.ch + d, 8), "seq": lax.rem(p.seq + e, 4)})
    return ids


def start_kernel(pack, tail, shard, consts, halo, full, packs, send, recv, halo_sems, *gather_sems):
    p = Place()
    ids = everyone(p)
    greet(ids)
    copies = [push(pack, packs.at[p.ch, p.seq], send.at[n], recv.at[n], one) for n, one in enumerate(ids)]
    copies.append(push(tail, halo, halo_sems.at[0], halo_sems.at[1], {"ch": lax.rem(p.ch + 1, 8)}))
    gather = Gather(p, [shard], [full], *gather_sems)
    gather.start()
    packs[p.ch, p.seq] = pack[...]
    wait_all(copies)
    row = lax.broadcasted_iota(jnp.int32, (16, 128), 0)
    for c in range(8):
        first = packs[c, 0]
        total = first + packs[c, 1] + packs[c, 2] + packs[c, 3]
        consts[:, c * 128 : (c + 1) * 128] = jnp.where(row < 10, first, total)
    gather.rest()


def start_call(pack, tail, shard):
    rows, cols = shard.shape
    consts, halo, full = pl.pallas_call(
        start_kernel,
        out_shape=[
            jax.ShapeDtypeStruct((16, 1024), F32),
            jax.ShapeDtypeStruct(tail.shape, BF),
            jax.ShapeDtypeStruct((4, 2, 2, 2, rows, cols), BF),
        ],
        in_specs=[VM, VM, ANYWHERE],
        out_specs=[VM, VM, ANYWHERE],
        scratch_shapes=[
            pltpu.VMEM((8, 4, 16, 128), F32),
            pltpu.SemaphoreType.DMA((31,)),
            pltpu.SemaphoreType.DMA((31,)),
            pltpu.SemaphoreType.DMA((2,)),
        ]
        + Gather.scratch(1),
        compiler_params=pltpu.CompilerParams(collective_id=4, has_side_effects=True, vmem_limit_bytes=VMEM_LIMIT),
    )(pack, tail, shard)
    return consts, halo, full.reshape(rows * 32, cols)


def lagged(u, buf, b, stream, lane, size, width):
    at = pl.ds(pl.multiple_of(stream * width + lane, 128), 128)
    rows = size * 2
    buf[pl.ds(0, 16)] = u[pl.ds(rows + 16 * b, 16), at].astype(F32)
    buf[pl.ds(16, size)] = u[pl.ds(b * size, size), at].astype(F32)
    return buf[pl.ds(16, size)], buf[pl.ds(15, size)], buf[pl.ds(14, size)]


def short_conv(u, buf, consts, b, stream, lane, size, width):
    now, one, two = lagged(u, buf, b, stream, lane, size, width)
    at = pl.ds(lane, 128)
    return consts[stream : stream + 1, at] * now + consts[3 + stream : 4 + stream, at] * one + consts[
        6 + stream : 7 + stream, at
    ] * two


def send_pieces(p, pieces, blocks_ref, send, recv, local, make):
    copies = []
    for d in range(8):
        block = lax.rem(p.ch + d + 1, 8)
        make(block)
        for b in range(2):
            dst = blocks_ref.at[p.ch, :, pl.ds(b * 128, 128)]
            if d < 7:
                copies.append(push(pieces.at[block, b], dst, send.at[d, b], recv.at[d, b], {"ch": block}))
            else:
                copy = pltpu.make_async_copy(pieces.at[block, b], dst, local.at[b])
                copy.start()
                copies.append(copy)
    return copies


def send_blocks(p, ys, blocks_ref, send, recv, local):
    copies = []
    for d in range(7):
        copies.append(
            push(ys.at[p.ch_ahead[d]], blocks_ref.at[p.ch], send.at[d], recv.at[d], {"ch": p.ch_ahead[d]})
        )
    copy = pltpu.make_async_copy(ys.at[p.ch], blocks_ref.at[p.ch], local)
    copy.start()
    return copies + [copy]


def forward_kernel(
    size,
    u,
    consts,
    mask,
    h_ref,
    fh,
    fl,
    th,
    tl,
    lanes,
    mixer,
    kept,
    convolved,
    xs,
    abc,
    ys,
    pieces,
    gates,
    mixes,
    bufs,
    send,
    recv,
    local,
    send_back,
    recv_back,
    local_back,
):
    p = Place()
    width = 1024
    greet([{"ch": one} for one in p.ch_ahead])

    def make(block):
        lane = pl.multiple_of(block * 128, 128)

        def step(b, carry):
            gates[block, b] = short_conv(u, bufs.at[0], consts, b, 0, lane, size, width)
            key = short_conv(u, bufs.at[1], consts, b, 1, lane, size, width)
            mix = key * short_conv(u, bufs.at[2], consts, b, 2, lane, size, width)
            mixes[block, b] = mix
            pieces[block, b] = mix.astype(BF)
            return carry

        for b in range(2):
            step(b, 0)

    arriving = send_pieces(p, pieces, kept, send, recv, local, make)
    filter_spectra(fh, fl, lanes, h_ref, abc, 8, size)
    wait_all(arriving)
    spectra(fh, fl, kept, xs, 8)
    products_forward(xs, abc, xs, 8, size)
    inverse_blocks(th, tl, xs, ys, 8)
    wait_all(send_blocks(p, ys, convolved, send_back, recv_back, local_back))
    for c in range(8):
        at = slice(c * 128, (c + 1) * 128)
        for b in range(2):
            rows = slice(b * size, (b + 1) * size)
            long_part = convolved[c, :, b * 128 : (b + 1) * 128].astype(F32) + consts[9:10, at] * mixes[c, b]
            mixer[rows, at] = (gates[c, b] * long_part * mask[rows]).astype(BF)


def backward_kernel(
    size,
    u,
    consts,
    mask,
    grad_mixer,
    convolved,
    kept,
    h_ref,
    fh,
    fl,
    th,
    tl,
    lanes,
    du,
    dh_ref,
    sums,
    xs,
    ds,
    abc,
    ys,
    pieces,
    arrived,
    returned,
    keys,
    values,
    dlongs,
    dcs,
    edge_in,
    bufs,
    send,
    recv,
    local,
    send_back,
    recv_back,
    local_back,
    edge_sems,
):
    p = Place()
    width = 1024
    greet([{"ch": one} for one in p.ch_ahead])
    sums[...] = jnp.zeros_like(sums)

    def make(block):
        lane = pl.multiple_of(block * 128, 128)
        at = pl.ds(lane, 128)
        skip = consts[9:10, at]
        total = jnp.zeros((1, 128), F32)
        for b in range(2):
            rows = pl.ds(b * size, size)
            gate = short_conv(u, bufs.at[0], consts, b, 0, lane, size, width)
            key = short_conv(u, bufs.at[1], consts, b, 1, lane, size, width)
            value = short_conv(u, bufs.at[2], consts, b, 2, lane, size, width)
            keys[block, b] = key
            values[block, b] = value
            mix = key * value
            masked = grad_mixer[rows, at].astype(F32) * mask[rows]
            dlong = masked * gate
            dlongs[block, b] = dlong
            pieces[block, b] = dlong.astype(BF)
            total = total + jnp.sum(dlong * mix, axis=0, keepdims=True)
            long_part = convolved[block, :, b * 128 : (b + 1) * 128].astype(F32) + skip * mix
            dcs[0, b, pl.ds(0, size), at] = masked * long_part
        sums[9:10, at] = total

    arriving = send_pieces(p, pieces, arrived, send, recv, local, make)
    filter_spectra(fh, fl, lanes, h_ref, abc, 8, size)
    spectra(fh, fl, kept, xs, 8)
    wait_all(arriving)
    spectra(fh, fl, arrived, ds, 8)
    products_backward(xs, ds, abc, ds, lanes, 8, size)
    inverse_blocks(th, tl, ds, ys, 8)
    leaving = send_blocks(p, ys, returned, send_back, recv_back, local_back)
    filter_gradient(th, tl, abc, dh_ref, 8, size)
    wait_all(leaving)

    def products(c, carry):
        at = pl.ds(pl.multiple_of(c * 128, 128), 128)
        skip = consts[9:10, at]
        for b in range(2):
            dmixed = returned[c, :, b * 128 : (b + 1) * 128].astype(F32) + skip * dlongs[c, b]
            dcs[1, b, pl.ds(0, size), at] = dmixed * values[c, b]
            dcs[2, b, pl.ds(0, size), at] = dmixed * keys[c, b]
        return carry

    lax.fori_loop(0, 8, products, 0)
    edge = push(
        dcs.at[:, :, pl.ds(0, 8)], edge_in, edge_sems.at[0], edge_sems.at[1], {"ch": lax.rem(p.ch + 7, 8)}
    )

    def taps(c, carry):
        lane = pl.multiple_of(c * 128, 128)
        at = pl.ds(lane, 128)
        for stream in range(3):
            totals = [jnp.zeros((1, 128), F32)] * 3
            for b in range(2):
                parts = lagged(u, bufs.at[stream], b, stream, lane, size, width)
                grad = dcs[stream, b, pl.ds(0, size), at]
                for lag in range(3):
                    totals[lag] = totals[lag] + jnp.sum(grad * parts[lag], axis=0, keepdims=True)
            for lag in range(3):
                row = 3 * lag + stream
                sums[row : row + 1, at] = totals[lag]
        return carry

    lax.fori_loop(0, 8, taps, 0)
    edge.wait()
    inside = jnp.where(p.ch < 7, 1.0, 0.0)

    def streams(c, carry):
        lane = pl.multiple_of(c * 128, 128)
        at = pl.ds(lane, 128)
        for stream in range(3):
            out = pl.ds(pl.multiple_of(stream * width + lane, 128), 128)
            for b in range(2):
                dcs[stream, b, pl.ds(size, 8), at] = edge_in[stream, b, :, at] * inside
                total = consts[stream : stream + 1, at] * dcs[stream, b, pl.ds(0, size), at]
                total = total + consts[3 + stream : 4 + stream, at] * dcs[stream, b, pl.ds(1, size), at]
                total = total + consts[6 + stream : 7 + stream, at] * dcs[stream, b, pl.ds(2, size), at]
                du[pl.ds(b * size, size), out] = total.astype(BF)
        return carry

    lax.fori_loop(0, 8, streams, 0)


def exchange_sems():
    pieces = [pltpu.SemaphoreType.DMA((7, 2))] * 2 + [pltpu.SemaphoreType.DMA((2,))]
    return pieces + [pltpu.SemaphoreType.DMA((7,))] * 2 + [pltpu.SemaphoreType.DMA]


def forward_call(u, consts, mask, filt, tables, size):
    rows = 2 * size
    block = (8, size, 256)
    piece = (8, 2, size, 128)
    operands = (u, consts, mask, filt) + tables
    return pl.pallas_call(
        functools.partial(forward_kernel, size),
        out_shape=[jax.ShapeDtypeStruct((rows, 1024), BF)] + [jax.ShapeDtypeStruct(block, BF)] * 2,
        in_specs=[VM] * len(operands),
        out_specs=[VM] * 3,
        scratch_shapes=[
            pltpu.VMEM((8, 2 * size, 256), F32),
            pltpu.VMEM((8, 3, size, 256), F32),
            pltpu.VMEM(block, BF),
            pltpu.VMEM(piece, BF),
            pltpu.VMEM(piece, F32),
            pltpu.VMEM(piece, F32),
            pltpu.VMEM((3, size + 16, 128), F32),
        ]
        + exchange_sems(),
        compiler_params=pltpu.CompilerParams(collective_id=1, has_side_effects=True, vmem_limit_bytes=VMEM_LIMIT),
    )(*operands)


def backward_call(u, consts, mask, grad_mixer, convolved, kept, filt, tables, size):
    rows = 2 * size
    block = (8, size, 256)
    piece = (8, 2, size, 128)
    operands = (u, consts, mask, grad_mixer, convolved, kept, filt) + tables
    return pl.pallas_call(
        functools.partial(backward_kernel, size),
        out_shape=[
            jax.ShapeDtypeStruct((rows, 3072), BF),
            jax.ShapeDtypeStruct(block, F32),
            jax.ShapeDtypeStruct((16, 1024), F32),
        ],
        in_specs=[VM] * len(operands),
        out_specs=[VM] * 3,
        scratch_shapes=[
            pltpu.VMEM((8, 2 * size, 256), F32),
            pltpu.VMEM((8, 2 * size, 256), F32),
            pltpu.VMEM((8, 3, size, 256), F32),
            pltpu.VMEM(block, BF),
            pltpu.VMEM(piece, BF),
            pltpu.VMEM(block, BF),
            pltpu.VMEM(block, BF),
            pltpu.VMEM(piece, F32),
            pltpu.VMEM(piece, F32),
            pltpu.VMEM(piece, F32),
            pltpu.VMEM((3, 2, size + 8, 1024), F32),
            pltpu.VMEM((3, 2, 8, 1024), F32),
            pltpu.VMEM((3, size + 16, 128), F32),
        ]
        + exchange_sems()
        + [pltpu.SemaphoreType.DMA((2,))],
        compiler_params=pltpu.CompilerParams(collective_id=2, has_side_effects=True, vmem_limit_bytes=VMEM_LIMIT),
    )(*operands)


def add_rows(target, other):
    return (target.astype(F32) + other.astype(F32)).astype(BF)


def scatter_kernel(count, *refs):
    grads = refs[:count]
    small_vec, small_sec, small_fst = refs[count : count + 3]
    outs = refs[count + 3 : 2 * count + 3]
    small_out = refs[2 * count + 3]
    rest = refs[2 * count + 4 :]
    own = rest[:count]
    acc = rest[count : 2 * count]
    one_a = rest[2 * count : 3 * count]
    one_b = rest[3 * count : 4 * count]
    two_a = rest[4 * count : 5 * count]
    two_b = rest[5 * count : 6 * count]
    three = rest[6 * count : 7 * count]
    gathered, joined, send, recv, local, small_send, small_recv = rest[7 * count :]

    p = Place()
    ch, seq, z, x, y, core = p.ch, p.seq, p.z, p.x, p.y, p.core
    sibling, along_y, along_x, along_z, others = p.sibling, p.along_y, p.along_x, p.along_z, p.others
    ch_ahead, seq_ahead = p.ch_ahead, p.seq_ahead
    ch_count, seq_count = 8, 4
    greet([{"ch": one} for one in ch_ahead] + [{"seq": one} for one in seq_ahead])

    def remote(src, dst, slot, array, device):
        copy = pltpu.make_async_remote_copy(
            src_ref=src,
            dst_ref=dst,
            send_sem=send.at[array, slot],
            recv_sem=recv.at[array, slot],
            device_id=device,
            device_id_type=MESH,
        )
        copy.start()
        return copy

    core_copies, own_copies = [], []
    for i in range(count):
        core_copies.append(remote(grads[i].at[:, :, :, 1 - core], acc[i], 0, i, sibling))
        copy = pltpu.make_async_copy(grads[i].at[:, :, :, core], own[i], local.at[i])
        copy.start()
        own_copies.append(copy)

    vec_rows = small_vec.shape[0]
    fst_rows = small_fst.shape[0]
    sec_rows = small_sec.shape[0]
    small_copies = []
    for d in range(ch_count - 1):
        lane = pl.multiple_of(ch_ahead[d] * 128, 128)
        pairs = (
            (small_vec.at[:, pl.ds(lane, 128)], gathered.at[ch, pl.ds(0, vec_rows)]),
            (small_fst, gathered.at[ch, pl.ds(vec_rows, fst_rows)]),
        )
        for s in range(2):
            copy = pltpu.make_async_remote_copy(
                src_ref=pairs[s][0],
                dst_ref=pairs[s][1],
                send_sem=small_send.at[2 * d + s],
                recv_sem=small_recv.at[2 * d + s],
                device_id={"ch": ch_ahead[d]},
                device_id_type=MESH,
            )
            copy.start()
            small_copies.append(copy)
    gathered[ch, :vec_rows] = small_vec[:, pl.ds(pl.multiple_of(ch * 128, 128), 128)]
    gathered[ch, vec_rows:] = small_fst[...]

    one_copies = [None] * count
    two_copies = [None] * count
    three_copies = [None] * count

    def stage_core(i):
        own_copies[i].wait()
        core_copies[i].wait()

        def step(n, carry):
            zz, xy = n // 4, lax.rem(n, 4)
            xx, yy = xy // 2, lax.rem(xy, 2)
            acc[i][zz, xx, yy] = add_rows(acc[i][zz, xx, yy], own[i][zz, xx, yy])
            return carry

        lax.fori_loop(0, 16, step, 0)
        half = acc[i].shape[3] // 2
        one_copies[i] = (
            remote(acc[i].at[:, :, 1 - y, pl.ds(0, half)], one_a[i], 1, i, along_y),
            remote(acc[i].at[:, 1 - x, :, pl.ds(half, half)], one_b[i], 2, i, along_x),
        )

    def stage_one(i):
        wait_all(one_copies[i])
        half = acc[i].shape[3] // 2

        def step(n, carry):
            zz, w = n // 2, lax.rem(n, 2)
            acc[i][zz, w, y, :half] = add_rows(acc[i][zz, w, y, :half], one_a[i][zz, w])
            acc[i][zz, x, w, half:] = add_rows(acc[i][zz, x, w, half:], one_b[i][zz, w])
            return carry

        lax.fori_loop(0, 8, step, 0)
        two_copies[i] = (
            remote(acc[i].at[:, 1 - x, y, pl.ds(0, half)], two_a[i], 3, i, along_x),
            remote(acc[i].at[:, x, 1 - y, pl.ds(half, half)], two_b[i], 4, i, along_y),
        )

    def stage_two(i):
        wait_all(two_copies[i])
        half = acc[i].shape[3] // 2

        def step(zz, carry):
            acc[i][zz, x, y, :half] = add_rows(acc[i][zz, x, y, :half], two_a[i][zz])
            acc[i][zz, x, y, half:] = add_rows(acc[i][zz, x, y, half:], two_b[i][zz])
            return carry

        lax.fori_loop(0, 4, step, 0)
        three_copies[i] = [
            remote(acc[i].at[others[d], x, y], three[i].at[d], 5 + d, i, along_z[d]) for d in range(3)
        ]

    def stage_three(i):
        wait_all(three_copies[i])
        total = acc[i][z, x, y].astype(F32)
        for d in range(3):
            total = total + three[i][d].astype(F32)
        outs[i][...] = total

    stages = (stage_core, stage_one, stage_two, stage_three)
    for time in range(count + 3):
        for s in range(4):
            if 0 <= time - s < count:
                stages[s](time - s)
        if time == 0:
            wait_all(small_copies)
            total = gathered[0]
            for n in range(1, ch_count):
                total = total + gathered[n]
            joined[seq, : vec_rows + fst_rows] = total
            joined[seq, vec_rows + fst_rows :] = small_sec[...]
            small_copies = []
            for d in range(seq_count - 1):
                copy = pltpu.make_async_remote_copy(
                    src_ref=joined.at[seq],
                    dst_ref=joined.at[seq],
                    send_sem=small_send.at[14 + d],
                    recv_sem=small_recv.at[14 + d],
                    device_id={"seq": seq_ahead[d]},
                    device_id_type=MESH,
                )
                copy.start()
                small_copies.append(copy)
    wait_all(small_copies)
    total = joined[0]
    for n in range(1, seq_count):
        total = total + joined[n]
    small_out[...] = total


def scatter_sums(grads, vec, sec, fst):
    count = len(grads)
    views = []
    outs = []
    bufs = [[] for _ in range(7)]
    for grad in grads:
        rows, cols = grad.shape[0] // 32, grad.shape[1]
        half = rows // 2
        views.append(grad.reshape(4, 2, 2, 2, rows, cols))
        outs.append(jax.ShapeDtypeStruct((rows, cols), F32))
        for place, shape in enumerate(
            (
                (4, 2, 2, rows, cols),
                (4, 2, 2, rows, cols),
                (4, 2, half, cols),
                (4, 2, half, cols),
                (4, half, cols),
                (4, half, cols),
                (3, rows, cols),
            )
        ):
            bufs[place].append(pltpu.VMEM(shape, BF))
    small = vec.shape[0] + fst.shape[0]
    scratch = [one for group in bufs for one in group]
    scratch += [
        pltpu.VMEM((8, small, 128), F32),
        pltpu.VMEM((4, small + sec.shape[0], 128), F32),
        pltpu.SemaphoreType.DMA((count, 8)),
        pltpu.SemaphoreType.DMA((count, 8)),
        pltpu.SemaphoreType.DMA((count,)),
        pltpu.SemaphoreType.DMA((17,)),
        pltpu.SemaphoreType.DMA((17,)),
    ]
    outs.append(jax.ShapeDtypeStruct((small + sec.shape[0], 128), F32))
    return pl.pallas_call(
        functools.partial(scatter_kernel, count),
        out_shape=outs,
        in_specs=[ANYWHERE] * count + [VM] * 3,
        out_specs=[VM] * (count + 1),
        scratch_shapes=scratch,
        compiler_params=pltpu.CompilerParams(
            collective_id=3, has_side_effects=True, vmem_limit_bytes=VMEM_LIMIT
        ),
    )(*views, vec, sec, fst)


def general_body(
    tokens,
    lengths,
    in_weight,
    out_weight,
    up_weight,
    down_weight,
    gain_one,
    gain_two,
    conv_taps,
    skip_gain,
    filter_first,
    filter_bias,
    frequency,
    filter_second,
    cotangent,
):
    ch_count = lax.axis_size("ch")
    ch_place = lax.axis_index("ch")
    size = tokens.shape[1]
    buckets = tokens.shape[2]
    width = tokens.shape[3]
    chans = skip_gain.shape[0]
    length = size * ch_count
    rows = size * buckets
    dims = (ch_count, size, buckets, chans)
    tables = tuple(jnp.asarray(one) for one in block_tables(size))

    def gather(shard):
        return lax.all_gather(shard, ("ch", "seq"), axis=0, tiled=True)

    full_in = gather(in_weight)
    full_gain_one = gather(gain_one).astype(F32)
    full_gain_two = gather(gain_two).astype(F32)
    full_out = gather(out_weight)
    full_up = gather(up_weight)
    full_down = gather(down_weight)

    local = ch_place * size + jnp.arange(size, dtype=jnp.int32)
    mask = (local[None, :] < lengths[0][:, None]).astype(F32).reshape(rows, 1)
    before = ch_place * size - 2 + jnp.arange(2, dtype=jnp.int32)
    mask_before = (before[None, :] < lengths[0][:, None]).astype(F32).reshape(2 * buckets, 1)
    chain = [(i, i + 1) for i in range(ch_count - 1)]
    halo = lax.ppermute(tokens[0, size - 2 :], "ch", chain)
    x_zero = jnp.swapaxes(tokens[0], 0, 1).reshape(rows, width).astype(F32) * mask
    x_before = jnp.swapaxes(halo, 0, 1).reshape(2 * buckets, width).astype(F32) * mask_before

    taps_full = lax.all_gather(conv_taps.reshape(9, chans), "ch", axis=1, tiled=True).reshape(3, 3, width)
    skip_full = lax.all_gather(skip_gain.reshape(1, chans), "ch", axis=1, tiled=True)

    table = positions_table(length, filter_first.shape[0])
    hidden = filter_hidden(filter_first, filter_bias, frequency, table)
    decay = decay_table(length, ch_place * chans, chans, width)
    filt = jnp.dot(hidden, filter_second, precision=HIGH) * decay
    filt_blocks = jnp.tile(filt.reshape(ch_count, size, chans), (1, 1, buckets))

    normed_one = layer_norm(x_zero, full_gain_one).astype(BF)
    normed_before = layer_norm(x_before, full_gain_one).astype(BF)
    streams = jnp.dot(normed_one, full_in, preferred_element_type=F32).astype(BF)
    streams_before = jnp.dot(normed_before, full_in, preferred_element_type=F32).astype(BF)
    lag = jnp.concatenate(
        [streams_before.reshape(buckets, 2, 3, width), streams.reshape(buckets, size, 3, width)], axis=1
    ).astype(F32)
    lag_zero, lag_one, lag_two = lag[:, 2:], lag[:, 1:-1], lag[:, :-2]
    conv = taps_full[0] * lag_zero + taps_full[1] * lag_one + taps_full[2] * lag_two
    gate = conv[:, :, 0].reshape(rows, width)
    key_part = conv[:, :, 1].reshape(rows, width)
    value_part = conv[:, :, 2].reshape(rows, width)
    mixed = key_part * value_part

    convolved, kept = conv_forward(mixed.astype(BF), filt_blocks, tables, dims)
    long_part = convolved.astype(F32) + skip_full * mixed
    mixer = (gate * long_part * mask).astype(BF)
    after_mix = x_zero + jnp.dot(mixer, full_out, preferred_element_type=F32)
    normed_two = layer_norm(after_mix, full_gain_two).astype(BF)
    inner_act = jnp.dot(normed_two, full_up, preferred_element_type=F32)
    active = jax.nn.gelu(inner_act).astype(BF)
    result = (after_mix + jnp.dot(active, full_down, preferred_element_type=F32)).astype(BF)
    result = jnp.swapaxes(result.reshape(buckets, size, width), 0, 1).reshape(1, size, buckets, width)

    grad_result = jnp.swapaxes(cotangent[0], 0, 1).reshape(rows, width)
    grad_active = jnp.dot(grad_result, full_down.T, preferred_element_type=F32)
    _, gelu_pull = jax.vjp(jax.nn.gelu, inner_act)
    grad_inner = gelu_pull(grad_active)[0].astype(BF)
    grad_down = jnp.dot(active.T, grad_result, preferred_element_type=F32)
    grad_up = jnp.dot(normed_two.T, grad_inner, preferred_element_type=F32)
    grad_normed_two = jnp.dot(grad_inner, full_up.T, preferred_element_type=F32)
    _, norm_two_pull = jax.vjp(layer_norm, after_mix, full_gain_two)
    grad_after_part, grad_gain_two = norm_two_pull(grad_normed_two)
    grad_after = grad_result.astype(F32) + grad_after_part
    grad_mix = grad_after.astype(BF)
    grad_out = jnp.dot(mixer.T, grad_mix, preferred_element_type=F32)
    grad_mixer = jnp.dot(grad_mix, full_out.T, preferred_element_type=F32).astype(BF)
    grad_masked = grad_mixer.astype(F32) * mask
    grad_gate = grad_masked * long_part
    grad_long = grad_masked * gate
    grad_skip = jnp.sum(grad_long * mixed, axis=0)
    grad_convolved, grad_filt = conv_backward(grad_long.astype(BF), kept, filt_blocks, tables, dims)
    grad_mixed = grad_convolved.astype(F32) + skip_full * grad_long
    grad_conv = jnp.stack([grad_gate, grad_mixed * value_part, grad_mixed * key_part], axis=1)
    grad_conv = grad_conv.reshape(buckets, size, 3, width)
    grad_taps = jnp.stack(
        [
            jnp.sum(grad_conv * lag_zero, axis=(0, 1)),
            jnp.sum(grad_conv * lag_one, axis=(0, 1)),
            jnp.sum(grad_conv * lag_two, axis=(0, 1)),
        ],
        axis=0,
    )
    next_rows = lax.ppermute(grad_conv[:, :2], "ch", [(j, i) for i, j in chain])
    ahead = jnp.concatenate([grad_conv, next_rows], axis=1)
    grad_streams = taps_full[0] * ahead[:, :-2] + taps_full[1] * ahead[:, 1:-1] + taps_full[2] * ahead[:, 2:]
    grad_projected = grad_streams.astype(BF).reshape(rows, 3 * width)
    grad_in = jnp.dot(normed_one.T, grad_projected, preferred_element_type=F32)
    grad_normed_one = jnp.dot(grad_projected, full_in.T, preferred_element_type=F32)
    _, norm_one_pull = jax.vjp(layer_norm, x_zero, full_gain_one)
    grad_zero_part, grad_gain_one = norm_one_pull(grad_normed_one)
    grad_input = ((grad_after + grad_zero_part) * mask).astype(BF)
    grad_input = jnp.swapaxes(grad_input.reshape(buckets, size, width), 0, 1).reshape(1, size, buckets, width)

    grad_filt = jnp.sum(grad_filt.reshape(length, buckets, chans), axis=1)
    grad_raw = grad_filt * decay
    grad_second = jnp.dot(hidden.T, grad_raw, precision=HIGH)
    grad_hidden = jnp.dot(grad_raw, filter_second.T, precision=HIGH)

    def hidden_of(first_layer, first_shift, freq_values):
        return filter_hidden(first_layer, first_shift, freq_values, table)

    _, hidden_pull = jax.vjp(hidden_of, filter_first, filter_bias, frequency)
    grad_first, grad_bias, grad_freq = hidden_pull(grad_hidden)

    sum_in, sum_out, sum_up, sum_down, sum_gain_one, sum_gain_two = (
        lax.psum_scatter(one, ("ch", "seq"), scatter_dimension=0, tiled=True)
        for one in (grad_in, grad_out, grad_up, grad_down, grad_gain_one, grad_gain_two)
    )
    sum_second = lax.psum(grad_second, "seq")
    all_taps, all_skip, sum_first, sum_bias, sum_freq = lax.psum(
        (grad_taps, grad_skip, grad_first, grad_bias, grad_freq), ("ch", "seq")
    )
    sum_taps = lax.dynamic_slice_in_dim(all_taps, ch_place * chans, chans, 2)
    sum_skip = lax.dynamic_slice_in_dim(all_skip, ch_place * chans, chans, 0)
    return (
        result,
        grad_input,
        sum_in,
        sum_out,
        sum_up,
        sum_down,
        sum_gain_one,
        sum_gain_two,
        sum_taps,
        sum_skip,
        sum_first,
        sum_bias,
        sum_freq,
        sum_second,
    )


def slice_body(
    tokens,
    lengths,
    in_weight,
    out_weight,
    up_weight,
    down_weight,
    gain_one,
    gain_two,
    conv_taps,
    skip_gain,
    filter_first,
    filter_bias,
    frequency,
    filter_second,
    cotangent,
):
    ch_place = lax.axis_index("ch")
    seq_place = lax.axis_index("seq")
    size = tokens.shape[1]
    buckets = tokens.shape[2]
    width = tokens.shape[3]
    chans = skip_gain.shape[0]
    length = size * 8
    rows = size * buckets
    part = gain_one.shape[0]
    emb, filt_width = filter_first.shape
    tables = tuple(jnp.asarray(one) for one in block_tables(size))

    lane = jnp.arange(chans) // part == seq_place
    gains = jnp.stack([gain_one, gain_two]).astype(F32)
    gains = jnp.where(lane[None, :], jnp.tile(gains, (1, chans // part)), 0.0)
    pack = jnp.concatenate([conv_taps.reshape(9, chans), skip_gain[None], gains, jnp.zeros((4, chans), F32)])
    by_bucket = jnp.swapaxes(tokens[0], 0, 1)
    consts, halo, full_in = start_call(pack, by_bucket[:, size - 16 :], in_weight)

    def gather(shard):
        return lax.all_gather(shard, ("ch", "seq"), axis=0, tiled=True)

    full_out = gather(out_weight)
    full_up = gather(up_weight)
    full_down = gather(down_weight)
    full_gain_one = consts[10]
    full_gain_two = consts[11]

    local = ch_place * size + jnp.arange(size, dtype=jnp.int32)
    mask = (local[None, :] < lengths[0][:, None]).astype(F32).reshape(rows, 1)
    before = ch_place * size - 16 + jnp.arange(16, dtype=jnp.int32)
    inside = (before[None, :] < lengths[0][:, None]) & (before >= 0)[None, :]
    x_zero = by_bucket.reshape(rows, width).astype(F32) * mask
    x_before = halo.reshape(16 * buckets, width).astype(F32) * inside.astype(F32).reshape(16 * buckets, 1)
    normed_one = layer_norm(x_zero, full_gain_one).astype(BF)
    normed_before = layer_norm(x_before, full_gain_one).astype(BF)
    streams = jnp.dot(
        jnp.concatenate([normed_one, normed_before]), full_in, preferred_element_type=F32
    ).astype(BF)

    table = positions_table(length, emb)
    hidden = filter_hidden(filter_first, filter_bias, frequency, table)
    decay = decay_table(length, ch_place * chans, chans, width)
    filt = jnp.dot(hidden, filter_second, precision=HIGH) * decay
    filt_blocks = jnp.tile(filt.reshape(8, size, chans), (1, 1, buckets))

    wide_mask = jnp.broadcast_to(mask, (rows, 128))
    mixer, kept, convolved = forward_call(streams, consts, wide_mask, filt_blocks, tables, size)
    after_mix = x_zero + jnp.dot(mixer, full_out, preferred_element_type=F32)
    normed_two = layer_norm(after_mix, full_gain_two).astype(BF)
    inner_act = jnp.dot(normed_two, full_up, preferred_element_type=F32)
    active = jax.nn.gelu(inner_act).astype(BF)
    result = (after_mix + jnp.dot(active, full_down, preferred_element_type=F32)).astype(BF)
    result = jnp.swapaxes(result.reshape(buckets, size, width), 0, 1).reshape(1, size, buckets, width)

    grad_result = jnp.swapaxes(cotangent[0], 0, 1).reshape(rows, width)
    grad_active = jnp.dot(grad_result, full_down.T, preferred_element_type=F32)
    _, gelu_pull = jax.vjp(jax.nn.gelu, inner_act)
    grad_inner = gelu_pull(grad_active)[0].astype(BF)
    grad_down = jnp.dot(active.T, grad_result, preferred_element_type=F32).astype(BF)
    grad_up = jnp.dot(normed_two.T, grad_inner, preferred_element_type=F32).astype(BF)
    grad_normed_two = jnp.dot(grad_inner, full_up.T, preferred_element_type=F32)
    _, norm_two_pull = jax.vjp(layer_norm, after_mix, full_gain_two)
    grad_after_part, grad_gain_two = norm_two_pull(grad_normed_two)
    grad_after = grad_result.astype(F32) + grad_after_part
    grad_mix = grad_after.astype(BF)
    grad_out = jnp.dot(mixer.T, grad_mix, preferred_element_type=F32).astype(BF)
    grad_mixer = jnp.dot(grad_mix, full_out.T, preferred_element_type=F32).astype(BF)

    grad_projected, grad_filt, sums = backward_call(
        streams, consts, wide_mask, grad_mixer, convolved, kept, filt_blocks, tables, size
    )
    grad_in = jnp.dot(normed_one.T, grad_projected, preferred_element_type=F32).astype(BF)
    grad_normed_one = jnp.dot(grad_projected, full_in.T, preferred_element_type=F32)
    _, norm_one_pull = jax.vjp(layer_norm, x_zero, full_gain_one)
    grad_zero_part, grad_gain_one = norm_one_pull(grad_normed_one)
    grad_input = ((grad_after + grad_zero_part) * mask).astype(BF)
    grad_input = jnp.swapaxes(grad_input.reshape(buckets, size, width), 0, 1).reshape(1, size, buckets, width)

    grad_filt = grad_filt.reshape(length, buckets * chans)
    grad_raw = (grad_filt[:, :chans] + grad_filt[:, chans:]) * decay
    grad_second = jnp.dot(hidden.T, grad_raw, precision=HIGH)
    grad_hidden = jnp.dot(grad_raw, filter_second.T, precision=HIGH)

    def hidden_of(first_layer, first_shift, freq_values):
        return filter_hidden(first_layer, first_shift, freq_values, table)

    _, hidden_pull = jax.vjp(hidden_of, filter_first, filter_bias, frequency)
    grad_first, grad_bias, grad_freq = hidden_pull(grad_hidden)
    vec = jnp.concatenate([sums[:10], grad_gain_one[None], grad_gain_two[None], jnp.zeros((4, width), F32)])
    fst = jnp.concatenate([grad_first, grad_bias[None], grad_freq[None]])
    fst = jnp.pad(fst, ((0, -fst.shape[0] % 8), (0, 128 - filt_width)))
    sum_down, sum_up, sum_in, sum_out, small = scatter_sums((grad_down, grad_up, grad_in, grad_out), vec, grad_second, fst)
    gain_sums = lax.dynamic_slice_in_dim(small[10:12], seq_place * part, part, 1)
    return (
        result,
        grad_input,
        sum_in,
        sum_out,
        sum_up,
        sum_down,
        gain_sums[0],
        gain_sums[1],
        small[:9].reshape(3, 3, chans),
        small[9],
        small[16 : 16 + emb, :filt_width],
        small[16 + emb, :filt_width],
        small[17 + emb, :filt_width],
        small[16 + fst.shape[0] :],
    )


def solution(mesh):
    placed = (
        P("seq", "ch", None, None),
        P("seq", None),
        P(("ch", "seq"), None),
        P(("ch", "seq"), None),
        P(("ch", "seq"), None),
        P(("ch", "seq"), None),
        P(("ch", "seq")),
        P(("ch", "seq")),
        P(None, None, "ch"),
        P("ch"),
        P(),
        P(),
        P(),
        P(None, "ch"),
        P("seq", "ch", None, None),
    )
    custom = dict(mesh.shape) == {"ch": 8, "seq": 4}
    return jax.shard_map(
        slice_body if custom else general_body,
        mesh=mesh,
        in_specs=placed,
        out_specs=(
            P("seq", "ch", None, None),
            P("seq", "ch", None, None),
            P(("ch", "seq"), None),
            P(("ch", "seq"), None),
            P(("ch", "seq"), None),
            P(("ch", "seq"), None),
            P(("ch", "seq")),
            P(("ch", "seq")),
            P(None, None, "ch"),
            P("ch"),
            P(),
            P(),
            P(),
            P(None, "ch"),
        ),
        check_vma=False,
    )
```

```python
import functools
import math

import jax
import jax.numpy as jnp
import numpy as np
from jax import lax
from jax.experimental import pallas as pl
from jax.experimental.pallas import tpu as pltpu
from jax.sharding import PartitionSpec as P

EPS = 1e-05
SLOW_RATE = math.log(100.0) / 1.5
FAST_RATE = math.log(100.0) / 0.3
HIGH = lax.Precision.HIGHEST
BF = jnp.bfloat16
F32 = jnp.float32
MESH = pl.DeviceIdType.MESH
VMEM_LIMIT = 62 << 20


def layer_norm(values, gain):
    centre = values - jnp.mean(values, axis=-1, keepdims=True)
    spread = jnp.mean(centre * centre, axis=-1, keepdims=True)
    return centre * lax.rsqrt(spread + EPS) * gain


def positions_table(length, features):
    steps = jnp.arange(length).astype(jnp.float32)
    scaled = steps / (length - 1)
    bands = (features - 1) // 2
    freqs = 0.0001 + (bands - 1 - 0.0001) * jnp.arange(bands).astype(jnp.float32) / (bands - 1)
    angles = freqs[None, :] * (2.0 * math.pi * steps / length)[:, None]
    return jnp.concatenate([scaled[:, None], jnp.cos(angles), -jnp.sin(angles)], axis=1)


def decay_table(length, chan_start, count, width):
    scaled = jnp.arange(length).astype(jnp.float32) / (length - 1)
    chans = (chan_start + jnp.arange(count)).astype(jnp.float32)
    rates = SLOW_RATE + (FAST_RATE - SLOW_RATE) * chans / (width - 1)
    return jnp.exp(-scaled[:, None] * rates[None, :])


def filter_hidden(filter_first, filter_bias, frequency, table):
    inner = jnp.dot(table, filter_first, precision=HIGH) + filter_bias
    return jnp.sin(frequency * inner)


def block_tables(size):
    k = np.arange(size)[:, None]
    t = np.arange(size)[None, :]
    angle = 2.0 * np.pi * ((k * t) % (2 * size)) / (2 * size)
    real = np.cos(angle)
    imag = -np.sin(angle)
    imag[0] = np.where(np.arange(size) % 2 == 0, 1.0, -1.0)
    full = np.concatenate([real, imag], axis=0).astype(np.float32)
    high = full.astype(jnp.bfloat16)
    low = (full - high.astype(np.float32)).astype(jnp.bfloat16)
    weight = np.full((size, 1), 1.0 / size, np.float32)
    weight[0] = 0.5 / size
    sign = np.where(np.arange(size) % 2 == 0, 1.0, -1.0).astype(np.float32)[:, None]
    lanes = np.zeros((size, 128), np.float32)
    lanes[:, 0:1] = weight
    lanes[:, 1:2] = sign
    lanes[:, 2] = 1.0
    lanes[0, 2] = 0.0
    return high, low, high.T.copy(), low.T.copy(), lanes


def split_high(values):
    high = values.astype(BF)
    return high, (values - high.astype(F32)).astype(BF)


def mm(a, b):
    return jnp.dot(a, b, preferred_element_type=F32)


def spectra(fh, fl, source, target, blocks, first=0):
    def step(i, carry):
        block = source[i]
        target[i] = mm(fh[...], block) + mm(fl[...], block)
        return carry

    lax.fori_loop(first, blocks, step, 0)


def filter_spectra(fh, fl, lanes, h_ref, abc, blocks, size):
    weight = lanes[:, 0:1]
    sign = lanes[:, 1:2]

    def step(j, carry):
        prev_re, prev_im = carry
        high, low = split_high(h_ref[j])
        now = mm(fh[...], high) + mm(fl[...], high) + mm(fh[...], low)
        now_re = now[:size]
        now_im = now[size:]
        abc[j, 0] = (now_re + sign * prev_re) * weight
        abc[j, 1] = (now_im + sign * prev_im) * weight
        return now_re, now_im

    zero = jnp.zeros((size, h_ref.shape[2]), F32)
    lax.fori_loop(0, blocks, step, (zero, zero))


def row_chunks(size, body):
    def step(i, carry):
        body(pl.multiple_of(i * 8, 8))
        return carry

    lax.fori_loop(0, size // 8, step, 0)


def load_filter(abc, lanes, here, blocks):
    keep = lanes[here, 2:3]
    a = [abc[j, 0, here] for j in range(blocks)]
    raw = [abc[j, 1, here] for j in range(blocks)]
    b = [one * keep for one in raw]
    c = [jnp.where(keep > 0.5, one, two) for one, two in zip(a, raw)]
    return a, b, c


def products_forward(xs, abc, lanes, out, blocks, size):
    width = abc.shape[3]
    for lane in range(0, xs.shape[2], width):
        piece = slice(lane, lane + width)

        def body(row, piece=piece):
            here, there = pl.ds(row, 8), pl.ds(size + row, 8)
            re = [xs[i, here, piece] for i in range(blocks)]
            im = [xs[i, there, piece] for i in range(blocks)]
            a, b, c = load_filter(abc, lanes, here, blocks)
            for m in range(blocks):
                sum_re = re[0] * a[m] - im[0] * b[m]
                sum_im = re[0] * b[m] + im[0] * c[m]
                for i in range(1, m + 1):
                    sum_re = sum_re + (re[i] * a[m - i] - im[i] * b[m - i])
                    sum_im = sum_im + (re[i] * b[m - i] + im[i] * c[m - i])
                out[m, here, piece] = sum_re
                out[m, there, piece] = sum_im

        row_chunks(size, body)


def products_backward(xs, ds, abc, gh, lanes, blocks, size):
    width = abc.shape[3]
    count = xs.shape[2] // width
    for n in range(count):
        piece = slice(n * width, (n + 1) * width)

        def body(row, n=n, piece=piece):
            here, there = pl.ds(row, 8), pl.ds(size + row, 8)
            d_re = [ds[i, here, piece] for i in range(blocks)]
            d_im = [ds[i, there, piece] for i in range(blocks)]
            a, b, c = load_filter(abc, lanes, here, blocks)
            for i in range(blocks):
                sum_re = d_re[i] * a[0] + d_im[i] * b[0]
                sum_im = d_im[i] * c[0] - d_re[i] * b[0]
                for m in range(i + 1, blocks):
                    sum_re = sum_re + (d_re[m] * a[m - i] + d_im[m] * b[m - i])
                    sum_im = sum_im + (d_im[m] * c[m - i] - d_re[m] * b[m - i])
                ds[i, here, piece] = sum_re
                ds[i, there, piece] = sum_im
            x_re = [xs[i, here, piece] for i in range(blocks)]
            x_im = [xs[i, there, piece] for i in range(blocks)]
            weight = lanes[here, 0:1]
            sign = lanes[here, 1:2]
            keep = lanes[here, 2:3] > 0.5
            later_re = None
            later_im = None
            for j in range(blocks - 1, -1, -1):
                rr = d_re[j] * x_re[0]
                ii = d_im[j] * x_im[0]
                cross = d_im[j] * x_re[0] - d_re[j] * x_im[0]
                for i in range(1, blocks - j):
                    rr = rr + d_re[i + j] * x_re[i]
                    ii = ii + d_im[i + j] * x_im[i]
                    cross = cross + (d_im[i + j] * x_re[i] - d_re[i + j] * x_im[i])
                g_re = jnp.where(keep, rr + ii, rr) * weight
                g_im = jnp.where(keep, cross, ii) * weight
                if n:
                    g_re = g_re + gh[j, 0, here]
                    g_im = g_im + gh[j, 1, here]
                if n == count - 1 and later_re is not None:
                    gh[j, 0, here] = g_re + sign * later_re
                    gh[j, 1, here] = g_im + sign * later_im
                else:
                    gh[j, 0, here] = g_re
                    gh[j, 1, here] = g_im
                later_re, later_im = g_re, g_im

        row_chunks(size, body)


def inverse_of(th, tl, values):
    high, low = split_high(values)
    return mm(th[...], high) + mm(tl[...], high) + mm(th[...], low)


def inverse_blocks(th, tl, source, target, blocks):
    def step(m, carry):
        target[m] = inverse_of(th, tl, source[m]).astype(target.dtype)
        return carry

    lax.fori_loop(0, blocks, step, 0)


def filter_gradient(th, tl, gh, out, blocks, size):
    def step(j, carry):
        re_high, re_low = split_high(gh[j, 0])
        im_high, im_low = split_high(gh[j, 1])
        left, right = th[:, :size], th[:, size:]
        total = mm(left, re_high) + mm(right, im_high) + mm(left, re_low) + mm(right, im_low)
        total = total + mm(tl[:, :size], re_high) + mm(tl[:, size:], im_high)
        out[j] = total
        return carry

    lax.fori_loop(0, blocks, step, 0)


def conv_forward_kernel(dims, x_ref, h_ref, fh, fl, th, tl, lanes, out, xs, abc):
    blocks, size, buckets, chans = dims
    filter_spectra(fh, fl, lanes, h_ref, abc, blocks, size)
    spectra(fh, fl, x_ref, xs, blocks)
    products_forward(xs, abc, lanes, xs, blocks, size)
    inverse_blocks(th, tl, xs, out, blocks)


def conv_backward_kernel(dims, d_ref, x_ref, h_ref, fh, fl, th, tl, lanes, out, dh_ref, xs, ds, abc, gh):
    blocks, size, buckets, chans = dims
    filter_spectra(fh, fl, lanes, h_ref, abc, blocks, size)
    spectra(fh, fl, x_ref, xs, blocks)
    spectra(fh, fl, d_ref, ds, blocks)
    products_backward(xs, ds, abc, gh, lanes, blocks, size)
    inverse_blocks(th, tl, ds, out, blocks)
    filter_gradient(th, tl, gh, dh_ref, blocks, size)


VM = pl.BlockSpec(memory_space=pltpu.VMEM)
ANYWHERE = pl.BlockSpec(memory_space=pl.ANY)


def conv_call(kernel, dims, operands, kinds, spectra_count):
    blocks, size, buckets, chans = dims
    cols = buckets * chans
    scratch = [pltpu.VMEM((blocks, 2 * size, cols), F32)] * spectra_count
    return pl.pallas_call(
        functools.partial(kernel, dims),
        out_shape=[jax.ShapeDtypeStruct((blocks, size, cols), kind) for kind in kinds],
        in_specs=[VM] * len(operands),
        out_specs=[VM] * len(kinds),
        scratch_shapes=scratch + [pltpu.VMEM((blocks, 2, size, cols), F32)] * spectra_count,
        compiler_params=pltpu.CompilerParams(vmem_limit_bytes=VMEM_LIMIT),
    )(*operands)


def rows_to_blocks(rows, dims):
    blocks, size, buckets, chans = dims
    moved = lax.all_to_all(rows.reshape(buckets, size, blocks, chans), "ch", split_axis=2, concat_axis=0)
    return jnp.transpose(moved, (0, 2, 1, 3)).reshape(blocks, size, buckets * chans)


def blocks_to_rows(values, dims):
    blocks, size, buckets, chans = dims
    moved = lax.all_to_all(values.reshape(blocks, size, buckets, chans), "ch", split_axis=0, concat_axis=0)
    return jnp.transpose(moved, (2, 1, 0, 3)).reshape(buckets * size, blocks * chans)


def conv_forward(rows, filt, tables, dims):
    kept = rows_to_blocks(rows, dims)
    (out,) = conv_call(conv_forward_kernel, dims, (kept, filt) + tables, (BF,), 1)
    return blocks_to_rows(out, dims), kept


def conv_backward(rows, kept, filt, tables, dims):
    moved = rows_to_blocks(rows, dims)
    out, dfilt = conv_call(conv_backward_kernel, dims, (moved, kept, filt) + tables, (BF, F32), 2)
    return blocks_to_rows(out, dims), dfilt


class Place:
    def __init__(self):
        self.ch = lax.axis_index("ch")
        self.seq = lax.axis_index("seq")
        self.z, self.x = self.ch // 2, lax.rem(self.ch, 2)
        self.y, self.core = self.seq // 2, lax.rem(self.seq, 2)
        self.sibling = {"seq": self.y * 2 + (1 - self.core)}
        self.along_y = {"seq": (1 - self.y) * 2 + self.core}
        self.along_x = {"ch": self.z * 2 + (1 - self.x)}
        self.others = [self.z + 1 - 2 * lax.rem(self.z, 2), lax.rem(self.z + 2, 4), 3 - self.z]
        self.along_z = [{"ch": one * 2 + self.x} for one in self.others]
        self.ch_ahead = [lax.rem(self.ch + d, 8) for d in range(1, 8)]
        self.seq_ahead = [lax.rem(self.seq + d, 4) for d in range(1, 4)]


def greet(ids):
    barrier = pltpu.get_barrier_semaphore()
    for one in ids:
        pl.semaphore_signal(barrier, inc=1, device_id=one, device_id_type=MESH)
    pl.semaphore_wait(barrier, len(ids))


def wait_all(copies):
    for copy in copies:
        copy.wait()


def push(src, dst, send, recv, device):
    copy = pltpu.make_async_remote_copy(
        src_ref=src, dst_ref=dst, send_sem=send, recv_sem=recv, device_id=device, device_id_type=MESH
    )
    copy.start()
    return copy


class Gather:
    SLOTS = 36

    def __init__(self, place, shards, fulls, send, recv, local):
        self.p, self.shards, self.fulls = place, shards, fulls
        self.send, self.recv, self.local = send, recv, local
        self.copies = {}

    def go(self, i, name, slot, src, dst, device):
        self.copies[(i, name)] = push(src, dst, self.send.at[i, slot], self.recv.at[i, slot], device)

    def start(self):
        p = self.p
        for i, shard in enumerate(self.shards):
            mine = self.fulls[i].at[p.z, p.x, p.y, p.core]
            self.go(i, ("z", 1), 1, shard, mine, p.along_z[1])
            self.go(i, ("z", 0), 0, shard, mine, p.along_z[0])
            self.go(i, ("x", 0), 3, shard, mine, p.along_x)
            self.go(i, ("y", 0), 7, shard, mine, p.along_y)
            self.go(i, ("c", 0), 19, shard, mine, p.sibling)
            copy = pltpu.make_async_copy(shard, mine, self.local.at[i])
            copy.start()
            self.copies[(i, "own")] = copy

    def pass_column(self, d):
        p = self.p
        for i in range(len(self.shards)):
            self.copies[(i, ("z", d))].wait_recv()
            here = self.fulls[i].at[p.others[d], p.x, p.y, p.core]
            if d == 1:
                self.go(i, ("z", 2), 2, here, here, p.along_z[0])
            self.go(i, ("x", d + 1), 4 + d, here, here, p.along_x)
            self.go(i, ("y", d + 1), 8 + d, here, here, p.along_y)
            self.go(i, ("c", d + 1), 20 + d, here, here, p.sibling)

    def pass_sides(self, n):
        p = self.p
        zz = p.z if n == 0 else p.others[n - 1]
        for i in range(len(self.shards)):
            half = self.shards[i].shape[0] // 2
            full = self.fulls[i]
            self.copies[(i, ("x", n))].wait_recv()
            top = full.at[zz, 1 - p.x, p.y, p.core, pl.ds(0, half)]
            self.go(i, ("top", n), 11 + n, top, top, p.along_y)
            whole = full.at[zz, 1 - p.x, p.y, p.core]
            self.go(i, ("c", 4 + n), 23 + n, whole, whole, p.sibling)
            self.copies[(i, ("y", n))].wait_recv()
            low = full.at[zz, p.x, 1 - p.y, p.core, pl.ds(half, half)]
            self.go(i, ("low", n), 15 + n, low, low, p.along_x)
            whole = full.at[zz, p.x, 1 - p.y, p.core]
            self.go(i, ("c", 8 + n), 27 + n, whole, whole, p.sibling)

    def pass_last(self, n):
        p = self.p
        zz = p.z if n == 0 else p.others[n - 1]
        for i in range(len(self.shards)):
            self.copies[(i, ("top", n))].wait_recv()
            self.copies[(i, ("low", n))].wait_recv()
            whole = self.fulls[i].at[zz, 1 - p.x, 1 - p.y, p.core]
            self.go(i, ("c", 12 + n), 31 + n, whole, whole, p.sibling)

    def finish(self):
        for (i, name), copy in self.copies.items():
            if name == "own":
                copy.wait()
            else:
                copy.wait_send()
                if name[0] == "c":
                    copy.wait_recv()

    def steps(self):
        return (
            [functools.partial(self.pass_column, 0), functools.partial(self.pass_column, 1)]
            + [functools.partial(self.pass_sides, 0), functools.partial(self.pass_column, 2)]
            + [functools.partial(self.pass_sides, n) for n in (1, 2, 3)]
            + [functools.partial(self.pass_last, n) for n in range(4)]
        )

    def rest(self, first=0):
        for step in self.steps()[first:]:
            step()
        self.finish()

    @classmethod
    def scratch(cls, count):
        return [
            pltpu.SemaphoreType.DMA((count, cls.SLOTS)),
            pltpu.SemaphoreType.DMA((count, cls.SLOTS)),
            pltpu.SemaphoreType.DMA((count,)),
        ]


def everyone(p):
    ids = []
    for d in range(8):
        for e in range(4):
            if d or e:
                ids.append({"ch": lax.rem(p.ch + d, 8), "seq": lax.rem(p.seq + e, 4)})
    return ids


def start_kernel(pack, tail, shard, consts, halo, full, packs, send, recv, halo_sems, *gather_sems):
    p = Place()
    ids = everyone(p)
    greet(ids)
    copies = [push(pack, packs.at[p.ch, p.seq], send.at[n], recv.at[n], one) for n, one in enumerate(ids)]
    copies.append(push(tail, halo, halo_sems.at[0], halo_sems.at[1], {"ch": lax.rem(p.ch + 1, 8)}))
    gather = Gather(p, [shard], [full], *gather_sems)
    gather.start()
    packs[p.ch, p.seq] = pack[...]
    wait_all(copies)
    row = lax.broadcasted_iota(jnp.int32, (16, 128), 0)
    for c in range(8):
        first = packs[c, 0]
        total = first + packs[c, 1] + packs[c, 2] + packs[c, 3]
        consts[:, c * 128 : (c + 1) * 128] = jnp.where(row < 10, first, total)
    gather.rest()


def start_call(pack, tail, shard):
    rows, cols = shard.shape
    consts, halo, full = pl.pallas_call(
        start_kernel,
        out_shape=[
            jax.ShapeDtypeStruct((16, 1024), F32),
            jax.ShapeDtypeStruct(tail.shape, BF),
            jax.ShapeDtypeStruct((4, 2, 2, 2, rows, cols), BF),
        ],
        in_specs=[VM, VM, ANYWHERE],
        out_specs=[VM, VM, ANYWHERE],
        scratch_shapes=[
            pltpu.VMEM((8, 4, 16, 128), F32),
            pltpu.SemaphoreType.DMA((31,)),
            pltpu.SemaphoreType.DMA((31,)),
            pltpu.SemaphoreType.DMA((2,)),
        ]
        + Gather.scratch(1),
        compiler_params=pltpu.CompilerParams(collective_id=4, has_side_effects=True, vmem_limit_bytes=VMEM_LIMIT),
    )(pack, tail, shard)
    return consts, halo, full.reshape(rows * 32, cols)


def lagged(u, buf, b, stream, lane, size, width):
    at = pl.ds(pl.multiple_of(stream * width + lane, 128), 128)
    rows = size * 2
    buf[pl.ds(0, 16)] = u[pl.ds(rows + 16 * b, 16), at].astype(F32)
    buf[pl.ds(16, size)] = u[pl.ds(b * size, size), at].astype(F32)
    return buf[pl.ds(16, size)], buf[pl.ds(15, size)], buf[pl.ds(14, size)]


def short_conv(u, buf, consts, b, stream, lane, size, width):
    now, one, two = lagged(u, buf, b, stream, lane, size, width)
    at = pl.ds(lane, 128)
    return consts[stream : stream + 1, at] * now + consts[3 + stream : 4 + stream, at] * one + consts[
        6 + stream : 7 + stream, at
    ] * two


def send_pieces(p, pieces, blocks_ref, send, recv, local, make):
    copies = []

    def piece(block, b):
        if len(pieces.shape) == 4:
            return pieces.at[block, b]
        return pieces.at[block, :, pl.ds(b * 128, 128)]

    for d in range(8):
        block = lax.rem(p.ch + d + 1, 8)
        make(block)
        for b in range(2):
            dst = blocks_ref.at[p.ch, :, pl.ds(b * 128, 128)]
            if d < 7:
                copies.append(push(piece(block, b), dst, send.at[d, b], recv.at[d, b], {"ch": block}))
            else:
                copy = pltpu.make_async_copy(piece(block, b), dst, local.at[b])
                copy.start()
                copies.append(copy)
    return copies


def send_blocks(p, ys, blocks_ref, send, recv, local):
    copies = []
    for d in range(7):
        copies.append(
            push(ys.at[p.ch_ahead[d]], blocks_ref.at[p.ch], send.at[d], recv.at[d], {"ch": p.ch_ahead[d]})
        )
    copy = pltpu.make_async_copy(ys.at[p.ch], blocks_ref.at[p.ch], local)
    copy.start()
    return copies + [copy]


def forward_kernel(size, *refs):
    u, consts, mask, h_ref, fh, fl, th, tl, lanes = refs[:9]
    shards = refs[9:12]
    mixer, kept, convolved = refs[12:15]
    fulls = refs[15:18]
    xs, abc, ys, pieces, gates, mixes, bufs = refs[18:25]
    send, recv, local, send_back, recv_back, local_back = refs[25:31]
    p = Place()
    width = 1024
    greet([{"ch": one} for one in p.ch_ahead] + [p.sibling, p.along_y])
    gather = Gather(p, shards, fulls, *refs[31:])

    def make(block):
        lane = pl.multiple_of(block * 128, 128)

        def step(b, carry):
            gates[block, b] = short_conv(u, bufs.at[0], consts, b, 0, lane, size, width)
            key = short_conv(u, bufs.at[1], consts, b, 1, lane, size, width)
            mix = key * short_conv(u, bufs.at[2], consts, b, 2, lane, size, width)
            mixes[block, b] = mix
            pieces[block, b] = mix.astype(BF)
            return carry

        for b in range(2):
            step(b, 0)

    arriving = send_pieces(p, pieces, kept, send, recv, local, make)
    gather.start()
    steps = gather.steps()
    filter_spectra(fh, fl, lanes, h_ref, abc, 8, size)
    wait_all(arriving)
    spectra(fh, fl, kept, xs, 8)
    steps[0]()
    products_forward(xs, abc, lanes, xs, 8, size)
    inverse_blocks(th, tl, xs, ys, 8)
    leaving = send_blocks(p, ys, convolved, send_back, recv_back, local_back)
    for step in steps[1:4]:
        step()
    wait_all(leaving)
    for c in range(8):
        at = slice(c * 128, (c + 1) * 128)
        for b in range(2):
            rows = slice(b * size, (b + 1) * size)
            long_part = convolved[c, :, b * 128 : (b + 1) * 128].astype(F32) + consts[9:10, at] * mixes[c, b]
            mixer[rows, at] = (gates[c, b] * long_part * mask[rows]).astype(BF)
    gather.rest(4)


def backward_kernel(size, count, *refs):
    u, consts, mask, grad_mixer, convolved, kept, h_ref, fh, fl, th, tl, lanes = refs[:12]
    grads = refs[12 : 12 + count]
    du, dh_ref, sums = refs[12 + count : 15 + count]
    outs = refs[15 + count : 15 + 2 * count]
    rest = refs[15 + 2 * count :]
    xs, ds, abc, gh, pieces, arrived, returned, keys, values, dlongs, dcs, edge_out, edge_in, bufs = rest[:14]
    send, recv, local, send_back, recv_back, local_back, edge_sems = rest[14:21]
    p = Place()
    width = 1024
    greet([{"ch": one} for one in p.ch_ahead] + [p.sibling, p.along_y])
    scatter = Scatter(p, [(one, 0, one.shape[5]) for one in grads], outs, rest[21:])
    scatter.start()
    sums[...] = jnp.zeros_like(sums)

    def grad_parts(block, b, rows, skip):
        at = pl.ds(pl.multiple_of(block * 128, 128), 128)
        take = max(rows, 16)
        masked = grad_mixer[pl.ds(b * size, take), at].astype(F32)[:rows] * mask[pl.ds(b * size, rows)]
        conv = convolved[block, :take, b * 128 : (b + 1) * 128].astype(F32)[:rows]
        return masked, conv + skip * (keys[block, b, :rows] * values[block, b, :rows])

    def make(block):
        lane = pl.multiple_of(block * 128, 128)
        at = pl.ds(lane, 128)
        total = jnp.zeros((1, 128), F32)
        for b in range(2):
            rows = pl.ds(b * size, size)
            gate = short_conv(u, bufs.at[0], consts, b, 0, lane, size, width)
            key = short_conv(u, bufs.at[1], consts, b, 1, lane, size, width)
            value = short_conv(u, bufs.at[2], consts, b, 2, lane, size, width)
            keys[block, b] = key
            values[block, b] = value
            dlong = grad_mixer[rows, at].astype(F32) * mask[rows] * gate
            dlongs[block, b] = dlong
            pieces[block, :, b * 128 : (b + 1) * 128] = dlong.astype(BF)
            total = total + jnp.sum(dlong * (key * value), axis=0, keepdims=True)
        sums[9:10, at] = total

    arriving = send_pieces(p, pieces, arrived, send, recv, local, make)
    filter_spectra(fh, fl, lanes, h_ref, abc, 8, size)
    spectra(fh, fl, kept, xs, 8)
    for i in range(count):
        scatter.core(i)
    wait_all(arriving)
    spectra(fh, fl, arrived, ds, 8)
    products_backward(xs, ds, abc, gh, lanes, 8, size)
    inverse_blocks(th, tl, ds, pieces, 8)
    leaving = send_blocks(p, pieces, returned, send_back, recv_back, local_back)
    filter_gradient(th, tl, gh, dh_ref, 8, size)
    for i in range(count):
        scatter.first(i)
    wait_all(leaving)

    def edges(c, carry):
        at = pl.ds(pl.multiple_of(c * 128, 128), 128)
        skip = consts[9:10, at]
        for b in range(2):
            masked, long_part = grad_parts(c, b, 8, skip)
            back = returned[c, :16, b * 128 : (b + 1) * 128].astype(F32)[:8]
            dmixed = back + skip * dlongs[c, b, :8]
            edge_out[0, b, :, at] = masked * long_part
            edge_out[1, b, :, at] = dmixed * values[c, b, :8]
            edge_out[2, b, :, at] = dmixed * keys[c, b, :8]
        return carry

    lax.fori_loop(0, 8, edges, 0)
    edge = push(edge_out, edge_in, edge_sems.at[0], edge_sems.at[1], {"ch": lax.rem(p.ch + 7, 8)})
    for i in range(count):
        scatter.second(i)
    edge.wait()
    inside = jnp.where(p.ch < 7, 1.0, 0.0)

    def streams(c, carry):
        lane = pl.multiple_of(c * 128, 128)
        at = pl.ds(lane, 128)
        skip = consts[9:10, at]
        for b in range(2):
            masked, long_part = grad_parts(c, b, size, skip)
            dmixed = returned[c, :, b * 128 : (b + 1) * 128].astype(F32) + skip * dlongs[c, b]
            dcs[0, b, pl.ds(0, size)] = masked * long_part
            dcs[1, b, pl.ds(0, size)] = dmixed * values[c, b]
            dcs[2, b, pl.ds(0, size)] = dmixed * keys[c, b]
        for stream in range(3):
            out = pl.ds(pl.multiple_of(stream * width + lane, 128), 128)
            totals = [jnp.zeros((1, 128), F32)] * 3
            for b in range(2):
                dcs[stream, b, pl.ds(size, 8)] = edge_in[stream, b, :, at] * inside
                parts = lagged(u, bufs.at[stream], b, stream, lane, size, width)
                grad = dcs[stream, b, pl.ds(0, size)]
                for lag in range(3):
                    totals[lag] = totals[lag] + jnp.sum(grad * parts[lag], axis=0, keepdims=True)
                total = consts[stream : stream + 1, at] * grad
                total = total + consts[3 + stream : 4 + stream, at] * dcs[stream, b, pl.ds(1, size)]
                total = total + consts[6 + stream : 7 + stream, at] * dcs[stream, b, pl.ds(2, size)]
                du[pl.ds(b * size, size), out] = total.astype(BF)
            for lag in range(3):
                row = 3 * lag + stream
                sums[row : row + 1, at] = totals[lag]
        return carry

    lax.fori_loop(0, 8, streams, 0)
    for i in range(count):
        scatter.third(i)
    for i in range(count):
        scatter.last(i)


def exchange_sems():
    pieces = [pltpu.SemaphoreType.DMA((7, 2))] * 2 + [pltpu.SemaphoreType.DMA((2,))]
    return pieces + [pltpu.SemaphoreType.DMA((7,))] * 2 + [pltpu.SemaphoreType.DMA]


def forward_call(u, consts, mask, filt, tables, shards, size):
    rows = 2 * size
    block = (8, size, 256)
    piece = (8, 2, size, 128)
    operands = (u, consts, mask, filt) + tables
    count = len(shards)
    whole = [jax.ShapeDtypeStruct((4, 2, 2, 2) + one.shape, BF) for one in shards]
    out = pl.pallas_call(
        functools.partial(forward_kernel, size),
        out_shape=[jax.ShapeDtypeStruct((rows, 1024), BF)] + [jax.ShapeDtypeStruct(block, BF)] * 2 + whole,
        in_specs=[VM] * len(operands) + [ANYWHERE] * count,
        out_specs=[VM] * 3 + [ANYWHERE] * count,
        scratch_shapes=[
            pltpu.VMEM((8, 2 * size, 256), F32),
            pltpu.VMEM((8, 2, size, 128), F32),
            pltpu.VMEM(block, BF),
            pltpu.VMEM(piece, BF),
            pltpu.VMEM(piece, F32),
            pltpu.VMEM(piece, F32),
            pltpu.VMEM((3, size + 16, 128), F32),
        ]
        + exchange_sems()
        + Gather.scratch(count),
        compiler_params=pltpu.CompilerParams(collective_id=1, has_side_effects=True, vmem_limit_bytes=VMEM_LIMIT),
    )(*operands, *shards)
    return out[:3], [one.reshape(-1, one.shape[-1]) for one in out[3:]]


def backward_call(u, consts, mask, grad_mixer, convolved, kept, filt, tables, grads, size):
    rows = 2 * size
    block = (8, size, 256)
    piece = (8, 2, size, 128)
    operands = (u, consts, mask, grad_mixer, convolved, kept, filt) + tables
    count = len(grads)
    shapes = [(one.shape[0] // 32, one.shape[1]) for one in grads]
    views = [one.reshape((4, 2, 2, 2) + shape) for one, shape in zip(grads, shapes)]
    out = pl.pallas_call(
        functools.partial(backward_kernel, size, count),
        out_shape=[
            jax.ShapeDtypeStruct((rows, 3072), BF),
            jax.ShapeDtypeStruct((8, size, 128), F32),
            jax.ShapeDtypeStruct((16, 1024), F32),
        ]
        + [jax.ShapeDtypeStruct(shape, F32) for shape in shapes],
        in_specs=[VM] * len(operands) + [ANYWHERE] * count,
        out_specs=[VM] * (3 + count),
        scratch_shapes=[
            pltpu.VMEM((8, 2 * size, 256), F32),
            pltpu.VMEM((8, 2 * size, 256), F32),
            pltpu.VMEM((8, 2, size, 128), F32),
            pltpu.VMEM((8, 2, size, 128), F32),
            pltpu.VMEM(block, BF),
            pltpu.VMEM(block, BF),
            pltpu.VMEM(block, BF),
            pltpu.VMEM(piece, F32),
            pltpu.VMEM(piece, F32),
            pltpu.VMEM(piece, F32),
            pltpu.VMEM((3, 2, size + 8, 128), F32),
            pltpu.VMEM((3, 2, 8, 1024), F32),
            pltpu.VMEM((3, 2, 8, 1024), F32),
            pltpu.VMEM((3, size + 16, 128), F32),
        ]
        + exchange_sems()
        + [pltpu.SemaphoreType.DMA((2,))]
        + Scatter.scratch(shapes),
        compiler_params=pltpu.CompilerParams(collective_id=2, has_side_effects=True, vmem_limit_bytes=VMEM_LIMIT),
    )(*operands, *views)
    return out[:3], out[3:]


def add_rows(target, other):
    return (target.astype(F32) + other.astype(F32)).astype(BF)


class Scatter:
    SLOTS = 11

    def __init__(self, place, grads, outs, refs):
        count = len(grads)
        self.p, self.grads, self.outs = place, grads, outs
        names = ("own", "acc", "one_a", "one_b", "two_a", "two_b", "three", "four")
        for n, name in enumerate(names):
            setattr(self, name, refs[n * count : (n + 1) * count])
        self.send, self.recv, self.local = refs[8 * count : 8 * count + 3]
        self.copies = {}

    def go(self, i, slot, src, dst, device):
        copy = push(src, dst, self.send.at[i, slot], self.recv.at[i, slot], device)
        self.copies[(i, slot)] = copy

    def done(self, i, *slots):
        for slot in slots:
            self.copies[(i, slot)].wait()

    def part(self, i, zz, core):
        ref, first, cols = self.grads[i]
        if cols == ref.shape[5]:
            return ref.at[zz, :, :, core]
        return ref.at[zz, :, :, core, :, pl.ds(first, cols)]

    def load(self, i, zz):
        copy = pltpu.make_async_copy(self.part(i, zz, self.p.core), self.own[i].at[zz % 2], self.local.at[i, zz])
        copy.start()
        self.copies[(i, "own", zz)] = copy

    def start(self):
        for i in range(len(self.grads)):
            for zz in range(4):
                self.go(i, zz, self.part(i, zz, 1 - self.p.core), self.acc[i].at[zz], self.p.sibling)
            self.load(i, 0)
            self.load(i, 1)

    def core(self, i):
        p, acc, own = self.p, self.acc[i], self.own[i]
        for zz in range(4):
            self.copies[(i, "own", zz)].wait()
            self.done(i, zz)

            def step(n, carry, zz=zz):
                xx, yy = n // 2, lax.rem(n, 2)
                acc[zz, xx, yy] = add_rows(acc[zz, xx, yy], own[zz % 2, xx, yy])
                return carry

            lax.fori_loop(0, 4, step, 0)
            if zz < 2:
                self.load(i, zz + 2)
        half = acc.shape[3] // 2
        self.go(i, 4, acc.at[:, :, 1 - p.y, pl.ds(0, half)], self.one_a[i], p.along_y)
        self.go(i, 5, acc.at[:, 1 - p.x, :, pl.ds(half, half)], self.one_b[i], p.along_x)

    def first(self, i):
        p, acc = self.p, self.acc[i]
        half = acc.shape[3] // 2
        self.done(i, 4, 5)

        def step(n, carry):
            zz, w = n // 2, lax.rem(n, 2)
            acc[zz, w, p.y, :half] = add_rows(acc[zz, w, p.y, :half], self.one_a[i][zz, w])
            acc[zz, p.x, w, half:] = add_rows(acc[zz, p.x, w, half:], self.one_b[i][zz, w])
            return carry

        lax.fori_loop(0, 8, step, 0)
        self.go(i, 6, acc.at[:, 1 - p.x, p.y, pl.ds(0, half)], self.two_a[i], p.along_x)
        self.go(i, 7, acc.at[:, p.x, 1 - p.y, pl.ds(half, half)], self.two_b[i], p.along_y)

    def second(self, i):
        p, acc = self.p, self.acc[i]
        half = acc.shape[3] // 2
        self.done(i, 6, 7)

        def step(zz, carry):
            acc[zz, p.x, p.y, :half] = add_rows(acc[zz, p.x, p.y, :half], self.two_a[i][zz])
            acc[zz, p.x, p.y, half:] = add_rows(acc[zz, p.x, p.y, half:], self.two_b[i][zz])
            return carry

        lax.fori_loop(0, 4, step, 0)
        self.go(i, 8, acc.at[p.others[2], p.x, p.y], self.three[i].at[0], p.along_z[0])
        self.go(i, 9, acc.at[p.others[0], p.x, p.y], self.three[i].at[1], p.along_z[0])

    def third(self, i):
        p, acc = self.p, self.acc[i]
        far = p.others[1]
        self.done(i, 8, 9)
        acc[far, p.x, p.y] = add_rows(acc[far, p.x, p.y], self.three[i][0])
        self.go(i, 10, acc.at[far, p.x, p.y], self.four[i], p.along_z[1])

    def last(self, i):
        p, acc = self.p, self.acc[i]
        self.done(i, 10)
        total = acc[p.z, p.x, p.y].astype(F32) + self.three[i][1].astype(F32) + self.four[i][...].astype(F32)
        cols = self.grads[i][2]
        first = self.grads[i][1]
        self.outs[i][:, first : first + cols] = total

    @classmethod
    def scratch(cls, shapes):
        count = len(shapes)
        bufs = [[] for _ in range(8)]
        for rows, cols in shapes:
            half = rows // 2
            for place, shape in enumerate(
                (
                    (2, 2, 2, rows, cols),
                    (4, 2, 2, rows, cols),
                    (4, 2, half, cols),
                    (4, 2, half, cols),
                    (4, half, cols),
                    (4, half, cols),
                    (2, rows, cols),
                    (rows, cols),
                )
            ):
                bufs[place].append(pltpu.VMEM(shape, BF))
        return [one for group in bufs for one in group] + [
            pltpu.SemaphoreType.DMA((count, cls.SLOTS)),
            pltpu.SemaphoreType.DMA((count, cls.SLOTS)),
            pltpu.SemaphoreType.DMA((count, 4)),
        ]


PARTS = 3


def scatter_kernel(grad, small_vec, small_sec, small_fst, out, small_out, gathered, joined, small_send, small_recv, *refs):
    p = Place()
    greet([{"ch": one} for one in p.ch_ahead] + [{"seq": one} for one in p.seq_ahead])
    cols = grad.shape[5] // PARTS
    scatter = Scatter(p, [(grad, n * cols, cols) for n in range(PARTS)], [out] * PARTS, refs)
    scatter.start()

    vec_rows = small_vec.shape[0]
    fst_rows = small_fst.shape[0]
    small_copies = []
    for d in range(7):
        lane = pl.multiple_of(p.ch_ahead[d] * 128, 128)
        pairs = (
            (small_vec.at[:, pl.ds(lane, 128)], gathered.at[p.ch, pl.ds(0, vec_rows)]),
            (small_fst, gathered.at[p.ch, pl.ds(vec_rows, fst_rows)]),
        )
        for n, (src, dst) in enumerate(pairs):
            slot = 2 * d + n
            small_copies.append(push(src, dst, small_send.at[slot], small_recv.at[slot], {"ch": p.ch_ahead[d]}))
    gathered[p.ch, :vec_rows] = small_vec[:, pl.ds(pl.multiple_of(p.ch * 128, 128), 128)]
    gathered[p.ch, vec_rows:] = small_fst[...]

    stages = (scatter.core, scatter.first, scatter.second, scatter.third, scatter.last)
    for time in range(PARTS + len(stages) - 1):
        for n, stage in enumerate(stages):
            if 0 <= time - n < PARTS:
                stage(time - n)
        if time == 0:
            wait_all(small_copies)
            total = gathered[0]
            for n in range(1, 8):
                total = total + gathered[n]
            joined[p.seq, : vec_rows + fst_rows] = total
            joined[p.seq, vec_rows + fst_rows :] = small_sec[...]
            small_copies = [
                push(joined.at[p.seq], joined.at[p.seq], small_send.at[14 + d], small_recv.at[14 + d], {"seq": p.seq_ahead[d]})
                for d in range(3)
            ]
    wait_all(small_copies)
    total = joined[0]
    for n in range(1, 4):
        total = total + joined[n]
    small_out[...] = total


def scatter_sums(grad, vec, sec, fst):
    rows, cols = grad.shape[0] // 32, grad.shape[1]
    small = vec.shape[0] + fst.shape[0]
    return pl.pallas_call(
        scatter_kernel,
        out_shape=[
            jax.ShapeDtypeStruct((rows, cols), F32),
            jax.ShapeDtypeStruct((small + sec.shape[0], 128), F32),
        ],
        in_specs=[ANYWHERE] + [VM] * 3,
        out_specs=[VM] * 2,
        scratch_shapes=[
            pltpu.VMEM((8, small, 128), F32),
            pltpu.VMEM((4, small + sec.shape[0], 128), F32),
            pltpu.SemaphoreType.DMA((17,)),
            pltpu.SemaphoreType.DMA((17,)),
        ]
        + Scatter.scratch([(rows, cols // PARTS)] * PARTS),
        compiler_params=pltpu.CompilerParams(collective_id=3, has_side_effects=True, vmem_limit_bytes=VMEM_LIMIT),
    )(grad.reshape(4, 2, 2, 2, rows, cols), vec, sec, fst)


def general_body(
    tokens,
    lengths,
    in_weight,
    out_weight,
    up_weight,
    down_weight,
    gain_one,
    gain_two,
    conv_taps,
    skip_gain,
    filter_first,
    filter_bias,
    frequency,
    filter_second,
    cotangent,
):
    ch_count = lax.axis_size("ch")
    ch_place = lax.axis_index("ch")
    size = tokens.shape[1]
    buckets = tokens.shape[2]
    width = tokens.shape[3]
    chans = skip_gain.shape[0]
    length = size * ch_count
    rows = size * buckets
    dims = (ch_count, size, buckets, chans)
    tables = tuple(jnp.asarray(one) for one in block_tables(size))

    def gather(shard):
        return lax.all_gather(shard, ("ch", "seq"), axis=0, tiled=True)

    full_in = gather(in_weight)
    full_gain_one = gather(gain_one).astype(F32)
    full_gain_two = gather(gain_two).astype(F32)
    full_out = gather(out_weight)
    full_up = gather(up_weight)
    full_down = gather(down_weight)

    local = ch_place * size + jnp.arange(size, dtype=jnp.int32)
    mask = (local[None, :] < lengths[0][:, None]).astype(F32).reshape(rows, 1)
    before = ch_place * size - 2 + jnp.arange(2, dtype=jnp.int32)
    mask_before = (before[None, :] < lengths[0][:, None]).astype(F32).reshape(2 * buckets, 1)
    chain = [(i, i + 1) for i in range(ch_count - 1)]
    halo = lax.ppermute(tokens[0, size - 2 :], "ch", chain)
    x_zero = jnp.swapaxes(tokens[0], 0, 1).reshape(rows, width).astype(F32) * mask
    x_before = jnp.swapaxes(halo, 0, 1).reshape(2 * buckets, width).astype(F32) * mask_before

    taps_full = lax.all_gather(conv_taps.reshape(9, chans), "ch", axis=1, tiled=True).reshape(3, 3, width)
    skip_full = lax.all_gather(skip_gain.reshape(1, chans), "ch", axis=1, tiled=True)

    table = positions_table(length, filter_first.shape[0])
    hidden = filter_hidden(filter_first, filter_bias, frequency, table)
    decay = decay_table(length, ch_place * chans, chans, width)
    filt = jnp.dot(hidden, filter_second, precision=HIGH) * decay
    filt_blocks = jnp.tile(filt.reshape(ch_count, size, chans), (1, 1, buckets))

    normed_one = layer_norm(x_zero, full_gain_one).astype(BF)
    normed_before = layer_norm(x_before, full_gain_one).astype(BF)
    streams = jnp.dot(normed_one, full_in, preferred_element_type=F32).astype(BF)
    streams_before = jnp.dot(normed_before, full_in, preferred_element_type=F32).astype(BF)
    lag = jnp.concatenate(
        [streams_before.reshape(buckets, 2, 3, width), streams.reshape(buckets, size, 3, width)], axis=1
    ).astype(F32)
    lag_zero, lag_one, lag_two = lag[:, 2:], lag[:, 1:-1], lag[:, :-2]
    conv = taps_full[0] * lag_zero + taps_full[1] * lag_one + taps_full[2] * lag_two
    gate = conv[:, :, 0].reshape(rows, width)
    key_part = conv[:, :, 1].reshape(rows, width)
    value_part = conv[:, :, 2].reshape(rows, width)
    mixed = key_part * value_part

    convolved, kept = conv_forward(mixed.astype(BF), filt_blocks, tables, dims)
    long_part = convolved.astype(F32) + skip_full * mixed
    mixer = (gate * long_part * mask).astype(BF)
    after_mix = x_zero + jnp.dot(mixer, full_out, preferred_element_type=F32)
    normed_two = layer_norm(after_mix, full_gain_two).astype(BF)
    inner_act = jnp.dot(normed_two, full_up, preferred_element_type=F32)
    active = jax.nn.gelu(inner_act).astype(BF)
    result = (after_mix + jnp.dot(active, full_down, preferred_element_type=F32)).astype(BF)
    result = jnp.swapaxes(result.reshape(buckets, size, width), 0, 1).reshape(1, size, buckets, width)

    grad_result = jnp.swapaxes(cotangent[0], 0, 1).reshape(rows, width)
    grad_active = jnp.dot(grad_result, full_down.T, preferred_element_type=F32)
    _, gelu_pull = jax.vjp(jax.nn.gelu, inner_act)
    grad_inner = gelu_pull(grad_active)[0].astype(BF)
    grad_down = jnp.dot(active.T, grad_result, preferred_element_type=F32)
    grad_up = jnp.dot(normed_two.T, grad_inner, preferred_element_type=F32)
    grad_normed_two = jnp.dot(grad_inner, full_up.T, preferred_element_type=F32)
    _, norm_two_pull = jax.vjp(layer_norm, after_mix, full_gain_two)
    grad_after_part, grad_gain_two = norm_two_pull(grad_normed_two)
    grad_after = grad_result.astype(F32) + grad_after_part
    grad_mix = grad_after.astype(BF)
    grad_out = jnp.dot(mixer.T, grad_mix, preferred_element_type=F32)
    grad_mixer = jnp.dot(grad_mix, full_out.T, preferred_element_type=F32).astype(BF)
    grad_masked = grad_mixer.astype(F32) * mask
    grad_gate = grad_masked * long_part
    grad_long = grad_masked * gate
    grad_skip = jnp.sum(grad_long * mixed, axis=0)
    grad_convolved, grad_filt = conv_backward(grad_long.astype(BF), kept, filt_blocks, tables, dims)
    grad_mixed = grad_convolved.astype(F32) + skip_full * grad_long
    grad_conv = jnp.stack([grad_gate, grad_mixed * value_part, grad_mixed * key_part], axis=1)
    grad_conv = grad_conv.reshape(buckets, size, 3, width)
    grad_taps = jnp.stack(
        [
            jnp.sum(grad_conv * lag_zero, axis=(0, 1)),
            jnp.sum(grad_conv * lag_one, axis=(0, 1)),
            jnp.sum(grad_conv * lag_two, axis=(0, 1)),
        ],
        axis=0,
    )
    next_rows = lax.ppermute(grad_conv[:, :2], "ch", [(j, i) for i, j in chain])
    ahead = jnp.concatenate([grad_conv, next_rows], axis=1)
    grad_streams = taps_full[0] * ahead[:, :-2] + taps_full[1] * ahead[:, 1:-1] + taps_full[2] * ahead[:, 2:]
    grad_projected = grad_streams.astype(BF).reshape(rows, 3 * width)
    grad_in = jnp.dot(normed_one.T, grad_projected, preferred_element_type=F32)
    grad_normed_one = jnp.dot(grad_projected, full_in.T, preferred_element_type=F32)
    _, norm_one_pull = jax.vjp(layer_norm, x_zero, full_gain_one)
    grad_zero_part, grad_gain_one = norm_one_pull(grad_normed_one)
    grad_input = ((grad_after + grad_zero_part) * mask).astype(BF)
    grad_input = jnp.swapaxes(grad_input.reshape(buckets, size, width), 0, 1).reshape(1, size, buckets, width)

    grad_filt = jnp.sum(grad_filt.reshape(length, buckets, chans), axis=1)
    grad_raw = grad_filt * decay
    grad_second = jnp.dot(hidden.T, grad_raw, precision=HIGH)
    grad_hidden = jnp.dot(grad_raw, filter_second.T, precision=HIGH)

    def hidden_of(first_layer, first_shift, freq_values):
        return filter_hidden(first_layer, first_shift, freq_values, table)

    _, hidden_pull = jax.vjp(hidden_of, filter_first, filter_bias, frequency)
    grad_first, grad_bias, grad_freq = hidden_pull(grad_hidden)

    sum_in, sum_out, sum_up, sum_down, sum_gain_one, sum_gain_two = (
        lax.psum_scatter(one, ("ch", "seq"), scatter_dimension=0, tiled=True)
        for one in (grad_in, grad_out, grad_up, grad_down, grad_gain_one, grad_gain_two)
    )
    sum_second = lax.psum(grad_second, "seq")
    all_taps, all_skip, sum_first, sum_bias, sum_freq = lax.psum(
        (grad_taps, grad_skip, grad_first, grad_bias, grad_freq), ("ch", "seq")
    )
    sum_taps = lax.dynamic_slice_in_dim(all_taps, ch_place * chans, chans, 2)
    sum_skip = lax.dynamic_slice_in_dim(all_skip, ch_place * chans, chans, 0)
    return (
        result,
        grad_input,
        sum_in,
        sum_out,
        sum_up,
        sum_down,
        sum_gain_one,
        sum_gain_two,
        sum_taps,
        sum_skip,
        sum_first,
        sum_bias,
        sum_freq,
        sum_second,
    )


def slice_body(
    tokens,
    lengths,
    in_weight,
    out_weight,
    up_weight,
    down_weight,
    gain_one,
    gain_two,
    conv_taps,
    skip_gain,
    filter_first,
    filter_bias,
    frequency,
    filter_second,
    cotangent,
):
    ch_place = lax.axis_index("ch")
    seq_place = lax.axis_index("seq")
    size = tokens.shape[1]
    buckets = tokens.shape[2]
    width = tokens.shape[3]
    chans = skip_gain.shape[0]
    length = size * 8
    rows = size * buckets
    part = gain_one.shape[0]
    emb, filt_width = filter_first.shape
    tables = tuple(jnp.asarray(one) for one in block_tables(size))

    lane = jnp.arange(chans) // part == seq_place
    gains = jnp.stack([gain_one, gain_two]).astype(F32)
    gains = jnp.where(lane[None, :], jnp.tile(gains, (1, chans // part)), 0.0)
    pack = jnp.concatenate([conv_taps.reshape(9, chans), skip_gain[None], gains, jnp.zeros((4, chans), F32)])
    by_bucket = jnp.swapaxes(tokens[0], 0, 1)
    consts, halo, full_in = start_call(pack, by_bucket[:, size - 16 :], in_weight)

    full_gain_one = consts[10]
    full_gain_two = consts[11]

    local = ch_place * size + jnp.arange(size, dtype=jnp.int32)
    mask = (local[None, :] < lengths[0][:, None]).astype(F32).reshape(rows, 1)
    before = ch_place * size - 16 + jnp.arange(16, dtype=jnp.int32)
    inside = (before[None, :] < lengths[0][:, None]) & (before >= 0)[None, :]
    x_zero = by_bucket.reshape(rows, width).astype(F32) * mask
    x_before = halo.reshape(16 * buckets, width).astype(F32) * inside.astype(F32).reshape(16 * buckets, 1)
    normed_one = layer_norm(x_zero, full_gain_one).astype(BF)
    normed_before = layer_norm(x_before, full_gain_one).astype(BF)
    streams = jnp.dot(
        jnp.concatenate([normed_one, normed_before]), full_in, preferred_element_type=F32
    ).astype(BF)

    table = positions_table(length, emb)
    hidden = filter_hidden(filter_first, filter_bias, frequency, table)
    decay = decay_table(length, ch_place * chans, chans, width)
    filt = jnp.dot(hidden, filter_second, precision=HIGH) * decay
    filt_blocks = filt.reshape(8, size, chans)

    wide_mask = jnp.broadcast_to(mask, (rows, 128))
    (mixer, kept, convolved), (full_out, full_up, full_down) = forward_call(
        streams, consts, wide_mask, filt_blocks, tables, (out_weight, up_weight, down_weight), size
    )
    after_mix = x_zero + jnp.dot(mixer, full_out, preferred_element_type=F32)
    normed_two = layer_norm(after_mix, full_gain_two).astype(BF)
    inner_act = jnp.dot(normed_two, full_up, preferred_element_type=F32)
    active = jax.nn.gelu(inner_act).astype(BF)
    result = (after_mix + jnp.dot(active, full_down, preferred_element_type=F32)).astype(BF)
    result = jnp.swapaxes(result.reshape(buckets, size, width), 0, 1).reshape(1, size, buckets, width)

    grad_result = jnp.swapaxes(cotangent[0], 0, 1).reshape(rows, width)
    grad_active = jnp.dot(grad_result, full_down.T, preferred_element_type=F32)
    _, gelu_pull = jax.vjp(jax.nn.gelu, inner_act)
    grad_inner = gelu_pull(grad_active)[0].astype(BF)
    grad_down = jnp.dot(active.T, grad_result, preferred_element_type=F32).astype(BF)
    grad_up = jnp.dot(normed_two.T, grad_inner, preferred_element_type=F32).astype(BF)
    grad_normed_two = jnp.dot(grad_inner, full_up.T, preferred_element_type=F32)
    _, norm_two_pull = jax.vjp(layer_norm, after_mix, full_gain_two)
    grad_after_part, grad_gain_two = norm_two_pull(grad_normed_two)
    grad_after = grad_result.astype(F32) + grad_after_part
    grad_mix = grad_after.astype(BF)
    grad_out = jnp.dot(mixer.T, grad_mix, preferred_element_type=F32).astype(BF)
    grad_mixer = jnp.dot(grad_mix, full_out.T, preferred_element_type=F32).astype(BF)

    (grad_projected, grad_filt, sums), (sum_down, sum_up, sum_out) = backward_call(
        streams, consts, wide_mask, grad_mixer, convolved, kept, filt_blocks, tables, (grad_down, grad_up, grad_out), size
    )
    grad_in = jnp.dot(normed_one.T, grad_projected, preferred_element_type=F32).astype(BF)
    grad_normed_one = jnp.dot(grad_projected, full_in.T, preferred_element_type=F32)
    _, norm_one_pull = jax.vjp(layer_norm, x_zero, full_gain_one)
    grad_zero_part, grad_gain_one = norm_one_pull(grad_normed_one)
    grad_input = ((grad_after + grad_zero_part) * mask).astype(BF)
    grad_input = jnp.swapaxes(grad_input.reshape(buckets, size, width), 0, 1).reshape(1, size, buckets, width)

    grad_raw = grad_filt.reshape(length, chans) * decay
    grad_second = jnp.dot(hidden.T, grad_raw, precision=HIGH)
    grad_hidden = jnp.dot(grad_raw, filter_second.T, precision=HIGH)

    def hidden_of(first_layer, first_shift, freq_values):
        return filter_hidden(first_layer, first_shift, freq_values, table)

    _, hidden_pull = jax.vjp(hidden_of, filter_first, filter_bias, frequency)
    grad_first, grad_bias, grad_freq = hidden_pull(grad_hidden)
    vec = jnp.concatenate([sums[:10], grad_gain_one[None], grad_gain_two[None], jnp.zeros((4, width), F32)])
    fst = jnp.concatenate([grad_first, grad_bias[None], grad_freq[None]])
    fst = jnp.pad(fst, ((0, -fst.shape[0] % 8), (0, 128 - filt_width)))
    sum_in, small = scatter_sums(grad_in, vec, grad_second, fst)
    gain_sums = lax.dynamic_slice_in_dim(small[10:12], seq_place * part, part, 1)
    return (
        result,
        grad_input,
        sum_in,
        sum_out,
        sum_up,
        sum_down,
        gain_sums[0],
        gain_sums[1],
        small[:9].reshape(3, 3, chans),
        small[9],
        small[16 : 16 + emb, :filt_width],
        small[16 + emb, :filt_width],
        small[17 + emb, :filt_width],
        small[16 + fst.shape[0] :],
    )


def solution(mesh):
    placed = (
        P("seq", "ch", None, None),
        P("seq", None),
        P(("ch", "seq"), None),
        P(("ch", "seq"), None),
        P(("ch", "seq"), None),
        P(("ch", "seq"), None),
        P(("ch", "seq")),
        P(("ch", "seq")),
        P(None, None, "ch"),
        P("ch"),
        P(),
        P(),
        P(),
        P(None, "ch"),
        P("seq", "ch", None, None),
    )
    custom = dict(mesh.shape) == {"ch": 8, "seq": 4}
    return jax.shard_map(
        slice_body if custom else general_body,
        mesh=mesh,
        in_specs=placed,
        out_specs=(
            P("seq", "ch", None, None),
            P("seq", "ch", None, None),
            P(("ch", "seq"), None),
            P(("ch", "seq"), None),
            P(("ch", "seq"), None),
            P(("ch", "seq"), None),
            P(("ch", "seq")),
            P(("ch", "seq")),
            P(None, None, "ch"),
            P("ch"),
            P(),
            P(),
            P(),
            P(None, "ch"),
        ),
        check_vma=False,
    )
```

```python
import functools
import math

import jax
import jax.numpy as jnp
import numpy as np
from jax import lax
from jax.experimental import pallas as pl
from jax.experimental.pallas import tpu as pltpu
from jax.sharding import PartitionSpec as P

EPS = 1e-05
SLOW_RATE = math.log(100.0) / 1.5
FAST_RATE = math.log(100.0) / 0.3
HIGH = lax.Precision.HIGHEST
BF = jnp.bfloat16
F32 = jnp.float32
MESH = pl.DeviceIdType.MESH
VMEM_LIMIT = 62 << 20
SHARE = 0.72
EARLY, LATE = range(0, 2), range(2, 4)


def layer_norm(values, gain):
    centre = values - jnp.mean(values, axis=-1, keepdims=True)
    spread = jnp.mean(centre * centre, axis=-1, keepdims=True)
    return centre * lax.rsqrt(spread + EPS) * gain


def positions_table(length, features):
    steps = jnp.arange(length).astype(jnp.float32)
    scaled = steps / (length - 1)
    bands = (features - 1) // 2
    freqs = 0.0001 + (bands - 1 - 0.0001) * jnp.arange(bands).astype(jnp.float32) / (bands - 1)
    angles = freqs[None, :] * (2.0 * math.pi * steps / length)[:, None]
    return jnp.concatenate([scaled[:, None], jnp.cos(angles), -jnp.sin(angles)], axis=1)


def decay_table(length, chan_start, count, width):
    scaled = jnp.arange(length).astype(jnp.float32) / (length - 1)
    chans = (chan_start + jnp.arange(count)).astype(jnp.float32)
    rates = SLOW_RATE + (FAST_RATE - SLOW_RATE) * chans / (width - 1)
    return jnp.exp(-scaled[:, None] * rates[None, :])


def filter_hidden(filter_first, filter_bias, frequency, table):
    inner = jnp.dot(table, filter_first, precision=HIGH) + filter_bias
    return jnp.sin(frequency * inner)


def block_tables(size):
    k = np.arange(size)[:, None]
    t = np.arange(size)[None, :]
    angle = 2.0 * np.pi * ((k * t) % (2 * size)) / (2 * size)
    real = np.cos(angle)
    imag = -np.sin(angle)
    imag[0] = np.where(np.arange(size) % 2 == 0, 1.0, -1.0)
    full = np.concatenate([real, imag], axis=0).astype(np.float32)
    high = full.astype(jnp.bfloat16)
    low = (full - high.astype(np.float32)).astype(jnp.bfloat16)
    weight = np.full((size, 1), 1.0 / size, np.float32)
    weight[0] = 0.5 / size
    sign = np.where(np.arange(size) % 2 == 0, 1.0, -1.0).astype(np.float32)[:, None]
    lanes = np.zeros((size, 128), np.float32)
    lanes[:, 0:1] = weight
    lanes[:, 1:2] = sign
    lanes[:, 2] = 1.0
    lanes[0, 2] = 0.0
    return high, low, high.T.copy(), low.T.copy(), lanes


def split_high(values):
    high = values.astype(BF)
    return high, (values - high.astype(F32)).astype(BF)


def mm(a, b):
    return jnp.dot(a, b, preferred_element_type=F32)


def spectra(fh, fl, source, target, blocks, first=0):
    def step(i, carry):
        block = source[i]
        target[i] = mm(fh[...], block) + mm(fl[...], block)
        return carry

    lax.fori_loop(first, blocks, step, 0)


def filter_spectra(fh, fl, lanes, h_ref, abc, blocks, size):
    weight = lanes[:, 0:1]
    sign = lanes[:, 1:2]

    def step(j, carry):
        prev_re, prev_im = carry
        high, low = split_high(h_ref[j])
        now = mm(fh[...], high) + mm(fl[...], high) + mm(fh[...], low)
        now_re = now[:size]
        now_im = now[size:]
        abc[j, 0] = (now_re + sign * prev_re) * weight
        abc[j, 1] = (now_im + sign * prev_im) * weight
        return now_re, now_im

    zero = jnp.zeros((size, h_ref.shape[2]), F32)
    lax.fori_loop(0, blocks, step, (zero, zero))


def row_chunks(size, body):
    def step(i, carry):
        body(pl.multiple_of(i * 8, 8))
        return carry

    lax.fori_loop(0, size // 8, step, 0)


def load_filter(abc, lanes, here, blocks):
    keep = lanes[here, 2:3]
    a = [abc[j, 0, here] for j in range(blocks)]
    raw = [abc[j, 1, here] for j in range(blocks)]
    b = [one * keep for one in raw]
    c = [jnp.where(keep > 0.5, one, two) for one, two in zip(a, raw)]
    return a, b, c


def products_forward(xs, abc, lanes, out, blocks, size):
    width = abc.shape[3]
    for lane in range(0, xs.shape[2], width):
        piece = slice(lane, lane + width)

        def body(row, piece=piece):
            here, there = pl.ds(row, 8), pl.ds(size + row, 8)
            re = [xs[i, here, piece] for i in range(blocks)]
            im = [xs[i, there, piece] for i in range(blocks)]
            a, b, c = load_filter(abc, lanes, here, blocks)
            for m in range(blocks):
                sum_re = re[0] * a[m] - im[0] * b[m]
                sum_im = re[0] * b[m] + im[0] * c[m]
                for i in range(1, m + 1):
                    sum_re = sum_re + (re[i] * a[m - i] - im[i] * b[m - i])
                    sum_im = sum_im + (re[i] * b[m - i] + im[i] * c[m - i])
                out[m, here, piece] = sum_re
                out[m, there, piece] = sum_im

        row_chunks(size, body)


def products_backward(xs, ds, abc, gh, lanes, blocks, size):
    width = abc.shape[3]
    count = xs.shape[2] // width
    for n in range(count):
        piece = slice(n * width, (n + 1) * width)

        def body(row, n=n, piece=piece):
            here, there = pl.ds(row, 8), pl.ds(size + row, 8)
            d_re = [ds[i, here, piece] for i in range(blocks)]
            d_im = [ds[i, there, piece] for i in range(blocks)]
            a, b, c = load_filter(abc, lanes, here, blocks)
            for i in range(blocks):
                sum_re = d_re[i] * a[0] + d_im[i] * b[0]
                sum_im = d_im[i] * c[0] - d_re[i] * b[0]
                for m in range(i + 1, blocks):
                    sum_re = sum_re + (d_re[m] * a[m - i] + d_im[m] * b[m - i])
                    sum_im = sum_im + (d_im[m] * c[m - i] - d_re[m] * b[m - i])
                ds[i, here, piece] = sum_re
                ds[i, there, piece] = sum_im
            x_re = [xs[i, here, piece] for i in range(blocks)]
            x_im = [xs[i, there, piece] for i in range(blocks)]
            weight = lanes[here, 0:1]
            sign = lanes[here, 1:2]
            keep = lanes[here, 2:3] > 0.5
            later_re = None
            later_im = None
            for j in range(blocks - 1, -1, -1):
                rr = d_re[j] * x_re[0]
                ii = d_im[j] * x_im[0]
                cross = d_im[j] * x_re[0] - d_re[j] * x_im[0]
                for i in range(1, blocks - j):
                    rr = rr + d_re[i + j] * x_re[i]
                    ii = ii + d_im[i + j] * x_im[i]
                    cross = cross + (d_im[i + j] * x_re[i] - d_re[i + j] * x_im[i])
                g_re = jnp.where(keep, rr + ii, rr) * weight
                g_im = jnp.where(keep, cross, ii) * weight
                if n:
                    g_re = g_re + gh[j, 0, here]
                    g_im = g_im + gh[j, 1, here]
                if n == count - 1 and later_re is not None:
                    gh[j, 0, here] = g_re + sign * later_re
                    gh[j, 1, here] = g_im + sign * later_im
                else:
                    gh[j, 0, here] = g_re
                    gh[j, 1, here] = g_im
                later_re, later_im = g_re, g_im

        row_chunks(size, body)


def inverse_of(th, tl, values):
    high, low = split_high(values)
    return mm(th[...], high) + mm(tl[...], high) + mm(th[...], low)


def inverse_blocks(th, tl, source, target, blocks):
    def step(m, carry):
        target[m] = inverse_of(th, tl, source[m]).astype(target.dtype)
        return carry

    lax.fori_loop(0, blocks, step, 0)


def filter_gradient(th, tl, gh, out, blocks, size):
    def step(j, carry):
        re_high, re_low = split_high(gh[j, 0])
        im_high, im_low = split_high(gh[j, 1])
        left, right = th[:, :size], th[:, size:]
        total = mm(left, re_high) + mm(right, im_high) + mm(left, re_low) + mm(right, im_low)
        total = total + mm(tl[:, :size], re_high) + mm(tl[:, size:], im_high)
        out[j] = total
        return carry

    lax.fori_loop(0, blocks, step, 0)


def conv_forward_kernel(dims, x_ref, h_ref, fh, fl, th, tl, lanes, out, xs, abc):
    blocks, size, buckets, chans = dims
    filter_spectra(fh, fl, lanes, h_ref, abc, blocks, size)
    spectra(fh, fl, x_ref, xs, blocks)
    products_forward(xs, abc, lanes, xs, blocks, size)
    inverse_blocks(th, tl, xs, out, blocks)


def conv_backward_kernel(dims, d_ref, x_ref, h_ref, fh, fl, th, tl, lanes, out, dh_ref, xs, ds, abc, gh):
    blocks, size, buckets, chans = dims
    filter_spectra(fh, fl, lanes, h_ref, abc, blocks, size)
    spectra(fh, fl, x_ref, xs, blocks)
    spectra(fh, fl, d_ref, ds, blocks)
    products_backward(xs, ds, abc, gh, lanes, blocks, size)
    inverse_blocks(th, tl, ds, out, blocks)
    filter_gradient(th, tl, gh, dh_ref, blocks, size)


VM = pl.BlockSpec(memory_space=pltpu.VMEM)
ANYWHERE = pl.BlockSpec(memory_space=pl.ANY)


def conv_call(kernel, dims, operands, kinds, spectra_count):
    blocks, size, buckets, chans = dims
    cols = buckets * chans
    scratch = [pltpu.VMEM((blocks, 2 * size, cols), F32)] * spectra_count
    return pl.pallas_call(
        functools.partial(kernel, dims),
        out_shape=[jax.ShapeDtypeStruct((blocks, size, cols), kind) for kind in kinds],
        in_specs=[VM] * len(operands),
        out_specs=[VM] * len(kinds),
        scratch_shapes=scratch + [pltpu.VMEM((blocks, 2, size, cols), F32)] * spectra_count,
        compiler_params=pltpu.CompilerParams(vmem_limit_bytes=VMEM_LIMIT),
    )(*operands)


def rows_to_blocks(rows, dims):
    blocks, size, buckets, chans = dims
    moved = lax.all_to_all(rows.reshape(buckets, size, blocks, chans), "ch", split_axis=2, concat_axis=0)
    return jnp.transpose(moved, (0, 2, 1, 3)).reshape(blocks, size, buckets * chans)


def blocks_to_rows(values, dims):
    blocks, size, buckets, chans = dims
    moved = lax.all_to_all(values.reshape(blocks, size, buckets, chans), "ch", split_axis=0, concat_axis=0)
    return jnp.transpose(moved, (2, 1, 0, 3)).reshape(buckets * size, blocks * chans)


def conv_forward(rows, filt, tables, dims):
    kept = rows_to_blocks(rows, dims)
    (out,) = conv_call(conv_forward_kernel, dims, (kept, filt) + tables, (BF,), 1)
    return blocks_to_rows(out, dims), kept


def conv_backward(rows, kept, filt, tables, dims):
    moved = rows_to_blocks(rows, dims)
    out, dfilt = conv_call(conv_backward_kernel, dims, (moved, kept, filt) + tables, (BF, F32), 2)
    return blocks_to_rows(out, dims), dfilt


class Place:
    def __init__(self):
        self.ch = lax.axis_index("ch")
        self.seq = lax.axis_index("seq")
        self.z, self.x = self.ch // 2, lax.rem(self.ch, 2)
        self.y, self.core = self.seq // 2, lax.rem(self.seq, 2)
        self.sibling = {"seq": self.y * 2 + (1 - self.core)}
        self.along_y = {"seq": (1 - self.y) * 2 + self.core}
        self.along_x = {"ch": self.z * 2 + (1 - self.x)}
        self.others = [self.z + 1 - 2 * lax.rem(self.z, 2), lax.rem(self.z + 2, 4), 3 - self.z]
        self.along_z = [{"ch": one * 2 + self.x} for one in self.others]
        self.ch_ahead = [lax.rem(self.ch + d, 8) for d in range(1, 8)]
        self.seq_ahead = [lax.rem(self.seq + d, 4) for d in range(1, 4)]


def greet(ids):
    barrier = pltpu.get_barrier_semaphore()
    for one in ids:
        pl.semaphore_signal(barrier, inc=1, device_id=one, device_id_type=MESH)
    pl.semaphore_wait(barrier, len(ids))


def wait_all(copies):
    for copy in copies:
        copy.wait()


def push(src, dst, send, recv, device):
    copy = pltpu.make_async_remote_copy(
        src_ref=src, dst_ref=dst, send_sem=send, recv_sem=recv, device_id=device, device_id_type=MESH
    )
    copy.start()
    return copy


def split_columns(cols, share):
    return int(cols * share / 128 + 0.5) * 128


class Columns:
    SLOTS = 3

    def __init__(self, place, shards, columns, send, recv, local):
        self.p, self.shards, self.columns = place, shards, columns
        self.send, self.recv, self.local = send, recv, local
        self.copies = {}

    def go(self, i, slot, src, dst, device):
        self.copies[(i, slot)] = push(src, dst, self.send.at[i, slot], self.recv.at[i, slot], device)

    def start(self):
        p = self.p
        for i, shard in enumerate(self.shards):
            mine = self.columns[i].at[p.z]
            self.go(i, 1, shard, mine, p.along_z[1])
            self.go(i, 0, shard, mine, p.along_z[0])
            copy = pltpu.make_async_copy(shard, mine, self.local.at[i])
            copy.start()
            self.copies[(i, 3)] = copy

    def pass_far(self):
        p = self.p
        for i in range(len(self.shards)):
            self.copies[(i, 1)].wait_recv()
            here = self.columns[i].at[p.others[1]]
            self.go(i, 2, here, here, p.along_z[0])

    def finish(self):
        for (i, slot), copy in self.copies.items():
            if slot == 1:
                copy.wait_send()
            else:
                copy.wait()

    @classmethod
    def scratch(cls, count):
        return [
            pltpu.SemaphoreType.DMA((count, cls.SLOTS)),
            pltpu.SemaphoreType.DMA((count, cls.SLOTS)),
            pltpu.SemaphoreType.DMA((count,)),
        ]


class Gather:
    SLOTS = 32

    def __init__(self, place, columns, fulls, share, send, recv, local, places=range(4), by_place=()):
        self.p, self.columns, self.fulls, self.share = place, columns, fulls, share
        self.places, self.by_place = places, by_place
        self.send, self.recv, self.local = send, recv, local
        self.copies = {}
        self.seen = set()

    def go(self, i, slot, src, dst, device):
        self.copies[(i, slot)] = push(src, dst, self.send.at[i, slot], self.recv.at[i, slot], device)

    def place(self, n):
        return self.p.z if n == 0 else self.p.others[n - 1]

    def arrays(self, n):
        return [i for i in range(len(self.fulls)) if i not in self.by_place or n in self.places]

    def plane(self, i, n):
        if i in self.by_place:
            return self.fulls[i].at[n - self.places[0]]
        return self.fulls[i].at[self.place(n)]

    def ends(self, i, n):
        p, zz = self.p, self.place(n)
        return self.columns[i].at[zz], self.plane(i, n).at[p.x, p.y, p.core]

    def start_y(self, places=range(4)):
        for n in places:
            for i in self.arrays(n):
                src, dst = self.ends(i, n)
                self.go(i, 4 + n, src, dst, self.p.along_y)
                self.go(i, 16 + n, src, dst, self.p.sibling)
                copy = pltpu.make_async_copy(src, dst, self.local.at[i, n])
                copy.start()
                self.copies[(i, 32 + n)] = copy

    def start_x(self, places=range(4)):
        for n in places:
            for i in self.arrays(n):
                src, dst = self.ends(i, n)
                self.go(i, n, src, dst, self.p.along_x)

    def pass_sides(self, n):
        p = self.p
        for i in self.arrays(n):
            full = self.plane(i, n)
            cols = full.shape[4]
            part = split_columns(cols, self.share)
            self.copies[(i, n)].wait_recv()
            whole = full.at[1 - p.x, p.y, p.core]
            some = full.at[1 - p.x, p.y, p.core, :, pl.ds(0, part)]
            self.go(i, 8 + n, some, some, p.along_y)
            self.go(i, 20 + n, whole, whole, p.sibling)
            self.copies[(i, 4 + n)].wait_recv()
            whole = full.at[p.x, 1 - p.y, p.core]
            some = full.at[p.x, 1 - p.y, p.core, :, pl.ds(part, cols - part)]
            self.go(i, 12 + n, some, some, p.along_x)
            self.go(i, 24 + n, whole, whole, p.sibling)

    def pass_last(self, n):
        p = self.p
        for i in self.arrays(n):
            self.copies[(i, 8 + n)].wait_recv()
            self.copies[(i, 12 + n)].wait_recv()
            whole = self.plane(i, n).at[1 - p.x, 1 - p.y, p.core]
            self.go(i, 28 + n, whole, whole, p.sibling)

    def arrived(self, n):
        for i in range(len(self.fulls)):
            for slot in (16, 20, 24, 28):
                self.copies[(i, slot + n)].wait_recv()
            self.copies.pop((i, 32 + n)).wait()
            self.seen.add((i, n))

    def finish(self):
        for (i, slot), copy in self.copies.items():
            if slot >= 32:
                copy.wait()
            else:
                copy.wait_send()
                if slot >= 16 and (i, slot % 4) not in self.seen:
                    copy.wait_recv()

    @classmethod
    def scratch(cls, count):
        return [
            pltpu.SemaphoreType.DMA((count, cls.SLOTS)),
            pltpu.SemaphoreType.DMA((count, cls.SLOTS)),
            pltpu.SemaphoreType.DMA((count, 4)),
        ]


def everyone(p):
    ids = []
    for d in range(8):
        for e in range(4):
            if d or e:
                ids.append({"ch": lax.rem(p.ch + d, 8), "seq": lax.rem(p.seq + e, 4)})
    return ids


def start_kernel(count, *refs):
    pack, tail = refs[:2]
    shards = refs[2 : 2 + count]
    consts, halo, full = refs[2 + count : 5 + count]
    columns = refs[5 + count : 4 + 2 * count]
    packs, send, recv, halo_sems, column_in = refs[4 + 2 * count : 9 + 2 * count]
    column_sems = refs[9 + 2 * count : 12 + 2 * count]
    gather_sems = refs[12 + 2 * count :]
    columns = [column_in] + list(columns)
    p = Place()
    ids = everyone(p)
    greet(ids)
    column = Columns(p, shards, columns, *column_sems)
    gather = Gather(p, columns[:1], [full], 0.5, *gather_sems)
    column.start()
    copies = [push(pack, packs.at[p.ch, p.seq], send.at[n], recv.at[n], one) for n, one in enumerate(ids)]
    copies.append(push(tail, halo, halo_sems.at[0], halo_sems.at[1], {"ch": lax.rem(p.ch + 1, 8)}))
    packs[p.ch, p.seq] = pack[...]
    column.copies.pop((0, 3)).wait()
    gather.start_x([0])
    gather.start_y([0])
    column.copies[(0, 0)].wait_recv()
    gather.start_x([1])
    gather.start_y([1])
    column.pass_far()
    gather.start_x([2])
    gather.start_y([2])
    gather.pass_sides(0)
    gather.pass_sides(1)
    column.copies[(0, 2)].wait_recv()
    gather.start_x([3])
    gather.start_y([3])
    wait_all(copies)
    row = lax.broadcasted_iota(jnp.int32, (16, 128), 0)
    for c in range(8):
        first = packs[c, 0]
        total = first + packs[c, 1] + packs[c, 2] + packs[c, 3]
        consts[:, c * 128 : (c + 1) * 128] = jnp.where(row < 10, first, total)
    gather.pass_sides(2)
    gather.pass_sides(3)
    for n in range(4):
        gather.pass_last(n)
    gather.finish()
    for slot in (0, 2):
        column.copies.pop((0, slot)).wait_send()
    column.finish()


def start_call(pack, tail, shards):
    rows, cols = shards[0].shape
    count = len(shards)
    out = pl.pallas_call(
        functools.partial(start_kernel, count),
        out_shape=[
            jax.ShapeDtypeStruct((16, 1024), F32),
            jax.ShapeDtypeStruct(tail.shape, BF),
            jax.ShapeDtypeStruct((4, 2, 2, 2, rows, cols), BF),
        ]
        + [jax.ShapeDtypeStruct((4,) + one.shape, BF) for one in shards[1:]],
        in_specs=[VM, VM] + [VM] * count,
        out_specs=[VM, VM, ANYWHERE] + [VM] * (count - 1),
        scratch_shapes=[
            pltpu.VMEM((8, 4, 16, 128), F32),
            pltpu.SemaphoreType.DMA((31,)),
            pltpu.SemaphoreType.DMA((31,)),
            pltpu.SemaphoreType.DMA((2,)),
            pltpu.VMEM((4, rows, cols), BF),
        ]
        + Columns.scratch(count)
        + Gather.scratch(1),
        compiler_params=pltpu.CompilerParams(collective_id=4, has_side_effects=True, vmem_limit_bytes=VMEM_LIMIT),
    )(pack, tail, *shards)
    return out[0], out[1], out[2].reshape(rows * 32, cols), out[3:]


def lagged(u, buf, b, stream, lane, size, width):
    at = pl.ds(pl.multiple_of(stream * width + lane, 128), 128)
    rows = size * 2
    buf[pl.ds(0, 16)] = u[pl.ds(rows + 16 * b, 16), at].astype(F32)
    buf[pl.ds(16, size)] = u[pl.ds(b * size, size), at].astype(F32)
    return buf[pl.ds(16, size)], buf[pl.ds(15, size)], buf[pl.ds(14, size)]


def short_conv(u, buf, consts, b, stream, lane, size, width):
    now, one, two = lagged(u, buf, b, stream, lane, size, width)
    at = pl.ds(lane, 128)
    return consts[stream : stream + 1, at] * now + consts[3 + stream : 4 + stream, at] * one + consts[
        6 + stream : 7 + stream, at
    ] * two


def send_pieces(p, pieces, blocks_ref, send, recv, local, make):
    copies = []

    def piece(block, b):
        if len(pieces.shape) == 4:
            return pieces.at[block, b]
        return pieces.at[block, :, pl.ds(b * 128, 128)]

    for d in range(8):
        block = lax.rem(p.ch + d + 1, 8)
        make(block)
        for b in range(2):
            dst = blocks_ref.at[p.ch, :, pl.ds(b * 128, 128)]
            if d < 7:
                copies.append(push(piece(block, b), dst, send.at[d, b], recv.at[d, b], {"ch": block}))
            else:
                copy = pltpu.make_async_copy(piece(block, b), dst, local.at[b])
                copy.start()
                copies.append(copy)
    return copies


def send_blocks(p, ys, blocks_ref, send, recv, local):
    copies = []
    for d in range(7):
        copies.append(
            push(ys.at[p.ch_ahead[d]], blocks_ref.at[p.ch], send.at[d], recv.at[d], {"ch": p.ch_ahead[d]})
        )
    copy = pltpu.make_async_copy(ys.at[p.ch], blocks_ref.at[p.ch], local)
    copy.start()
    return copies + [copy]


def forward_kernel(size, *refs):
    u, consts, mask, h_ref, fh, fl, th, tl, lanes = refs[:9]
    columns = refs[9:12]
    mixer, kept, convolved = refs[12:15]
    fulls = refs[15:18]
    xs, abc, ys, pieces, gates, mixes, bufs = refs[18:25]
    send, recv, local, send_back, recv_back, local_back = refs[25:31]
    p = Place()
    width = 1024
    greet([{"ch": one} for one in p.ch_ahead] + [p.sibling, p.along_y])
    gather = Gather(p, columns, fulls, SHARE, *refs[31:], places=EARLY, by_place=(2,))
    gather.start_y()

    def make(block):
        lane = pl.multiple_of(block * 128, 128)

        def step(b, carry):
            gates[block, b] = short_conv(u, bufs.at[0], consts, b, 0, lane, size, width)
            key = short_conv(u, bufs.at[1], consts, b, 1, lane, size, width)
            mix = key * short_conv(u, bufs.at[2], consts, b, 2, lane, size, width)
            mixes[block, b] = mix
            pieces[block, b] = mix.astype(BF)
            return carry

        for b in range(2):
            step(b, 0)

    arriving = send_pieces(p, pieces, kept, send, recv, local, make)
    gather.start_x()
    filter_spectra(fh, fl, lanes, h_ref, abc, 8, size)
    wait_all(arriving)
    spectra(fh, fl, kept, xs, 8)
    products_forward(xs, abc, lanes, xs, 8, size)
    inverse_blocks(th, tl, xs, ys, 8)
    leaving = send_blocks(p, ys, convolved, send_back, recv_back, local_back)
    for n in range(4):
        gather.pass_sides(n)
    wait_all(leaving)
    for c in range(8):
        at = slice(c * 128, (c + 1) * 128)
        for b in range(2):
            rows = slice(b * size, (b + 1) * size)
            long_part = convolved[c, :, b * 128 : (b + 1) * 128].astype(F32) + consts[9:10, at] * mixes[c, b]
            mixer[rows, at] = (gates[c, b] * long_part * mask[rows]).astype(BF)
    for n in range(4):
        gather.pass_last(n)
    gather.finish()


def backward_kernel(size, count, *refs):
    u, consts, mask, grad_mixer, convolved, kept, h_ref, fh, fl, th, tl, lanes = refs[:12]
    grads = refs[12 : 12 + count]
    du, dh_ref, sums = refs[12 + count : 15 + count]
    outs = refs[15 + count : 15 + 2 * count]
    rest = refs[15 + 2 * count :]
    xs, ds, abc, gh, pieces, arrived, returned, keys, values, dlongs, dcs, edge_out, edge_in, bufs = rest[:14]
    send, recv, local, send_back, recv_back, local_back, edge_sems = rest[14:21]
    p = Place()
    width = 1024
    greet([{"ch": one} for one in p.ch_ahead] + [p.sibling, p.along_y])
    whole = [grads[0]] + [(one, 0, one.shape[5]) for one in grads[1:]]
    stops = [None] + list(outs[1:])
    scatter = Scatter(p, whole, [outs[0]] + [None] * (count - 1), stops, SHARE, rest[21:])
    scatter.start(1)
    scatter.start(2)
    sums[...] = jnp.zeros_like(sums)

    def grad_parts(block, b, rows, skip):
        at = pl.ds(pl.multiple_of(block * 128, 128), 128)
        take = max(rows, 16)
        masked = grad_mixer[pl.ds(b * size, take), at].astype(F32)[:rows] * mask[pl.ds(b * size, rows)]
        conv = convolved[block, :take, b * 128 : (b + 1) * 128].astype(F32)[:rows]
        return masked, conv + skip * (keys[block, b, :rows] * values[block, b, :rows])

    def make(block):
        lane = pl.multiple_of(block * 128, 128)
        at = pl.ds(lane, 128)
        total = jnp.zeros((1, 128), F32)
        for b in range(2):
            rows = pl.ds(b * size, size)
            gate = short_conv(u, bufs.at[0], consts, b, 0, lane, size, width)
            key = short_conv(u, bufs.at[1], consts, b, 1, lane, size, width)
            value = short_conv(u, bufs.at[2], consts, b, 2, lane, size, width)
            keys[block, b] = key
            values[block, b] = value
            dlong = grad_mixer[rows, at].astype(F32) * mask[rows] * gate
            dlongs[block, b] = dlong
            pieces[block, :, b * 128 : (b + 1) * 128] = dlong.astype(BF)
            total = total + jnp.sum(dlong * (key * value), axis=0, keepdims=True)
        sums[9:10, at] = total

    arriving = send_pieces(p, pieces, arrived, send, recv, local, make)
    scatter.turn(0)
    scatter.core(1)
    filter_spectra(fh, fl, lanes, h_ref, abc, 8, size)
    scatter.core(2)
    spectra(fh, fl, kept, xs, 8)
    wait_all(arriving)
    spectra(fh, fl, arrived, ds, 8)
    products_backward(xs, ds, abc, gh, lanes, 8, size)
    inverse_blocks(th, tl, ds, pieces, 8)
    leaving = send_blocks(p, pieces, returned, send_back, recv_back, local_back)
    filter_gradient(th, tl, gh, dh_ref, 8, size)
    scatter.third(0)
    scatter.first(1)
    wait_all(leaving)

    def edges(c, carry):
        at = pl.ds(pl.multiple_of(c * 128, 128), 128)
        skip = consts[9:10, at]
        for b in range(2):
            masked, long_part = grad_parts(c, b, 8, skip)
            back = returned[c, :16, b * 128 : (b + 1) * 128].astype(F32)[:8]
            dmixed = back + skip * dlongs[c, b, :8]
            edge_out[0, b, :, at] = masked * long_part
            edge_out[1, b, :, at] = dmixed * values[c, b, :8]
            edge_out[2, b, :, at] = dmixed * keys[c, b, :8]
        return carry

    lax.fori_loop(0, 8, edges, 0)
    edge = push(edge_out, edge_in, edge_sems.at[0], edge_sems.at[1], {"ch": lax.rem(p.ch + 7, 8)})
    scatter.first(2)
    edge.wait()
    inside = jnp.where(p.ch < 7, 1.0, 0.0)

    def streams(c, carry):
        lane = pl.multiple_of(c * 128, 128)
        at = pl.ds(lane, 128)
        skip = consts[9:10, at]
        for b in range(2):
            masked, long_part = grad_parts(c, b, size, skip)
            dmixed = returned[c, :, b * 128 : (b + 1) * 128].astype(F32) + skip * dlongs[c, b]
            dcs[0, b, pl.ds(0, size)] = masked * long_part
            dcs[1, b, pl.ds(0, size)] = dmixed * values[c, b]
            dcs[2, b, pl.ds(0, size)] = dmixed * keys[c, b]
        for stream in range(3):
            out = pl.ds(pl.multiple_of(stream * width + lane, 128), 128)
            totals = [jnp.zeros((1, 128), F32)] * 3
            for b in range(2):
                dcs[stream, b, pl.ds(size, 8)] = edge_in[stream, b, :, at] * inside
                parts = lagged(u, bufs.at[stream], b, stream, lane, size, width)
                grad = dcs[stream, b, pl.ds(0, size)]
                for lag in range(3):
                    totals[lag] = totals[lag] + jnp.sum(grad * parts[lag], axis=0, keepdims=True)
                total = consts[stream : stream + 1, at] * grad
                total = total + consts[3 + stream : 4 + stream, at] * dcs[stream, b, pl.ds(1, size)]
                total = total + consts[6 + stream : 7 + stream, at] * dcs[stream, b, pl.ds(2, size)]
                du[pl.ds(b * size, size), out] = total.astype(BF)
            for lag in range(3):
                row = 3 * lag + stream
                sums[row : row + 1, at] = totals[lag]
        return carry

    lax.fori_loop(0, 8, streams, 0)
    scatter.second(1)
    scatter.second(2)
    scatter.last(0)


def nt(a, b):
    return lax.dot_general(a, b, (((1,), (1,)), ((), ())), preferred_element_type=F32)


def tn(a, b):
    return lax.dot_general(a, b, (((0,), (0,)), ((), ())), preferred_element_type=F32)


GELU_ONE = math.sqrt(2.0 / math.pi)
GELU_THREE = GELU_ONE * 0.044715


class Planes:
    def __init__(self, place, column, acc, one_a, one_b, two_a, two_b, send, recv):
        self.p, self.column = place, column
        self.acc, self.one_a, self.one_b, self.two_a, self.two_b = acc, one_a, one_b, two_a, two_b
        self.send, self.recv = send, recv
        self.copies = {}
        cols = acc.shape[4]
        half = split_columns(cols, 0.5)
        self.low, self.high = pl.ds(0, half), pl.ds(half, cols - half)

    def go(self, n, slot, src, dst, device):
        self.copies[(n, slot)] = push(src, dst, self.send.at[n, slot], self.recv.at[n, slot], device)

    def done(self, n, *slots):
        for slot in slots:
            self.copies[(n, slot)].wait()

    def core(self, n, made):
        self.go(n, 0, made.at[:, :, 1 - self.p.core], self.acc.at[n], self.p.sibling)

    def sides(self, n, made):
        p, acc = self.p, self.acc.at[n]
        self.done(n, 0)

        def step(k, carry):
            xx, yy = k // 2, lax.rem(k, 2)
            acc[xx, yy] = add_rows(acc[xx, yy], made[xx, yy, p.core])
            return carry

        lax.fori_loop(0, 4, step, 0)
        self.go(n, 1, acc.at[:, 1 - p.y, :, self.low], self.one_a.at[n], p.along_y)
        self.go(n, 2, acc.at[1 - p.x, :, :, self.high], self.one_b.at[n], p.along_x)

    def cross(self, n):
        p, acc = self.p, self.acc.at[n]
        low, high = self.low, self.high
        self.done(n, 1, 2)
        for k in range(2):
            acc[k, p.y, :, low] = add_rows(acc[k, p.y, :, low], self.one_a[n, k])
            acc[p.x, k, :, high] = add_rows(acc[p.x, k, :, high], self.one_b[n, k])
        self.go(n, 3, acc.at[1 - p.x, p.y, :, low], self.two_a.at[n], p.along_x)
        self.go(n, 4, acc.at[p.x, 1 - p.y, :, high], self.two_b.at[n], p.along_y)

    def last(self, n, zz):
        p, acc = self.p, self.acc.at[n]
        low, high = self.low, self.high
        self.done(n, 3, 4)
        self.column[zz, :, low] = add_rows(acc[p.x, p.y, :, low], self.two_a[n])
        self.column[zz, :, high] = add_rows(acc[p.x, p.y, :, high], self.two_b[n])

    @staticmethod
    def scratch(rows, cols):
        half = split_columns(cols, 0.5)
        return [
            pltpu.VMEM((4, 2, 2, rows, cols), BF),
            pltpu.VMEM((4, 2, rows, half), BF),
            pltpu.VMEM((4, 2, rows, cols - half), BF),
            pltpu.VMEM((4, rows, half), BF),
            pltpu.VMEM((4, rows, cols - half), BF),
            pltpu.SemaphoreType.DMA((4, 5)),
            pltpu.SemaphoreType.DMA((4, 5)),
        ]


def feed_forward_kernel(*refs):
    mixer, tokens, mask, cot, consts, w_out, w_up, early, column = refs[:9]
    result, grad_after, grad_mixer, grad_gain, grad_out, sum_column, grad_up = refs[9:16]
    up, planes, late, total, unit, scale, normed, turned, da, pre, dact, act, dpre, kept_down, kept_up = refs[16:31]
    up_sem, plane_sems, out_sems = refs[31:34]
    gather_sems, scatter_refs = refs[34:37], refs[37:]
    p = Place()
    greet([p.along_x, p.along_y, p.sibling])
    gather = Gather(p, [column], [late], 0.5, *gather_sems, places=LATE, by_place=(0,))
    gather.start_x()
    gather.start_y()
    sums = Planes(p, sum_column, *scatter_refs)
    loads = [pltpu.make_async_copy(w_up, up, up_sem)]
    loads += [pltpu.make_async_copy(early.at[n], planes.at[n], plane_sems.at[n]) for n in EARLY]
    for load in loads:
        load.start()
    gain = consts[11:12, :]
    total[...] = mm(mixer[...], w_out[...])

    def norm(i, carry):
        rows = pl.ds(pl.multiple_of(i * 32, 32), 32)
        zero = tokens[rows].astype(F32) * mask[rows, 0:1]
        value = zero + total[rows]
        total[rows] = value
        centre = value - jnp.mean(value, axis=1, keepdims=True)
        inverse = lax.rsqrt(jnp.mean(centre * centre, axis=1, keepdims=True) + EPS)
        one = centre * inverse
        unit[rows] = one
        scale[rows] = jnp.broadcast_to(inverse, (32, 128))
        normed[rows] = (one * gain).astype(BF)
        return carry

    lax.fori_loop(0, 16, norm, 0)
    turned[...] = normed[...].T
    wait_all(loads)
    writes = [None] * 4
    for n in range(4):
        zz = gather.place(n)
        cols = pl.ds(pl.multiple_of(zz * 1024, 1024), 1024)
        slot = n % 2
        made = kept_down.at[slot]
        pre[...] = mm(normed[...], up[:, cols])
        if n < 2:
            gather.pass_sides(n + 2)
            plane = planes.at[n]
        else:
            gather.arrived(n)
            plane = late.at[n - 2]
        if n > 0:
            sums.sides(n - 1, kept_down.at[1 - slot])
        dact[...] = nt(cot[...], plane[...].reshape(1024, 1024))

        def gelu(i, carry):
            rows = pl.ds(pl.multiple_of(i * 16, 16), 16)
            x = pre[rows]
            square = x * x
            t = jnp.tanh(x * (GELU_ONE + GELU_THREE * square))
            half = 0.5 + 0.5 * t
            value = x * half
            act[rows] = value.astype(BF)
            slope = half + value * (1.0 - t) * (GELU_ONE + 3.0 * GELU_THREE * square)
            dpre[rows] = (dact[rows] * slope).astype(BF)
            return carry

        lax.fori_loop(0, 32, gelu, 0)
        if n > 1:
            wait_all(writes[n - 2])
        made[...] = tn(act[...], cot[...]).astype(BF).reshape(2, 2, 2, 128, 1024)
        sums.core(n, made)
        total[...] += mm(act[...], plane[...].reshape(1024, 1024))
        if n > 1:
            sums.cross(n - 2)
        else:
            gather.pass_last(n + 2)
        back = nt(dpre[...], up[:, cols])
        da[...] = back if n == 0 else da[...] + back
        kept_up[slot] = mm(turned[...], dpre[...]).astype(BF)
        writes[n] = [pltpu.make_async_copy(kept_up.at[slot], grad_up.at[:, cols], out_sems.at[n])]
        for copy in writes[n]:
            copy.start()
    sums.sides(3, kept_down.at[1])
    sums.cross(2)
    sums.last(0, gather.place(0))

    def finish(i, gain_sum):
        rows = pl.ds(pl.multiple_of(i * 32, 32), 32)
        result[rows] = total[rows].astype(BF)
        one = unit[rows]
        back = da[rows]
        e = back * gain
        inner = e - jnp.mean(e, axis=1, keepdims=True) - one * jnp.mean(e * one, axis=1, keepdims=True)
        after = cot[rows].astype(F32) + scale[rows, 0:1] * inner
        grad_after[rows] = after
        normed[rows] = after.astype(BF)
        return gain_sum + jnp.sum(back * one, axis=0, keepdims=True)

    grad_gain[...] = lax.fori_loop(0, 16, finish, jnp.zeros((1, 1024), F32))
    grad_mixer[...] = nt(normed[...], w_out[...]).astype(BF)
    sums.cross(3)
    sums.last(1, gather.place(1))
    sums.last(2, gather.place(2))
    grad_out[...] = tn(mixer[...], normed[...]).astype(BF)
    for n in (2, 3):
        wait_all(writes[n])
    gather.finish()
    sums.last(3, gather.place(3))


def feed_forward_call(mixer, tokens, mask, cot, consts, w_out, w_up, early, column):
    rows, width = mixer.shape
    hidden = w_up.shape[1]
    wide = (rows, width)
    square = (width, width)
    part = column.shape[1:]
    return pl.pallas_call(
        feed_forward_kernel,
        out_shape=[
            jax.ShapeDtypeStruct(wide, BF),
            jax.ShapeDtypeStruct(wide, F32),
            jax.ShapeDtypeStruct(wide, BF),
            jax.ShapeDtypeStruct((1, width), F32),
            jax.ShapeDtypeStruct(square, BF),
            jax.ShapeDtypeStruct((4,) + part, BF),
            jax.ShapeDtypeStruct((width, hidden), BF),
        ],
        in_specs=[VM] * 6 + [ANYWHERE] * 3,
        out_specs=[VM] * 6 + [ANYWHERE],
        scratch_shapes=[
            pltpu.VMEM((width, hidden), BF),
            pltpu.VMEM((len(EARLY), 2, 2, 2) + part, BF),
            pltpu.VMEM((len(LATE), 2, 2, 2) + part, BF),
            pltpu.VMEM(wide, F32),
            pltpu.VMEM(wide, F32),
            pltpu.VMEM((rows, 128), F32),
            pltpu.VMEM(wide, BF),
            pltpu.VMEM((width, rows), BF),
            pltpu.VMEM(wide, F32),
            pltpu.VMEM(wide, F32),
            pltpu.VMEM(wide, F32),
            pltpu.VMEM(wide, BF),
            pltpu.VMEM(wide, BF),
            pltpu.VMEM((2, 2, 2, 2) + part, BF),
            pltpu.VMEM((2,) + square, BF),
            pltpu.SemaphoreType.DMA,
            pltpu.SemaphoreType.DMA((len(EARLY),)),
            pltpu.SemaphoreType.DMA((4,)),
        ]
        + Gather.scratch(1)
        + Planes.scratch(*part),
        compiler_params=pltpu.CompilerParams(collective_id=5, has_side_effects=True, vmem_limit_bytes=VMEM_LIMIT),
    )(mixer, tokens, mask, cot, consts, w_out, w_up, early, column)


def exchange_sems():
    pieces = [pltpu.SemaphoreType.DMA((7, 2))] * 2 + [pltpu.SemaphoreType.DMA((2,))]
    return pieces + [pltpu.SemaphoreType.DMA((7,))] * 2 + [pltpu.SemaphoreType.DMA]


def forward_call(u, consts, mask, filt, tables, columns, size):
    rows = 2 * size
    block = (8, size, 256)
    piece = (8, 2, size, 128)
    operands = (u, consts, mask, filt) + tables
    count = len(columns)
    whole = [jax.ShapeDtypeStruct((4, 2, 2, 2) + one.shape[1:], BF) for one in columns[:2]]
    whole.append(jax.ShapeDtypeStruct((len(EARLY), 2, 2, 2) + columns[2].shape[1:], BF))
    out = pl.pallas_call(
        functools.partial(forward_kernel, size),
        out_shape=[jax.ShapeDtypeStruct((rows, 1024), BF)] + [jax.ShapeDtypeStruct(block, BF)] * 2 + whole,
        in_specs=[VM] * (len(operands) + count),
        out_specs=[VM] * 3 + [ANYWHERE] * count,
        scratch_shapes=[
            pltpu.VMEM((8, 2 * size, 256), F32),
            pltpu.VMEM((8, 2, size, 128), F32),
            pltpu.VMEM(block, BF),
            pltpu.VMEM(piece, BF),
            pltpu.VMEM(piece, F32),
            pltpu.VMEM(piece, F32),
            pltpu.VMEM((3, size + 16, 128), F32),
        ]
        + exchange_sems()
        + Gather.scratch(count),
        compiler_params=pltpu.CompilerParams(collective_id=1, has_side_effects=True, vmem_limit_bytes=VMEM_LIMIT),
    )(*operands, *columns)
    return out[:3], [one.reshape(-1, one.shape[-1]) for one in out[3:5]] + [out[5]]


def backward_call(u, consts, mask, grad_mixer, convolved, kept, filt, tables, grads, size):
    rows = 2 * size
    block = (8, size, 256)
    piece = (8, 2, size, 128)
    operands = (u, consts, mask, grad_mixer, convolved, kept, filt) + tables
    count = len(grads)
    shapes = [grads[0].shape[1:]] + [(one.shape[0] // 32, one.shape[1]) for one in grads[1:]]
    views = [grads[0]] + [one.reshape((4, 2, 2, 2) + shape) for one, shape in zip(grads[1:], shapes[1:])]
    out = pl.pallas_call(
        functools.partial(backward_kernel, size, count),
        out_shape=[
            jax.ShapeDtypeStruct((rows, 3072), BF),
            jax.ShapeDtypeStruct((8, size, 128), F32),
            jax.ShapeDtypeStruct((16, 1024), F32),
        ]
        + [jax.ShapeDtypeStruct(shapes[0], F32)]
        + [jax.ShapeDtypeStruct((4,) + shape, BF) for shape in shapes[1:]],
        in_specs=[VM] * (len(operands) + 1) + [ANYWHERE] * (count - 1),
        out_specs=[VM] * (3 + count),
        scratch_shapes=[
            pltpu.VMEM((8, 2 * size, 256), F32),
            pltpu.VMEM((8, 2 * size, 256), F32),
            pltpu.VMEM((8, 2, size, 128), F32),
            pltpu.VMEM((8, 2, size, 128), F32),
            pltpu.VMEM(block, BF),
            pltpu.VMEM(block, BF),
            pltpu.VMEM(block, BF),
            pltpu.VMEM(piece, F32),
            pltpu.VMEM(piece, F32),
            pltpu.VMEM(piece, F32),
            pltpu.VMEM((3, 2, size + 8, 128), F32),
            pltpu.VMEM((3, 2, 8, 1024), F32),
            pltpu.VMEM((3, 2, 8, 1024), F32),
            pltpu.VMEM((3, size + 16, 128), F32),
        ]
        + exchange_sems()
        + [pltpu.SemaphoreType.DMA((2,))]
        + Scatter.scratch([shape + (n > 0, n > 0) for n, shape in enumerate(shapes)], SHARE),
        compiler_params=pltpu.CompilerParams(collective_id=2, has_side_effects=True, vmem_limit_bytes=VMEM_LIMIT),
    )(*operands, *views)
    return out[:3], out[3:]


def add_rows(target, other):
    return (target.astype(F32) + other.astype(F32)).astype(BF)


class Scatter:
    SLOTS = 11

    def __init__(self, place, grads, outs, columns, share, refs):
        self.p, self.grads, self.outs, self.columns, self.share = place, grads, outs, columns, share
        count = len(grads)
        self.bufs = []
        at = 0
        for one, column in zip(grads, columns):
            names = Scatter.names(isinstance(one, tuple), column is not None)
            self.bufs.append(dict(zip(names, refs[at : at + len(names)])))
            at += len(names)
        self.send, self.recv, self.local = refs[at : at + 3]
        self.copies = {}

    @staticmethod
    def names(whole, stops):
        before = ("own", "acc", "one_a", "one_b", "two_a", "two_b") if whole else ()
        return before + (() if stops else ("three", "four"))

    def go(self, i, slot, src, dst, device):
        copy = push(src, dst, self.send.at[i, slot], self.recv.at[i, slot], device)
        self.copies[(i, slot)] = copy

    def done(self, i, *slots):
        for slot in slots:
            self.copies[(i, slot)].wait()

    def part(self, i, zz, core):
        ref, first, cols = self.grads[i]
        if cols == ref.shape[5]:
            return ref.at[zz, :, :, core]
        return ref.at[zz, :, :, core, :, pl.ds(first, cols)]

    def load(self, i, zz):
        own = self.bufs[i]["own"]
        copy = pltpu.make_async_copy(self.part(i, zz, self.p.core), own.at[zz % 2], self.local.at[i, zz])
        copy.start()
        self.copies[(i, "own", zz)] = copy

    def start(self, i):
        for zz in range(4):
            self.go(i, zz, self.part(i, zz, 1 - self.p.core), self.bufs[i]["acc"].at[zz], self.p.sibling)
        self.load(i, 0)
        self.load(i, 1)

    def halves(self, i):
        cols = self.grads[i][2]
        part = split_columns(cols, self.share)
        return pl.ds(0, part), pl.ds(part, cols - part)

    def core(self, i):
        p, acc, own = self.p, self.bufs[i]["acc"], self.bufs[i]["own"]
        for zz in range(4):
            self.copies[(i, "own", zz)].wait()
            self.done(i, zz)

            def step(n, carry, zz=zz):
                xx, yy = n // 2, lax.rem(n, 2)
                acc[zz, xx, yy] = add_rows(acc[zz, xx, yy], own[zz % 2, xx, yy])
                return carry

            lax.fori_loop(0, 4, step, 0)
            if zz < 2:
                self.load(i, zz + 2)
        low, high = self.halves(i)
        self.go(i, 4, acc.at[:, :, 1 - p.y, :, low], self.bufs[i]["one_a"], p.along_y)
        self.go(i, 5, acc.at[:, 1 - p.x, :, :, high], self.bufs[i]["one_b"], p.along_x)

    def first(self, i):
        p, acc = self.p, self.bufs[i]["acc"]
        one_a, one_b = self.bufs[i]["one_a"], self.bufs[i]["one_b"]
        low, high = self.halves(i)
        self.done(i, 4, 5)

        def step(n, carry):
            zz, w = n // 2, lax.rem(n, 2)
            acc[zz, w, p.y, :, low] = add_rows(acc[zz, w, p.y, :, low], one_a[zz, w])
            acc[zz, p.x, w, :, high] = add_rows(acc[zz, p.x, w, :, high], one_b[zz, w])
            return carry

        lax.fori_loop(0, 8, step, 0)
        self.go(i, 6, acc.at[:, 1 - p.x, p.y, :, low], self.bufs[i]["two_a"], p.along_x)
        self.go(i, 7, acc.at[:, p.x, 1 - p.y, :, high], self.bufs[i]["two_b"], p.along_y)

    def second(self, i):
        p, acc = self.p, self.bufs[i]["acc"]
        two_a, two_b = self.bufs[i]["two_a"], self.bufs[i]["two_b"]
        low, high = self.halves(i)
        self.done(i, 6, 7)
        column = self.columns[i]

        def step(zz, carry):
            here = acc.at[zz, p.x, p.y] if column is None else column.at[zz]
            here[:, low] = add_rows(acc[zz, p.x, p.y, :, low], two_a[zz])
            here[:, high] = add_rows(acc[zz, p.x, p.y, :, high], two_b[zz])
            return carry

        lax.fori_loop(0, 4, step, 0)
        if column is None:
            self.turn(i)

    def sums(self, i, zz):
        if isinstance(self.grads[i], tuple):
            return self.bufs[i]["acc"].at[zz, self.p.x, self.p.y]
        return self.grads[i].at[zz]

    def turn(self, i):
        p, three = self.p, self.bufs[i]["three"]
        self.go(i, 8, self.sums(i, p.others[2]), three.at[0], p.along_z[0])
        self.go(i, 9, self.sums(i, p.others[0]), three.at[1], p.along_z[0])

    def third(self, i):
        p, three = self.p, self.bufs[i]["three"]
        self.done(i, 8, 9)
        far = self.sums(i, p.others[1])
        three[0] = add_rows(far[...], three[0])
        self.go(i, 10, three.at[0], self.bufs[i]["four"], p.along_z[1])

    def last(self, i):
        three, four = self.bufs[i]["three"], self.bufs[i]["four"]
        self.done(i, 10)
        total = self.sums(i, self.p.z)[...].astype(F32) + three[1].astype(F32) + four[...].astype(F32)
        if isinstance(self.grads[i], tuple):
            _, first, cols = self.grads[i]
            self.outs[i][:, first : first + cols] = total
        else:
            self.outs[i][...] = total

    @classmethod
    def scratch(cls, kinds, share):
        count = len(kinds)
        bufs = []
        for rows, cols, whole, stops in kinds:
            part = split_columns(cols, share)
            shapes = {
                "own": (2, 2, 2, rows, cols),
                "acc": (4, 2, 2, rows, cols),
                "one_a": (4, 2, rows, part),
                "one_b": (4, 2, rows, cols - part),
                "two_a": (4, rows, part),
                "two_b": (4, rows, cols - part),
                "three": (2, rows, cols),
                "four": (rows, cols),
            }
            bufs += [pltpu.VMEM(shapes[name], BF) for name in cls.names(whole, stops)]
        return bufs + [
            pltpu.SemaphoreType.DMA((count, cls.SLOTS)),
            pltpu.SemaphoreType.DMA((count, cls.SLOTS)),
            pltpu.SemaphoreType.DMA((count, 4)),
        ]


PARTS = 3


def scatter_kernel(count, *refs):
    grad, small_vec, small_sec, small_fst = refs[:4]
    columns = refs[4 : 4 + count]
    out, small_out = refs[4 + count : 6 + count]
    outs = refs[6 + count : 6 + 2 * count]
    gathered, joined, small_send, small_recv = refs[6 + 2 * count : 10 + 2 * count]
    p = Place()
    greet([{"ch": one} for one in p.ch_ahead] + [{"seq": one} for one in p.seq_ahead])
    cols = grad.shape[5] // PARTS
    parts = [(grad, n * cols, cols) for n in range(PARTS)]
    scatter = Scatter(
        p, parts + list(columns), [out] * PARTS + list(outs), [None] * (PARTS + count), 0.5, refs[10 + 2 * count :]
    )
    for n in range(PARTS):
        scatter.start(n)
    for n in range(count):
        scatter.turn(PARTS + n)

    vec_rows = small_vec.shape[0]
    fst_rows = small_fst.shape[0]
    small_copies = []
    for d in range(7):
        lane = pl.multiple_of(p.ch_ahead[d] * 128, 128)
        pairs = (
            (small_vec.at[:, pl.ds(lane, 128)], gathered.at[p.ch, pl.ds(0, vec_rows)]),
            (small_fst, gathered.at[p.ch, pl.ds(vec_rows, fst_rows)]),
        )
        for n, (src, dst) in enumerate(pairs):
            slot = 2 * d + n
            small_copies.append(push(src, dst, small_send.at[slot], small_recv.at[slot], {"ch": p.ch_ahead[d]}))
    gathered[p.ch, :vec_rows] = small_vec[:, pl.ds(pl.multiple_of(p.ch * 128, 128), 128)]
    gathered[p.ch, vec_rows:] = small_fst[...]

    stages = (scatter.core, scatter.first, scatter.second, scatter.third, scatter.last)
    later = [functools.partial(stage, PARTS + n) for stage in (scatter.third, scatter.last) for n in range(count)]
    for time in range(PARTS + len(stages) - 1):
        for n, stage in enumerate(stages):
            if 0 <= time - n < PARTS:
                stage(time - n)
        if time == 0:
            wait_all(small_copies)
            total = gathered[0]
            for n in range(1, 8):
                total = total + gathered[n]
            joined[p.seq, : vec_rows + fst_rows] = total
            joined[p.seq, vec_rows + fst_rows :] = small_sec[...]
            small_copies = [
                push(joined.at[p.seq], joined.at[p.seq], small_send.at[14 + d], small_recv.at[14 + d], {"seq": p.seq_ahead[d]})
                for d in range(3)
            ]
        if time > 0 and later:
            later.pop(0)()
    for step in later:
        step()
    wait_all(small_copies)
    total = joined[0]
    for n in range(1, 4):
        total = total + joined[n]
    small_out[...] = total


def scatter_sums(grad, vec, sec, fst, columns):
    rows, cols = grad.shape[0] // 32, grad.shape[1]
    small = vec.shape[0] + fst.shape[0]
    count = len(columns)
    kinds = [(rows, cols // PARTS, True, False)] * PARTS + [one.shape[1:] + (False, False) for one in columns]
    out = pl.pallas_call(
        functools.partial(scatter_kernel, count),
        out_shape=[
            jax.ShapeDtypeStruct((rows, cols), F32),
            jax.ShapeDtypeStruct((small + sec.shape[0], 128), F32),
        ]
        + [jax.ShapeDtypeStruct(one.shape[1:], F32) for one in columns],
        in_specs=[ANYWHERE] + [VM] * (3 + count),
        out_specs=[VM] * (2 + count),
        scratch_shapes=[
            pltpu.VMEM((8, small, 128), F32),
            pltpu.VMEM((4, small + sec.shape[0], 128), F32),
            pltpu.SemaphoreType.DMA((17,)),
            pltpu.SemaphoreType.DMA((17,)),
        ]
        + Scatter.scratch(kinds, 0.5),
        compiler_params=pltpu.CompilerParams(collective_id=3, has_side_effects=True, vmem_limit_bytes=VMEM_LIMIT),
    )(grad.reshape(4, 2, 2, 2, rows, cols), vec, sec, fst, *columns)
    return out[0], out[1], out[2:]


def general_body(
    tokens,
    lengths,
    in_weight,
    out_weight,
    up_weight,
    down_weight,
    gain_one,
    gain_two,
    conv_taps,
    skip_gain,
    filter_first,
    filter_bias,
    frequency,
    filter_second,
    cotangent,
):
    ch_count = lax.axis_size("ch")
    ch_place = lax.axis_index("ch")
    size = tokens.shape[1]
    buckets = tokens.shape[2]
    width = tokens.shape[3]
    chans = skip_gain.shape[0]
    length = size * ch_count
    rows = size * buckets
    dims = (ch_count, size, buckets, chans)
    tables = tuple(jnp.asarray(one) for one in block_tables(size))

    def gather(shard):
        return lax.all_gather(shard, ("ch", "seq"), axis=0, tiled=True)

    full_in = gather(in_weight)
    full_gain_one = gather(gain_one).astype(F32)
    full_gain_two = gather(gain_two).astype(F32)
    full_out = gather(out_weight)
    full_up = gather(up_weight)
    full_down = gather(down_weight)

    local = ch_place * size + jnp.arange(size, dtype=jnp.int32)
    mask = (local[None, :] < lengths[0][:, None]).astype(F32).reshape(rows, 1)
    before = ch_place * size - 2 + jnp.arange(2, dtype=jnp.int32)
    mask_before = (before[None, :] < lengths[0][:, None]).astype(F32).reshape(2 * buckets, 1)
    chain = [(i, i + 1) for i in range(ch_count - 1)]
    halo = lax.ppermute(tokens[0, size - 2 :], "ch", chain)
    x_zero = jnp.swapaxes(tokens[0], 0, 1).reshape(rows, width).astype(F32) * mask
    x_before = jnp.swapaxes(halo, 0, 1).reshape(2 * buckets, width).astype(F32) * mask_before

    taps_full = lax.all_gather(conv_taps.reshape(9, chans), "ch", axis=1, tiled=True).reshape(3, 3, width)
    skip_full = lax.all_gather(skip_gain.reshape(1, chans), "ch", axis=1, tiled=True)

    table = positions_table(length, filter_first.shape[0])
    hidden = filter_hidden(filter_first, filter_bias, frequency, table)
    decay = decay_table(length, ch_place * chans, chans, width)
    filt = jnp.dot(hidden, filter_second, precision=HIGH) * decay
    filt_blocks = jnp.tile(filt.reshape(ch_count, size, chans), (1, 1, buckets))

    normed_one = layer_norm(x_zero, full_gain_one).astype(BF)
    normed_before = layer_norm(x_before, full_gain_one).astype(BF)
    streams = jnp.dot(normed_one, full_in, preferred_element_type=F32).astype(BF)
    streams_before = jnp.dot(normed_before, full_in, preferred_element_type=F32).astype(BF)
    lag = jnp.concatenate(
        [streams_before.reshape(buckets, 2, 3, width), streams.reshape(buckets, size, 3, width)], axis=1
    ).astype(F32)
    lag_zero, lag_one, lag_two = lag[:, 2:], lag[:, 1:-1], lag[:, :-2]
    conv = taps_full[0] * lag_zero + taps_full[1] * lag_one + taps_full[2] * lag_two
    gate = conv[:, :, 0].reshape(rows, width)
    key_part = conv[:, :, 1].reshape(rows, width)
    value_part = conv[:, :, 2].reshape(rows, width)
    mixed = key_part * value_part

    convolved, kept = conv_forward(mixed.astype(BF), filt_blocks, tables, dims)
    long_part = convolved.astype(F32) + skip_full * mixed
    mixer = (gate * long_part * mask).astype(BF)
    after_mix = x_zero + jnp.dot(mixer, full_out, preferred_element_type=F32)
    normed_two = layer_norm(after_mix, full_gain_two).astype(BF)
    inner_act = jnp.dot(normed_two, full_up, preferred_element_type=F32)
    active = jax.nn.gelu(inner_act).astype(BF)
    result = (after_mix + jnp.dot(active, full_down, preferred_element_type=F32)).astype(BF)
    result = jnp.swapaxes(result.reshape(buckets, size, width), 0, 1).reshape(1, size, buckets, width)

    grad_result = jnp.swapaxes(cotangent[0], 0, 1).reshape(rows, width)
    grad_active = jnp.dot(grad_result, full_down.T, preferred_element_type=F32)
    _, gelu_pull = jax.vjp(jax.nn.gelu, inner_act)
    grad_inner = gelu_pull(grad_active)[0].astype(BF)
    grad_down = jnp.dot(active.T, grad_result, preferred_element_type=F32)
    grad_up = jnp.dot(normed_two.T, grad_inner, preferred_element_type=F32)
    grad_normed_two = jnp.dot(grad_inner, full_up.T, preferred_element_type=F32)
    _, norm_two_pull = jax.vjp(layer_norm, after_mix, full_gain_two)
    grad_after_part, grad_gain_two = norm_two_pull(grad_normed_two)
    grad_after = grad_result.astype(F32) + grad_after_part
    grad_mix = grad_after.astype(BF)
    grad_out = jnp.dot(mixer.T, grad_mix, preferred_element_type=F32)
    grad_mixer = jnp.dot(grad_mix, full_out.T, preferred_element_type=F32).astype(BF)
    grad_masked = grad_mixer.astype(F32) * mask
    grad_gate = grad_masked * long_part
    grad_long = grad_masked * gate
    grad_skip = jnp.sum(grad_long * mixed, axis=0)
    grad_convolved, grad_filt = conv_backward(grad_long.astype(BF), kept, filt_blocks, tables, dims)
    grad_mixed = grad_convolved.astype(F32) + skip_full * grad_long
    grad_conv = jnp.stack([grad_gate, grad_mixed * value_part, grad_mixed * key_part], axis=1)
    grad_conv = grad_conv.reshape(buckets, size, 3, width)
    grad_taps = jnp.stack(
        [
            jnp.sum(grad_conv * lag_zero, axis=(0, 1)),
            jnp.sum(grad_conv * lag_one, axis=(0, 1)),
            jnp.sum(grad_conv * lag_two, axis=(0, 1)),
        ],
        axis=0,
    )
    next_rows = lax.ppermute(grad_conv[:, :2], "ch", [(j, i) for i, j in chain])
    ahead = jnp.concatenate([grad_conv, next_rows], axis=1)
    grad_streams = taps_full[0] * ahead[:, :-2] + taps_full[1] * ahead[:, 1:-1] + taps_full[2] * ahead[:, 2:]
    grad_projected = grad_streams.astype(BF).reshape(rows, 3 * width)
    grad_in = jnp.dot(normed_one.T, grad_projected, preferred_element_type=F32)
    grad_normed_one = jnp.dot(grad_projected, full_in.T, preferred_element_type=F32)
    _, norm_one_pull = jax.vjp(layer_norm, x_zero, full_gain_one)
    grad_zero_part, grad_gain_one = norm_one_pull(grad_normed_one)
    grad_input = ((grad_after + grad_zero_part) * mask).astype(BF)
    grad_input = jnp.swapaxes(grad_input.reshape(buckets, size, width), 0, 1).reshape(1, size, buckets, width)

    grad_filt = jnp.sum(grad_filt.reshape(length, buckets, chans), axis=1)
    grad_raw = grad_filt * decay
    grad_second = jnp.dot(hidden.T, grad_raw, precision=HIGH)
    grad_hidden = jnp.dot(grad_raw, filter_second.T, precision=HIGH)

    def hidden_of(first_layer, first_shift, freq_values):
        return filter_hidden(first_layer, first_shift, freq_values, table)

    _, hidden_pull = jax.vjp(hidden_of, filter_first, filter_bias, frequency)
    grad_first, grad_bias, grad_freq = hidden_pull(grad_hidden)

    sum_in, sum_out, sum_up, sum_down, sum_gain_one, sum_gain_two = (
        lax.psum_scatter(one, ("ch", "seq"), scatter_dimension=0, tiled=True)
        for one in (grad_in, grad_out, grad_up, grad_down, grad_gain_one, grad_gain_two)
    )
    sum_second = lax.psum(grad_second, "seq")
    all_taps, all_skip, sum_first, sum_bias, sum_freq = lax.psum(
        (grad_taps, grad_skip, grad_first, grad_bias, grad_freq), ("ch", "seq")
    )
    sum_taps = lax.dynamic_slice_in_dim(all_taps, ch_place * chans, chans, 2)
    sum_skip = lax.dynamic_slice_in_dim(all_skip, ch_place * chans, chans, 0)
    return (
        result,
        grad_input,
        sum_in,
        sum_out,
        sum_up,
        sum_down,
        sum_gain_one,
        sum_gain_two,
        sum_taps,
        sum_skip,
        sum_first,
        sum_bias,
        sum_freq,
        sum_second,
    )


def slice_body(
    tokens,
    lengths,
    in_weight,
    out_weight,
    up_weight,
    down_weight,
    gain_one,
    gain_two,
    conv_taps,
    skip_gain,
    filter_first,
    filter_bias,
    frequency,
    filter_second,
    cotangent,
):
    ch_place = lax.axis_index("ch")
    seq_place = lax.axis_index("seq")
    size = tokens.shape[1]
    buckets = tokens.shape[2]
    width = tokens.shape[3]
    chans = skip_gain.shape[0]
    length = size * 8
    rows = size * buckets
    part = gain_one.shape[0]
    emb, filt_width = filter_first.shape
    tables = tuple(jnp.asarray(one) for one in block_tables(size))

    lane = jnp.arange(chans) // part == seq_place
    gains = jnp.stack([gain_one, gain_two]).astype(F32)
    gains = jnp.where(lane[None, :], jnp.tile(gains, (1, chans // part)), 0.0)
    pack = jnp.concatenate([conv_taps.reshape(9, chans), skip_gain[None], gains, jnp.zeros((4, chans), F32)])
    by_bucket = jnp.swapaxes(tokens[0], 0, 1)
    consts, halo, full_in, columns = start_call(
        pack, by_bucket[:, size - 16 :], (in_weight, out_weight, up_weight, down_weight)
    )

    full_gain_one = consts[10]

    local = ch_place * size + jnp.arange(size, dtype=jnp.int32)
    mask = (local[None, :] < lengths[0][:, None]).astype(F32).reshape(rows, 1)
    before = ch_place * size - 16 + jnp.arange(16, dtype=jnp.int32)
    inside = (before[None, :] < lengths[0][:, None]) & (before >= 0)[None, :]
    x_zero = by_bucket.reshape(rows, width).astype(F32) * mask
    x_before = halo.reshape(16 * buckets, width).astype(F32) * inside.astype(F32).reshape(16 * buckets, 1)
    normed_one = layer_norm(x_zero, full_gain_one).astype(BF)
    normed_before = layer_norm(x_before, full_gain_one).astype(BF)
    streams = jnp.dot(
        jnp.concatenate([normed_one, normed_before]), full_in, preferred_element_type=F32
    ).astype(BF)

    table = positions_table(length, emb)
    hidden = filter_hidden(filter_first, filter_bias, frequency, table)
    decay = decay_table(length, ch_place * chans, chans, width)
    filt = jnp.dot(hidden, filter_second, precision=HIGH) * decay
    filt_blocks = filt.reshape(8, size, chans)

    wide_mask = jnp.broadcast_to(mask, (rows, 128))
    (mixer, kept, convolved), (full_out, full_up, early) = forward_call(
        streams, consts, wide_mask, filt_blocks, tables, columns, size
    )
    grad_result = jnp.swapaxes(cotangent[0], 0, 1).reshape(rows, width)
    result, grad_after, grad_mixer, grad_gain_two, grad_out, column_down, grad_up = feed_forward_call(
        mixer, by_bucket.reshape(rows, width), wide_mask, grad_result, consts, full_out, full_up, early, columns[2]
    )
    result = jnp.swapaxes(result.reshape(buckets, size, width), 0, 1).reshape(1, size, buckets, width)

    (grad_projected, grad_filt, sums), (sum_down, *late) = backward_call(
        streams, consts, wide_mask, grad_mixer, convolved, kept, filt_blocks, tables, (column_down, grad_up, grad_out), size
    )
    grad_in = jnp.dot(normed_one.T, grad_projected, preferred_element_type=F32).astype(BF)
    grad_normed_one = jnp.dot(grad_projected, full_in.T, preferred_element_type=F32)
    _, norm_one_pull = jax.vjp(layer_norm, x_zero, full_gain_one)
    grad_zero_part, grad_gain_one = norm_one_pull(grad_normed_one)
    grad_input = ((grad_after + grad_zero_part) * mask).astype(BF)
    grad_input = jnp.swapaxes(grad_input.reshape(buckets, size, width), 0, 1).reshape(1, size, buckets, width)

    grad_raw = grad_filt.reshape(length, chans) * decay
    grad_second = jnp.dot(hidden.T, grad_raw, precision=HIGH)
    grad_hidden = jnp.dot(grad_raw, filter_second.T, precision=HIGH)

    def hidden_of(first_layer, first_shift, freq_values):
        return filter_hidden(first_layer, first_shift, freq_values, table)

    _, hidden_pull = jax.vjp(hidden_of, filter_first, filter_bias, frequency)
    grad_first, grad_bias, grad_freq = hidden_pull(grad_hidden)
    vec = jnp.concatenate([sums[:10], grad_gain_one[None], grad_gain_two, jnp.zeros((4, width), F32)])
    fst = jnp.concatenate([grad_first, grad_bias[None], grad_freq[None]])
    fst = jnp.pad(fst, ((0, -fst.shape[0] % 8), (0, 128 - filt_width)))
    sum_in, small, (sum_up, sum_out) = scatter_sums(grad_in, vec, grad_second, fst, late)
    gain_sums = lax.dynamic_slice_in_dim(small[10:12], seq_place * part, part, 1)
    return (
        result,
        grad_input,
        sum_in,
        sum_out,
        sum_up,
        sum_down,
        gain_sums[0],
        gain_sums[1],
        small[:9].reshape(3, 3, chans),
        small[9],
        small[16 : 16 + emb, :filt_width],
        small[16 + emb, :filt_width],
        small[17 + emb, :filt_width],
        small[16 + fst.shape[0] :],
    )


def solution(mesh):
    placed = (
        P("seq", "ch", None, None),
        P("seq", None),
        P(("ch", "seq"), None),
        P(("ch", "seq"), None),
        P(("ch", "seq"), None),
        P(("ch", "seq"), None),
        P(("ch", "seq")),
        P(("ch", "seq")),
        P(None, None, "ch"),
        P("ch"),
        P(),
        P(),
        P(),
        P(None, "ch"),
        P("seq", "ch", None, None),
    )
    custom = dict(mesh.shape) == {"ch": 8, "seq": 4}
    return jax.shard_map(
        slice_body if custom else general_body,
        mesh=mesh,
        in_specs=placed,
        out_specs=(
            P("seq", "ch", None, None),
            P("seq", "ch", None, None),
            P(("ch", "seq"), None),
            P(("ch", "seq"), None),
            P(("ch", "seq"), None),
            P(("ch", "seq"), None),
            P(("ch", "seq")),
            P(("ch", "seq")),
            P(None, None, "ch"),
            P("ch"),
            P(),
            P(),
            P(),
            P(None, "ch"),
        ),
        check_vma=False,
    )
```

```python
import functools
import math

import jax
import jax.numpy as jnp
import numpy as np
from jax import lax
from jax.experimental import pallas as pl
from jax.experimental.pallas import tpu as pltpu
from jax.sharding import PartitionSpec as P

EPS = 1e-05
SLOW_RATE = math.log(100.0) / 1.5
FAST_RATE = math.log(100.0) / 0.3
HIGH = lax.Precision.HIGHEST
BF = jnp.bfloat16
F32 = jnp.float32
MESH = pl.DeviceIdType.MESH
VMEM_LIMIT = 62 << 20
OWN = 256
SHARE = 0.72
SHARE_BACK = 0.56
EARLY, LATE = range(0, 2), range(2, 4)


def layer_norm(values, gain):
    centre = values - jnp.mean(values, axis=-1, keepdims=True)
    spread = jnp.mean(centre * centre, axis=-1, keepdims=True)
    return centre * lax.rsqrt(spread + EPS) * gain


def positions_table(length, features):
    steps = jnp.arange(length).astype(jnp.float32)
    scaled = steps / (length - 1)
    bands = (features - 1) // 2
    freqs = 0.0001 + (bands - 1 - 0.0001) * jnp.arange(bands).astype(jnp.float32) / (bands - 1)
    angles = freqs[None, :] * (2.0 * math.pi * steps / length)[:, None]
    return jnp.concatenate([scaled[:, None], jnp.cos(angles), -jnp.sin(angles)], axis=1)


def decay_table(length, chan_start, count, width):
    scaled = jnp.arange(length).astype(jnp.float32) / (length - 1)
    chans = (chan_start + jnp.arange(count)).astype(jnp.float32)
    rates = SLOW_RATE + (FAST_RATE - SLOW_RATE) * chans / (width - 1)
    return jnp.exp(-scaled[:, None] * rates[None, :])


def filter_hidden(filter_first, filter_bias, frequency, table):
    inner = jnp.dot(table, filter_first, precision=HIGH) + filter_bias
    return jnp.sin(frequency * inner)


def block_tables(size):
    k = np.arange(size)[:, None]
    t = np.arange(size)[None, :]
    angle = 2.0 * np.pi * ((k * t) % (2 * size)) / (2 * size)
    real = np.cos(angle)
    imag = -np.sin(angle)
    imag[0] = np.where(np.arange(size) % 2 == 0, 1.0, -1.0)
    full = np.concatenate([real, imag], axis=0).astype(np.float32)
    high = full.astype(jnp.bfloat16)
    low = (full - high.astype(np.float32)).astype(jnp.bfloat16)
    weight = np.full((size, 1), 1.0 / size, np.float32)
    weight[0] = 0.5 / size
    sign = np.where(np.arange(size) % 2 == 0, 1.0, -1.0).astype(np.float32)[:, None]
    lanes = np.zeros((size, 128), np.float32)
    lanes[:, 0:1] = weight
    lanes[:, 1:2] = sign
    lanes[:, 2] = 1.0
    lanes[0, 2] = 0.0
    return high, low, high.T.copy(), low.T.copy(), lanes


def split_high(values):
    high = values.astype(BF)
    return high, (values - high.astype(F32)).astype(BF)


def mm(a, b):
    return jnp.dot(a, b, preferred_element_type=F32)


def spectra(fh, fl, source, target, blocks, piece=slice(None)):
    def step(i, carry):
        block = source[i, :, piece]
        target[i, :, piece] = mm(fh[...], block) + mm(fl[...], block)
        return carry

    lax.fori_loop(0, blocks, step, 0)


def filter_spectra(fh, fl, lanes, h_ref, abc, blocks, size):
    weight = lanes[:, 0:1]
    sign = lanes[:, 1:2]

    def step(j, carry):
        prev_re, prev_im = carry
        high, low = split_high(h_ref[j])
        now = mm(fh[...], high) + mm(fl[...], high) + mm(fh[...], low)
        now_re = now[:size]
        now_im = now[size:]
        abc[j, 0] = (now_re + sign * prev_re) * weight
        abc[j, 1] = (now_im + sign * prev_im) * weight
        return now_re, now_im

    zero = jnp.zeros((size, h_ref.shape[2]), F32)
    lax.fori_loop(0, blocks, step, (zero, zero))


def row_chunks(size, body):
    def step(i, carry):
        body(pl.multiple_of(i * 8, 8))
        return carry

    lax.fori_loop(0, size // 8, step, 0)


def load_filter(abc, lanes, here, blocks):
    keep = lanes[here, 2:3]
    a = [abc[j, 0, here] for j in range(blocks)]
    raw = [abc[j, 1, here] for j in range(blocks)]
    b = [one * keep for one in raw]
    c = [jnp.where(keep > 0.5, one, two) for one, two in zip(a, raw)]
    return a, b, c


def products_forward(xs, abc, lanes, out, blocks, size, pieces=None):
    width = abc.shape[3]
    for n in range(xs.shape[2] // width) if pieces is None else pieces:
        piece = slice(n * width, (n + 1) * width)

        def body(row, piece=piece):
            here, there = pl.ds(row, 8), pl.ds(size + row, 8)
            re = [xs[i, here, piece] for i in range(blocks)]
            im = [xs[i, there, piece] for i in range(blocks)]
            a, b, c = load_filter(abc, lanes, here, blocks)
            for m in range(blocks):
                sum_re = re[0] * a[m] - im[0] * b[m]
                sum_im = re[0] * b[m] + im[0] * c[m]
                for i in range(1, m + 1):
                    sum_re = sum_re + (re[i] * a[m - i] - im[i] * b[m - i])
                    sum_im = sum_im + (re[i] * b[m - i] + im[i] * c[m - i])
                out[m, here, piece] = sum_re
                out[m, there, piece] = sum_im

        row_chunks(size, body)


def products_backward(xs, ds, abc, gh, lanes, blocks, size, pieces=None):
    width = abc.shape[3]
    count = xs.shape[2] // width
    for n in range(count) if pieces is None else pieces:
        piece = slice(n * width, (n + 1) * width)

        def body(row, n=n, piece=piece):
            here, there = pl.ds(row, 8), pl.ds(size + row, 8)
            d_re = [ds[i, here, piece] for i in range(blocks)]
            d_im = [ds[i, there, piece] for i in range(blocks)]
            a, b, c = load_filter(abc, lanes, here, blocks)
            for i in range(blocks):
                sum_re = d_re[i] * a[0] + d_im[i] * b[0]
                sum_im = d_im[i] * c[0] - d_re[i] * b[0]
                for m in range(i + 1, blocks):
                    sum_re = sum_re + (d_re[m] * a[m - i] + d_im[m] * b[m - i])
                    sum_im = sum_im + (d_im[m] * c[m - i] - d_re[m] * b[m - i])
                ds[i, here, piece] = sum_re
                ds[i, there, piece] = sum_im
            x_re = [xs[i, here, piece] for i in range(blocks)]
            x_im = [xs[i, there, piece] for i in range(blocks)]
            weight = lanes[here, 0:1]
            sign = lanes[here, 1:2]
            keep = lanes[here, 2:3] > 0.5
            later_re = None
            later_im = None
            for j in range(blocks - 1, -1, -1):
                rr = d_re[j] * x_re[0]
                ii = d_im[j] * x_im[0]
                cross = d_im[j] * x_re[0] - d_re[j] * x_im[0]
                for i in range(1, blocks - j):
                    rr = rr + d_re[i + j] * x_re[i]
                    ii = ii + d_im[i + j] * x_im[i]
                    cross = cross + (d_im[i + j] * x_re[i] - d_re[i + j] * x_im[i])
                g_re = jnp.where(keep, rr + ii, rr) * weight
                g_im = jnp.where(keep, cross, ii) * weight
                if n:
                    g_re = g_re + gh[j, 0, here]
                    g_im = g_im + gh[j, 1, here]
                if n == count - 1 and later_re is not None:
                    gh[j, 0, here] = g_re + sign * later_re
                    gh[j, 1, here] = g_im + sign * later_im
                else:
                    gh[j, 0, here] = g_re
                    gh[j, 1, here] = g_im
                later_re, later_im = g_re, g_im

        row_chunks(size, body)


def inverse_of(th, tl, values):
    high, low = split_high(values)
    return mm(th[...], high) + mm(tl[...], high) + mm(th[...], low)


def inverse_blocks(th, tl, source, target, blocks, piece=slice(None)):
    def step(m, carry):
        target[m, :, piece] = inverse_of(th, tl, source[m, :, piece]).astype(target.dtype)
        return carry

    lax.fori_loop(0, blocks, step, 0)


def filter_gradient(th, tl, gh, out, blocks, size):
    def step(j, carry):
        re_high, re_low = split_high(gh[j, 0])
        im_high, im_low = split_high(gh[j, 1])
        left, right = th[:, :size], th[:, size:]
        total = mm(left, re_high) + mm(right, im_high) + mm(left, re_low) + mm(right, im_low)
        total = total + mm(tl[:, :size], re_high) + mm(tl[:, size:], im_high)
        out[j] = total
        return carry

    lax.fori_loop(0, blocks, step, 0)


def conv_forward_kernel(dims, x_ref, h_ref, fh, fl, th, tl, lanes, out, xs, abc):
    blocks, size, buckets, chans = dims
    filter_spectra(fh, fl, lanes, h_ref, abc, blocks, size)
    spectra(fh, fl, x_ref, xs, blocks)
    products_forward(xs, abc, lanes, xs, blocks, size)
    inverse_blocks(th, tl, xs, out, blocks)


def conv_backward_kernel(dims, d_ref, x_ref, h_ref, fh, fl, th, tl, lanes, out, dh_ref, xs, ds, abc, gh):
    blocks, size, buckets, chans = dims
    filter_spectra(fh, fl, lanes, h_ref, abc, blocks, size)
    spectra(fh, fl, x_ref, xs, blocks)
    spectra(fh, fl, d_ref, ds, blocks)
    products_backward(xs, ds, abc, gh, lanes, blocks, size)
    inverse_blocks(th, tl, ds, out, blocks)
    filter_gradient(th, tl, gh, dh_ref, blocks, size)


VM = pl.BlockSpec(memory_space=pltpu.VMEM)
ANYWHERE = pl.BlockSpec(memory_space=pl.ANY)


def conv_call(kernel, dims, operands, kinds, spectra_count):
    blocks, size, buckets, chans = dims
    cols = buckets * chans
    scratch = [pltpu.VMEM((blocks, 2 * size, cols), F32)] * spectra_count
    return pl.pallas_call(
        functools.partial(kernel, dims),
        out_shape=[jax.ShapeDtypeStruct((blocks, size, cols), kind) for kind in kinds],
        in_specs=[VM] * len(operands),
        out_specs=[VM] * len(kinds),
        scratch_shapes=scratch + [pltpu.VMEM((blocks, 2, size, cols), F32)] * spectra_count,
        compiler_params=pltpu.CompilerParams(vmem_limit_bytes=VMEM_LIMIT),
    )(*operands)


def rows_to_blocks(rows, dims):
    blocks, size, buckets, chans = dims
    moved = lax.all_to_all(rows.reshape(buckets, size, blocks, chans), "ch", split_axis=2, concat_axis=0)
    return jnp.transpose(moved, (0, 2, 1, 3)).reshape(blocks, size, buckets * chans)


def blocks_to_rows(values, dims):
    blocks, size, buckets, chans = dims
    moved = lax.all_to_all(values.reshape(blocks, size, buckets, chans), "ch", split_axis=0, concat_axis=0)
    return jnp.transpose(moved, (2, 1, 0, 3)).reshape(buckets * size, blocks * chans)


def conv_forward(rows, filt, tables, dims):
    kept = rows_to_blocks(rows, dims)
    (out,) = conv_call(conv_forward_kernel, dims, (kept, filt) + tables, (BF,), 1)
    return blocks_to_rows(out, dims), kept


def conv_backward(rows, kept, filt, tables, dims):
    moved = rows_to_blocks(rows, dims)
    out, dfilt = conv_call(conv_backward_kernel, dims, (moved, kept, filt) + tables, (BF, F32), 2)
    return blocks_to_rows(out, dims), dfilt


class Place:
    def __init__(self):
        self.ch = lax.axis_index("ch")
        self.seq = lax.axis_index("seq")
        self.z, self.x = self.ch // 2, lax.rem(self.ch, 2)
        self.y, self.core = self.seq // 2, lax.rem(self.seq, 2)
        self.sibling = {"seq": self.y * 2 + (1 - self.core)}
        self.along_y = {"seq": (1 - self.y) * 2 + self.core}
        self.along_x = {"ch": self.z * 2 + (1 - self.x)}
        self.others = [self.z + 1 - 2 * lax.rem(self.z, 2), lax.rem(self.z + 2, 4), 3 - self.z]
        self.along_z = [{"ch": one * 2 + self.x} for one in self.others]
        self.ch_ahead = [lax.rem(self.ch + d, 8) for d in range(1, 8)]
        self.seq_ahead = [lax.rem(self.seq + d, 4) for d in range(1, 4)]


def greet(ids):
    barrier = pltpu.get_barrier_semaphore()
    for one in ids:
        pl.semaphore_signal(barrier, inc=1, device_id=one, device_id_type=MESH)
    pl.semaphore_wait(barrier, len(ids))


def wait_all(copies):
    for copy in copies:
        copy.wait()


def fetching(kernel, fetch):
    def wrapped(*refs):
        count = len(fetch)
        refs, places, sems = list(refs[: -2 * count]), refs[-2 * count : -count], refs[-count:]
        loads = {}
        for n, i in enumerate(fetch):
            loads[i] = pltpu.make_async_copy(refs[i], places[n], sems[n])
            loads[i].start()
            refs[i] = places[n]
        return kernel(loads, *refs)

    return wrapped


def fetch_scratch(operands, fetch):
    places = [pltpu.VMEM(operands[i].shape, operands[i].dtype) for i in fetch]
    return places + [pltpu.SemaphoreType.DMA] * len(fetch)


def fetch_specs(operands, fetch):
    return [ANYWHERE if i in fetch else VM for i in range(len(operands))]


def push(src, dst, send, recv, device):
    copy = pltpu.make_async_remote_copy(
        src_ref=src, dst_ref=dst, send_sem=send, recv_sem=recv, device_id=device, device_id_type=MESH
    )
    copy.start()
    return copy


def split_columns(cols, share):
    return int(cols * share / 128 + 0.5) * 128


class Columns:
    SLOTS = 3

    def __init__(self, place, shards, columns, send, recv, local):
        self.p, self.shards, self.columns = place, shards, columns
        self.send, self.recv, self.local = send, recv, local
        self.copies = {}

    def go(self, i, slot, src, dst, device):
        self.copies[(i, slot)] = push(src, dst, self.send.at[i, slot], self.recv.at[i, slot], device)

    def start(self):
        p = self.p
        for i, shard in enumerate(self.shards):
            mine = self.columns[i].at[p.z]
            self.go(i, 1, shard, mine, p.along_z[1])
            self.go(i, 0, shard, mine, p.along_z[0])
            copy = pltpu.make_async_copy(shard, mine, self.local.at[i])
            copy.start()
            self.copies[(i, 3)] = copy

    def pass_far(self):
        p = self.p
        for i in range(len(self.shards)):
            self.copies[(i, 1)].wait_recv()
            here = self.columns[i].at[p.others[1]]
            self.go(i, 2, here, here, p.along_z[0])

    def finish(self):
        for (i, slot), copy in self.copies.items():
            if slot == 1:
                copy.wait_send()
            else:
                copy.wait()

    @classmethod
    def scratch(cls, count):
        return [
            pltpu.SemaphoreType.DMA((count, cls.SLOTS)),
            pltpu.SemaphoreType.DMA((count, cls.SLOTS)),
            pltpu.SemaphoreType.DMA((count,)),
        ]


class Gather:
    SLOTS = 32

    def __init__(self, place, columns, fulls, share, send, recv, local, places=range(4), by_place=()):
        self.p, self.columns, self.fulls, self.share = place, columns, fulls, share
        self.places, self.by_place = places, by_place
        self.send, self.recv, self.local = send, recv, local
        self.copies = {}
        self.seen = set()

    def go(self, i, slot, src, dst, device):
        self.copies[(i, slot)] = push(src, dst, self.send.at[i, slot], self.recv.at[i, slot], device)

    def place(self, n):
        return self.p.z if n == 0 else self.p.others[n - 1]

    def arrays(self, n):
        return [i for i in range(len(self.fulls)) if i not in self.by_place or n in self.places]

    def plane(self, i, n):
        if i in self.by_place:
            return self.fulls[i].at[n - self.places[0]]
        return self.fulls[i].at[self.place(n)]

    def ends(self, i, n):
        p, zz = self.p, self.place(n)
        return self.columns[i].at[zz], self.plane(i, n).at[p.x, p.y, p.core]

    def start_y(self, places=range(4), arrays=None):
        for n in places:
            for i in self.arrays(n) if arrays is None else arrays:
                src, dst = self.ends(i, n)
                self.go(i, 4 + n, src, dst, self.p.along_y)
                self.go(i, 16 + n, src, dst, self.p.sibling)
                copy = pltpu.make_async_copy(src, dst, self.local.at[i, n])
                copy.start()
                self.copies[(i, 32 + n)] = copy

    def start_x(self, places=range(4), arrays=None):
        for n in places:
            for i in self.arrays(n) if arrays is None else arrays:
                src, dst = self.ends(i, n)
                self.go(i, n, src, dst, self.p.along_x)

    def pass_sides(self, n):
        p = self.p
        for i in self.arrays(n):
            full = self.plane(i, n)
            cols = full.shape[4]
            part = split_columns(cols, self.share)
            self.copies[(i, n)].wait_recv()
            whole = full.at[1 - p.x, p.y, p.core]
            some = full.at[1 - p.x, p.y, p.core, :, pl.ds(0, part)]
            self.go(i, 8 + n, some, some, p.along_y)
            self.go(i, 20 + n, whole, whole, p.sibling)
            self.copies[(i, 4 + n)].wait_recv()
            whole = full.at[p.x, 1 - p.y, p.core]
            some = full.at[p.x, 1 - p.y, p.core, :, pl.ds(part, cols - part)]
            self.go(i, 12 + n, some, some, p.along_x)
            self.go(i, 24 + n, whole, whole, p.sibling)

    def pass_last(self, n):
        p = self.p
        for i in self.arrays(n):
            self.copies[(i, 8 + n)].wait_recv()
            self.copies[(i, 12 + n)].wait_recv()
            whole = self.plane(i, n).at[1 - p.x, 1 - p.y, p.core]
            self.go(i, 28 + n, whole, whole, p.sibling)

    def arrived(self, n):
        for i in range(len(self.fulls)):
            for slot in (16, 20, 24, 28):
                self.copies[(i, slot + n)].wait_recv()
            self.copies.pop((i, 32 + n)).wait()
            self.seen.add((i, n))

    def finish(self):
        for (i, slot), copy in self.copies.items():
            if slot >= 32:
                copy.wait()
            else:
                copy.wait_send()
                if slot >= 16 and (i, slot % 4) not in self.seen:
                    copy.wait_recv()

    @classmethod
    def scratch(cls, count):
        return [
            pltpu.SemaphoreType.DMA((count, cls.SLOTS)),
            pltpu.SemaphoreType.DMA((count, cls.SLOTS)),
            pltpu.SemaphoreType.DMA((count, 4)),
        ]


def everyone(p):
    ids = []
    for d in range(8):
        for e in range(4):
            if d or e:
                ids.append({"ch": lax.rem(p.ch + d, 8), "seq": lax.rem(p.seq + e, 4)})
    return ids


def make_filter(p, table, first, second, shift, speed, hidden, filt, size):
    length = 8 * size
    lane = (lax.broadcasted_iota(jnp.int32, (1, 128), 1) + p.ch * 128).astype(F32)
    rate = SLOW_RATE + (FAST_RATE - SLOW_RATE) * lane / 1023.0

    def step(j, carry):
        rows = pl.ds(pl.multiple_of(j * size, size), size)
        inner = jnp.dot(table[rows], first[...], precision=HIGH, preferred_element_type=F32) + shift[...]
        wave = jnp.sin(speed[...] * inner)
        hidden[rows] = wave
        place = (lax.broadcasted_iota(jnp.int32, (size, 1), 0) + j * size).astype(F32) / (length - 1)
        filt[j] = jnp.dot(wave, second[...], precision=HIGH, preferred_element_type=F32) * jnp.exp(-place * rate)
        return carry

    lax.fori_loop(0, 8, step, 0)


def start_kernel(size, *refs):
    taps, skip, gains, tokens, table, first, second, shift, speed = refs[:9]
    shards = refs[9:12]
    consts, halo, hidden, filt, full = refs[12:17]
    columns = list(refs[17:19])
    pack, packs, send, recv, halo_sems, column_in, first_wide = refs[19:26]
    column_sems, later_sems, gather_sems = refs[26:29], refs[29:32], refs[32:]
    p = Place()
    ids = everyone(p)
    greet(ids)
    column = Columns(p, shards[:1], [column_in], *column_sems)
    later = Columns(p, shards[1:], columns, *later_sems)
    gather = Gather(p, [column_in], [full], 0.5, *gather_sems)
    column.start()
    pack[...] = jnp.zeros_like(pack)
    part = gains.shape[1]
    pack[10:12, :part] = gains[...].astype(F32)
    moved = pltpu.roll(pack[8:16], p.seq * part, 1)
    pack[8:16] = moved
    for n in range(9):
        pack[n : n + 1] = taps[n // 3, n % 3 : n % 3 + 1]
    pack[9:10] = skip[...]
    column.copies[(0, 3)].wait()
    gather.start_x([0])
    gather.start_y([0])
    copies = [push(pack, packs.at[p.ch, p.seq], send.at[n], recv.at[n], one) for n, one in enumerate(ids)]
    copies.append(push(tokens.at[:, pl.ds(size - 16, 16)], halo, halo_sems.at[0], halo_sems.at[1], {"ch": lax.rem(p.ch + 1, 8)}))
    packs[p.ch, p.seq] = pack[...]
    column.copies[(0, 0)].wait_recv()
    gather.start_x([1])
    gather.start_y([1])
    column.pass_far()
    gather.start_x([2])
    gather.start_y([2])
    gather.pass_sides(0)
    column.copies[(0, 2)].wait_recv()
    gather.start_x([3])
    gather.start_y([3])
    later.start()
    first_wide[...] = jnp.zeros_like(first_wide)
    first_wide[: first.shape[0]] = first[...]
    make_filter(p, table, first_wide, second, shift, speed, hidden, filt, size)
    later.pass_far()
    for n in range(1, 4):
        gather.pass_sides(n)
    for n in range(4):
        gather.pass_last(n)
    wait_all(copies)
    row = lax.broadcasted_iota(jnp.int32, (16, 128), 0)
    for c in range(8):
        one = packs[c, 0]
        total = one + packs[c, 1] + packs[c, 2] + packs[c, 3]
        consts[:, c * 128 : (c + 1) * 128] = jnp.where(row < 10, one, total)
    gather.finish()
    for slot in (0, 1, 2):
        column.copies[(0, slot)].wait_send()
    later.finish()


def start_call(taps, skip, gains, tokens, table, first, second, shift, speed, shards, size):
    rows, cols = shards[0].shape
    filt_width = second.shape[0]
    out = pl.pallas_call(
        functools.partial(start_kernel, size),
        out_shape=[
            jax.ShapeDtypeStruct((16, 1024), F32),
            jax.ShapeDtypeStruct((2, 16, 1024), BF),
            jax.ShapeDtypeStruct((8 * size, filt_width), F32),
            jax.ShapeDtypeStruct((8, size, 128), F32),
            jax.ShapeDtypeStruct((4, 2, 2, 2, rows, cols), BF),
        ]
        + [jax.ShapeDtypeStruct((4,) + one.shape, BF) for one in shards[1:]],
        in_specs=[VM] * 12,
        out_specs=[VM] * 4 + [ANYWHERE] + [VM] * 2,
        scratch_shapes=[
            pltpu.VMEM((16, 128), F32),
            pltpu.VMEM((8, 4, 16, 128), F32),
            pltpu.SemaphoreType.DMA((31,)),
            pltpu.SemaphoreType.DMA((31,)),
            pltpu.SemaphoreType.DMA((2,)),
            pltpu.VMEM((4, rows, cols), BF),
            pltpu.VMEM((table.shape[1], filt_width), F32),
        ]
        + Columns.scratch(1)
        + Columns.scratch(2)
        + Gather.scratch(1),
        compiler_params=pltpu.CompilerParams(collective_id=4, has_side_effects=True, vmem_limit_bytes=VMEM_LIMIT),
    )(taps, skip, gains, tokens, table, first, second, shift, speed, *shards)
    return out[:4], out[4].reshape(rows * 32, cols), out[5:]


def lagged(u, buf, b, stream, lane, size, width):
    at = pl.ds(pl.multiple_of(stream * width + lane, 128), 128)
    rows = size * 2
    buf[pl.ds(0, 16)] = u[pl.ds(rows + 16 * b, 16), at].astype(F32)
    buf[pl.ds(16, size)] = u[pl.ds(b * size, size), at].astype(F32)
    return buf[pl.ds(16, size)], buf[pl.ds(15, size)], buf[pl.ds(14, size)]


def short_conv(u, buf, consts, b, stream, lane, size, width):
    now, one, two = lagged(u, buf, b, stream, lane, size, width)
    at = pl.ds(lane, 128)
    return consts[stream : stream + 1, at] * now + consts[3 + stream : 4 + stream, at] * one + consts[
        6 + stream : 7 + stream, at
    ] * two


def make_pieces(p, make):
    for d in (1, 2, 3, 0):
        make(lax.rem(p.ch // 2 + d, 4))


def send_pieces(p, pieces, blocks_ref, b, send, recv, local, make=None):
    copies = []
    mine = p.ch // 2
    at = pl.ds(b * 128, 128)
    for d in (1, 2, 3, 0):
        pair = lax.rem(mine + d, 4)
        if make is not None:
            make(pair)
        for k in range(2):
            block = 2 * pair + k if d else (p.ch + 1 - 2 * lax.rem(p.ch, 2) if k == 0 else p.ch)
            far = lax.rem(block - p.ch + 8, 8)
            src, dst = pieces.at[block, :, at], blocks_ref.at[p.ch, :, at]
            if d == 0 and k == 1:
                copy = pltpu.make_async_copy(src, dst, local.at[b])
                copy.start()
                copies.append(copy)
            else:
                copies.append(push(src, dst, send.at[far, b], recv.at[far, b], {"ch": block}))
    return copies


def send_blocks(p, ys, blocks_ref, b, send, recv, local):
    at = pl.ds(b * 128, 128)
    copies = []
    for d in range(7):
        src, dst = ys.at[p.ch_ahead[d], :, at], blocks_ref.at[p.ch, :, at]
        copies.append(push(src, dst, send.at[d, b], recv.at[d, b], {"ch": p.ch_ahead[d]}))
    copy = pltpu.make_async_copy(ys.at[p.ch, :, at], blocks_ref.at[p.ch, :, at], local.at[b])
    copy.start()
    return copies + [copy]


def half(b):
    return slice(b * 128, (b + 1) * 128)


def fill_mask(p, lengths, mask, size, first):
    for b in range(2):
        place = lax.broadcasted_iota(jnp.int32, (size, 128), 0) + (p.ch * OWN + first)
        inside = jnp.where(place < lengths[0, b], 1.0, 0.0)
        mask[pl.ds(b * size, size)] = jnp.where(place < 0, 0.0, inside)


def norm_rows(values, gain):
    centre = values - jnp.mean(values, axis=1, keepdims=True)
    inverse = lax.rsqrt(jnp.mean(centre * centre, axis=1, keepdims=True) + EPS)
    return centre * inverse, inverse


def forward_kernel(size, loads, *refs):
    lengths, tokens, halo, consts, h_ref, fh, fl, th, tl, lanes, down_shard = refs[:11]
    columns = list(refs[11:13])
    w_in = refs[13]
    normed, u, mixer, kept, convolved, column_down, mask = refs[14:21]
    fulls = refs[21:24]
    weight, xs, abc, ys, pieces, gates, mixes, bufs, mask_before = refs[24:33]
    send, recv, local, send_back, recv_back, local_back = refs[33:39]
    weight_sems, column_sems, gather_sems = refs[39], refs[40:43], refs[43:]
    p = Place()
    width = 1024
    rows = 2 * size
    load = pltpu.make_async_copy(w_in, weight, weight_sems)
    load.start()
    greet([{"ch": one} for one in p.ch_ahead] + [p.sibling, p.along_y])
    column = Columns(p, [down_shard], [column_down], *column_sems)
    gather = Gather(p, columns + [column_down], fulls, SHARE, *gather_sems, places=EARLY, by_place=(2,))
    for i in (10, 11, 12):
        loads[i].wait()
    column.start()
    gather.start_x([0], arrays=(0, 1))
    gather.start_y([0], arrays=(0, 1))
    column.copies[(0, 3)].wait()
    gather.start_x([0], arrays=(2,))
    gather.start_y([0], arrays=(2,))
    gather.start_y([1], arrays=(0, 1))
    loads[1].wait()
    fill_mask(p, lengths, mask, size, 0)
    fill_mask(p, lengths, mask_before, 16, -16)
    gain = consts[10:11, :]

    def norm(i, carry):
        here = pl.ds(pl.multiple_of(i * 32, 32), 32)
        one, _ = norm_rows(tokens[here].astype(F32) * mask[here, 0:1], gain)
        normed[here] = (one * gain).astype(BF)
        return carry

    lax.fori_loop(0, rows // 32, norm, 0)
    before = halo[...].reshape(32, width).astype(F32) * mask_before[:, 0:1]
    before = (norm_rows(before, gain)[0] * gain).astype(BF)
    load.wait()

    def make(pair):
        for stream in range(3):
            at = pl.ds(pl.multiple_of(stream * width + pair * 256, 256), 256)
            u[pl.ds(0, rows), at] = mm(normed[...], weight[:, at]).astype(BF)
            u[pl.ds(rows, 32), at] = mm(before, weight[:, at]).astype(BF)
        for k in range(2):
            block = 2 * pair + k
            lane = pl.multiple_of(block * 128, 128)
            for b in range(2):
                gates[block, b] = short_conv(u, bufs.at[0], consts, b, 0, lane, size, width)
                key = short_conv(u, bufs.at[1], consts, b, 1, lane, size, width)
                mix = key * short_conv(u, bufs.at[2], consts, b, 2, lane, size, width)
                mixes[block, b] = mix
                pieces[block, :, half(b)] = mix.astype(BF)

    arriving = [send_pieces(p, pieces, kept, 0, send, recv, local, make)]
    arriving.append(send_pieces(p, pieces, kept, 1, send, recv, local))
    gather.start_x([1], arrays=(0, 1))
    loads[4].wait()
    filter_spectra(fh, fl, lanes, h_ref, abc, 8, size)
    gather.pass_sides(0)
    gather.start_y([2], arrays=(0, 1))
    leaving = []
    for b in range(2):
        wait_all(arriving[b])
        spectra(fh, fl, kept, xs, 8, half(b))
        products_forward(xs, abc, lanes, xs, 8, size, (b,))
        inverse_blocks(th, tl, xs, ys, 8, half(b))
        leaving.append(send_blocks(p, ys, convolved, b, send_back, recv_back, local_back))
        if b == 0:
            column.copies[(0, 0)].wait_recv()
            gather.start_x([1], arrays=(2,))
            gather.start_y([1], arrays=(2,))
            gather.start_x([2], arrays=(0, 1))
            column.pass_far()
    gather.pass_sides(1)
    gather.start_x([3], arrays=(0, 1))
    gather.start_y([3], arrays=(0, 1))
    gather.pass_sides(2)
    for b in range(2):
        rows = slice(b * size, (b + 1) * size)
        wait_all(leaving[b])
        for c in range(8):
            at = half(c)
            long_part = convolved[c, :, half(b)].astype(F32) + consts[9:10, at] * mixes[c, b]
            mixer[rows, at] = (gates[c, b] * long_part * mask[rows]).astype(BF)
    gather.pass_sides(3)
    for n in range(4):
        gather.pass_last(n)
    gather.finish()
    for slot in (0, 1, 2):
        column.copies[(0, slot)].wait_send()
    column.copies[(0, 2)].wait_recv()


def backward_kernel(size, count, loads, *refs):
    u, consts, mask, grad_mixer, convolved, kept, h_ref, fh, fl, th, tl, lanes = refs[:12]
    grads = refs[12 : 12 + count]
    du, dh_ref, sums = refs[12 + count : 15 + count]
    outs = refs[15 + count : 15 + 2 * count]
    rest = refs[15 + 2 * count :]
    xs, ds, abc, gh, pieces, arrived, returned, keys, values, dlongs, dcs, edge_out, edge_in, ends, bufs = rest[:15]
    send, recv, local, send_back, recv_back, local_back, edge_sems = rest[15:22]
    p = Place()
    width = 1024
    greet([{"ch": one} for one in p.ch_ahead] + [p.sibling, p.along_y])
    for i in (0, 2, 3):
        loads[i].wait()
    whole = [grads[0]] + [(one, 0, one.shape[5]) for one in grads[1:]]
    stops = [None] + list(outs[1:])
    scatter = Scatter(p, whole, [outs[0]] + [None] * (count - 1), stops, SHARE_BACK, rest[22:])
    scatter.start(1)
    scatter.start(2)
    sums[...] = jnp.zeros_like(sums)

    def grad_parts(block, b, rows, skip):
        at = pl.ds(pl.multiple_of(block * 128, 128), 128)
        take = max(rows, 16)
        masked = grad_mixer[pl.ds(b * size, take), at].astype(F32)[:rows] * mask[pl.ds(b * size, rows)]
        conv = convolved[block, :take, b * 128 : (b + 1) * 128].astype(F32)[:rows]
        return masked, conv + skip * (keys[block, b, :rows] * values[block, b, :rows])

    def make(pair):
        for k in range(2):
            make_block(2 * pair + k)

    def make_block(block):
        lane = pl.multiple_of(block * 128, 128)
        at = pl.ds(lane, 128)
        total = jnp.zeros((1, 128), F32)
        for b in range(2):
            rows = pl.ds(b * size, size)
            gate = short_conv(u, bufs.at[0], consts, b, 0, lane, size, width)
            key = short_conv(u, bufs.at[1], consts, b, 1, lane, size, width)
            value = short_conv(u, bufs.at[2], consts, b, 2, lane, size, width)
            keys[block, b] = key
            values[block, b] = value
            dlong = grad_mixer[rows, at].astype(F32) * mask[rows] * gate
            dlongs[block, b] = dlong
            pieces[block, :, b * 128 : (b + 1) * 128] = dlong.astype(BF)
            total = total + jnp.sum(dlong * (key * value), axis=0, keepdims=True)
        sums[9:10, at] = total

    arriving = [send_pieces(p, pieces, arrived, 0, send, recv, local, make)]
    arriving.append(send_pieces(p, pieces, arrived, 1, send, recv, local))
    scatter.core(1)
    loads[12].wait()
    scatter.turn(0)
    loads[6].wait()
    filter_spectra(fh, fl, lanes, h_ref, abc, 8, size)
    scatter.core(2)
    loads[5].wait()
    spectra(fh, fl, kept, xs, 8)
    leaving = []
    for b in range(2):
        wait_all(arriving[b])
        spectra(fh, fl, arrived, ds, 8, half(b))
        products_backward(xs, ds, abc, gh, lanes, 8, size, (b,))
        inverse_blocks(th, tl, ds, pieces, 8, half(b))
        leaving.append(send_blocks(p, pieces, returned, b, send_back, recv_back, local_back))
    filter_gradient(th, tl, gh, dh_ref, 8, size)
    scatter.third(0)
    loads[4].wait()
    wait_all(leaving[0])
    wait_all(leaving[1])

    def edges(c, carry):
        at = pl.ds(pl.multiple_of(c * 128, 128), 128)
        skip = consts[9:10, at]
        for b in range(2):
            masked, long_part = grad_parts(c, b, 8, skip)
            back = returned[c, :16, b * 128 : (b + 1) * 128].astype(F32)[:8]
            dmixed = back + skip * dlongs[c, b, :8]
            dmixed = dmixed[:2]
            edge_out[2 * b : 2 * b + 2, at] = (masked * long_part)[:2]
            edge_out[4 + 2 * b : 6 + 2 * b, at] = dmixed * values[c, b, :8][:2]
            edge_out[8 + 2 * b : 10 + 2 * b, at] = dmixed * keys[c, b, :8][:2]
        return carry

    lax.fori_loop(0, 8, edges, 0)
    edge = push(edge_out, edge_in, edge_sems.at[0], edge_sems.at[1], {"ch": lax.rem(p.ch + 7, 8)})
    scatter.first(1)
    scatter.first(2)

    def streams(c, carry):
        lane = pl.multiple_of(c * 128, 128)
        at = pl.ds(lane, 128)
        skip = consts[9:10, at]
        for b in range(2):
            masked, long_part = grad_parts(c, b, size, skip)
            dmixed = returned[c, :, b * 128 : (b + 1) * 128].astype(F32) + skip * dlongs[c, b]
            dcs[0, b, pl.ds(0, size)] = masked * long_part
            dcs[1, b, pl.ds(0, size)] = dmixed * values[c, b]
            dcs[2, b, pl.ds(0, size)] = dmixed * keys[c, b]
        for stream in range(3):
            out = pl.ds(pl.multiple_of(stream * width + lane, 128), 128)
            totals = [jnp.zeros((1, 128), F32)] * 3
            for b in range(2):
                dcs[stream, b, pl.ds(size, 8)] = jnp.zeros((8, 128), F32)
                parts = lagged(u, bufs.at[stream], b, stream, lane, size, width)
                grad = dcs[stream, b, pl.ds(0, size)]
                for lag in range(3):
                    totals[lag] = totals[lag] + jnp.sum(grad * parts[lag], axis=0, keepdims=True)
                total = consts[stream : stream + 1, at] * grad
                total = total + consts[3 + stream : 4 + stream, at] * dcs[stream, b, pl.ds(1, size)]
                total = total + consts[6 + stream : 7 + stream, at] * dcs[stream, b, pl.ds(2, size)]
                du[pl.ds(b * size, size), out] = total.astype(BF)
                ends[stream, b, :, at] = total[size - 16 :]
            for lag in range(3):
                row = 3 * lag + stream
                sums[row : row + 1, at] = totals[lag]
        return carry

    lax.fori_loop(0, 8, streams, 0)
    edge.wait()

    inside = jnp.where(p.ch < 7, 1.0, 0.0)
    for stream in range(3):
        one = consts[3 + stream : 4 + stream, :] * inside
        two = consts[6 + stream : 7 + stream, :] * inside
        out = slice(stream * width, (stream + 1) * width)
        for b in range(2):
            row = 4 * stream + 2 * b
            near, far = edge_in[row : row + 1, :], edge_in[row + 1 : row + 2, :]
            ends[stream, b, 14:15] = ends[stream, b, 14:15] + two * near
            ends[stream, b, 15:16] = ends[stream, b, 15:16] + one * near + two * far
            du[(b + 1) * size - 16 : (b + 1) * size, out] = ends[stream, b].astype(BF)
    scatter.second(1)
    scatter.second(2)
    scatter.last(0)


def nt(a, b):
    return lax.dot_general(a, b, (((1,), (1,)), ((), ())), preferred_element_type=F32)


def tn(a, b):
    return lax.dot_general(a, b, (((0,), (0,)), ((), ())), preferred_element_type=F32)


GELU_ONE = math.sqrt(2.0 / math.pi)
GELU_THREE = GELU_ONE * 0.044715


class Planes:
    def __init__(self, place, column, acc, one_a, one_b, two_a, two_b, send, recv):
        self.p, self.column = place, column
        self.acc, self.one_a, self.one_b, self.two_a, self.two_b = acc, one_a, one_b, two_a, two_b
        self.send, self.recv = send, recv
        self.copies = {}
        cols = acc.shape[4]
        half = split_columns(cols, 0.5)
        self.low, self.high = pl.ds(0, half), pl.ds(half, cols - half)

    def go(self, n, slot, src, dst, device):
        self.copies[(n, slot)] = push(src, dst, self.send.at[n, slot], self.recv.at[n, slot], device)

    def done(self, n, *slots):
        for slot in slots:
            self.copies[(n, slot)].wait()

    def core(self, n, made):
        self.go(n, 0, made.at[:, :, 1 - self.p.core], self.acc.at[n], self.p.sibling)

    def sides(self, n, made):
        p, acc = self.p, self.acc.at[n]
        self.done(n, 0)

        def step(k, carry):
            xx, yy = k // 2, lax.rem(k, 2)
            acc[xx, yy] = add_rows(acc[xx, yy], made[xx, yy, p.core])
            return carry

        lax.fori_loop(0, 4, step, 0)
        self.go(n, 1, acc.at[:, 1 - p.y, :, self.low], self.one_a.at[n], p.along_y)
        self.go(n, 2, acc.at[1 - p.x, :, :, self.high], self.one_b.at[n], p.along_x)

    def cross(self, n):
        p, acc = self.p, self.acc.at[n]
        low, high = self.low, self.high
        self.done(n, 1, 2)
        for k in range(2):
            acc[k, p.y, :, low] = add_rows(acc[k, p.y, :, low], self.one_a[n, k])
            acc[p.x, k, :, high] = add_rows(acc[p.x, k, :, high], self.one_b[n, k])
        self.go(n, 3, acc.at[1 - p.x, p.y, :, low], self.two_a.at[n], p.along_x)
        self.go(n, 4, acc.at[p.x, 1 - p.y, :, high], self.two_b.at[n], p.along_y)

    def last(self, n, zz):
        p, acc = self.p, self.acc.at[n]
        low, high = self.low, self.high
        self.done(n, 3, 4)
        self.column[zz, :, low] = add_rows(acc[p.x, p.y, :, low], self.two_a[n])
        self.column[zz, :, high] = add_rows(acc[p.x, p.y, :, high], self.two_b[n])

    @staticmethod
    def scratch(rows, cols):
        half = split_columns(cols, 0.5)
        return [
            pltpu.VMEM((4, 2, 2, rows, cols), BF),
            pltpu.VMEM((4, 2, rows, half), BF),
            pltpu.VMEM((4, 2, rows, cols - half), BF),
            pltpu.VMEM((4, rows, half), BF),
            pltpu.VMEM((4, rows, cols - half), BF),
            pltpu.SemaphoreType.DMA((4, 5)),
            pltpu.SemaphoreType.DMA((4, 5)),
        ]


def feed_forward_kernel(loads, *refs):
    mixer, tokens, mask, cot, consts, w_out, w_up, early, column = refs[:9]
    result, grad_after, grad_mixer, grad_gain, grad_out, sum_column, grad_up = refs[9:16]
    up, planes, late, total, unit, scale, normed, turned, da, pre, dact, act, dpre, kept_down, kept_up = refs[16:31]
    up_sem, plane_sems, out_sems = refs[31:34]
    gather_sems, scatter_refs = refs[34:37], refs[37:44]
    p = Place()
    greet([p.along_x, p.along_y, p.sibling])
    loads[8].wait()
    gather = Gather(p, [column], [late], 0.5, *gather_sems, places=LATE, by_place=(0,))
    gather.start_x(LATE)
    gather.start_y(LATE)
    sums = Planes(p, sum_column, *scatter_refs)
    weights = [pltpu.make_async_copy(w_up, up, up_sem)]
    weights += [pltpu.make_async_copy(early.at[n], planes.at[n], plane_sems.at[n]) for n in EARLY]
    for load in weights:
        load.start()
    gain = consts[11:12, :]
    loads[0].wait()
    loads[5].wait()
    total[...] = mm(mixer[...], w_out[...])
    loads[1].wait()
    loads[2].wait()
    loads[3].wait()

    def norm(i, carry):
        rows = pl.ds(pl.multiple_of(i * 32, 32), 32)
        zero = tokens[rows].astype(F32) * mask[rows, 0:1]
        value = zero + total[rows]
        total[rows] = value
        centre = value - jnp.mean(value, axis=1, keepdims=True)
        inverse = lax.rsqrt(jnp.mean(centre * centre, axis=1, keepdims=True) + EPS)
        one = centre * inverse
        unit[rows] = one
        scale[rows] = jnp.broadcast_to(inverse, (32, 128))
        normed[rows] = (one * gain).astype(BF)
        return carry

    lax.fori_loop(0, 16, norm, 0)
    turned[...] = normed[...].T
    wait_all(weights)
    writes = [None] * 4
    for n in range(4):
        zz = gather.place(n)
        cols = pl.ds(pl.multiple_of(zz * 1024, 1024), 1024)
        slot = n % 2
        made = kept_down.at[slot]
        pre[...] = mm(normed[...], up[:, cols])
        if n < 2:
            gather.pass_sides(n + 2)
            plane = planes.at[n]
        else:
            gather.arrived(n)
            plane = late.at[n - 2]
        if n > 0:
            sums.sides(n - 1, kept_down.at[1 - slot])
        dact[...] = nt(cot[...], plane[...].reshape(1024, 1024))

        def gelu(i, carry):
            rows = pl.ds(pl.multiple_of(i * 16, 16), 16)
            x = pre[rows]
            square = x * x
            t = jnp.tanh(x * (GELU_ONE + GELU_THREE * square))
            half = 0.5 + 0.5 * t
            value = x * half
            act[rows] = value.astype(BF)
            slope = half + value * (1.0 - t) * (GELU_ONE + 3.0 * GELU_THREE * square)
            dpre[rows] = (dact[rows] * slope).astype(BF)
            return carry

        lax.fori_loop(0, 32, gelu, 0)
        if n > 1:
            wait_all(writes[n - 2])
        made[...] = tn(act[...], cot[...]).astype(BF).reshape(2, 2, 2, 128, 1024)
        sums.core(n, made)
        total[...] += mm(act[...], plane[...].reshape(1024, 1024))
        if n > 1:
            sums.cross(n - 2)
        else:
            gather.pass_last(n + 2)
        back = nt(dpre[...], up[:, cols])
        da[...] = back if n == 0 else da[...] + back
        kept_up[slot] = mm(turned[...], dpre[...]).astype(BF)
        writes[n] = [pltpu.make_async_copy(kept_up.at[slot], grad_up.at[:, cols], out_sems.at[n])]
        for copy in writes[n]:
            copy.start()
    sums.sides(3, kept_down.at[1])
    sums.cross(2)
    sums.last(0, gather.place(0))

    def finish(i, gain_sum):
        rows = pl.ds(pl.multiple_of(i * 32, 32), 32)
        result[rows] = total[rows].astype(BF)
        one = unit[rows]
        back = da[rows]
        e = back * gain
        inner = e - jnp.mean(e, axis=1, keepdims=True) - one * jnp.mean(e * one, axis=1, keepdims=True)
        after = cot[rows].astype(F32) + scale[rows, 0:1] * inner
        grad_after[rows] = after
        normed[rows] = after.astype(BF)
        return gain_sum + jnp.sum(back * one, axis=0, keepdims=True)

    grad_gain[...] = lax.fori_loop(0, 16, finish, jnp.zeros((1, 1024), F32))
    grad_mixer[...] = nt(normed[...], w_out[...]).astype(BF)
    sums.cross(3)
    sums.last(1, gather.place(1))
    sums.last(2, gather.place(2))
    grad_out[...] = tn(mixer[...], normed[...]).astype(BF)
    for n in (2, 3):
        wait_all(writes[n])
    gather.finish()
    sums.last(3, gather.place(3))


def feed_forward_call(mixer, tokens, mask, cot, consts, w_out, w_up, early, column):
    rows, width = mixer.shape
    hidden = w_up.shape[1]
    wide = (rows, width)
    square = (width, width)
    part = column.shape[1:]
    operands = (mixer, tokens, mask, cot, consts, w_out, w_up, early, column)
    fetch = (0, 1, 2, 3, 5, 8)
    return pl.pallas_call(
        fetching(feed_forward_kernel, fetch),
        out_shape=[
            jax.ShapeDtypeStruct(wide, BF),
            jax.ShapeDtypeStruct(wide, F32),
            jax.ShapeDtypeStruct(wide, BF),
            jax.ShapeDtypeStruct((1, width), F32),
            jax.ShapeDtypeStruct(square, BF),
            jax.ShapeDtypeStruct((4,) + part, BF),
            jax.ShapeDtypeStruct((width, hidden), BF),
        ],
        in_specs=fetch_specs(operands[:6], fetch) + [ANYWHERE] * 3,
        out_specs=[VM] * 6 + [ANYWHERE],
        scratch_shapes=[
            pltpu.VMEM((width, hidden), BF),
            pltpu.VMEM((len(EARLY), 2, 2, 2) + part, BF),
            pltpu.VMEM((len(LATE), 2, 2, 2) + part, BF),
            pltpu.VMEM(wide, F32),
            pltpu.VMEM(wide, F32),
            pltpu.VMEM((rows, 128), F32),
            pltpu.VMEM(wide, BF),
            pltpu.VMEM((width, rows), BF),
            pltpu.VMEM(wide, F32),
            pltpu.VMEM(wide, F32),
            pltpu.VMEM(wide, F32),
            pltpu.VMEM(wide, BF),
            pltpu.VMEM(wide, BF),
            pltpu.VMEM((2, 2, 2, 2) + part, BF),
            pltpu.VMEM((2,) + square, BF),
            pltpu.SemaphoreType.DMA,
            pltpu.SemaphoreType.DMA((len(EARLY),)),
            pltpu.SemaphoreType.DMA((4,)),
        ]
        + Gather.scratch(1)
        + Planes.scratch(*part)
        + fetch_scratch(operands, fetch),
        compiler_params=pltpu.CompilerParams(collective_id=5, has_side_effects=True, vmem_limit_bytes=VMEM_LIMIT),
    )(*operands)


def exchange_sems():
    pieces = [pltpu.SemaphoreType.DMA((8, 2))] * 2 + [pltpu.SemaphoreType.DMA((2,))]
    return pieces + [pltpu.SemaphoreType.DMA((7, 2))] * 2 + [pltpu.SemaphoreType.DMA((2,))]


def forward_call(lengths, tokens, halo, consts, filt, tables, down_shard, columns, w_in, size):
    rows = 2 * size
    block = (8, size, 256)
    piece = (8, 2, size, 128)
    operands = (lengths, tokens, halo, consts, filt) + tables + (down_shard,) + tuple(columns)
    whole = [jax.ShapeDtypeStruct((4, 2, 2, 2) + one.shape[1:], BF) for one in columns]
    whole.append(jax.ShapeDtypeStruct((len(EARLY), 2, 2, 2) + down_shard.shape, BF))
    fetch = (1, 4, 10, 11, 12)
    out = pl.pallas_call(
        fetching(functools.partial(forward_kernel, size), fetch),
        out_shape=[
            jax.ShapeDtypeStruct((rows, 1024), BF),
            jax.ShapeDtypeStruct((rows + 32, 3072), BF),
            jax.ShapeDtypeStruct((rows, 1024), BF),
            jax.ShapeDtypeStruct(block, BF),
            jax.ShapeDtypeStruct(block, BF),
            jax.ShapeDtypeStruct((4,) + down_shard.shape, BF),
            jax.ShapeDtypeStruct((rows, 128), F32),
        ]
        + whole,
        in_specs=[pl.BlockSpec(memory_space=pltpu.SMEM)] + fetch_specs(operands, fetch)[1:] + [ANYWHERE],
        out_specs=[VM] * 7 + [ANYWHERE] * 3,
        scratch_shapes=[
            pltpu.VMEM(w_in.shape, BF),
            pltpu.VMEM((8, 2 * size, 256), F32),
            pltpu.VMEM((8, 2, size, 128), F32),
            pltpu.VMEM(block, BF),
            pltpu.VMEM(block, BF),
            pltpu.VMEM(piece, F32),
            pltpu.VMEM(piece, F32),
            pltpu.VMEM((3, size + 16, 128), F32),
            pltpu.VMEM((32, 128), F32),
        ]
        + exchange_sems()
        + [pltpu.SemaphoreType.DMA]
        + Columns.scratch(1)
        + Gather.scratch(3)
        + fetch_scratch(operands, fetch),
        compiler_params=pltpu.CompilerParams(collective_id=1, has_side_effects=True, vmem_limit_bytes=VMEM_LIMIT),
    )(*operands, w_in)
    return out[:7], [one.reshape(-1, one.shape[-1]) for one in out[7:9]] + [out[9]]


def backward_call(u, consts, mask, grad_mixer, convolved, kept, filt, tables, grads, size):
    rows = 2 * size
    block = (8, size, 256)
    piece = (8, 2, size, 128)
    operands = (u, consts, mask, grad_mixer, convolved, kept, filt) + tables
    count = len(grads)
    shapes = [grads[0].shape[1:]] + [(one.shape[0] // 32, one.shape[1]) for one in grads[1:]]
    views = [grads[0]] + [one.reshape((4, 2, 2, 2) + shape) for one, shape in zip(grads[1:], shapes[1:])]
    fetch = (0, 2, 3, 4, 5, 6, 12)
    operands = operands + tuple(views[:1])
    out = pl.pallas_call(
        fetching(functools.partial(backward_kernel, size, count), fetch),
        out_shape=[
            jax.ShapeDtypeStruct((rows, 3072), BF),
            jax.ShapeDtypeStruct((8, size, 128), F32),
            jax.ShapeDtypeStruct((16, 1024), F32),
        ]
        + [jax.ShapeDtypeStruct(shapes[0], F32)]
        + [jax.ShapeDtypeStruct((4,) + shape, BF) for shape in shapes[1:]],
        in_specs=fetch_specs(operands, fetch) + [ANYWHERE] * (count - 1),
        out_specs=[VM] * (3 + count),
        scratch_shapes=[
            pltpu.VMEM((8, 2 * size, 256), F32),
            pltpu.VMEM((8, 2 * size, 256), F32),
            pltpu.VMEM((8, 2, size, 128), F32),
            pltpu.VMEM((8, 2, size, 128), F32),
            pltpu.VMEM(block, BF),
            pltpu.VMEM(block, BF),
            pltpu.VMEM(block, BF),
            pltpu.VMEM(piece, F32),
            pltpu.VMEM(piece, F32),
            pltpu.VMEM(piece, F32),
            pltpu.VMEM((3, 2, size + 8, 128), F32),
            pltpu.VMEM((16, 1024), F32),
            pltpu.VMEM((16, 1024), F32),
            pltpu.VMEM((3, 2, 16, 1024), F32),
            pltpu.VMEM((3, size + 16, 128), F32),
        ]
        + exchange_sems()
        + [pltpu.SemaphoreType.DMA((2,))]
        + Scatter.scratch([shape + ("load" if n else "", n > 0) for n, shape in enumerate(shapes)], SHARE_BACK)
        + fetch_scratch(operands, fetch),
        compiler_params=pltpu.CompilerParams(collective_id=2, has_side_effects=True, vmem_limit_bytes=VMEM_LIMIT),
    )(*operands, *views[1:])
    return out[:3], out[3:]


def add_rows(target, other):
    return (target.astype(F32) + other.astype(F32)).astype(BF)


class Scatter:
    SLOTS = 11

    def __init__(self, place, grads, outs, columns, share, refs):
        self.p, self.grads, self.outs, self.columns, self.share = place, grads, outs, columns, share
        count = len(grads)
        self.bufs = []
        at = 0
        for one, column in zip(grads, columns):
            names = Scatter.names(self.kind(one), column is not None)
            self.bufs.append(dict(zip(names, refs[at : at + len(names)])))
            at += len(names)
        self.send, self.recv, self.local = refs[at : at + 3]
        self.copies = {}

    @staticmethod
    def kind(grad):
        if not isinstance(grad, tuple):
            return ""
        return "load" if len(grad) == 3 else "made"

    @staticmethod
    def names(whole, stops):
        before = ("acc", "one_a", "one_b", "two_a", "two_b") if whole else ()
        if whole == "load":
            before += ("own",)
        return before + (() if stops else ("three", "four"))

    def go(self, i, slot, src, dst, device):
        copy = push(src, dst, self.send.at[i, slot], self.recv.at[i, slot], device)
        self.copies[(i, slot)] = copy

    def done(self, i, *slots):
        for slot in slots:
            self.copies[(i, slot)].wait()

    def part(self, i, zz, core):
        ref, first, cols = self.grads[i]
        if cols == ref.shape[5]:
            return ref.at[zz, :, :, core]
        return ref.at[zz, :, :, core, :, pl.ds(first, cols)]

    def load(self, i, zz):
        own = self.bufs[i]["own"]
        copy = pltpu.make_async_copy(self.part(i, zz, self.p.core), own.at[zz % 2], self.local.at[i, zz])
        copy.start()
        self.copies[(i, "own", zz)] = copy

    def start(self, i):
        if self.kind(self.grads[i]) == "made":
            self.go(i, 0, self.grads[i][0].at[:, :, :, 1 - self.p.core], self.bufs[i]["acc"], self.p.sibling)
            return
        for zz in range(4):
            self.go(i, zz, self.part(i, zz, 1 - self.p.core), self.bufs[i]["acc"].at[zz], self.p.sibling)
        self.load(i, 0)
        self.load(i, 1)

    def halves(self, i):
        cols = self.grads[i][2]
        part = split_columns(cols, self.share)
        return pl.ds(0, part), pl.ds(part, cols - part)

    def core(self, i):
        p, acc = self.p, self.bufs[i]["acc"]
        if self.kind(self.grads[i]) == "made":
            made = self.grads[i][0]
            self.done(i, 0)

            def add(n, carry):
                zz, xx, yy = n // 4, lax.rem(n // 2, 2), lax.rem(n, 2)
                acc[zz, xx, yy] = add_rows(acc[zz, xx, yy], made[zz, xx, yy, p.core])
                return carry

            lax.fori_loop(0, 16, add, 0)
        else:
            self.add_loaded(i)
        low, high = self.halves(i)
        self.go(i, 4, acc.at[:, :, 1 - p.y, :, low], self.bufs[i]["one_a"], p.along_y)
        self.go(i, 5, acc.at[:, 1 - p.x, :, :, high], self.bufs[i]["one_b"], p.along_x)

    def add_loaded(self, i):
        acc, own = self.bufs[i]["acc"], self.bufs[i]["own"]
        for zz in range(4):
            self.copies[(i, "own", zz)].wait()
            self.done(i, zz)

            def step(n, carry, zz=zz):
                xx, yy = n // 2, lax.rem(n, 2)
                acc[zz, xx, yy] = add_rows(acc[zz, xx, yy], own[zz % 2, xx, yy])
                return carry

            lax.fori_loop(0, 4, step, 0)
            if zz < 2:
                self.load(i, zz + 2)

    def first(self, i):
        p, acc = self.p, self.bufs[i]["acc"]
        one_a, one_b = self.bufs[i]["one_a"], self.bufs[i]["one_b"]
        low, high = self.halves(i)
        self.done(i, 4, 5)

        def step(n, carry):
            zz, w = n // 2, lax.rem(n, 2)
            acc[zz, w, p.y, :, low] = add_rows(acc[zz, w, p.y, :, low], one_a[zz, w])
            acc[zz, p.x, w, :, high] = add_rows(acc[zz, p.x, w, :, high], one_b[zz, w])
            return carry

        lax.fori_loop(0, 8, step, 0)
        self.go(i, 6, acc.at[:, 1 - p.x, p.y, :, low], self.bufs[i]["two_a"], p.along_x)
        self.go(i, 7, acc.at[:, p.x, 1 - p.y, :, high], self.bufs[i]["two_b"], p.along_y)

    def second(self, i):
        p, acc = self.p, self.bufs[i]["acc"]
        two_a, two_b = self.bufs[i]["two_a"], self.bufs[i]["two_b"]
        low, high = self.halves(i)
        self.done(i, 6, 7)
        column = self.columns[i]

        def step(zz, carry):
            here = acc.at[zz, p.x, p.y] if column is None else column.at[zz]
            here[:, low] = add_rows(acc[zz, p.x, p.y, :, low], two_a[zz])
            here[:, high] = add_rows(acc[zz, p.x, p.y, :, high], two_b[zz])
            return carry

        lax.fori_loop(0, 4, step, 0)
        if column is None:
            self.turn(i)

    def sums(self, i, zz):
        if isinstance(self.grads[i], tuple):
            return self.bufs[i]["acc"].at[zz, self.p.x, self.p.y]
        return self.grads[i].at[zz]

    def turn(self, i):
        p, three = self.p, self.bufs[i]["three"]
        self.go(i, 8, self.sums(i, p.others[2]), three.at[0], p.along_z[0])
        self.go(i, 9, self.sums(i, p.others[0]), three.at[1], p.along_z[0])

    def third(self, i):
        p, three = self.p, self.bufs[i]["three"]
        self.done(i, 8, 9)
        far = self.sums(i, p.others[1])
        three[0] = add_rows(far[...], three[0])
        self.go(i, 10, three.at[0], self.bufs[i]["four"], p.along_z[1])

    def last(self, i):
        three, four = self.bufs[i]["three"], self.bufs[i]["four"]
        self.done(i, 10)
        total = self.sums(i, self.p.z)[...].astype(F32) + three[1].astype(F32) + four[...].astype(F32)
        if isinstance(self.grads[i], tuple):
            first, cols = self.grads[i][1:3]
            self.outs[i][:, first : first + cols] = total
        else:
            self.outs[i][...] = total

    @classmethod
    def scratch(cls, kinds, share):
        count = len(kinds)
        bufs = []
        for rows, cols, whole, stops in kinds:
            part = split_columns(cols, share)
            shapes = {
                "own": (2, 2, 2, rows, cols),
                "acc": (4, 2, 2, rows, cols),
                "one_a": (4, 2, rows, part),
                "one_b": (4, 2, rows, cols - part),
                "two_a": (4, rows, part),
                "two_b": (4, rows, cols - part),
                "three": (2, rows, cols),
                "four": (rows, cols),
            }
            bufs += [pltpu.VMEM(shapes[name], BF) for name in cls.names(whole, stops)]
        return bufs + [
            pltpu.SemaphoreType.DMA((count, cls.SLOTS)),
            pltpu.SemaphoreType.DMA((count, cls.SLOTS)),
            pltpu.SemaphoreType.DMA((count, 4)),
        ]


def small_sums(p, vec, sec, fst, gathered, send, recv):
    rows, more = vec.shape[0], fst.shape[0]
    copies = []
    for d in range(7):
        lane = pl.multiple_of(p.ch_ahead[d] * 128, 128)
        pairs = (
            (vec.at[:, pl.ds(lane, 128)], gathered.at[p.ch, pl.ds(0, rows)]),
            (fst, gathered.at[p.ch, pl.ds(rows, more)]),
        )
        for n, (src, dst) in enumerate(pairs):
            copies.append(push(src, dst, send.at[2 * d + n], recv.at[2 * d + n], {"ch": p.ch_ahead[d]}))
    gathered[p.ch, :rows] = vec[:, pl.ds(pl.multiple_of(p.ch * 128, 128), 128)]
    gathered[p.ch, rows:] = fst[...]
    return copies


def join_sums(p, sec, gathered, joined, send, recv):
    rows = gathered.shape[1]
    total = gathered[0]
    for n in range(1, 8):
        total = total + gathered[n]
    joined[p.seq, :rows] = total
    joined[p.seq, rows:] = sec[...]
    return [
        push(joined.at[p.seq], joined.at[p.seq], send.at[14 + d], recv.at[14 + d], {"seq": p.seq_ahead[d]})
        for d in range(3)
    ]


def tail_kernel(size, loads, *refs):
    normed, du, tokens, mask, consts, grad_after, sums, gain_two = refs[:8]
    dh, hidden, table, first, second, shift, speed = refs[8:15]
    columns = list(refs[15:17])
    w_in = refs[17]
    grad_input, out, small_out = refs[18:21]
    outs = list(refs[21:23])
    weight, turned, made, da, vec, sec, fst, gathered, joined, first_wide = refs[23:33]
    weight_sem, small_send, small_recv = refs[33:36]
    width = 1024
    p = Place()
    load = pltpu.make_async_copy(w_in, weight, weight_sem)
    load.start()
    greet([{"ch": one} for one in p.ch_ahead] + [{"seq": one} for one in p.seq_ahead])
    grads = [(made.at[n], n * width, width, None) for n in range(3)] + columns
    scatter = Scatter(p, grads, [out] * 3 + outs, [None] * 5, 0.5, refs[36:])
    loads[15].wait()
    loads[16].wait()
    for n in (3, 4):
        scatter.turn(n)
    loads[0].wait()
    turned[...] = normed[...].T
    loads[1].wait()

    def part(stream):
        made[stream] = mm(turned[...], du[:, stream * width : (stream + 1) * width]).astype(BF).reshape(made.shape[1:])
        scatter.start(stream)

    def back(stream):
        at = slice(stream * width, (stream + 1) * width)
        one = nt(du[:, at], weight[:, at])
        da[...] = one if stream == 0 else da[...] + one

    part(0)
    part(1)
    scatter.core(0)
    part(2)
    scatter.core(1)
    scatter.core(2)

    length = 8 * size
    lane = (lax.broadcasted_iota(jnp.int32, (1, 128), 1) + p.ch * 128).astype(F32)
    rate = SLOW_RATE + (FAST_RATE - SLOW_RATE) * lane / 1023.0
    emb, filt_width = first_wide.shape
    first_wide[...] = jnp.zeros_like(first_wide)
    first_wide[: first.shape[0]] = first[...]
    sec[...] = jnp.zeros_like(sec)
    fst[...] = jnp.zeros_like(fst)

    def high(a, b, dims):
        return lax.dot_general(a, b, ((dims), ((), ())), precision=HIGH, preferred_element_type=F32)

    def step(j, carry):
        rows = pl.ds(pl.multiple_of(j * size, size), size)
        place = (lax.broadcasted_iota(jnp.int32, (size, 1), 0) + j * size).astype(F32) / (length - 1)
        draw = dh[j] * jnp.exp(-place * rate)
        sec[...] += high(hidden[rows], draw, ((0,), (0,)))
        inner = high(table[rows], first_wide[...], ((1,), (0,))) + shift[...]
        q = high(draw, second[...], ((1,), (1,))) * jnp.cos(speed[...] * inner)
        scaled = q * speed[...]
        fst[:emb, :filt_width] += high(table[rows], scaled, ((0,), (0,)))
        fst[emb : emb + 1, :filt_width] += jnp.sum(scaled, axis=0, keepdims=True)
        fst[emb + 1 : emb + 2, :filt_width] += jnp.sum(q * inner, axis=0, keepdims=True)
        return carry

    for i in (8, 9, 10):
        loads[i].wait()
    load.wait()
    back(0)
    scatter.first(0)
    lax.fori_loop(0, 8, step, 0)
    scatter.first(1)
    back(1)
    back(2)
    scatter.second(0)
    scatter.first(2)
    for i in (2, 3, 5):
        loads[i].wait()
    gain = consts[10:11, :]

    def norm(i, total):
        rows = pl.ds(pl.multiple_of(i * 32, 32), 32)
        one, inverse = norm_rows(tokens[rows].astype(F32) * mask[rows, 0:1], gain)
        grad = da[rows]
        e = grad * gain
        inner = e - jnp.mean(e, axis=1, keepdims=True) - one * jnp.mean(e * one, axis=1, keepdims=True)
        grad_input[rows] = ((grad_after[rows] + inverse * inner) * mask[rows, 0:1]).astype(BF)
        return total + jnp.sum(grad * one, axis=0, keepdims=True)

    gain_one = lax.fori_loop(0, normed.shape[0] // 32, norm, jnp.zeros((1, width), F32))
    vec[...] = jnp.zeros_like(vec)
    vec[:10] = sums[:10]
    vec[10:11] = gain_one
    vec[11:12] = gain_two[...]
    small = small_sums(p, vec, sec, fst, gathered, small_send, small_recv)
    scatter.second(1)
    for n in (3, 4):
        scatter.third(n)
    scatter.third(0)
    scatter.second(2)
    scatter.third(1)
    wait_all(small)
    small = join_sums(p, sec, gathered, joined, small_send, small_recv)
    scatter.third(2)
    for n in (3, 4):
        scatter.last(n)
    scatter.last(0)
    scatter.last(1)
    scatter.last(2)
    wait_all(small)
    total = joined[0]
    for n in range(1, 4):
        total = total + joined[n]
    small_out[...] = total


def tail_call(operands, columns, w_in, size):
    rows, width = operands[0].shape
    emb, filt_width = operands[10].shape[1], operands[11].shape[1]
    part = w_in.shape[0] // 32
    small = 16 + emb + 8
    kinds = [(part, width, "made", False)] * 3 + [one.shape[1:] + ("", False) for one in columns]
    operands = tuple(operands) + tuple(columns)
    fetch = (0, 1, 2, 3, 5, 8, 9, 10, 15, 16)
    return pl.pallas_call(
        fetching(functools.partial(tail_kernel, size), fetch),
        out_shape=[
            jax.ShapeDtypeStruct((rows, width), BF),
            jax.ShapeDtypeStruct((part, 3 * width), F32),
            jax.ShapeDtypeStruct((small + filt_width, 128), F32),
        ]
        + [jax.ShapeDtypeStruct(one.shape[1:], F32) for one in columns],
        in_specs=fetch_specs(operands, fetch) + [ANYWHERE],
        out_specs=[VM] * 5,
        scratch_shapes=[
            pltpu.VMEM(w_in.shape, BF),
            pltpu.VMEM((width, rows), BF),
            pltpu.VMEM((3, 4, 2, 2, 2, part, width), BF),
            pltpu.VMEM((rows, width), F32),
            pltpu.VMEM((16, width), F32),
            pltpu.VMEM((filt_width, 128), F32),
            pltpu.VMEM((emb + 8, 128), F32),
            pltpu.VMEM((8, small, 128), F32),
            pltpu.VMEM((4, small + filt_width, 128), F32),
            pltpu.VMEM((emb, filt_width), F32),
            pltpu.SemaphoreType.DMA,
            pltpu.SemaphoreType.DMA((17,)),
            pltpu.SemaphoreType.DMA((17,)),
        ]
        + Scatter.scratch(kinds, 0.5)
        + fetch_scratch(operands, fetch),
        compiler_params=pltpu.CompilerParams(collective_id=3, has_side_effects=True, vmem_limit_bytes=VMEM_LIMIT),
    )(*operands, w_in)


def general_body(
    tokens,
    lengths,
    in_weight,
    out_weight,
    up_weight,
    down_weight,
    gain_one,
    gain_two,
    conv_taps,
    skip_gain,
    filter_first,
    filter_bias,
    frequency,
    filter_second,
    cotangent,
):
    ch_count = lax.axis_size("ch")
    ch_place = lax.axis_index("ch")
    size = tokens.shape[1]
    buckets = tokens.shape[2]
    width = tokens.shape[3]
    chans = skip_gain.shape[0]
    length = size * ch_count
    rows = size * buckets
    dims = (ch_count, size, buckets, chans)
    tables = tuple(jnp.asarray(one) for one in block_tables(size))

    def gather(shard):
        return lax.all_gather(shard, ("ch", "seq"), axis=0, tiled=True)

    full_in = gather(in_weight)
    full_gain_one = gather(gain_one).astype(F32)
    full_gain_two = gather(gain_two).astype(F32)
    full_out = gather(out_weight)
    full_up = gather(up_weight)
    full_down = gather(down_weight)

    local = ch_place * size + jnp.arange(size, dtype=jnp.int32)
    mask = (local[None, :] < lengths[0][:, None]).astype(F32).reshape(rows, 1)
    before = ch_place * size - 2 + jnp.arange(2, dtype=jnp.int32)
    mask_before = (before[None, :] < lengths[0][:, None]).astype(F32).reshape(2 * buckets, 1)
    chain = [(i, i + 1) for i in range(ch_count - 1)]
    halo = lax.ppermute(tokens[0, size - 2 :], "ch", chain)
    x_zero = jnp.swapaxes(tokens[0], 0, 1).reshape(rows, width).astype(F32) * mask
    x_before = jnp.swapaxes(halo, 0, 1).reshape(2 * buckets, width).astype(F32) * mask_before

    taps_full = lax.all_gather(conv_taps.reshape(9, chans), "ch", axis=1, tiled=True).reshape(3, 3, width)
    skip_full = lax.all_gather(skip_gain.reshape(1, chans), "ch", axis=1, tiled=True)

    table = positions_table(length, filter_first.shape[0])
    hidden = filter_hidden(filter_first, filter_bias, frequency, table)
    decay = decay_table(length, ch_place * chans, chans, width)
    filt = jnp.dot(hidden, filter_second, precision=HIGH) * decay
    filt_blocks = jnp.tile(filt.reshape(ch_count, size, chans), (1, 1, buckets))

    normed_one = layer_norm(x_zero, full_gain_one).astype(BF)
    normed_before = layer_norm(x_before, full_gain_one).astype(BF)
    streams = jnp.dot(normed_one, full_in, preferred_element_type=F32).astype(BF)
    streams_before = jnp.dot(normed_before, full_in, preferred_element_type=F32).astype(BF)
    lag = jnp.concatenate(
        [streams_before.reshape(buckets, 2, 3, width), streams.reshape(buckets, size, 3, width)], axis=1
    ).astype(F32)
    lag_zero, lag_one, lag_two = lag[:, 2:], lag[:, 1:-1], lag[:, :-2]
    conv = taps_full[0] * lag_zero + taps_full[1] * lag_one + taps_full[2] * lag_two
    gate = conv[:, :, 0].reshape(rows, width)
    key_part = conv[:, :, 1].reshape(rows, width)
    value_part = conv[:, :, 2].reshape(rows, width)
    mixed = key_part * value_part

    convolved, kept = conv_forward(mixed.astype(BF), filt_blocks, tables, dims)
    long_part = convolved.astype(F32) + skip_full * mixed
    mixer = (gate * long_part * mask).astype(BF)
    after_mix = x_zero + jnp.dot(mixer, full_out, preferred_element_type=F32)
    normed_two = layer_norm(after_mix, full_gain_two).astype(BF)
    inner_act = jnp.dot(normed_two, full_up, preferred_element_type=F32)
    active = jax.nn.gelu(inner_act).astype(BF)
    result = (after_mix + jnp.dot(active, full_down, preferred_element_type=F32)).astype(BF)
    result = jnp.swapaxes(result.reshape(buckets, size, width), 0, 1).reshape(1, size, buckets, width)

    grad_result = jnp.swapaxes(cotangent[0], 0, 1).reshape(rows, width)
    grad_active = jnp.dot(grad_result, full_down.T, preferred_element_type=F32)
    _, gelu_pull = jax.vjp(jax.nn.gelu, inner_act)
    grad_inner = gelu_pull(grad_active)[0].astype(BF)
    grad_down = jnp.dot(active.T, grad_result, preferred_element_type=F32)
    grad_up = jnp.dot(normed_two.T, grad_inner, preferred_element_type=F32)
    grad_normed_two = jnp.dot(grad_inner, full_up.T, preferred_element_type=F32)
    _, norm_two_pull = jax.vjp(layer_norm, after_mix, full_gain_two)
    grad_after_part, grad_gain_two = norm_two_pull(grad_normed_two)
    grad_after = grad_result.astype(F32) + grad_after_part
    grad_mix = grad_after.astype(BF)
    grad_out = jnp.dot(mixer.T, grad_mix, preferred_element_type=F32)
    grad_mixer = jnp.dot(grad_mix, full_out.T, preferred_element_type=F32).astype(BF)
    grad_masked = grad_mixer.astype(F32) * mask
    grad_gate = grad_masked * long_part
    grad_long = grad_masked * gate
    grad_skip = jnp.sum(grad_long * mixed, axis=0)
    grad_convolved, grad_filt = conv_backward(grad_long.astype(BF), kept, filt_blocks, tables, dims)
    grad_mixed = grad_convolved.astype(F32) + skip_full * grad_long
    grad_conv = jnp.stack([grad_gate, grad_mixed * value_part, grad_mixed * key_part], axis=1)
    grad_conv = grad_conv.reshape(buckets, size, 3, width)
    grad_taps = jnp.stack(
        [
            jnp.sum(grad_conv * lag_zero, axis=(0, 1)),
            jnp.sum(grad_conv * lag_one, axis=(0, 1)),
            jnp.sum(grad_conv * lag_two, axis=(0, 1)),
        ],
        axis=0,
    )
    next_rows = lax.ppermute(grad_conv[:, :2], "ch", [(j, i) for i, j in chain])
    ahead = jnp.concatenate([grad_conv, next_rows], axis=1)
    grad_streams = taps_full[0] * ahead[:, :-2] + taps_full[1] * ahead[:, 1:-1] + taps_full[2] * ahead[:, 2:]
    grad_projected = grad_streams.astype(BF).reshape(rows, 3 * width)
    grad_in = jnp.dot(normed_one.T, grad_projected, preferred_element_type=F32)
    grad_normed_one = jnp.dot(grad_projected, full_in.T, preferred_element_type=F32)
    _, norm_one_pull = jax.vjp(layer_norm, x_zero, full_gain_one)
    grad_zero_part, grad_gain_one = norm_one_pull(grad_normed_one)
    grad_input = ((grad_after + grad_zero_part) * mask).astype(BF)
    grad_input = jnp.swapaxes(grad_input.reshape(buckets, size, width), 0, 1).reshape(1, size, buckets, width)

    grad_filt = jnp.sum(grad_filt.reshape(length, buckets, chans), axis=1)
    grad_raw = grad_filt * decay
    grad_second = jnp.dot(hidden.T, grad_raw, precision=HIGH)
    grad_hidden = jnp.dot(grad_raw, filter_second.T, precision=HIGH)

    def hidden_of(first_layer, first_shift, freq_values):
        return filter_hidden(first_layer, first_shift, freq_values, table)

    _, hidden_pull = jax.vjp(hidden_of, filter_first, filter_bias, frequency)
    grad_first, grad_bias, grad_freq = hidden_pull(grad_hidden)

    sum_in, sum_out, sum_up, sum_down, sum_gain_one, sum_gain_two = (
        lax.psum_scatter(one, ("ch", "seq"), scatter_dimension=0, tiled=True)
        for one in (grad_in, grad_out, grad_up, grad_down, grad_gain_one, grad_gain_two)
    )
    sum_second = lax.psum(grad_second, "seq")
    all_taps, all_skip, sum_first, sum_bias, sum_freq = lax.psum(
        (grad_taps, grad_skip, grad_first, grad_bias, grad_freq), ("ch", "seq")
    )
    sum_taps = lax.dynamic_slice_in_dim(all_taps, ch_place * chans, chans, 2)
    sum_skip = lax.dynamic_slice_in_dim(all_skip, ch_place * chans, chans, 0)
    return (
        result,
        grad_input,
        sum_in,
        sum_out,
        sum_up,
        sum_down,
        sum_gain_one,
        sum_gain_two,
        sum_taps,
        sum_skip,
        sum_first,
        sum_bias,
        sum_freq,
        sum_second,
    )


def by_position(values, size):
    first, second = values[:size, None], values[size:, None]
    bucket = lax.broadcasted_iota(jnp.int32, (size, 2, values.shape[1]), 1)
    return jnp.where(bucket == 0, first, second)[None]


def filter_table(length, features):
    steps = np.arange(length).astype(np.float32)
    scaled = steps / np.float32(length - 1)
    bands = (features - 1) // 2
    freqs = np.float32(0.0001) + np.float32(bands - 1 - 0.0001) * np.arange(bands).astype(np.float32) / np.float32(bands - 1)
    angles = freqs[None, :] * (np.float32(2.0 * math.pi) * steps / np.float32(length))[:, None]
    table = np.concatenate([scaled[:, None], np.cos(angles), -np.sin(angles)], axis=1)
    return np.pad(table, ((0, 0), (0, -features % 8)))


def slice_body(
    tokens,
    lengths,
    in_weight,
    out_weight,
    up_weight,
    down_weight,
    gain_one,
    gain_two,
    conv_taps,
    skip_gain,
    filter_first,
    filter_bias,
    frequency,
    filter_second,
    cotangent,
):
    seq_place = lax.axis_index("seq")
    size = tokens.shape[1]
    buckets = tokens.shape[2]
    width = tokens.shape[3]
    chans = skip_gain.shape[0]
    length = size * 8
    rows = size * buckets
    part = gain_one.shape[0]
    emb, filt_width = filter_first.shape
    tables = tuple(jnp.asarray(one) for one in block_tables(size))

    by_bucket = jnp.swapaxes(tokens[0], 0, 1)
    flat = by_bucket.reshape(rows, width)
    wide_table = jnp.asarray(filter_table(length, emb))
    pads = wide_table.shape[1] - emb
    (consts, halo, hidden, filt), full_in, columns = start_call(
        conv_taps,
        skip_gain[None],
        jnp.stack([gain_one, gain_two]),
        by_bucket,
        wide_table,
        filter_first,
        filter_second,
        filter_bias[None],
        frequency[None],
        (in_weight, out_weight, up_weight),
        size,
    )
    (normed_one, streams, mixer, kept, convolved, column_down, wide_mask), (full_out, full_up, early) = forward_call(
        lengths, flat, halo, consts, filt, tables, down_weight, columns, full_in, size
    )
    grad_result = jnp.swapaxes(cotangent[0], 0, 1).reshape(rows, width)
    result, grad_after, grad_mixer, grad_gain_two, grad_out, sum_column, grad_up = feed_forward_call(
        mixer, flat, wide_mask, grad_result, consts, full_out, full_up, early, column_down
    )
    result = by_position(result, size)

    (grad_projected, grad_filt, sums), (sum_down, *late) = backward_call(
        streams, consts, wide_mask, grad_mixer, convolved, kept, filt, tables, (sum_column, grad_up, grad_out), size
    )
    grad_input, sum_in, small, sum_up, sum_out = tail_call(
        (normed_one, grad_projected, flat, wide_mask, consts, grad_after, sums, grad_gain_two)
        + (grad_filt, hidden, wide_table, filter_first, filter_second, filter_bias[None], frequency[None]),
        late,
        full_in,
        size,
    )
    grad_input = by_position(grad_input, size)
    after = 16 + emb + pads
    gain_sums = lax.dynamic_slice_in_dim(small[10:12], seq_place * part, part, 1)
    return (
        result,
        grad_input,
        sum_in,
        sum_out,
        sum_up,
        sum_down,
        gain_sums[0],
        gain_sums[1],
        small[:9].reshape(3, 3, chans),
        small[9],
        small[16 : 16 + emb, :filt_width],
        small[after, :filt_width],
        small[after + 1, :filt_width],
        small[after + 8 :],
    )


def solution(mesh):
    placed = (
        P("seq", "ch", None, None),
        P("seq", None),
        P(("ch", "seq"), None),
        P(("ch", "seq"), None),
        P(("ch", "seq"), None),
        P(("ch", "seq"), None),
        P(("ch", "seq")),
        P(("ch", "seq")),
        P(None, None, "ch"),
        P("ch"),
        P(),
        P(),
        P(),
        P(None, "ch"),
        P("seq", "ch", None, None),
    )
    custom = dict(mesh.shape) == {"ch": 8, "seq": 4}
    return jax.shard_map(
        slice_body if custom else general_body,
        mesh=mesh,
        in_specs=placed,
        out_specs=(
            P("seq", "ch", None, None),
            P("seq", "ch", None, None),
            P(("ch", "seq"), None),
            P(("ch", "seq"), None),
            P(("ch", "seq"), None),
            P(("ch", "seq"), None),
            P(("ch", "seq")),
            P(("ch", "seq")),
            P(None, None, "ch"),
            P("ch"),
            P(),
            P(),
            P(),
            P(None, "ch"),
        ),
        check_vma=False,
    )
```

```python
import functools
import math

import jax
import jax.numpy as jnp
import numpy as np
from jax import lax
from jax.experimental import pallas as pl
from jax.experimental.pallas import tpu as pltpu
from jax.sharding import PartitionSpec as P

EPS = 1e-05
SLOW_RATE = math.log(100.0) / 1.5
FAST_RATE = math.log(100.0) / 0.3
HIGH = lax.Precision.HIGHEST
BF = jnp.bfloat16
F32 = jnp.float32
MESH = pl.DeviceIdType.MESH
VMEM_LIMIT = 62 << 20
OWN = 256
SHARE = 0.85
SHARE_BACK = 0.69
EARLY, LATE = range(0, 1), range(1, 4)


def layer_norm(values, gain):
    centre = values - jnp.mean(values, axis=-1, keepdims=True)
    spread = jnp.mean(centre * centre, axis=-1, keepdims=True)
    return centre * lax.rsqrt(spread + EPS) * gain


def positions_table(length, features):
    steps = jnp.arange(length).astype(jnp.float32)
    scaled = steps / (length - 1)
    bands = (features - 1) // 2
    freqs = 0.0001 + (bands - 1 - 0.0001) * jnp.arange(bands).astype(jnp.float32) / (bands - 1)
    angles = freqs[None, :] * (2.0 * math.pi * steps / length)[:, None]
    return jnp.concatenate([scaled[:, None], jnp.cos(angles), -jnp.sin(angles)], axis=1)


def decay_table(length, chan_start, count, width):
    scaled = jnp.arange(length).astype(jnp.float32) / (length - 1)
    chans = (chan_start + jnp.arange(count)).astype(jnp.float32)
    rates = SLOW_RATE + (FAST_RATE - SLOW_RATE) * chans / (width - 1)
    return jnp.exp(-scaled[:, None] * rates[None, :])


def filter_hidden(filter_first, filter_bias, frequency, table):
    inner = jnp.dot(table, filter_first, precision=HIGH) + filter_bias
    return jnp.sin(frequency * inner)


def block_tables(size):
    k = np.arange(size)[:, None]
    t = np.arange(size)[None, :]
    angle = 2.0 * np.pi * ((k * t) % (2 * size)) / (2 * size)
    real = np.cos(angle)
    imag = -np.sin(angle)
    imag[0] = np.where(np.arange(size) % 2 == 0, 1.0, -1.0)
    full = np.concatenate([real, imag], axis=0).astype(np.float32)
    high = full.astype(jnp.bfloat16)
    low = (full - high.astype(np.float32)).astype(jnp.bfloat16)
    weight = np.full((size, 1), 1.0 / size, np.float32)
    weight[0] = 0.5 / size
    sign = np.where(np.arange(size) % 2 == 0, 1.0, -1.0).astype(np.float32)[:, None]
    lanes = np.zeros((size, 128), np.float32)
    lanes[:, 0:1] = weight
    lanes[:, 1:2] = sign
    lanes[:, 2] = 1.0
    lanes[0, 2] = 0.0
    return high, low, high.T.copy(), low.T.copy(), lanes


def split_high(values):
    high = values.astype(BF)
    return high, (values - high.astype(F32)).astype(BF)


def mm(a, b):
    return jnp.dot(a, b, preferred_element_type=F32)


def spectra(fh, fl, source, target, blocks, piece=slice(None)):
    def step(i, carry):
        block = source[i, :, piece]
        target[i, :, piece] = mm(fh[...], block) + mm(fl[...], block)
        return carry

    lax.fori_loop(0, blocks, step, 0)


def filter_spectra(fh, fl, lanes, h_ref, abc, blocks, size):
    weight = lanes[:, 0:1]
    sign = lanes[:, 1:2]

    def step(j, carry):
        prev_re, prev_im = carry
        high, low = split_high(h_ref[j])
        now = mm(fh[...], high) + mm(fl[...], high) + mm(fh[...], low)
        now_re = now[:size]
        now_im = now[size:]
        abc[j, 0] = (now_re + sign * prev_re) * weight
        abc[j, 1] = (now_im + sign * prev_im) * weight
        return now_re, now_im

    zero = jnp.zeros((size, h_ref.shape[2]), F32)
    lax.fori_loop(0, blocks, step, (zero, zero))


def row_chunks(size, body):
    def step(i, carry):
        body(pl.multiple_of(i * 8, 8))
        return carry

    lax.fori_loop(0, size // 8, step, 0)


def load_filter(abc, lanes, here, blocks):
    keep = lanes[here, 2:3]
    a = [abc[j, 0, here] for j in range(blocks)]
    raw = [abc[j, 1, here] for j in range(blocks)]
    b = [one * keep for one in raw]
    c = [jnp.where(keep > 0.5, one, two) for one, two in zip(a, raw)]
    return a, b, c


def products_forward(xs, abc, lanes, out, blocks, size, pieces=None):
    width = abc.shape[3]
    for n in range(xs.shape[2] // width) if pieces is None else pieces:
        piece = slice(n * width, (n + 1) * width)

        def body(row, piece=piece):
            here, there = pl.ds(row, 8), pl.ds(size + row, 8)
            re = [xs[i, here, piece] for i in range(blocks)]
            im = [xs[i, there, piece] for i in range(blocks)]
            a, b, c = load_filter(abc, lanes, here, blocks)
            for m in range(blocks):
                sum_re = re[0] * a[m] - im[0] * b[m]
                sum_im = re[0] * b[m] + im[0] * c[m]
                for i in range(1, m + 1):
                    sum_re = sum_re + (re[i] * a[m - i] - im[i] * b[m - i])
                    sum_im = sum_im + (re[i] * b[m - i] + im[i] * c[m - i])
                out[m, here, piece] = sum_re
                out[m, there, piece] = sum_im

        row_chunks(size, body)


def products_backward(xs, ds, abc, gh, lanes, blocks, size, pieces=None):
    width = abc.shape[3]
    count = xs.shape[2] // width
    for n in range(count) if pieces is None else pieces:
        piece = slice(n * width, (n + 1) * width)

        def body(row, n=n, piece=piece):
            here, there = pl.ds(row, 8), pl.ds(size + row, 8)
            d_re = [ds[i, here, piece] for i in range(blocks)]
            d_im = [ds[i, there, piece] for i in range(blocks)]
            a, b, c = load_filter(abc, lanes, here, blocks)
            for i in range(blocks):
                sum_re = d_re[i] * a[0] + d_im[i] * b[0]
                sum_im = d_im[i] * c[0] - d_re[i] * b[0]
                for m in range(i + 1, blocks):
                    sum_re = sum_re + (d_re[m] * a[m - i] + d_im[m] * b[m - i])
                    sum_im = sum_im + (d_im[m] * c[m - i] - d_re[m] * b[m - i])
                ds[i, here, piece] = sum_re
                ds[i, there, piece] = sum_im
            x_re = [xs[i, here, piece] for i in range(blocks)]
            x_im = [xs[i, there, piece] for i in range(blocks)]
            weight = lanes[here, 0:1]
            sign = lanes[here, 1:2]
            keep = lanes[here, 2:3] > 0.5
            later_re = None
            later_im = None
            for j in range(blocks - 1, -1, -1):
                rr = d_re[j] * x_re[0]
                ii = d_im[j] * x_im[0]
                cross = d_im[j] * x_re[0] - d_re[j] * x_im[0]
                for i in range(1, blocks - j):
                    rr = rr + d_re[i + j] * x_re[i]
                    ii = ii + d_im[i + j] * x_im[i]
                    cross = cross + (d_im[i + j] * x_re[i] - d_re[i + j] * x_im[i])
                g_re = jnp.where(keep, rr + ii, rr) * weight
                g_im = jnp.where(keep, cross, ii) * weight
                if n:
                    g_re = g_re + gh[j, 0, here]
                    g_im = g_im + gh[j, 1, here]
                if n == count - 1 and later_re is not None:
                    gh[j, 0, here] = g_re + sign * later_re
                    gh[j, 1, here] = g_im + sign * later_im
                else:
                    gh[j, 0, here] = g_re
                    gh[j, 1, here] = g_im
                later_re, later_im = g_re, g_im

        row_chunks(size, body)


def inverse_of(th, tl, values):
    high, low = split_high(values)
    return mm(th[...], high) + mm(tl[...], high) + mm(th[...], low)


def inverse_blocks(th, tl, source, target, blocks, piece=slice(None)):
    def step(m, carry):
        target[m, :, piece] = inverse_of(th, tl, source[m, :, piece]).astype(target.dtype)
        return carry

    lax.fori_loop(0, blocks, step, 0)


def filter_gradient(th, tl, gh, out, blocks, size):
    def step(j, carry):
        re_high, re_low = split_high(gh[j, 0])
        im_high, im_low = split_high(gh[j, 1])
        left, right = th[:, :size], th[:, size:]
        total = mm(left, re_high) + mm(right, im_high) + mm(left, re_low) + mm(right, im_low)
        total = total + mm(tl[:, :size], re_high) + mm(tl[:, size:], im_high)
        out[j] = total
        return carry

    lax.fori_loop(0, blocks, step, 0)


def conv_forward_kernel(dims, x_ref, h_ref, fh, fl, th, tl, lanes, out, xs, abc):
    blocks, size, buckets, chans = dims
    filter_spectra(fh, fl, lanes, h_ref, abc, blocks, size)
    spectra(fh, fl, x_ref, xs, blocks)
    products_forward(xs, abc, lanes, xs, blocks, size)
    inverse_blocks(th, tl, xs, out, blocks)


def conv_backward_kernel(dims, d_ref, x_ref, h_ref, fh, fl, th, tl, lanes, out, dh_ref, xs, ds, abc, gh):
    blocks, size, buckets, chans = dims
    filter_spectra(fh, fl, lanes, h_ref, abc, blocks, size)
    spectra(fh, fl, x_ref, xs, blocks)
    spectra(fh, fl, d_ref, ds, blocks)
    products_backward(xs, ds, abc, gh, lanes, blocks, size)
    inverse_blocks(th, tl, ds, out, blocks)
    filter_gradient(th, tl, gh, dh_ref, blocks, size)


VM = pl.BlockSpec(memory_space=pltpu.VMEM)
ANYWHERE = pl.BlockSpec(memory_space=pl.ANY)


def conv_call(kernel, dims, operands, kinds, spectra_count):
    blocks, size, buckets, chans = dims
    cols = buckets * chans
    scratch = [pltpu.VMEM((blocks, 2 * size, cols), F32)] * spectra_count
    return pl.pallas_call(
        functools.partial(kernel, dims),
        out_shape=[jax.ShapeDtypeStruct((blocks, size, cols), kind) for kind in kinds],
        in_specs=[VM] * len(operands),
        out_specs=[VM] * len(kinds),
        scratch_shapes=scratch + [pltpu.VMEM((blocks, 2, size, cols), F32)] * spectra_count,
        compiler_params=pltpu.CompilerParams(vmem_limit_bytes=VMEM_LIMIT),
    )(*operands)


def rows_to_blocks(rows, dims):
    blocks, size, buckets, chans = dims
    moved = lax.all_to_all(rows.reshape(buckets, size, blocks, chans), "ch", split_axis=2, concat_axis=0)
    return jnp.transpose(moved, (0, 2, 1, 3)).reshape(blocks, size, buckets * chans)


def blocks_to_rows(values, dims):
    blocks, size, buckets, chans = dims
    moved = lax.all_to_all(values.reshape(blocks, size, buckets, chans), "ch", split_axis=0, concat_axis=0)
    return jnp.transpose(moved, (2, 1, 0, 3)).reshape(buckets * size, blocks * chans)


def conv_forward(rows, filt, tables, dims):
    kept = rows_to_blocks(rows, dims)
    (out,) = conv_call(conv_forward_kernel, dims, (kept, filt) + tables, (BF,), 1)
    return blocks_to_rows(out, dims), kept


def conv_backward(rows, kept, filt, tables, dims):
    moved = rows_to_blocks(rows, dims)
    out, dfilt = conv_call(conv_backward_kernel, dims, (moved, kept, filt) + tables, (BF, F32), 2)
    return blocks_to_rows(out, dims), dfilt


class Place:
    def __init__(self):
        self.ch = lax.axis_index("ch")
        self.seq = lax.axis_index("seq")
        self.z, self.x = self.ch // 2, lax.rem(self.ch, 2)
        self.y, self.core = self.seq // 2, lax.rem(self.seq, 2)
        self.sibling = {"seq": self.y * 2 + (1 - self.core)}
        self.along_y = {"seq": (1 - self.y) * 2 + self.core}
        self.along_x = {"ch": self.z * 2 + (1 - self.x)}
        self.others = [self.z + 1 - 2 * lax.rem(self.z, 2), lax.rem(self.z + 2, 4), 3 - self.z]
        self.along_z = [{"ch": one * 2 + self.x} for one in self.others]
        self.ch_ahead = [lax.rem(self.ch + d, 8) for d in range(1, 8)]
        self.seq_ahead = [lax.rem(self.seq + d, 4) for d in range(1, 4)]


def greet(ids):
    barrier = pltpu.get_barrier_semaphore()
    for one in ids:
        pl.semaphore_signal(barrier, inc=1, device_id=one, device_id_type=MESH)
    pl.semaphore_wait(barrier, len(ids))


def wait_all(copies):
    for copy in copies:
        copy.wait()


def fetching(kernel, fetch, store=()):
    def wrapped(*refs):
        moved = tuple(fetch) + tuple(store)
        count = len(moved)
        refs, places, sems = list(refs[: -2 * count]), refs[-2 * count : -count], refs[-count:]
        moves = {}
        for n, i in enumerate(moved):
            ends = (refs[i], places[n]) if n < len(fetch) else (places[n], refs[i])
            moves[i] = pltpu.make_async_copy(*ends, sems[n])
            if n < len(fetch):
                moves[i].start()
            refs[i] = places[n]
        kernel(moves, *refs)
        for i in store:
            moves[i].wait()

    return wrapped


def fetch_scratch(operands, fetch, outs=(), store=()):
    arrays = [operands[i] for i in fetch] + [outs[i] for i in store]
    return [pltpu.VMEM(one.shape, one.dtype) for one in arrays] + [pltpu.SemaphoreType.DMA] * len(arrays)


def fetch_specs(operands, fetch):
    return [ANYWHERE if i in fetch else VM for i in range(len(operands))]


def push(src, dst, send, recv, device):
    copy = pltpu.make_async_remote_copy(
        src_ref=src, dst_ref=dst, send_sem=send, recv_sem=recv, device_id=device, device_id_type=MESH
    )
    copy.start()
    return copy


def split_columns(cols, share):
    return int(cols * share / 128 + 0.5) * 128


class Columns:
    SLOTS = 3

    def __init__(self, place, shards, columns, send, recv, local):
        self.p, self.shards, self.columns = place, shards, columns
        self.send, self.recv, self.local = send, recv, local
        self.copies = {}

    def go(self, i, slot, src, dst, device):
        self.copies[(i, slot)] = push(src, dst, self.send.at[i, slot], self.recv.at[i, slot], device)

    def start(self):
        p = self.p
        for i, shard in enumerate(self.shards):
            mine = self.columns[i].at[p.z]
            self.go(i, 1, shard, mine, p.along_z[1])
            self.go(i, 0, shard, mine, p.along_z[0])
            copy = pltpu.make_async_copy(shard, mine, self.local.at[i])
            copy.start()
            self.copies[(i, 3)] = copy

    def pass_far(self):
        p = self.p
        for i in range(len(self.shards)):
            self.copies[(i, 1)].wait_recv()
            here = self.columns[i].at[p.others[1]]
            self.go(i, 2, here, here, p.along_z[0])

    def finish(self):
        for (i, slot), copy in self.copies.items():
            if slot == 1:
                copy.wait_send()
            else:
                copy.wait()

    @classmethod
    def scratch(cls, count):
        return [
            pltpu.SemaphoreType.DMA((count, cls.SLOTS)),
            pltpu.SemaphoreType.DMA((count, cls.SLOTS)),
            pltpu.SemaphoreType.DMA((count,)),
        ]


class Gather:
    SLOTS = 32

    def __init__(self, place, columns, fulls, share, send, recv, local, places=range(4), by_place=()):
        self.p, self.columns, self.fulls, self.share = place, columns, fulls, share
        self.places, self.by_place = places, by_place
        self.send, self.recv, self.local = send, recv, local
        self.copies = {}
        self.seen = set()

    def go(self, i, slot, src, dst, device):
        self.copies[(i, slot)] = push(src, dst, self.send.at[i, slot], self.recv.at[i, slot], device)

    def place(self, n):
        return self.p.z if n == 0 else self.p.others[n - 1]

    def arrays(self, n):
        return [i for i in range(len(self.fulls)) if i not in self.by_place or n in self.places]

    def plane(self, i, n):
        if i in self.by_place:
            return self.fulls[i].at[n - self.places[0]]
        return self.fulls[i].at[self.place(n)]

    def ends(self, i, n):
        p, zz = self.p, self.place(n)
        return self.columns[i].at[zz], self.plane(i, n).at[p.x, p.y, p.core]

    def start_y(self, places=range(4), arrays=None):
        for n in places:
            for i in self.arrays(n) if arrays is None else arrays:
                src, dst = self.ends(i, n)
                self.go(i, 4 + n, src, dst, self.p.along_y)
                self.go(i, 16 + n, src, dst, self.p.sibling)
                copy = pltpu.make_async_copy(src, dst, self.local.at[i, n])
                copy.start()
                self.copies[(i, 32 + n)] = copy

    def start_x(self, places=range(4), arrays=None):
        for n in places:
            for i in self.arrays(n) if arrays is None else arrays:
                src, dst = self.ends(i, n)
                self.go(i, n, src, dst, self.p.along_x)

    def pass_sides(self, n):
        p = self.p
        for i in self.arrays(n):
            full = self.plane(i, n)
            cols = full.shape[4]
            part = split_columns(cols, self.share)
            self.copies[(i, n)].wait_recv()
            whole = full.at[1 - p.x, p.y, p.core]
            some = full.at[1 - p.x, p.y, p.core, :, pl.ds(0, part)]
            self.go(i, 8 + n, some, some, p.along_y)
            self.go(i, 20 + n, whole, whole, p.sibling)
            self.copies[(i, 4 + n)].wait_recv()
            whole = full.at[p.x, 1 - p.y, p.core]
            some = full.at[p.x, 1 - p.y, p.core, :, pl.ds(part, cols - part)]
            self.go(i, 12 + n, some, some, p.along_x)
            self.go(i, 24 + n, whole, whole, p.sibling)

    def pass_last(self, n):
        p = self.p
        for i in self.arrays(n):
            self.copies[(i, 8 + n)].wait_recv()
            self.copies[(i, 12 + n)].wait_recv()
            whole = self.plane(i, n).at[1 - p.x, 1 - p.y, p.core]
            self.go(i, 28 + n, whole, whole, p.sibling)

    def arrived(self, n):
        for i in range(len(self.fulls)):
            for slot in (16, 20, 24, 28):
                self.copies[(i, slot + n)].wait_recv()
            self.copies.pop((i, 32 + n)).wait()
            self.seen.add((i, n))

    def finish(self):
        for (i, slot), copy in self.copies.items():
            if slot >= 32:
                copy.wait()
            else:
                copy.wait_send()
                if slot >= 16 and (i, slot % 4) not in self.seen:
                    copy.wait_recv()

    @classmethod
    def scratch(cls, count):
        return [
            pltpu.SemaphoreType.DMA((count, cls.SLOTS)),
            pltpu.SemaphoreType.DMA((count, cls.SLOTS)),
            pltpu.SemaphoreType.DMA((count, 4)),
        ]


def everyone(p):
    ids = []
    for d in range(8):
        for e in range(4):
            if d or e:
                ids.append({"ch": lax.rem(p.ch + d, 8), "seq": lax.rem(p.seq + e, 4)})
    return ids


def make_filter(p, table, first, second, shift, speed, hidden, filt, size, start, stop):
    length = 8 * size
    lane = (lax.broadcasted_iota(jnp.int32, (1, 128), 1) + p.ch * 128).astype(F32)
    rate = SLOW_RATE + (FAST_RATE - SLOW_RATE) * lane / 1023.0

    def step(j, carry):
        rows = pl.ds(pl.multiple_of(j * size, size), size)
        inner = jnp.dot(table[rows], first[...], precision=HIGH, preferred_element_type=F32) + shift[...]
        wave = jnp.sin(speed[...] * inner)
        hidden[rows] = wave
        place = (lax.broadcasted_iota(jnp.int32, (size, 1), 0) + j * size).astype(F32) / (length - 1)
        filt[j] = jnp.dot(wave, second[...], precision=HIGH, preferred_element_type=F32) * jnp.exp(-place * rate)
        return carry

    lax.fori_loop(start, stop, step, 0)


def start_kernel(size, *refs):
    taps, skip, gains, tokens, table, first, second, shift, speed = refs[:9]
    shards = refs[9:12]
    consts, halo, hidden, filt = refs[12:16]
    full = refs[16]
    columns = list(refs[17:19])
    pack, packs, send, recv, halo_sems, column_in, first_wide = refs[19:26]
    column_sems, later_sems, gather_sems = refs[26:29], refs[29:32], refs[32:35]
    p = Place()
    ids = everyone(p)
    greet(ids)
    column = Columns(p, shards[:1], [column_in], *column_sems)
    later = Columns(p, shards[1:], columns, *later_sems)
    gather = Gather(p, [column_in], [full], 0.5, *gather_sems)
    column.start()
    pack[...] = jnp.zeros_like(pack)
    part = gains.shape[1]
    pack[10:12, :part] = gains[...].astype(F32)
    moved = pltpu.roll(pack[8:16], p.seq * part, 1)
    pack[8:16] = moved
    for n in range(9):
        pack[n : n + 1] = taps[n // 3, n % 3 : n % 3 + 1]
    pack[9:10] = skip[...]
    column.copies[(0, 3)].wait()
    gather.start_x([0])
    gather.start_y([0])
    copies = [push(pack, packs.at[p.ch, p.seq], send.at[n], recv.at[n], one) for n, one in enumerate(ids)]
    copies.append(push(tokens.at[:, pl.ds(size - 16, 16)], halo, halo_sems.at[0], halo_sems.at[1], {"ch": lax.rem(p.ch + 1, 8)}))
    packs[p.ch, p.seq] = pack[...]
    column.copies[(0, 0)].wait_recv()
    gather.start_x([1])
    gather.start_y([1])
    column.pass_far()
    gather.start_x([2])
    gather.start_y([2])
    gather.pass_sides(0)
    first_wide[...] = jnp.zeros_like(first_wide)
    first_wide[: first.shape[0]] = first[...]

    def filter_part(start):
        make_filter(p, table, first_wide, second, shift, speed, hidden, filt, size, start, start + 2)

    filter_part(0)
    filter_part(2)
    column.copies[(0, 2)].wait_recv()
    gather.start_x([3])
    gather.start_y([3])
    later.start()
    gather.pass_sides(1)
    gather.pass_sides(2)
    filter_part(4)
    gather.pass_sides(3)
    gather.pass_last(0)
    gather.pass_last(1)
    filter_part(6)
    gather.pass_last(2)
    later.pass_far()
    gather.pass_last(3)
    wait_all(copies)
    row = lax.broadcasted_iota(jnp.int32, (16, 128), 0)
    for c in range(8):
        one = packs[c, 0]
        total = one + packs[c, 1] + packs[c, 2] + packs[c, 3]
        consts[:, c * 128 : (c + 1) * 128] = jnp.where(row < 10, one, total)
    gather.finish()
    for slot in (0, 1, 2):
        column.copies[(0, slot)].wait_send()
    later.finish()


def start_call(taps, skip, gains, tokens, table, first, second, shift, speed, shards, size):
    rows, cols = shards[0].shape
    filt_width = second.shape[0]
    out = pl.pallas_call(
        functools.partial(start_kernel, size),
        out_shape=[
            jax.ShapeDtypeStruct((16, 1024), F32),
            jax.ShapeDtypeStruct((2, 16, 1024), BF),
            jax.ShapeDtypeStruct((8 * size, filt_width), F32),
            jax.ShapeDtypeStruct((8, size, 128), F32),
            jax.ShapeDtypeStruct((4, 2, 2, 2, rows, cols), BF),
            jax.ShapeDtypeStruct((4,) + shards[1].shape, BF),
            jax.ShapeDtypeStruct((4,) + shards[2].shape, BF),
        ],
        in_specs=[VM] * 12,
        out_specs=[VM] * 4 + [ANYWHERE] + [VM] * 2,
        scratch_shapes=[
            pltpu.VMEM((16, 128), F32),
            pltpu.VMEM((8, 4, 16, 128), F32),
            pltpu.SemaphoreType.DMA((31,)),
            pltpu.SemaphoreType.DMA((31,)),
            pltpu.SemaphoreType.DMA((2,)),
            pltpu.VMEM((4, rows, cols), BF),
            pltpu.VMEM((table.shape[1], filt_width), F32),
        ]
        + Columns.scratch(1)
        + Columns.scratch(2)
        + Gather.scratch(1),
        compiler_params=pltpu.CompilerParams(collective_id=4, has_side_effects=True, vmem_limit_bytes=VMEM_LIMIT),
    )(taps, skip, gains, tokens, table, first, second, shift, speed, *shards)
    return out[:4], out[4].reshape(rows * 32, cols), out[5:]


def lagged(u, buf, b, stream, lane, size, width):
    at = pl.ds(pl.multiple_of(stream * width + lane, 128), 128)
    rows = size * 2
    buf[pl.ds(0, 16)] = u[pl.ds(rows + 16 * b, 16), at].astype(F32)
    buf[pl.ds(16, size)] = u[pl.ds(b * size, size), at].astype(F32)
    return buf[pl.ds(16, size)], buf[pl.ds(15, size)], buf[pl.ds(14, size)]


def short_conv(u, buf, consts, b, stream, lane, size, width):
    now, one, two = lagged(u, buf, b, stream, lane, size, width)
    at = pl.ds(lane, 128)
    return consts[stream : stream + 1, at] * now + consts[3 + stream : 4 + stream, at] * one + consts[
        6 + stream : 7 + stream, at
    ] * two


def make_pieces(p, make):
    for d in (1, 2, 3, 0):
        make(lax.rem(p.ch // 2 + d, 4))


def send_pieces(p, pieces, blocks_ref, b, send, recv, local, make=None):
    copies = []
    mine = p.ch // 2
    at = pl.ds(b * 128, 128)
    for d in (1, 2, 3, 0):
        pair = lax.rem(mine + d, 4)
        if make is not None:
            make(pair)
        for k in range(2):
            block = 2 * pair + k if d else (p.ch + 1 - 2 * lax.rem(p.ch, 2) if k == 0 else p.ch)
            far = lax.rem(block - p.ch + 8, 8)
            src, dst = pieces.at[block, :, at], blocks_ref.at[p.ch, :, at]
            if d == 0 and k == 1:
                copy = pltpu.make_async_copy(src, dst, local.at[b])
                copy.start()
                copies.append(copy)
            else:
                copies.append(push(src, dst, send.at[far, b], recv.at[far, b], {"ch": block}))
    return copies


def send_blocks(p, ys, blocks_ref, b, send, recv, local):
    at = pl.ds(b * 128, 128)
    copies = []
    for d in range(7):
        src, dst = ys.at[p.ch_ahead[d], :, at], blocks_ref.at[p.ch, :, at]
        copies.append(push(src, dst, send.at[d, b], recv.at[d, b], {"ch": p.ch_ahead[d]}))
    copy = pltpu.make_async_copy(ys.at[p.ch, :, at], blocks_ref.at[p.ch, :, at], local.at[b])
    copy.start()
    return copies + [copy]


def half(b):
    return slice(b * 128, (b + 1) * 128)


def fill_mask(p, lengths, mask, size, first):
    for b in range(2):
        place = lax.broadcasted_iota(jnp.int32, (size, 128), 0) + (p.ch * OWN + first)
        inside = jnp.where(place < lengths[0, b], 1.0, 0.0)
        mask[pl.ds(b * size, size)] = jnp.where(place < 0, 0.0, inside)


def norm_rows(values, gain):
    centre = values - jnp.mean(values, axis=1, keepdims=True)
    inverse = lax.rsqrt(jnp.mean(centre * centre, axis=1, keepdims=True) + EPS)
    return centre * inverse, inverse


def forward_kernel(size, loads, *refs):
    lengths, tokens, halo, consts, h_ref, fh, fl, th, tl, lanes, down_shard = refs[:11]
    columns = list(refs[11:13])
    w_in = refs[13]
    normed, u, mixer, kept, convolved, column_down, mask = refs[14:21]
    fulls = refs[21:24]
    weight, xs, abc, ys, pieces, gates, mixes, bufs, mask_before = refs[24:33]
    send, recv, local, send_back, recv_back, local_back = refs[33:39]
    weight_sems, column_sems, gather_sems = refs[39], refs[40:43], refs[43:]
    p = Place()
    width = 1024
    rows = 2 * size
    load = pltpu.make_async_copy(w_in, weight, weight_sems)
    load.start()
    greet([{"ch": one} for one in p.ch_ahead] + [p.sibling, p.along_y])
    column = Columns(p, [down_shard], [column_down], *column_sems)
    gather = Gather(p, columns + [column_down], fulls, SHARE, *gather_sems, places=EARLY, by_place=(2,))
    for i in (10, 11, 12):
        loads[i].wait()
    column.start()
    gather.start_x([0], arrays=(0, 1))
    gather.start_y([0], arrays=(0, 1))
    column.copies[(0, 3)].wait()
    gather.start_x([0], arrays=(2,))
    gather.start_y([0], arrays=(2,))
    gather.start_y([1], arrays=(0, 1))
    loads[1].wait()
    fill_mask(p, lengths, mask, size, 0)
    fill_mask(p, lengths, mask_before, 16, -16)
    gain = consts[10:11, :]

    def norm(i, carry):
        here = pl.ds(pl.multiple_of(i * 32, 32), 32)
        one, _ = norm_rows(tokens[here].astype(F32) * mask[here, 0:1], gain)
        normed[here] = (one * gain).astype(BF)
        return carry

    lax.fori_loop(0, rows // 32, norm, 0)
    before = halo[...].reshape(32, width).astype(F32) * mask_before[:, 0:1]
    before = (norm_rows(before, gain)[0] * gain).astype(BF)
    load.wait()

    def make(pair):
        for stream in range(3):
            at = pl.ds(pl.multiple_of(stream * width + pair * 256, 256), 256)
            u[pl.ds(0, rows), at] = mm(normed[...], weight[:, at]).astype(BF)
            u[pl.ds(rows, 32), at] = mm(before, weight[:, at]).astype(BF)
        for k in range(2):
            block = 2 * pair + k
            lane = pl.multiple_of(block * 128, 128)
            for b in range(2):
                gates[block, b] = short_conv(u, bufs.at[0], consts, b, 0, lane, size, width)
                key = short_conv(u, bufs.at[1], consts, b, 1, lane, size, width)
                mix = key * short_conv(u, bufs.at[2], consts, b, 2, lane, size, width)
                mixes[block, b] = mix
                pieces[block, :, half(b)] = mix.astype(BF)

    arriving = [send_pieces(p, pieces, kept, 0, send, recv, local, make)]
    arriving.append(send_pieces(p, pieces, kept, 1, send, recv, local))
    gather.start_x([1], arrays=(0, 1))
    loads[4].wait()
    loads[14].start()
    loads[15].start()
    filter_spectra(fh, fl, lanes, h_ref, abc, 8, size)
    gather.pass_sides(0)
    gather.start_y([2], arrays=(0, 1))
    leaving = []
    for b in range(2):
        wait_all(arriving[b])
        if b == 1:
            loads[17].start()
        spectra(fh, fl, kept, xs, 8, half(b))
        products_forward(xs, abc, lanes, xs, 8, size, (b,))
        inverse_blocks(th, tl, xs, ys, 8, half(b))
        leaving.append(send_blocks(p, ys, convolved, b, send_back, recv_back, local_back))
        if b == 0:
            gather.start_x([2], arrays=(0, 1))
            gather.pass_sides(1)
            gather.start_y([3], arrays=(0, 1))
            column.pass_far()
    gather.start_x([3], arrays=(0, 1))
    gather.pass_sides(2)
    gather.pass_last(0)
    for b in range(2):
        rows = slice(b * size, (b + 1) * size)
        wait_all(leaving[b])
        for c in range(8):
            at = half(c)
            long_part = convolved[c, :, half(b)].astype(F32) + consts[9:10, at] * mixes[c, b]
            mixer[rows, at] = (gates[c, b] * long_part * mask[rows]).astype(BF)
    gather.pass_sides(3)
    for n in range(1, 4):
        gather.pass_last(n)
    gather.finish()
    for slot in (0, 1, 2):
        column.copies[(0, slot)].wait_send()
    column.copies[(0, 0)].wait_recv()
    column.copies[(0, 2)].wait_recv()


def backward_kernel(size, count, loads, *refs):
    u, consts, mask, grad_mixer, convolved, kept, h_ref, fh, fl, th, tl, lanes = refs[:12]
    grads, plane = list(refs[12 : 13 + count]), refs[13]
    del grads[1]
    refs = refs[1:]
    du, dh_ref, sums = refs[12 + count : 15 + count]
    outs, far_out = refs[15 + count : 15 + 2 * count], refs[15 + 2 * count]
    rest = refs[16 + 2 * count :]
    xs, ds, abc, gh, pieces, arrived, returned, keys, values, dlongs, dcs, edge_out, edge_in, ends, bufs = rest[:15]
    send, recv, local, send_back, recv_back, local_back, edge_sems = rest[15:22]
    p = Place()
    width = 1024
    greet([{"ch": one} for one in p.ch_ahead] + [p.sibling, p.along_y])
    for i in (0, 2, 3):
        loads[i].wait()
    up_cols = grads[1].shape[5]
    whole = [grads[0], (grads[1], 0, up_cols // 2), (grads[1], up_cols // 2, up_cols // 2), (grads[2], 0, grads[2].shape[5])]
    stops = [None, outs[1], outs[1], outs[2]]
    scatter = Scatter(p, whole, [outs[0]] + [None] * 3, stops, SHARE_BACK, rest[28:])
    planes = Planes(p, grads[0], plane, *rest[22:28])
    loads[13].wait()
    planes.turn(0)
    scatter.start(1)
    scatter.start(2)
    scatter.start(3)
    sums[...] = jnp.zeros_like(sums)

    def grad_parts(block, b, rows, skip):
        at = pl.ds(pl.multiple_of(block * 128, 128), 128)
        take = max(rows, 16)
        masked = grad_mixer[pl.ds(b * size, take), at].astype(F32)[:rows] * mask[pl.ds(b * size, rows)]
        conv = convolved[block, :take, b * 128 : (b + 1) * 128].astype(F32)[:rows]
        return masked, conv + skip * (keys[block, b, :rows] * values[block, b, :rows])

    def make(pair):
        for k in range(2):
            make_block(2 * pair + k)

    def make_block(block):
        lane = pl.multiple_of(block * 128, 128)
        at = pl.ds(lane, 128)
        total = jnp.zeros((1, 128), F32)
        for b in range(2):
            rows = pl.ds(b * size, size)
            gate = short_conv(u, bufs.at[0], consts, b, 0, lane, size, width)
            key = short_conv(u, bufs.at[1], consts, b, 1, lane, size, width)
            value = short_conv(u, bufs.at[2], consts, b, 2, lane, size, width)
            keys[block, b] = key
            values[block, b] = value
            dlong = grad_mixer[rows, at].astype(F32) * mask[rows] * gate
            dlongs[block, b] = dlong
            pieces[block, :, b * 128 : (b + 1) * 128] = dlong.astype(BF)
            total = total + jnp.sum(dlong * (key * value), axis=0, keepdims=True)
        sums[9:10, at] = total

    arriving = [send_pieces(p, pieces, arrived, 0, send, recv, local, make)]
    arriving.append(send_pieces(p, pieces, arrived, 1, send, recv, local))
    scatter.core(1)
    loads[6].wait()
    filter_spectra(fh, fl, lanes, h_ref, abc, 8, size)
    loads[5].wait()
    spectra(fh, fl, kept, xs, 8)
    leaving = []
    for b in range(2):
        wait_all(arriving[b])
        spectra(fh, fl, arrived, ds, 8, half(b))
        products_backward(xs, ds, abc, gh, lanes, 8, size, (b,))
        inverse_blocks(th, tl, ds, pieces, 8, half(b))
        leaving.append(send_blocks(p, pieces, returned, b, send_back, recv_back, local_back))
        if b == 0:
            scatter.core(2)
            scatter.core(3)
            planes.cross(0)
    scatter.first(1)
    filter_gradient(th, tl, gh, dh_ref, 8, size)
    loads[17].start()
    loads[12].wait()
    planes.last(0, p.others[2])
    scatter.turn(0)
    loads[4].wait()
    wait_all(leaving[0])
    wait_all(leaving[1])

    def edges(c, carry):
        at = pl.ds(pl.multiple_of(c * 128, 128), 128)
        skip = consts[9:10, at]
        for b in range(2):
            masked, long_part = grad_parts(c, b, 8, skip)
            back = returned[c, :16, b * 128 : (b + 1) * 128].astype(F32)[:8]
            dmixed = back + skip * dlongs[c, b, :8]
            dmixed = dmixed[:2]
            edge_out[2 * b : 2 * b + 2, at] = (masked * long_part)[:2]
            edge_out[4 + 2 * b : 6 + 2 * b, at] = dmixed * values[c, b, :8][:2]
            edge_out[8 + 2 * b : 10 + 2 * b, at] = dmixed * keys[c, b, :8][:2]
        return carry

    lax.fori_loop(0, 8, edges, 0)
    edge = push(edge_out, edge_in, edge_sems.at[0], edge_sems.at[1], {"ch": lax.rem(p.ch + 7, 8)})
    scatter.first(2)
    scatter.first(3)

    def streams(c, carry):
        lane = pl.multiple_of(c * 128, 128)
        at = pl.ds(lane, 128)
        skip = consts[9:10, at]
        for b in range(2):
            masked, long_part = grad_parts(c, b, size, skip)
            dmixed = returned[c, :, b * 128 : (b + 1) * 128].astype(F32) + skip * dlongs[c, b]
            dcs[0, b, pl.ds(0, size)] = masked * long_part
            dcs[1, b, pl.ds(0, size)] = dmixed * values[c, b]
            dcs[2, b, pl.ds(0, size)] = dmixed * keys[c, b]
        for stream in range(3):
            out = pl.ds(pl.multiple_of(stream * width + lane, 128), 128)
            totals = [jnp.zeros((1, 128), F32)] * 3
            for b in range(2):
                dcs[stream, b, pl.ds(size, 8)] = jnp.zeros((8, 128), F32)
                parts = lagged(u, bufs.at[stream], b, stream, lane, size, width)
                grad = dcs[stream, b, pl.ds(0, size)]
                for lag in range(3):
                    totals[lag] = totals[lag] + jnp.sum(grad * parts[lag], axis=0, keepdims=True)
                total = consts[stream : stream + 1, at] * grad
                total = total + consts[3 + stream : 4 + stream, at] * dcs[stream, b, pl.ds(1, size)]
                total = total + consts[6 + stream : 7 + stream, at] * dcs[stream, b, pl.ds(2, size)]
                du[pl.ds(b * size, size), out] = total.astype(BF)
                ends[stream, b, :, at] = total[size - 16 :]
            for lag in range(3):
                row = 3 * lag + stream
                sums[row : row + 1, at] = totals[lag]
        return carry

    lax.fori_loop(0, 8, streams, 0)
    edge.wait()

    inside = jnp.where(p.ch < 7, 1.0, 0.0)
    for stream in range(3):
        one = consts[3 + stream : 4 + stream, :] * inside
        two = consts[6 + stream : 7 + stream, :] * inside
        out = slice(stream * width, (stream + 1) * width)
        for b in range(2):
            row = 4 * stream + 2 * b
            near, far = edge_in[row : row + 1, :], edge_in[row + 1 : row + 2, :]
            ends[stream, b, 14:15] = ends[stream, b, 14:15] + two * near
            ends[stream, b, 15:16] = ends[stream, b, 15:16] + one * near + two * far
            du[(b + 1) * size - 16 : (b + 1) * size, out] = ends[stream, b].astype(BF)
    loads[16].start()
    scatter.second(1)
    scatter.second(2)
    scatter.second(3)
    scatter.near(0, outs[0], far_out)


def nt(a, b):
    return lax.dot_general(a, b, (((1,), (1,)), ((), ())), preferred_element_type=F32)


def tn(a, b):
    return lax.dot_general(a, b, (((0,), (0,)), ((), ())), preferred_element_type=F32)


GELU_ONE = math.sqrt(2.0 / math.pi)
GELU_THREE = GELU_ONE * 0.044715


class Planes:
    def __init__(self, place, column, acc, one_a, one_b, two_a, two_b, send, recv):
        self.p, self.column = place, column
        self.acc, self.one_a, self.one_b, self.two_a, self.two_b = acc, one_a, one_b, two_a, two_b
        self.send, self.recv = send, recv
        self.copies = {}
        cols = acc.shape[4]
        half = split_columns(cols, 0.5)
        self.low, self.high = pl.ds(0, half), pl.ds(half, cols - half)

    def go(self, n, slot, src, dst, device):
        self.copies[(n, slot)] = push(src, dst, self.send.at[n, slot], self.recv.at[n, slot], device)

    def done(self, n, *slots):
        for slot in slots:
            self.copies[(n, slot)].wait()

    def core(self, n, made):
        self.go(n, 0, made.at[:, :, 1 - self.p.core], self.acc.at[n], self.p.sibling)

    def sides(self, n, made):
        p, acc = self.p, self.acc.at[n]
        self.done(n, 0)

        def step(k, carry):
            xx, yy = k // 2, lax.rem(k, 2)
            acc[xx, yy] = add_rows(acc[xx, yy], made[xx, yy, p.core])
            return carry

        lax.fori_loop(0, 4, step, 0)

    def turn(self, n):
        p, acc = self.p, self.acc.at[n]
        self.go(n, 1, acc.at[:, 1 - p.y, :, self.low], self.one_a.at[n], p.along_y)
        self.go(n, 2, acc.at[1 - p.x, :, :, self.high], self.one_b.at[n], p.along_x)

    def cross(self, n):
        p, acc = self.p, self.acc.at[n]
        low, high = self.low, self.high
        self.done(n, 1, 2)
        for k in range(2):
            acc[k, p.y, :, low] = add_rows(acc[k, p.y, :, low], self.one_a[n, k])
            acc[p.x, k, :, high] = add_rows(acc[p.x, k, :, high], self.one_b[n, k])
        self.go(n, 3, acc.at[1 - p.x, p.y, :, low], self.two_a.at[n], p.along_x)
        self.go(n, 4, acc.at[p.x, 1 - p.y, :, high], self.two_b.at[n], p.along_y)

    def last(self, n, zz):
        p, acc = self.p, self.acc.at[n]
        low, high = self.low, self.high
        self.done(n, 3, 4)
        self.column[zz, :, low] = add_rows(acc[p.x, p.y, :, low], self.two_a[n])
        self.column[zz, :, high] = add_rows(acc[p.x, p.y, :, high], self.two_b[n])

    @staticmethod
    def scratch(count, rows, cols):
        half = split_columns(cols, 0.5)
        return [
            pltpu.VMEM((count, 2, rows, half), BF),
            pltpu.VMEM((count, 2, rows, cols - half), BF),
            pltpu.VMEM((count, rows, half), BF),
            pltpu.VMEM((count, rows, cols - half), BF),
            pltpu.SemaphoreType.DMA((count + 1, 5)),
            pltpu.SemaphoreType.DMA((count + 1, 5)),
        ]


def feed_forward_kernel(loads, *refs):
    mixer, tokens, mask, cot, consts, w_out, w_up, early, column = refs[:9]
    result, grad_after, grad_mixer, grad_gain, grad_out, sum_column, sum_last, grad_up = refs[9:17]
    up, planes, late, total, unit, scale, normed, turned, da, pre, dact, act, dpre, kept_down, kept_up = refs[17:32]
    up_sem, plane_sems, out_sems, sum_acc = refs[32:36]
    gather_sems, scatter_refs = refs[36:39], refs[39:45]
    p = Place()
    greet([p.along_x, p.along_y, p.sibling])
    loads[8].wait()
    gather = Gather(p, [column], [late], 0.5, *gather_sems, places=LATE, by_place=(0,))
    gather.start_x([1, 2])
    gather.start_y([1, 2])
    sums = Planes(p, sum_column, sum_acc, *scatter_refs)
    weights = [pltpu.make_async_copy(w_up, up, up_sem)]
    weights += [pltpu.make_async_copy(early.at[n], planes.at[n], plane_sems.at[n]) for n in EARLY]
    for load in weights:
        load.start()
    gain = consts[11:12, :]
    loads[0].wait()
    loads[5].wait()
    total[...] = mm(mixer[...], w_out[...])
    loads[1].wait()
    loads[2].wait()
    loads[3].wait()

    def norm(i, carry):
        rows = pl.ds(pl.multiple_of(i * 32, 32), 32)
        zero = tokens[rows].astype(F32) * mask[rows, 0:1]
        value = zero + total[rows]
        total[rows] = value
        centre = value - jnp.mean(value, axis=1, keepdims=True)
        inverse = lax.rsqrt(jnp.mean(centre * centre, axis=1, keepdims=True) + EPS)
        one = centre * inverse
        unit[rows] = one
        scale[rows] = jnp.broadcast_to(inverse, (32, 128))
        normed[rows] = (one * gain).astype(BF)
        return carry

    lax.fori_loop(0, 16, norm, 0)
    turned[...] = normed[...].T
    wait_all(weights)
    writes = [None] * 4
    for n in range(4):
        zz = gather.place(n)
        cols = pl.ds(pl.multiple_of(zz * 1024, 1024), 1024)
        slot = n % 2
        made = kept_down.at[slot]
        pre[...] = mm(normed[...], up[:, cols])
        if n == 0:
            gather.pass_sides(1)
            gather.start_x([3])
            gather.start_y([3])
            plane = planes.at[0]
        else:
            gather.arrived(n)
            plane = late.at[n - 1]
        if n > 0:
            sums.sides(n - 1, kept_down.at[1 - slot])
            sums.turn(n - 1)
        dact[...] = nt(cot[...], plane[...].reshape(1024, 1024))

        def gelu(i, carry):
            rows = pl.ds(pl.multiple_of(i * 16, 16), 16)
            x = pre[rows]
            square = x * x
            t = jnp.tanh(x * (GELU_ONE + GELU_THREE * square))
            half = 0.5 + 0.5 * t
            value = x * half
            act[rows] = value.astype(BF)
            slope = half + value * (1.0 - t) * (GELU_ONE + 3.0 * GELU_THREE * square)
            dpre[rows] = (dact[rows] * slope).astype(BF)
            return carry

        lax.fori_loop(0, 32, gelu, 0)
        if n > 1:
            wait_all(writes[n - 2])
        made[...] = tn(act[...], cot[...]).astype(BF).reshape(2, 2, 2, 128, 1024)
        sums.core(n, made)
        total[...] += mm(act[...], plane[...].reshape(1024, 1024))
        if n > 1:
            sums.cross(n - 2)
        if n < 2:
            gather.pass_sides(n + 2)
        if n < 3:
            gather.pass_last(n + 1)
        back = nt(dpre[...], up[:, cols])
        da[...] = back if n == 0 else da[...] + back
        kept_up[slot] = mm(turned[...], dpre[...]).astype(BF)
        writes[n] = [pltpu.make_async_copy(kept_up.at[slot], grad_up.at[:, cols], out_sems.at[n])]
        for copy in writes[n]:
            copy.start()
    sums.sides(3, kept_down.at[1])
    sum_last[0] = sum_acc[3]
    sums.last(0, gather.place(0))

    def finish(i, gain_sum):
        rows = pl.ds(pl.multiple_of(i * 32, 32), 32)
        result[rows] = total[rows].astype(BF)
        one = unit[rows]
        back = da[rows]
        e = back * gain
        inner = e - jnp.mean(e, axis=1, keepdims=True) - one * jnp.mean(e * one, axis=1, keepdims=True)
        after = cot[rows].astype(F32) + scale[rows, 0:1] * inner
        grad_after[rows] = after
        normed[rows] = after.astype(BF)
        return gain_sum + jnp.sum(back * one, axis=0, keepdims=True)

    grad_gain[...] = lax.fori_loop(0, 16, finish, jnp.zeros((1, 1024), F32))
    loads[9].start()
    loads[10].start()
    grad_mixer[...] = nt(normed[...], w_out[...]).astype(BF)
    loads[11].start()
    sums.cross(2)
    sums.last(1, gather.place(1))
    grad_out[...] = tn(mixer[...], normed[...]).astype(BF)
    for n in (2, 3):
        wait_all(writes[n])
    gather.finish()
    sums.last(2, gather.place(2))
    sum_column[gather.place(3)] = sum_acc[3, 0, 0]


def feed_forward_call(mixer, tokens, mask, cot, consts, w_out, w_up, early, column):
    rows, width = mixer.shape
    hidden = w_up.shape[1]
    wide = (rows, width)
    square = (width, width)
    part = column.shape[1:]
    operands = (mixer, tokens, mask, cot, consts, w_out, w_up, early, column)
    fetch = (0, 1, 2, 3, 5, 8)
    store = (0, 1, 2)
    outs = [
        jax.ShapeDtypeStruct(wide, BF),
        jax.ShapeDtypeStruct(wide, F32),
        jax.ShapeDtypeStruct(wide, BF),
        jax.ShapeDtypeStruct((1, width), F32),
        jax.ShapeDtypeStruct(square, BF),
        jax.ShapeDtypeStruct((4,) + part, BF),
        jax.ShapeDtypeStruct((1, 2, 2) + part, BF),
        jax.ShapeDtypeStruct((width, hidden), BF),
        ]
    return pl.pallas_call(
        fetching(feed_forward_kernel, fetch, [len(operands) + i for i in store]),
        out_shape=outs,
        in_specs=fetch_specs(operands[:6], fetch) + [ANYWHERE] * 3,
        out_specs=fetch_specs(outs[:7], store) + [ANYWHERE],
        scratch_shapes=[
            pltpu.VMEM((width, hidden), BF),
            pltpu.VMEM((len(EARLY), 2, 2, 2) + part, BF),
            pltpu.VMEM((len(LATE), 2, 2, 2) + part, BF),
            pltpu.VMEM(wide, F32),
            pltpu.VMEM(wide, F32),
            pltpu.VMEM((rows, 128), F32),
            pltpu.VMEM(wide, BF),
            pltpu.VMEM((width, rows), BF),
            pltpu.VMEM(wide, F32),
            pltpu.VMEM(wide, F32),
            pltpu.VMEM(wide, F32),
            pltpu.VMEM(wide, BF),
            pltpu.VMEM(wide, BF),
            pltpu.VMEM((2, 2, 2, 2) + part, BF),
            pltpu.VMEM((2,) + square, BF),
            pltpu.SemaphoreType.DMA,
            pltpu.SemaphoreType.DMA((len(EARLY),)),
            pltpu.SemaphoreType.DMA((4,)),
            pltpu.VMEM((4, 2, 2) + part, BF),
        ]
        + Gather.scratch(1)
        + Planes.scratch(3, *part)
        + fetch_scratch(operands, fetch, outs, store),
        compiler_params=pltpu.CompilerParams(collective_id=5, has_side_effects=True, vmem_limit_bytes=VMEM_LIMIT),
    )(*operands)


def exchange_sems():
    pieces = [pltpu.SemaphoreType.DMA((8, 2))] * 2 + [pltpu.SemaphoreType.DMA((2,))]
    return pieces + [pltpu.SemaphoreType.DMA((7, 2))] * 2 + [pltpu.SemaphoreType.DMA((2,))]


def forward_call(lengths, tokens, halo, consts, filt, tables, down_shard, columns, w_in, size):
    rows = 2 * size
    block = (8, size, 256)
    piece = (8, 2, size, 128)
    operands = (lengths, tokens, halo, consts, filt) + tables + (down_shard,) + tuple(columns)
    whole = [jax.ShapeDtypeStruct((4, 2, 2, 2) + one.shape[1:], BF) for one in columns]
    whole.append(jax.ShapeDtypeStruct((len(EARLY), 2, 2, 2) + down_shard.shape, BF))
    fetch = (1, 4, 10, 11, 12)
    store = (0, 1, 3)
    outs = [
        jax.ShapeDtypeStruct((rows, 1024), BF),
        jax.ShapeDtypeStruct((rows + 32, 3072), BF),
        jax.ShapeDtypeStruct((rows, 1024), BF),
        jax.ShapeDtypeStruct(block, BF),
        jax.ShapeDtypeStruct(block, BF),
        jax.ShapeDtypeStruct((4,) + down_shard.shape, BF),
        jax.ShapeDtypeStruct((rows, 128), F32),
    ]
    first = len(operands) + 1
    out = pl.pallas_call(
        fetching(functools.partial(forward_kernel, size), fetch, [first + i for i in store]),
        out_shape=outs + whole,
        in_specs=[pl.BlockSpec(memory_space=pltpu.SMEM)] + fetch_specs(operands, fetch)[1:] + [ANYWHERE],
        out_specs=fetch_specs(outs, store) + [ANYWHERE] * 3,
        scratch_shapes=[
            pltpu.VMEM(w_in.shape, BF),
            pltpu.VMEM((8, 2 * size, 256), F32),
            pltpu.VMEM((8, 2, size, 128), F32),
            pltpu.VMEM(block, BF),
            pltpu.VMEM(block, BF),
            pltpu.VMEM(piece, F32),
            pltpu.VMEM(piece, F32),
            pltpu.VMEM((3, size + 16, 128), F32),
            pltpu.VMEM((32, 128), F32),
        ]
        + exchange_sems()
        + [pltpu.SemaphoreType.DMA]
        + Columns.scratch(1)
        + Gather.scratch(3)
        + fetch_scratch(operands, fetch, outs, store),
        compiler_params=pltpu.CompilerParams(collective_id=1, has_side_effects=True, vmem_limit_bytes=VMEM_LIMIT),
    )(*operands, w_in)
    return out[:7], [one.reshape(-1, one.shape[-1]) for one in out[7:9]], out[9]


def backward_call(u, consts, mask, grad_mixer, convolved, kept, filt, tables, grads, plane, size):
    rows = 2 * size
    block = (8, size, 256)
    piece = (8, 2, size, 128)
    operands = (u, consts, mask, grad_mixer, convolved, kept, filt) + tables
    count = len(grads)
    shapes = [grads[0].shape[1:]] + [(one.shape[0] // 32, one.shape[1]) for one in grads[1:]]
    views = [grads[0]] + [one.reshape((4, 2, 2, 2) + shape) for one, shape in zip(grads[1:], shapes[1:])]
    fetch = (0, 2, 3, 4, 5, 6, 12, 13)
    store = (0, 1)
    outs = [
        jax.ShapeDtypeStruct((rows, 3072), BF),
        jax.ShapeDtypeStruct((8, size, 128), F32),
        jax.ShapeDtypeStruct((16, 1024), F32),
    ]
    (up_rows, up_cols), out_kind = shapes[1], shapes[2]
    kinds = [shapes[0] + ("", False)] + [(up_rows, up_cols // 2, "load", True)] * 2 + [out_kind + ("load", True)]
    operands = operands + (views[0], plane)
    out = pl.pallas_call(
        fetching(functools.partial(backward_kernel, size, count), fetch, [len(operands) + count - 1 + i for i in store]),
        out_shape=outs
        + [jax.ShapeDtypeStruct(shapes[0], F32)]
        + [jax.ShapeDtypeStruct((4,) + shape, BF) for shape in shapes[1:]]
        + [jax.ShapeDtypeStruct(shapes[0], BF)],
        in_specs=fetch_specs(operands, fetch) + [ANYWHERE] * (count - 1),
        out_specs=fetch_specs(outs, store) + [VM] * (1 + count),
        scratch_shapes=[
            pltpu.VMEM((8, 2 * size, 256), F32),
            pltpu.VMEM((8, 2 * size, 256), F32),
            pltpu.VMEM((8, 2, size, 128), F32),
            pltpu.VMEM((8, 2, size, 128), F32),
            pltpu.VMEM(block, BF),
            pltpu.VMEM(block, BF),
            pltpu.VMEM(block, BF),
            pltpu.VMEM(piece, F32),
            pltpu.VMEM(piece, F32),
            pltpu.VMEM(piece, F32),
            pltpu.VMEM((3, 2, size + 8, 128), F32),
            pltpu.VMEM((16, 1024), F32),
            pltpu.VMEM((16, 1024), F32),
            pltpu.VMEM((3, 2, 16, 1024), F32),
            pltpu.VMEM((3, size + 16, 128), F32),
        ]
        + exchange_sems()
        + [pltpu.SemaphoreType.DMA((2,))]
        + Planes.scratch(1, *shapes[0])
        + Scatter.scratch(kinds, SHARE_BACK)
        + fetch_scratch(operands, fetch, outs, store),
        compiler_params=pltpu.CompilerParams(collective_id=2, has_side_effects=True, vmem_limit_bytes=VMEM_LIMIT),
    )(*operands, *views[1:])
    return out[:3], out[3:]


def add_rows(target, other):
    return (target.astype(F32) + other.astype(F32)).astype(BF)


class Scatter:
    SLOTS = 11

    def __init__(self, place, grads, outs, columns, share, refs):
        self.p, self.grads, self.outs, self.columns, self.share = place, grads, outs, columns, share
        count = len(grads)
        self.bufs = []
        at = 0
        for one, column in zip(grads, columns):
            names = Scatter.names(self.kind(one), column is not None)
            self.bufs.append(dict(zip(names, refs[at : at + len(names)])))
            at += len(names)
        self.send, self.recv, self.local = refs[at : at + 3]
        self.copies = {}

    @staticmethod
    def kind(grad):
        if not isinstance(grad, tuple):
            return ""
        return "load" if len(grad) == 3 else "made"

    @staticmethod
    def names(whole, stops):
        before = ("acc", "one_a", "one_b", "two_a", "two_b") if whole else ()
        if whole == "load":
            before += ("own",)
        return before + (() if stops else ("three", "four"))

    def go(self, i, slot, src, dst, device):
        copy = push(src, dst, self.send.at[i, slot], self.recv.at[i, slot], device)
        self.copies[(i, slot)] = copy

    def done(self, i, *slots):
        for slot in slots:
            self.copies[(i, slot)].wait()

    def part(self, i, zz, core):
        ref, first, cols = self.grads[i]
        if cols == ref.shape[5]:
            return ref.at[zz, :, :, core]
        return ref.at[zz, :, :, core, :, pl.ds(first, cols)]

    def load(self, i, zz):
        own = self.bufs[i]["own"]
        copy = pltpu.make_async_copy(self.part(i, zz, self.p.core), own.at[zz % 2], self.local.at[i, zz])
        copy.start()
        self.copies[(i, "own", zz)] = copy

    def start(self, i):
        if self.kind(self.grads[i]) == "made":
            self.go(i, 0, self.grads[i][0].at[:, :, :, 1 - self.p.core], self.bufs[i]["acc"], self.p.sibling)
            return
        for zz in range(4):
            self.go(i, zz, self.part(i, zz, 1 - self.p.core), self.bufs[i]["acc"].at[zz], self.p.sibling)
        self.load(i, 0)
        self.load(i, 1)

    def halves(self, i):
        cols = self.grads[i][2]
        part = split_columns(cols, self.share)
        return pl.ds(0, part), pl.ds(part, cols - part)

    def core(self, i):
        p, acc = self.p, self.bufs[i]["acc"]
        if self.kind(self.grads[i]) == "made":
            made = self.grads[i][0]
            self.done(i, 0)

            def add(n, carry):
                zz, xx, yy = n // 4, lax.rem(n // 2, 2), lax.rem(n, 2)
                acc[zz, xx, yy] = add_rows(acc[zz, xx, yy], made[zz, xx, yy, p.core])
                return carry

            lax.fori_loop(0, 16, add, 0)
        else:
            self.add_loaded(i)
        low, high = self.halves(i)
        self.go(i, 4, acc.at[:, :, 1 - p.y, :, low], self.bufs[i]["one_a"], p.along_y)
        self.go(i, 5, acc.at[:, 1 - p.x, :, :, high], self.bufs[i]["one_b"], p.along_x)

    def add_loaded(self, i):
        acc, own = self.bufs[i]["acc"], self.bufs[i]["own"]
        for zz in range(4):
            self.copies[(i, "own", zz)].wait()
            self.done(i, zz)

            def step(n, carry, zz=zz):
                xx, yy = n // 2, lax.rem(n, 2)
                acc[zz, xx, yy] = add_rows(acc[zz, xx, yy], own[zz % 2, xx, yy])
                return carry

            lax.fori_loop(0, 4, step, 0)
            if zz < 2:
                self.load(i, zz + 2)

    def first(self, i):
        p, acc = self.p, self.bufs[i]["acc"]
        one_a, one_b = self.bufs[i]["one_a"], self.bufs[i]["one_b"]
        low, high = self.halves(i)
        self.done(i, 4, 5)

        def step(n, carry):
            zz, w = n // 2, lax.rem(n, 2)
            acc[zz, w, p.y, :, low] = add_rows(acc[zz, w, p.y, :, low], one_a[zz, w])
            acc[zz, p.x, w, :, high] = add_rows(acc[zz, p.x, w, :, high], one_b[zz, w])
            return carry

        lax.fori_loop(0, 8, step, 0)
        self.go(i, 6, acc.at[:, 1 - p.x, p.y, :, low], self.bufs[i]["two_a"], p.along_x)
        self.go(i, 7, acc.at[:, p.x, 1 - p.y, :, high], self.bufs[i]["two_b"], p.along_y)

    def second(self, i):
        p, acc = self.p, self.bufs[i]["acc"]
        two_a, two_b = self.bufs[i]["two_a"], self.bufs[i]["two_b"]
        low, high = self.halves(i)
        self.done(i, 6, 7)
        column = self.columns[i]

        first, cols = (0, 0) if column is None else self.grads[i][1:3]

        def step(zz, carry):
            here = acc.at[zz, p.x, p.y] if column is None else column.at[zz, :, pl.ds(first, cols)]
            here[:, low] = add_rows(acc[zz, p.x, p.y, :, low], two_a[zz])
            here[:, high] = add_rows(acc[zz, p.x, p.y, :, high], two_b[zz])
            return carry

        lax.fori_loop(0, 4, step, 0)
        if column is None:
            self.turn(i)

    def sums(self, i, zz):
        if isinstance(self.grads[i], tuple):
            return self.bufs[i]["acc"].at[zz, self.p.x, self.p.y]
        return self.grads[i].at[zz]

    def turn(self, i):
        p, three = self.p, self.bufs[i]["three"]
        self.go(i, 8, self.sums(i, p.others[2]), three.at[0], p.along_z[0])
        self.go(i, 9, self.sums(i, p.others[0]), three.at[1], p.along_z[0])

    def third(self, i):
        p, three = self.p, self.bufs[i]["three"]
        self.done(i, 8, 9)
        far = self.sums(i, p.others[1])
        three[0] = add_rows(far[...], three[0])
        self.go(i, 10, three.at[0], self.bufs[i]["four"], p.along_z[1])

    def near(self, i, mine, far):
        three = self.bufs[i]["three"]
        self.done(i, 8, 9)
        far[...] = add_rows(self.sums(i, self.p.others[1])[...], three[0])
        mine[...] = self.sums(i, self.p.z)[...].astype(F32) + three[1].astype(F32)

    def last(self, i):
        three, four = self.bufs[i]["three"], self.bufs[i]["four"]
        self.done(i, 10)
        total = self.sums(i, self.p.z)[...].astype(F32) + three[1].astype(F32) + four[...].astype(F32)
        if isinstance(self.grads[i], tuple):
            first, cols = self.grads[i][1:3]
            self.outs[i][:, first : first + cols] = total
        else:
            self.outs[i][...] = total

    @classmethod
    def scratch(cls, kinds, share):
        count = len(kinds)
        bufs = []
        for rows, cols, whole, stops in kinds:
            part = split_columns(cols, share)
            shapes = {
                "own": (2, 2, 2, rows, cols),
                "acc": (4, 2, 2, rows, cols),
                "one_a": (4, 2, rows, part),
                "one_b": (4, 2, rows, cols - part),
                "two_a": (4, rows, part),
                "two_b": (4, rows, cols - part),
                "three": (2, rows, cols),
                "four": (rows, cols),
            }
            bufs += [pltpu.VMEM(shapes[name], BF) for name in cls.names(whole, stops)]
        return bufs + [
            pltpu.SemaphoreType.DMA((count, cls.SLOTS)),
            pltpu.SemaphoreType.DMA((count, cls.SLOTS)),
            pltpu.SemaphoreType.DMA((count, 4)),
        ]


def small_sums(p, vec, sec, fst, gathered, send, recv):
    rows, more = vec.shape[0], fst.shape[0]
    copies = []
    for d in range(7):
        lane = pl.multiple_of(p.ch_ahead[d] * 128, 128)
        pairs = (
            (vec.at[:, pl.ds(lane, 128)], gathered.at[p.ch, pl.ds(0, rows)]),
            (fst, gathered.at[p.ch, pl.ds(rows, more)]),
        )
        for n, (src, dst) in enumerate(pairs):
            copies.append(push(src, dst, send.at[2 * d + n], recv.at[2 * d + n], {"ch": p.ch_ahead[d]}))
    gathered[p.ch, :rows] = vec[:, pl.ds(pl.multiple_of(p.ch * 128, 128), 128)]
    gathered[p.ch, rows:] = fst[...]
    return copies


def join_sums(p, sec, gathered, joined, send, recv):
    rows = gathered.shape[1]
    total = gathered[0]
    for n in range(1, 8):
        total = total + gathered[n]
    joined[p.seq, :rows] = total
    joined[p.seq, rows:] = sec[...]
    return [
        push(joined.at[p.seq], joined.at[p.seq], send.at[14 + d], recv.at[14 + d], {"seq": p.seq_ahead[d]})
        for d in range(3)
    ]


def tail_kernel(size, loads, *refs):
    normed, du, tokens, mask, consts, grad_after, sums, gain_two = refs[:8]
    dh, hidden, table, first, second, shift, speed = refs[8:15]
    columns = list(refs[15:17])
    down_mine, down_far = refs[17:19]
    w_in = refs[19]
    grad_input, out, small_out = refs[20:23]
    outs = list(refs[23:25])
    down_out = refs[25]
    weight, turned, made, da, vec, sec, fst, gathered, joined, first_wide, down_last = refs[26:37]
    weight_sem, small_send, small_recv, down_sems = refs[37:41]
    width = 1024
    p = Place()
    load = pltpu.make_async_copy(w_in, weight, weight_sem)
    load.start()
    greet([{"ch": one} for one in p.ch_ahead] + [{"seq": one} for one in p.seq_ahead])
    grads = [(made.at[n], n * width, width, None) for n in range(3)] + columns
    scatter = Scatter(p, grads, [out] * 3 + outs, [None] * 5, 0.5, refs[41:])
    loads[15].wait()
    loads[16].wait()
    for n in (3, 4):
        scatter.turn(n)
    loads[18].wait()
    down = push(down_far, down_last, down_sems.at[0], down_sems.at[1], p.along_z[1])
    loads[0].wait()
    turned[...] = normed[...].T
    loads[1].wait()

    def part(stream):
        made[stream] = mm(turned[...], du[:, stream * width : (stream + 1) * width]).astype(BF).reshape(made.shape[1:])
        scatter.start(stream)

    def back(stream):
        at = slice(stream * width, (stream + 1) * width)
        one = nt(du[:, at], weight[:, at])
        da[...] = one if stream == 0 else da[...] + one

    part(0)
    part(1)
    scatter.core(0)
    part(2)
    scatter.core(1)
    scatter.core(2)

    length = 8 * size
    lane = (lax.broadcasted_iota(jnp.int32, (1, 128), 1) + p.ch * 128).astype(F32)
    rate = SLOW_RATE + (FAST_RATE - SLOW_RATE) * lane / 1023.0
    emb, filt_width = first_wide.shape
    first_wide[...] = jnp.zeros_like(first_wide)
    first_wide[: first.shape[0]] = first[...]
    sec[...] = jnp.zeros_like(sec)
    fst[...] = jnp.zeros_like(fst)

    def high(a, b, dims):
        return lax.dot_general(a, b, ((dims), ((), ())), precision=HIGH, preferred_element_type=F32)

    def step(j, carry):
        rows = pl.ds(pl.multiple_of(j * size, size), size)
        place = (lax.broadcasted_iota(jnp.int32, (size, 1), 0) + j * size).astype(F32) / (length - 1)
        draw = dh[j] * jnp.exp(-place * rate)
        sec[...] += high(hidden[rows], draw, ((0,), (0,)))
        inner = high(table[rows], first_wide[...], ((1,), (0,))) + shift[...]
        q = high(draw, second[...], ((1,), (1,))) * jnp.cos(speed[...] * inner)
        scaled = q * speed[...]
        fst[:emb, :filt_width] += high(table[rows], scaled, ((0,), (0,)))
        fst[emb : emb + 1, :filt_width] += jnp.sum(scaled, axis=0, keepdims=True)
        fst[emb + 1 : emb + 2, :filt_width] += jnp.sum(q * inner, axis=0, keepdims=True)
        return carry

    for i in (8, 9, 10):
        loads[i].wait()
    load.wait()
    back(0)
    back(1)
    back(2)
    scatter.first(0)
    lax.fori_loop(0, 4, step, 0)
    scatter.first(1)
    for n in (3, 4):
        scatter.third(n)
    scatter.first(2)
    for i in (2, 3, 5):
        loads[i].wait()
    gain = consts[10:11, :]

    def norm(i, total):
        rows = pl.ds(pl.multiple_of(i * 32, 32), 32)
        one, inverse = norm_rows(tokens[rows].astype(F32) * mask[rows, 0:1], gain)
        grad = da[rows]
        e = grad * gain
        inner = e - jnp.mean(e, axis=1, keepdims=True) - one * jnp.mean(e * one, axis=1, keepdims=True)
        grad_input[rows] = ((grad_after[rows] + inverse * inner) * mask[rows, 0:1]).astype(BF)
        return total + jnp.sum(grad * one, axis=0, keepdims=True)

    gain_one = lax.fori_loop(0, normed.shape[0] // 32, norm, jnp.zeros((1, width), F32))
    loads[20].start()
    vec[...] = jnp.zeros_like(vec)
    vec[:10] = sums[:10]
    vec[10:11] = gain_one
    vec[11:12] = gain_two[...]
    scatter.second(0)
    scatter.second(1)
    lax.fori_loop(4, 8, step, 0)
    small = small_sums(p, vec, sec, fst, gathered, small_send, small_recv)
    scatter.second(2)
    scatter.third(0)
    scatter.third(1)
    wait_all(small)
    small = join_sums(p, sec, gathered, joined, small_send, small_recv)
    scatter.third(2)
    for n in (3, 4):
        scatter.last(n)
    scatter.last(0)
    scatter.last(1)
    down.wait()
    loads[17].wait()
    down_out[...] = down_mine[...] + down_last[...].astype(F32)
    scatter.last(2)
    wait_all(small)
    total = joined[0]
    for n in range(1, 4):
        total = total + joined[n]
    small_out[...] = total


def tail_call(operands, columns, down, w_in, size):
    rows, width = operands[0].shape
    emb, filt_width = operands[10].shape[1], operands[11].shape[1]
    part = w_in.shape[0] // 32
    small = 16 + emb + 8
    kinds = [(part, width, "made", False)] * 3 + [one.shape[1:] + ("", False) for one in columns]
    operands = tuple(operands) + tuple(columns) + tuple(down)
    fetch = (0, 1, 2, 3, 5, 8, 9, 10, 15, 16, 17, 18)
    return pl.pallas_call(
        fetching(functools.partial(tail_kernel, size), fetch, [len(operands) + 1]),
        out_shape=[
            jax.ShapeDtypeStruct((rows, width), BF),
            jax.ShapeDtypeStruct((part, 3 * width), F32),
            jax.ShapeDtypeStruct((small + filt_width, 128), F32),
        ]
        + [jax.ShapeDtypeStruct(one.shape[1:], F32) for one in columns]
        + [jax.ShapeDtypeStruct(down[0].shape, F32)],
        in_specs=fetch_specs(operands, fetch) + [ANYWHERE],
        out_specs=[ANYWHERE] + [VM] * 5,
        scratch_shapes=[
            pltpu.VMEM(w_in.shape, BF),
            pltpu.VMEM((width, rows), BF),
            pltpu.VMEM((3, 4, 2, 2, 2, part, width), BF),
            pltpu.VMEM((rows, width), F32),
            pltpu.VMEM((16, width), F32),
            pltpu.VMEM((filt_width, 128), F32),
            pltpu.VMEM((emb + 8, 128), F32),
            pltpu.VMEM((8, small, 128), F32),
            pltpu.VMEM((4, small + filt_width, 128), F32),
            pltpu.VMEM((emb, filt_width), F32),
            pltpu.VMEM(down[1].shape, BF),
            pltpu.SemaphoreType.DMA,
            pltpu.SemaphoreType.DMA((17,)),
            pltpu.SemaphoreType.DMA((17,)),
            pltpu.SemaphoreType.DMA((2,)),
        ]
        + Scatter.scratch(kinds, 0.5)
        + fetch_scratch(operands, fetch, [jax.ShapeDtypeStruct((rows, width), BF)], (0,)),
        compiler_params=pltpu.CompilerParams(collective_id=3, has_side_effects=True, vmem_limit_bytes=VMEM_LIMIT),
    )(*operands, w_in)


def general_body(
    tokens,
    lengths,
    in_weight,
    out_weight,
    up_weight,
    down_weight,
    gain_one,
    gain_two,
    conv_taps,
    skip_gain,
    filter_first,
    filter_bias,
    frequency,
    filter_second,
    cotangent,
):
    ch_count = lax.axis_size("ch")
    ch_place = lax.axis_index("ch")
    size = tokens.shape[1]
    buckets = tokens.shape[2]
    width = tokens.shape[3]
    chans = skip_gain.shape[0]
    length = size * ch_count
    rows = size * buckets
    dims = (ch_count, size, buckets, chans)
    tables = tuple(jnp.asarray(one) for one in block_tables(size))

    def gather(shard):
        return lax.all_gather(shard, ("ch", "seq"), axis=0, tiled=True)

    full_in = gather(in_weight)
    full_gain_one = gather(gain_one).astype(F32)
    full_gain_two = gather(gain_two).astype(F32)
    full_out = gather(out_weight)
    full_up = gather(up_weight)
    full_down = gather(down_weight)

    local = ch_place * size + jnp.arange(size, dtype=jnp.int32)
    mask = (local[None, :] < lengths[0][:, None]).astype(F32).reshape(rows, 1)
    before = ch_place * size - 2 + jnp.arange(2, dtype=jnp.int32)
    mask_before = (before[None, :] < lengths[0][:, None]).astype(F32).reshape(2 * buckets, 1)
    chain = [(i, i + 1) for i in range(ch_count - 1)]
    halo = lax.ppermute(tokens[0, size - 2 :], "ch", chain)
    x_zero = jnp.swapaxes(tokens[0], 0, 1).reshape(rows, width).astype(F32) * mask
    x_before = jnp.swapaxes(halo, 0, 1).reshape(2 * buckets, width).astype(F32) * mask_before

    taps_full = lax.all_gather(conv_taps.reshape(9, chans), "ch", axis=1, tiled=True).reshape(3, 3, width)
    skip_full = lax.all_gather(skip_gain.reshape(1, chans), "ch", axis=1, tiled=True)

    table = positions_table(length, filter_first.shape[0])
    hidden = filter_hidden(filter_first, filter_bias, frequency, table)
    decay = decay_table(length, ch_place * chans, chans, width)
    filt = jnp.dot(hidden, filter_second, precision=HIGH) * decay
    filt_blocks = jnp.tile(filt.reshape(ch_count, size, chans), (1, 1, buckets))

    normed_one = layer_norm(x_zero, full_gain_one).astype(BF)
    normed_before = layer_norm(x_before, full_gain_one).astype(BF)
    streams = jnp.dot(normed_one, full_in, preferred_element_type=F32).astype(BF)
    streams_before = jnp.dot(normed_before, full_in, preferred_element_type=F32).astype(BF)
    lag = jnp.concatenate(
        [streams_before.reshape(buckets, 2, 3, width), streams.reshape(buckets, size, 3, width)], axis=1
    ).astype(F32)
    lag_zero, lag_one, lag_two = lag[:, 2:], lag[:, 1:-1], lag[:, :-2]
    conv = taps_full[0] * lag_zero + taps_full[1] * lag_one + taps_full[2] * lag_two
    gate = conv[:, :, 0].reshape(rows, width)
    key_part = conv[:, :, 1].reshape(rows, width)
    value_part = conv[:, :, 2].reshape(rows, width)
    mixed = key_part * value_part

    convolved, kept = conv_forward(mixed.astype(BF), filt_blocks, tables, dims)
    long_part = convolved.astype(F32) + skip_full * mixed
    mixer = (gate * long_part * mask).astype(BF)
    after_mix = x_zero + jnp.dot(mixer, full_out, preferred_element_type=F32)
    normed_two = layer_norm(after_mix, full_gain_two).astype(BF)
    inner_act = jnp.dot(normed_two, full_up, preferred_element_type=F32)
    active = jax.nn.gelu(inner_act).astype(BF)
    result = (after_mix + jnp.dot(active, full_down, preferred_element_type=F32)).astype(BF)
    result = jnp.swapaxes(result.reshape(buckets, size, width), 0, 1).reshape(1, size, buckets, width)

    grad_result = jnp.swapaxes(cotangent[0], 0, 1).reshape(rows, width)
    grad_active = jnp.dot(grad_result, full_down.T, preferred_element_type=F32)
    _, gelu_pull = jax.vjp(jax.nn.gelu, inner_act)
    grad_inner = gelu_pull(grad_active)[0].astype(BF)
    grad_down = jnp.dot(active.T, grad_result, preferred_element_type=F32)
    grad_up = jnp.dot(normed_two.T, grad_inner, preferred_element_type=F32)
    grad_normed_two = jnp.dot(grad_inner, full_up.T, preferred_element_type=F32)
    _, norm_two_pull = jax.vjp(layer_norm, after_mix, full_gain_two)
    grad_after_part, grad_gain_two = norm_two_pull(grad_normed_two)
    grad_after = grad_result.astype(F32) + grad_after_part
    grad_mix = grad_after.astype(BF)
    grad_out = jnp.dot(mixer.T, grad_mix, preferred_element_type=F32)
    grad_mixer = jnp.dot(grad_mix, full_out.T, preferred_element_type=F32).astype(BF)
    grad_masked = grad_mixer.astype(F32) * mask
    grad_gate = grad_masked * long_part
    grad_long = grad_masked * gate
    grad_skip = jnp.sum(grad_long * mixed, axis=0)
    grad_convolved, grad_filt = conv_backward(grad_long.astype(BF), kept, filt_blocks, tables, dims)
    grad_mixed = grad_convolved.astype(F32) + skip_full * grad_long
    grad_conv = jnp.stack([grad_gate, grad_mixed * value_part, grad_mixed * key_part], axis=1)
    grad_conv = grad_conv.reshape(buckets, size, 3, width)
    grad_taps = jnp.stack(
        [
            jnp.sum(grad_conv * lag_zero, axis=(0, 1)),
            jnp.sum(grad_conv * lag_one, axis=(0, 1)),
            jnp.sum(grad_conv * lag_two, axis=(0, 1)),
        ],
        axis=0,
    )
    next_rows = lax.ppermute(grad_conv[:, :2], "ch", [(j, i) for i, j in chain])
    ahead = jnp.concatenate([grad_conv, next_rows], axis=1)
    grad_streams = taps_full[0] * ahead[:, :-2] + taps_full[1] * ahead[:, 1:-1] + taps_full[2] * ahead[:, 2:]
    grad_projected = grad_streams.astype(BF).reshape(rows, 3 * width)
    grad_in = jnp.dot(normed_one.T, grad_projected, preferred_element_type=F32)
    grad_normed_one = jnp.dot(grad_projected, full_in.T, preferred_element_type=F32)
    _, norm_one_pull = jax.vjp(layer_norm, x_zero, full_gain_one)
    grad_zero_part, grad_gain_one = norm_one_pull(grad_normed_one)
    grad_input = ((grad_after + grad_zero_part) * mask).astype(BF)
    grad_input = jnp.swapaxes(grad_input.reshape(buckets, size, width), 0, 1).reshape(1, size, buckets, width)

    grad_filt = jnp.sum(grad_filt.reshape(length, buckets, chans), axis=1)
    grad_raw = grad_filt * decay
    grad_second = jnp.dot(hidden.T, grad_raw, precision=HIGH)
    grad_hidden = jnp.dot(grad_raw, filter_second.T, precision=HIGH)

    def hidden_of(first_layer, first_shift, freq_values):
        return filter_hidden(first_layer, first_shift, freq_values, table)

    _, hidden_pull = jax.vjp(hidden_of, filter_first, filter_bias, frequency)
    grad_first, grad_bias, grad_freq = hidden_pull(grad_hidden)

    sum_in, sum_out, sum_up, sum_down, sum_gain_one, sum_gain_two = (
        lax.psum_scatter(one, ("ch", "seq"), scatter_dimension=0, tiled=True)
        for one in (grad_in, grad_out, grad_up, grad_down, grad_gain_one, grad_gain_two)
    )
    sum_second = lax.psum(grad_second, "seq")
    all_taps, all_skip, sum_first, sum_bias, sum_freq = lax.psum(
        (grad_taps, grad_skip, grad_first, grad_bias, grad_freq), ("ch", "seq")
    )
    sum_taps = lax.dynamic_slice_in_dim(all_taps, ch_place * chans, chans, 2)
    sum_skip = lax.dynamic_slice_in_dim(all_skip, ch_place * chans, chans, 0)
    return (
        result,
        grad_input,
        sum_in,
        sum_out,
        sum_up,
        sum_down,
        sum_gain_one,
        sum_gain_two,
        sum_taps,
        sum_skip,
        sum_first,
        sum_bias,
        sum_freq,
        sum_second,
    )


def by_position(values, size):
    first, second = values[:size, None], values[size:, None]
    bucket = lax.broadcasted_iota(jnp.int32, (size, 2, values.shape[1]), 1)
    return jnp.where(bucket == 0, first, second)[None]


def filter_table(length, features):
    steps = np.arange(length).astype(np.float32)
    scaled = steps / np.float32(length - 1)
    bands = (features - 1) // 2
    freqs = np.float32(0.0001) + np.float32(bands - 1 - 0.0001) * np.arange(bands).astype(np.float32) / np.float32(bands - 1)
    angles = freqs[None, :] * (np.float32(2.0 * math.pi) * steps / np.float32(length))[:, None]
    table = np.concatenate([scaled[:, None], np.cos(angles), -np.sin(angles)], axis=1)
    return np.pad(table, ((0, 0), (0, -features % 8)))


def slice_body(
    tokens,
    lengths,
    in_weight,
    out_weight,
    up_weight,
    down_weight,
    gain_one,
    gain_two,
    conv_taps,
    skip_gain,
    filter_first,
    filter_bias,
    frequency,
    filter_second,
    cotangent,
):
    seq_place = lax.axis_index("seq")
    size = tokens.shape[1]
    buckets = tokens.shape[2]
    width = tokens.shape[3]
    chans = skip_gain.shape[0]
    length = size * 8
    rows = size * buckets
    part = gain_one.shape[0]
    emb, filt_width = filter_first.shape
    tables = tuple(jnp.asarray(one) for one in block_tables(size))

    by_bucket = jnp.swapaxes(tokens[0], 0, 1)
    flat = by_bucket.reshape(rows, width)
    wide_table = jnp.asarray(filter_table(length, emb))
    pads = wide_table.shape[1] - emb
    (consts, halo, hidden, filt), full_in, columns = start_call(
        conv_taps,
        skip_gain[None],
        jnp.stack([gain_one, gain_two]),
        by_bucket,
        wide_table,
        filter_first,
        filter_second,
        filter_bias[None],
        frequency[None],
        (in_weight, out_weight, up_weight),
        size,
    )
    (normed_one, streams, mixer, kept, convolved, column_down, wide_mask), (full_out, full_up), early = forward_call(
        lengths, flat, halo, consts, filt, tables, down_weight, columns, full_in, size
    )
    grad_result = jnp.swapaxes(cotangent[0], 0, 1).reshape(rows, width)
    result, grad_after, grad_mixer, grad_gain_two, grad_out, sum_column, sum_last, grad_up = feed_forward_call(
        mixer, flat, wide_mask, grad_result, consts, full_out, full_up, early, column_down
    )
    result = by_position(result, size)

    (grad_projected, grad_filt, sums), (down_mine, *late, down_far) = backward_call(
        streams, consts, wide_mask, grad_mixer, convolved, kept, filt, tables, (sum_column, grad_up, grad_out), sum_last, size
    )
    grad_input, sum_in, small, sum_up, sum_out, sum_down = tail_call(
        (normed_one, grad_projected, flat, wide_mask, consts, grad_after, sums, grad_gain_two)
        + (grad_filt, hidden, wide_table, filter_first, filter_second, filter_bias[None], frequency[None]),
        late,
        (down_mine, down_far),
        full_in,
        size,
    )
    grad_input = by_position(grad_input, size)
    after = 16 + emb + pads
    gain_sums = lax.dynamic_slice_in_dim(small[10:12], seq_place * part, part, 1)
    return (
        result,
        grad_input,
        sum_in,
        sum_out,
        sum_up,
        sum_down,
        gain_sums[0],
        gain_sums[1],
        small[:9].reshape(3, 3, chans),
        small[9],
        small[16 : 16 + emb, :filt_width],
        small[after, :filt_width],
        small[after + 1, :filt_width],
        small[after + 8 :],
    )


def solution(mesh):
    placed = (
        P("seq", "ch", None, None),
        P("seq", None),
        P(("ch", "seq"), None),
        P(("ch", "seq"), None),
        P(("ch", "seq"), None),
        P(("ch", "seq"), None),
        P(("ch", "seq")),
        P(("ch", "seq")),
        P(None, None, "ch"),
        P("ch"),
        P(),
        P(),
        P(),
        P(None, "ch"),
        P("seq", "ch", None, None),
    )
    custom = dict(mesh.shape) == {"ch": 8, "seq": 4}
    return jax.shard_map(
        slice_body if custom else general_body,
        mesh=mesh,
        in_specs=placed,
        out_specs=(
            P("seq", "ch", None, None),
            P("seq", "ch", None, None),
            P(("ch", "seq"), None),
            P(("ch", "seq"), None),
            P(("ch", "seq"), None),
            P(("ch", "seq"), None),
            P(("ch", "seq")),
            P(("ch", "seq")),
            P(None, None, "ch"),
            P("ch"),
            P(),
            P(),
            P(),
            P(None, "ch"),
        ),
        check_vma=False,
    )
```

```python
import functools
import math

import jax
import jax.numpy as jnp
import numpy as np
from jax import lax
from jax.experimental import pallas as pl
from jax.experimental.pallas import tpu as pltpu
from jax.sharding import PartitionSpec as P

EPS = 1e-05
SLOW_RATE = math.log(100.0) / 1.5
FAST_RATE = math.log(100.0) / 0.3
HIGH = lax.Precision.HIGHEST
BF = jnp.bfloat16
F32 = jnp.float32
MESH = pl.DeviceIdType.MESH
VMEM_LIMIT = 62 << 20
OWN = 256
SHARE = 0.85
SHARE_BACK = 0.69
EARLY, LATE = range(0, 1), range(1, 4)


def layer_norm(values, gain):
    centre = values - jnp.mean(values, axis=-1, keepdims=True)
    spread = jnp.mean(centre * centre, axis=-1, keepdims=True)
    return centre * lax.rsqrt(spread + EPS) * gain


def positions_table(length, features):
    steps = jnp.arange(length).astype(jnp.float32)
    scaled = steps / (length - 1)
    bands = (features - 1) // 2
    freqs = 0.0001 + (bands - 1 - 0.0001) * jnp.arange(bands).astype(jnp.float32) / (bands - 1)
    angles = freqs[None, :] * (2.0 * math.pi * steps / length)[:, None]
    return jnp.concatenate([scaled[:, None], jnp.cos(angles), -jnp.sin(angles)], axis=1)


def decay_table(length, chan_start, count, width):
    scaled = jnp.arange(length).astype(jnp.float32) / (length - 1)
    chans = (chan_start + jnp.arange(count)).astype(jnp.float32)
    rates = SLOW_RATE + (FAST_RATE - SLOW_RATE) * chans / (width - 1)
    return jnp.exp(-scaled[:, None] * rates[None, :])


def filter_hidden(filter_first, filter_bias, frequency, table):
    inner = jnp.dot(table, filter_first, precision=HIGH) + filter_bias
    return jnp.sin(frequency * inner)


def block_tables(size):
    k = np.arange(size)[:, None]
    t = np.arange(size)[None, :]
    angle = 2.0 * np.pi * ((k * t) % (2 * size)) / (2 * size)
    real = np.cos(angle)
    imag = -np.sin(angle)
    imag[0] = np.where(np.arange(size) % 2 == 0, 1.0, -1.0)
    full = np.concatenate([real, imag], axis=0).astype(np.float32)
    high = full.astype(jnp.bfloat16)
    low = (full - high.astype(np.float32)).astype(jnp.bfloat16)
    weight = np.full((size, 1), 1.0 / size, np.float32)
    weight[0] = 0.5 / size
    sign = np.where(np.arange(size) % 2 == 0, 1.0, -1.0).astype(np.float32)[:, None]
    lanes = np.zeros((size, 128), np.float32)
    lanes[:, 0:1] = weight
    lanes[:, 1:2] = sign
    lanes[:, 2] = 1.0
    lanes[0, 2] = 0.0
    return high, low, high.T.copy(), low.T.copy(), lanes


def split_high(values):
    high = values.astype(BF)
    return high, (values - high.astype(F32)).astype(BF)


def mm(a, b):
    return jnp.dot(a, b, preferred_element_type=F32)


def spectra(fh, fl, source, target, blocks, piece=slice(None)):
    def step(i, carry):
        block = source[i, :, piece]
        target[i, :, piece] = mm(fh[...], block) + mm(fl[...], block)
        return carry

    lax.fori_loop(0, blocks, step, 0)


def filter_spectra(fh, fl, lanes, h_ref, abc, blocks, size):
    weight = lanes[:, 0:1]
    sign = lanes[:, 1:2]

    def step(j, carry):
        prev_re, prev_im = carry
        high, low = split_high(h_ref[j])
        now = mm(fh[...], high) + mm(fl[...], high) + mm(fh[...], low)
        now_re = now[:size]
        now_im = now[size:]
        abc[j, 0] = (now_re + sign * prev_re) * weight
        abc[j, 1] = (now_im + sign * prev_im) * weight
        return now_re, now_im

    zero = jnp.zeros((size, h_ref.shape[2]), F32)
    lax.fori_loop(0, blocks, step, (zero, zero))


def row_chunks(size, body):
    def step(i, carry):
        body(pl.multiple_of(i * 8, 8))
        return carry

    lax.fori_loop(0, size // 8, step, 0)


def load_filter(abc, lanes, here, blocks):
    keep = lanes[here, 2:3]
    a = [abc[j, 0, here] for j in range(blocks)]
    raw = [abc[j, 1, here] for j in range(blocks)]
    b = [one * keep for one in raw]
    c = [jnp.where(keep > 0.5, one, two) for one, two in zip(a, raw)]
    return a, b, c


def products_forward(xs, abc, lanes, out, blocks, size, pieces=None):
    width = abc.shape[3]
    for n in range(xs.shape[2] // width) if pieces is None else pieces:
        piece = slice(n * width, (n + 1) * width)

        def body(row, piece=piece):
            here, there = pl.ds(row, 8), pl.ds(size + row, 8)
            re = [xs[i, here, piece] for i in range(blocks)]
            im = [xs[i, there, piece] for i in range(blocks)]
            a, b, c = load_filter(abc, lanes, here, blocks)
            for m in range(blocks):
                sum_re = re[0] * a[m] - im[0] * b[m]
                sum_im = re[0] * b[m] + im[0] * c[m]
                for i in range(1, m + 1):
                    sum_re = sum_re + (re[i] * a[m - i] - im[i] * b[m - i])
                    sum_im = sum_im + (re[i] * b[m - i] + im[i] * c[m - i])
                out[m, here, piece] = sum_re
                out[m, there, piece] = sum_im

        row_chunks(size, body)


def products_backward(xs, ds, abc, gh, lanes, blocks, size, pieces=None):
    width = abc.shape[3]
    count = xs.shape[2] // width
    for n in range(count) if pieces is None else pieces:
        piece = slice(n * width, (n + 1) * width)

        def body(row, n=n, piece=piece):
            here, there = pl.ds(row, 8), pl.ds(size + row, 8)
            d_re = [ds[i, here, piece] for i in range(blocks)]
            d_im = [ds[i, there, piece] for i in range(blocks)]
            a, b, c = load_filter(abc, lanes, here, blocks)
            for i in range(blocks):
                sum_re = d_re[i] * a[0] + d_im[i] * b[0]
                sum_im = d_im[i] * c[0] - d_re[i] * b[0]
                for m in range(i + 1, blocks):
                    sum_re = sum_re + (d_re[m] * a[m - i] + d_im[m] * b[m - i])
                    sum_im = sum_im + (d_im[m] * c[m - i] - d_re[m] * b[m - i])
                ds[i, here, piece] = sum_re
                ds[i, there, piece] = sum_im
            x_re = [xs[i, here, piece] for i in range(blocks)]
            x_im = [xs[i, there, piece] for i in range(blocks)]
            weight = lanes[here, 0:1]
            sign = lanes[here, 1:2]
            keep = lanes[here, 2:3] > 0.5
            later_re = None
            later_im = None
            for j in range(blocks - 1, -1, -1):
                rr = d_re[j] * x_re[0]
                ii = d_im[j] * x_im[0]
                cross = d_im[j] * x_re[0] - d_re[j] * x_im[0]
                for i in range(1, blocks - j):
                    rr = rr + d_re[i + j] * x_re[i]
                    ii = ii + d_im[i + j] * x_im[i]
                    cross = cross + (d_im[i + j] * x_re[i] - d_re[i + j] * x_im[i])
                g_re = jnp.where(keep, rr + ii, rr) * weight
                g_im = jnp.where(keep, cross, ii) * weight
                if n:
                    g_re = g_re + gh[j, 0, here]
                    g_im = g_im + gh[j, 1, here]
                if n == count - 1 and later_re is not None:
                    gh[j, 0, here] = g_re + sign * later_re
                    gh[j, 1, here] = g_im + sign * later_im
                else:
                    gh[j, 0, here] = g_re
                    gh[j, 1, here] = g_im
                later_re, later_im = g_re, g_im

        row_chunks(size, body)


def inverse_of(th, tl, values):
    high, low = split_high(values)
    return mm(th[...], high) + mm(tl[...], high) + mm(th[...], low)


def inverse_blocks(th, tl, source, target, blocks, piece=slice(None)):
    def step(m, carry):
        target[m, :, piece] = inverse_of(th, tl, source[m, :, piece]).astype(target.dtype)
        return carry

    lax.fori_loop(0, blocks, step, 0)


def filter_gradient(th, tl, gh, out, blocks, size):
    def step(j, carry):
        re_high, re_low = split_high(gh[j, 0])
        im_high, im_low = split_high(gh[j, 1])
        left, right = th[:, :size], th[:, size:]
        total = mm(left, re_high) + mm(right, im_high) + mm(left, re_low) + mm(right, im_low)
        total = total + mm(tl[:, :size], re_high) + mm(tl[:, size:], im_high)
        out[j] = total
        return carry

    lax.fori_loop(0, blocks, step, 0)


def conv_forward_kernel(dims, x_ref, h_ref, fh, fl, th, tl, lanes, out, xs, abc):
    blocks, size, buckets, chans = dims
    filter_spectra(fh, fl, lanes, h_ref, abc, blocks, size)
    spectra(fh, fl, x_ref, xs, blocks)
    products_forward(xs, abc, lanes, xs, blocks, size)
    inverse_blocks(th, tl, xs, out, blocks)


def conv_backward_kernel(dims, d_ref, x_ref, h_ref, fh, fl, th, tl, lanes, out, dh_ref, xs, ds, abc, gh):
    blocks, size, buckets, chans = dims
    filter_spectra(fh, fl, lanes, h_ref, abc, blocks, size)
    spectra(fh, fl, x_ref, xs, blocks)
    spectra(fh, fl, d_ref, ds, blocks)
    products_backward(xs, ds, abc, gh, lanes, blocks, size)
    inverse_blocks(th, tl, ds, out, blocks)
    filter_gradient(th, tl, gh, dh_ref, blocks, size)


VM = pl.BlockSpec(memory_space=pltpu.VMEM)
ANYWHERE = pl.BlockSpec(memory_space=pl.ANY)


def conv_call(kernel, dims, operands, kinds, spectra_count):
    blocks, size, buckets, chans = dims
    cols = buckets * chans
    scratch = [pltpu.VMEM((blocks, 2 * size, cols), F32)] * spectra_count
    return pl.pallas_call(
        functools.partial(kernel, dims),
        out_shape=[jax.ShapeDtypeStruct((blocks, size, cols), kind) for kind in kinds],
        in_specs=[VM] * len(operands),
        out_specs=[VM] * len(kinds),
        scratch_shapes=scratch + [pltpu.VMEM((blocks, 2, size, cols), F32)] * spectra_count,
        compiler_params=pltpu.CompilerParams(vmem_limit_bytes=VMEM_LIMIT),
    )(*operands)


def rows_to_blocks(rows, dims):
    blocks, size, buckets, chans = dims
    moved = lax.all_to_all(rows.reshape(buckets, size, blocks, chans), "ch", split_axis=2, concat_axis=0)
    return jnp.transpose(moved, (0, 2, 1, 3)).reshape(blocks, size, buckets * chans)


def blocks_to_rows(values, dims):
    blocks, size, buckets, chans = dims
    moved = lax.all_to_all(values.reshape(blocks, size, buckets, chans), "ch", split_axis=0, concat_axis=0)
    return jnp.transpose(moved, (2, 1, 0, 3)).reshape(buckets * size, blocks * chans)


def conv_forward(rows, filt, tables, dims):
    kept = rows_to_blocks(rows, dims)
    (out,) = conv_call(conv_forward_kernel, dims, (kept, filt) + tables, (BF,), 1)
    return blocks_to_rows(out, dims), kept


def conv_backward(rows, kept, filt, tables, dims):
    moved = rows_to_blocks(rows, dims)
    out, dfilt = conv_call(conv_backward_kernel, dims, (moved, kept, filt) + tables, (BF, F32), 2)
    return blocks_to_rows(out, dims), dfilt


class Place:
    def __init__(self):
        self.ch = lax.axis_index("ch")
        self.seq = lax.axis_index("seq")
        self.z, self.x = self.ch // 2, lax.rem(self.ch, 2)
        self.y, self.core = self.seq // 2, lax.rem(self.seq, 2)
        self.sibling = {"seq": self.y * 2 + (1 - self.core)}
        self.along_y = {"seq": (1 - self.y) * 2 + self.core}
        self.along_x = {"ch": self.z * 2 + (1 - self.x)}
        self.others = [self.z + 1 - 2 * lax.rem(self.z, 2), lax.rem(self.z + 2, 4), 3 - self.z]
        self.along_z = [{"ch": one * 2 + self.x} for one in self.others]
        self.ch_ahead = [lax.rem(self.ch + d, 8) for d in range(1, 8)]
        self.seq_ahead = [lax.rem(self.seq + d, 4) for d in range(1, 4)]


def greet(ids):
    barrier = pltpu.get_barrier_semaphore()
    for one in ids:
        pl.semaphore_signal(barrier, inc=1, device_id=one, device_id_type=MESH)
    pl.semaphore_wait(barrier, len(ids))


def wait_all(copies):
    for copy in copies:
        copy.wait()


def fetching(kernel, fetch, store=()):
    def wrapped(*refs):
        moved = tuple(fetch) + tuple(store)
        count = len(moved)
        refs, places, sems = list(refs[: -2 * count]), refs[-2 * count : -count], refs[-count:]
        moves = {}
        for n, i in enumerate(moved):
            ends = (refs[i], places[n]) if n < len(fetch) else (places[n], refs[i])
            moves[i] = pltpu.make_async_copy(*ends, sems[n])
            if n < len(fetch):
                moves[i].start()
            refs[i] = places[n]
        kernel(moves, *refs)
        for i in store:
            moves[i].wait()

    return wrapped


def fetch_scratch(operands, fetch, outs=(), store=()):
    arrays = [operands[i] for i in fetch] + [outs[i] for i in store]
    return [pltpu.VMEM(one.shape, one.dtype) for one in arrays] + [pltpu.SemaphoreType.DMA] * len(arrays)


def fetch_specs(operands, fetch):
    return [ANYWHERE if i in fetch else VM for i in range(len(operands))]


def push(src, dst, send, recv, device):
    copy = pltpu.make_async_remote_copy(
        src_ref=src, dst_ref=dst, send_sem=send, recv_sem=recv, device_id=device, device_id_type=MESH
    )
    copy.start()
    return copy


def split_columns(cols, share):
    return int(cols * share / 128 + 0.5) * 128


class Columns:
    SLOTS = 3

    def __init__(self, place, shards, columns, send, recv, local):
        self.p, self.shards, self.columns = place, shards, columns
        self.send, self.recv, self.local = send, recv, local
        self.copies = {}

    def go(self, i, slot, src, dst, device):
        self.copies[(i, slot)] = push(src, dst, self.send.at[i, slot], self.recv.at[i, slot], device)

    def start(self):
        p = self.p
        for i, shard in enumerate(self.shards):
            mine = self.columns[i].at[p.z]
            self.go(i, 1, shard, mine, p.along_z[1])
            self.go(i, 0, shard, mine, p.along_z[0])
            copy = pltpu.make_async_copy(shard, mine, self.local.at[i])
            copy.start()
            self.copies[(i, 3)] = copy

    def pass_far(self):
        p = self.p
        for i in range(len(self.shards)):
            self.copies[(i, 1)].wait_recv()
            here = self.columns[i].at[p.others[1]]
            self.go(i, 2, here, here, p.along_z[0])

    def finish(self):
        for (i, slot), copy in self.copies.items():
            if slot == 1:
                copy.wait_send()
            else:
                copy.wait()

    @classmethod
    def scratch(cls, count):
        return [
            pltpu.SemaphoreType.DMA((count, cls.SLOTS)),
            pltpu.SemaphoreType.DMA((count, cls.SLOTS)),
            pltpu.SemaphoreType.DMA((count,)),
        ]


class Gather:
    SLOTS = 32

    def __init__(self, place, columns, fulls, share, send, recv, local, places=range(4), by_place=()):
        self.source = {}
        self.p, self.columns, self.fulls, self.share = place, columns, fulls, share
        self.places, self.by_place = places, by_place
        self.send, self.recv, self.local = send, recv, local
        self.copies = {}
        self.seen = set()

    def go(self, i, slot, src, dst, device):
        self.copies[(i, slot)] = push(src, dst, self.send.at[i, slot], self.recv.at[i, slot], device)

    def place(self, n):
        return self.p.z if n == 0 else self.p.others[n - 1]

    def arrays(self, n):
        return [i for i in range(len(self.fulls)) if i not in self.by_place or n in self.places]

    def plane(self, i, n):
        if i in self.by_place:
            return self.fulls[i].at[n - self.places[0]]
        return self.fulls[i].at[self.place(n)]

    def ends(self, i, n):
        p, zz = self.p, self.place(n)
        src = self.source[i, n] if (i, n) in self.source else self.columns[i].at[zz]
        return src, self.plane(i, n).at[p.x, p.y, p.core]

    def start_y(self, places=range(4), arrays=None):
        for n in places:
            for i in self.arrays(n) if arrays is None else arrays:
                src, dst = self.ends(i, n)
                self.go(i, 4 + n, src, dst, self.p.along_y)
                self.go(i, 16 + n, src, dst, self.p.sibling)
                copy = pltpu.make_async_copy(src, dst, self.local.at[i, n])
                copy.start()
                self.copies[(i, 32 + n)] = copy

    def start_x(self, places=range(4), arrays=None):
        for n in places:
            for i in self.arrays(n) if arrays is None else arrays:
                src, dst = self.ends(i, n)
                self.go(i, n, src, dst, self.p.along_x)

    def pass_sides(self, n):
        p = self.p
        for i in self.arrays(n):
            full = self.plane(i, n)
            cols = full.shape[4]
            part = split_columns(cols, self.share)
            self.copies[(i, n)].wait_recv()
            whole = full.at[1 - p.x, p.y, p.core]
            some = full.at[1 - p.x, p.y, p.core, :, pl.ds(0, part)]
            self.go(i, 8 + n, some, some, p.along_y)
            self.go(i, 20 + n, whole, whole, p.sibling)
            self.copies[(i, 4 + n)].wait_recv()
            whole = full.at[p.x, 1 - p.y, p.core]
            some = full.at[p.x, 1 - p.y, p.core, :, pl.ds(part, cols - part)]
            self.go(i, 12 + n, some, some, p.along_x)
            self.go(i, 24 + n, whole, whole, p.sibling)

    def pass_last(self, n):
        p = self.p
        for i in self.arrays(n):
            self.copies[(i, 8 + n)].wait_recv()
            self.copies[(i, 12 + n)].wait_recv()
            whole = self.plane(i, n).at[1 - p.x, 1 - p.y, p.core]
            self.go(i, 28 + n, whole, whole, p.sibling)

    def arrived(self, n):
        for i in range(len(self.fulls)):
            for slot in (16, 20, 24, 28):
                self.copies[(i, slot + n)].wait_recv()
            self.copies.pop((i, 32 + n)).wait()
            self.seen.add((i, n))

    def finish(self):
        for (i, slot), copy in self.copies.items():
            if slot >= 32:
                copy.wait()
            else:
                copy.wait_send()
                if slot >= 16 and (i, slot % 4) not in self.seen:
                    copy.wait_recv()

    @classmethod
    def scratch(cls, count):
        return [
            pltpu.SemaphoreType.DMA((count, cls.SLOTS)),
            pltpu.SemaphoreType.DMA((count, cls.SLOTS)),
            pltpu.SemaphoreType.DMA((count, 4)),
        ]


def everyone(p):
    ids = []
    for d in range(8):
        for e in range(4):
            if d or e:
                ids.append({"ch": lax.rem(p.ch + d, 8), "seq": lax.rem(p.seq + e, 4)})
    return ids


def make_filter(p, table, first, second, shift, speed, hidden, filt, size, start, stop):
    length = 8 * size
    lane = (lax.broadcasted_iota(jnp.int32, (1, 128), 1) + p.ch * 128).astype(F32)
    rate = SLOW_RATE + (FAST_RATE - SLOW_RATE) * lane / 1023.0

    def step(j, carry):
        rows = pl.ds(pl.multiple_of(j * size, size), size)
        inner = jnp.dot(table[rows], first[...], precision=HIGH, preferred_element_type=F32) + shift[...]
        wave = jnp.sin(speed[...] * inner)
        hidden[rows] = wave
        place = (lax.broadcasted_iota(jnp.int32, (size, 1), 0) + j * size).astype(F32) / (length - 1)
        filt[j] = jnp.dot(wave, second[...], precision=HIGH, preferred_element_type=F32) * jnp.exp(-place * rate)
        return carry

    lax.fori_loop(start, stop, step, 0)


def start_kernel(size, *refs):
    taps, skip, gains, tokens, table, first, second, shift, speed = refs[:9]
    shards = refs[9:12]
    consts, halo, hidden, filt = refs[12:16]
    full = refs[16]
    columns = list(refs[17:19])
    pack, packs, send, recv, halo_sems, column_in, first_wide = refs[19:26]
    column_sems, later_sems, gather_sems = refs[26:29], refs[29:32], refs[32:35]
    p = Place()
    ids = everyone(p)
    greet(ids)
    column = Columns(p, shards[:1], [column_in], *column_sems)
    later = Columns(p, shards[1:], columns, *later_sems)
    gather = Gather(p, [column_in], [full], 0.5, *gather_sems)
    column.start()
    pack[...] = jnp.zeros_like(pack)
    part = gains.shape[1]
    pack[10:12, :part] = gains[...].astype(F32)
    moved = pltpu.roll(pack[8:16], p.seq * part, 1)
    pack[8:16] = moved
    for n in range(9):
        pack[n : n + 1] = taps[n // 3, n % 3 : n % 3 + 1]
    pack[9:10] = skip[...]
    column.copies[(0, 3)].wait()
    gather.start_x([0])
    gather.start_y([0])
    copies = [push(pack, packs.at[p.ch, p.seq], send.at[n], recv.at[n], one) for n, one in enumerate(ids)]
    copies.append(push(tokens.at[:, pl.ds(size - 16, 16)], halo, halo_sems.at[0], halo_sems.at[1], {"ch": lax.rem(p.ch + 1, 8)}))
    packs[p.ch, p.seq] = pack[...]
    column.copies[(0, 0)].wait_recv()
    gather.start_x([1])
    gather.start_y([1])
    column.pass_far()
    gather.start_x([2])
    gather.start_y([2])
    gather.pass_sides(0)
    first_wide[...] = jnp.zeros_like(first_wide)
    first_wide[: first.shape[0]] = first[...]

    def filter_part(start):
        make_filter(p, table, first_wide, second, shift, speed, hidden, filt, size, start, start + 2)

    filter_part(0)
    filter_part(2)
    column.copies[(0, 2)].wait_recv()
    gather.start_x([3])
    gather.start_y([3])
    later.start()
    gather.pass_sides(1)
    gather.pass_sides(2)
    filter_part(4)
    gather.pass_sides(3)
    gather.pass_last(0)
    gather.pass_last(1)
    filter_part(6)
    gather.pass_last(2)
    gather.pass_last(3)
    wait_all(copies)
    row = lax.broadcasted_iota(jnp.int32, (16, 128), 0)
    for c in range(8):
        one = packs[c, 0]
        total = one + packs[c, 1] + packs[c, 2] + packs[c, 3]
        consts[:, c * 128 : (c + 1) * 128] = jnp.where(row < 10, one, total)
    gather.finish()
    for slot in (0, 1, 2):
        column.copies[(0, slot)].wait_send()
    for i in range(2):
        for slot in (0, 1, 3):
            later.copies[(i, slot)].wait()


def start_call(taps, skip, gains, tokens, table, first, second, shift, speed, shards, size):
    rows, cols = shards[0].shape
    filt_width = second.shape[0]
    out = pl.pallas_call(
        functools.partial(start_kernel, size),
        out_shape=[
            jax.ShapeDtypeStruct((16, 1024), F32),
            jax.ShapeDtypeStruct((2, 16, 1024), BF),
            jax.ShapeDtypeStruct((8 * size, filt_width), F32),
            jax.ShapeDtypeStruct((8, size, 128), F32),
            jax.ShapeDtypeStruct((4, 2, 2, 2, rows, cols), BF),
            jax.ShapeDtypeStruct((4,) + shards[1].shape, BF),
            jax.ShapeDtypeStruct((4,) + shards[2].shape, BF),
        ],
        in_specs=[VM] * 12,
        out_specs=[VM] * 4 + [ANYWHERE] + [VM] * 2,
        scratch_shapes=[
            pltpu.VMEM((16, 128), F32),
            pltpu.VMEM((8, 4, 16, 128), F32),
            pltpu.SemaphoreType.DMA((31,)),
            pltpu.SemaphoreType.DMA((31,)),
            pltpu.SemaphoreType.DMA((2,)),
            pltpu.VMEM((4, rows, cols), BF),
            pltpu.VMEM((table.shape[1], filt_width), F32),
        ]
        + Columns.scratch(1)
        + Columns.scratch(2)
        + Gather.scratch(1),
        compiler_params=pltpu.CompilerParams(collective_id=4, has_side_effects=True, vmem_limit_bytes=VMEM_LIMIT),
    )(taps, skip, gains, tokens, table, first, second, shift, speed, *shards)
    return out[:4], out[4].reshape(rows * 32, cols), out[5:]


def lagged(u, buf, b, stream, lane, size, width):
    at = pl.ds(pl.multiple_of(stream * width + lane, 128), 128)
    rows = size * 2
    buf[pl.ds(0, 16)] = u[pl.ds(rows + 16 * b, 16), at].astype(F32)
    buf[pl.ds(16, size)] = u[pl.ds(b * size, size), at].astype(F32)
    return buf[pl.ds(16, size)], buf[pl.ds(15, size)], buf[pl.ds(14, size)]


def short_conv(u, buf, consts, b, stream, lane, size, width):
    now, one, two = lagged(u, buf, b, stream, lane, size, width)
    at = pl.ds(lane, 128)
    return consts[stream : stream + 1, at] * now + consts[3 + stream : 4 + stream, at] * one + consts[
        6 + stream : 7 + stream, at
    ] * two


def make_pieces(p, make):
    for d in (1, 2, 3, 0):
        make(lax.rem(p.ch // 2 + d, 4))


def send_pieces(p, pieces, blocks_ref, b, send, recv, local, make=None):
    copies = []
    mine = p.ch // 2
    at = pl.ds(b * 128, 128)
    for d in (1, 2, 3, 0):
        pair = lax.rem(mine + d, 4)
        if make is not None:
            make(pair)
        for k in range(2):
            block = 2 * pair + k if d else (p.ch + 1 - 2 * lax.rem(p.ch, 2) if k == 0 else p.ch)
            far = lax.rem(block - p.ch + 8, 8)
            src, dst = pieces.at[block, :, at], blocks_ref.at[p.ch, :, at]
            if d == 0 and k == 1:
                copy = pltpu.make_async_copy(src, dst, local.at[b])
                copy.start()
                copies.append(copy)
            else:
                copies.append(push(src, dst, send.at[far, b], recv.at[far, b], {"ch": block}))
    return copies


def send_blocks(p, ys, blocks_ref, b, send, recv, local):
    at = pl.ds(b * 128, 128)
    copies = []
    for d in range(7):
        src, dst = ys.at[p.ch_ahead[d], :, at], blocks_ref.at[p.ch, :, at]
        copies.append(push(src, dst, send.at[d, b], recv.at[d, b], {"ch": p.ch_ahead[d]}))
    copy = pltpu.make_async_copy(ys.at[p.ch, :, at], blocks_ref.at[p.ch, :, at], local.at[b])
    copy.start()
    return copies + [copy]


def half(b):
    return slice(b * 128, (b + 1) * 128)


def fill_mask(p, lengths, mask, size, first):
    for b in range(2):
        place = lax.broadcasted_iota(jnp.int32, (size, 128), 0) + (p.ch * OWN + first)
        inside = jnp.where(place < lengths[0, b], 1.0, 0.0)
        mask[pl.ds(b * size, size)] = jnp.where(place < 0, 0.0, inside)


def norm_rows(values, gain):
    centre = values - jnp.mean(values, axis=1, keepdims=True)
    inverse = lax.rsqrt(jnp.mean(centre * centre, axis=1, keepdims=True) + EPS)
    return centre * inverse, inverse


def forward_kernel(size, loads, *refs):
    lengths, tokens, halo, consts, h_ref, fh, fl, th, tl, lanes, down_shard = refs[:11]
    columns = list(refs[11:13])
    w_in = refs[13]
    normed, u, mixer, kept, convolved, mask, column_down = refs[14:21]
    fulls = refs[21:24]
    weight, xs, abc, ys, pieces, gates, mixes, bufs, mask_before, far_out, far_up = refs[24:35]
    send, recv, local, send_back, recv_back, local_back = refs[35:41]
    weight_sems, far_sems, column_sems, gather_sems = refs[41], refs[42], refs[43:46], refs[46:]
    p = Place()
    width = 1024
    rows = 2 * size
    load = pltpu.make_async_copy(w_in, weight, weight_sems)
    load.start()
    greet([{"ch": one} for one in p.ch_ahead] + [p.sibling, p.along_y])
    gather = Gather(p, columns, fulls, SHARE, *gather_sems, places=EARLY, by_place=(2,))
    for i in (10, 11, 12):
        loads[i].wait()
    gather.source = {(2, 0): down_shard, (0, 3): far_out, (1, 3): far_up}
    fars = []
    for i, place in enumerate((far_out, far_up)):
        fars.append(push(columns[i].at[p.others[1]], place, far_sems.at[i, 0], far_sems.at[i, 1], p.along_z[0]))
    gather.start_x([0])
    gather.start_y([0])
    gather.start_y([1], arrays=(0, 1))
    loads[1].wait()
    fill_mask(p, lengths, mask, size, 0)
    fill_mask(p, lengths, mask_before, 16, -16)
    gain = consts[10:11, :]

    def norm(i, carry):
        here = pl.ds(pl.multiple_of(i * 32, 32), 32)
        one, _ = norm_rows(tokens[here].astype(F32) * mask[here, 0:1], gain)
        normed[here] = (one * gain).astype(BF)
        return carry

    lax.fori_loop(0, rows // 32, norm, 0)
    before = halo[...].reshape(32, width).astype(F32) * mask_before[:, 0:1]
    before = (norm_rows(before, gain)[0] * gain).astype(BF)
    load.wait()

    def make(pair):
        for stream in range(3):
            at = pl.ds(pl.multiple_of(stream * width + pair * 256, 256), 256)
            u[pl.ds(0, rows), at] = mm(normed[...], weight[:, at]).astype(BF)
            u[pl.ds(rows, 32), at] = mm(before, weight[:, at]).astype(BF)
        for k in range(2):
            block = 2 * pair + k
            lane = pl.multiple_of(block * 128, 128)
            for b in range(2):
                gates[block, b] = short_conv(u, bufs.at[0], consts, b, 0, lane, size, width)
                key = short_conv(u, bufs.at[1], consts, b, 1, lane, size, width)
                mix = key * short_conv(u, bufs.at[2], consts, b, 2, lane, size, width)
                mixes[block, b] = mix
                pieces[block, :, half(b)] = mix.astype(BF)

    arriving = [send_pieces(p, pieces, kept, 0, send, recv, local, make)]
    arriving.append(send_pieces(p, pieces, kept, 1, send, recv, local))
    gather.start_x([1], arrays=(0, 1))
    loads[4].wait()
    loads[14].start()
    loads[15].start()
    filter_spectra(fh, fl, lanes, h_ref, abc, 8, size)
    gather.pass_sides(0)
    gather.start_y([2], arrays=(0, 1))
    leaving = []
    for b in range(2):
        wait_all(arriving[b])
        if b == 1:
            loads[17].start()
        spectra(fh, fl, kept, xs, 8, half(b))
        products_forward(xs, abc, lanes, xs, 8, size, (b,))
        inverse_blocks(th, tl, xs, ys, 8, half(b))
        leaving.append(send_blocks(p, ys, convolved, b, send_back, recv_back, local_back))
        if b == 0:
            gather.start_x([2], arrays=(0, 1))
            gather.pass_sides(1)
            wait_all(fars)
            gather.start_y([3], arrays=(0, 1))
    gather.start_x([3], arrays=(0, 1))
    gather.pass_sides(2)
    gather.pass_last(0)
    for b in range(2):
        rows = slice(b * size, (b + 1) * size)
        wait_all(leaving[b])
        for c in range(8):
            at = half(c)
            long_part = convolved[c, :, half(b)].astype(F32) + consts[9:10, at] * mixes[c, b]
            mixer[rows, at] = (gates[c, b] * long_part * mask[rows]).astype(BF)
        if b == 1:
            column = Columns(p, [down_shard], [column_down], *column_sems)
            column.start()
    gather.pass_sides(3)
    for n in range(1, 4):
        gather.pass_last(n)
    gather.finish()
    for slot in (0, 1, 3):
        column.copies[(0, slot)].wait()


def backward_kernel(size, count, loads, *refs):
    u, consts, mask, grad_mixer, convolved, kept, h_ref, fh, fl, th, tl, lanes = refs[:12]
    grads, plane = list(refs[12 : 13 + count]), refs[13]
    del grads[1]
    refs = refs[1:]
    du, dh_ref, sums = refs[12 + count : 15 + count]
    outs, far_out = refs[15 + count : 15 + 2 * count], refs[15 + 2 * count]
    rest = refs[16 + 2 * count :]
    xs, ds, abc, gh, pieces, arrived, returned, keys, values, dlongs, dcs, edge_out, edge_in, ends, bufs = rest[:15]
    send, recv, local, send_back, recv_back, local_back, edge_sems = rest[15:22]
    p = Place()
    width = 1024
    greet([{"ch": one} for one in p.ch_ahead] + [p.sibling, p.along_y])
    for i in (0, 2, 3):
        loads[i].wait()
    up_cols = grads[1].shape[5]
    whole = [grads[0], (grads[1], 0, up_cols // 2), (grads[1], up_cols // 2, up_cols // 2), (grads[2], 0, grads[2].shape[5])]
    stops = [None, outs[1], outs[1], outs[2]]
    scatter = Scatter(p, whole, [outs[0]] + [None] * 3, stops, SHARE_BACK, rest[28:])
    planes = Planes(p, grads[0], plane, *rest[22:28])
    loads[13].wait()
    planes.turn(0)
    scatter.start(1)
    scatter.start(2)
    scatter.start(3)
    sums[...] = jnp.zeros_like(sums)

    def grad_parts(block, b, rows, skip):
        at = pl.ds(pl.multiple_of(block * 128, 128), 128)
        take = max(rows, 16)
        masked = grad_mixer[pl.ds(b * size, take), at].astype(F32)[:rows] * mask[pl.ds(b * size, rows)]
        conv = convolved[block, :take, b * 128 : (b + 1) * 128].astype(F32)[:rows]
        return masked, conv + skip * (keys[block, b, :rows] * values[block, b, :rows])

    def make(pair):
        for k in range(2):
            make_block(2 * pair + k)

    def make_block(block):
        lane = pl.multiple_of(block * 128, 128)
        at = pl.ds(lane, 128)
        total = jnp.zeros((1, 128), F32)
        for b in range(2):
            rows = pl.ds(b * size, size)
            gate = short_conv(u, bufs.at[0], consts, b, 0, lane, size, width)
            key = short_conv(u, bufs.at[1], consts, b, 1, lane, size, width)
            value = short_conv(u, bufs.at[2], consts, b, 2, lane, size, width)
            keys[block, b] = key
            values[block, b] = value
            dlong = grad_mixer[rows, at].astype(F32) * mask[rows] * gate
            dlongs[block, b] = dlong
            pieces[block, :, b * 128 : (b + 1) * 128] = dlong.astype(BF)
            total = total + jnp.sum(dlong * (key * value), axis=0, keepdims=True)
        sums[9:10, at] = total

    arriving = [send_pieces(p, pieces, arrived, 0, send, recv, local, make)]
    arriving.append(send_pieces(p, pieces, arrived, 1, send, recv, local))
    scatter.core(1)
    loads[6].wait()
    filter_spectra(fh, fl, lanes, h_ref, abc, 8, size)
    loads[5].wait()
    spectra(fh, fl, kept, xs, 8)
    leaving = []
    for b in range(2):
        wait_all(arriving[b])
        spectra(fh, fl, arrived, ds, 8, half(b))
        products_backward(xs, ds, abc, gh, lanes, 8, size, (b,))
        inverse_blocks(th, tl, ds, pieces, 8, half(b))
        leaving.append(send_blocks(p, pieces, returned, b, send_back, recv_back, local_back))
        if b == 0:
            scatter.core(2)
            scatter.core(3)
            planes.cross(0)
    scatter.first(1)
    filter_gradient(th, tl, gh, dh_ref, 8, size)
    loads[17].start()
    loads[12].wait()
    planes.last(0, p.others[2])
    scatter.turn(0)
    loads[4].wait()
    wait_all(leaving[0])
    wait_all(leaving[1])

    def edges(c, carry):
        at = pl.ds(pl.multiple_of(c * 128, 128), 128)
        skip = consts[9:10, at]
        for b in range(2):
            masked, long_part = grad_parts(c, b, 8, skip)
            back = returned[c, :16, b * 128 : (b + 1) * 128].astype(F32)[:8]
            dmixed = back + skip * dlongs[c, b, :8]
            dmixed = dmixed[:2]
            edge_out[2 * b : 2 * b + 2, at] = (masked * long_part)[:2]
            edge_out[4 + 2 * b : 6 + 2 * b, at] = dmixed * values[c, b, :8][:2]
            edge_out[8 + 2 * b : 10 + 2 * b, at] = dmixed * keys[c, b, :8][:2]
        return carry

    lax.fori_loop(0, 8, edges, 0)
    edge = push(edge_out, edge_in, edge_sems.at[0], edge_sems.at[1], {"ch": lax.rem(p.ch + 7, 8)})
    scatter.first(2)
    scatter.first(3)

    def streams(c, carry):
        lane = pl.multiple_of(c * 128, 128)
        at = pl.ds(lane, 128)
        skip = consts[9:10, at]
        for b in range(2):
            masked, long_part = grad_parts(c, b, size, skip)
            dmixed = returned[c, :, b * 128 : (b + 1) * 128].astype(F32) + skip * dlongs[c, b]
            dcs[0, b, pl.ds(0, size)] = masked * long_part
            dcs[1, b, pl.ds(0, size)] = dmixed * values[c, b]
            dcs[2, b, pl.ds(0, size)] = dmixed * keys[c, b]
        for stream in range(3):
            out = pl.ds(pl.multiple_of(stream * width + lane, 128), 128)
            totals = [jnp.zeros((1, 128), F32)] * 3
            for b in range(2):
                dcs[stream, b, pl.ds(size, 8)] = jnp.zeros((8, 128), F32)
                parts = lagged(u, bufs.at[stream], b, stream, lane, size, width)
                grad = dcs[stream, b, pl.ds(0, size)]
                for lag in range(3):
                    totals[lag] = totals[lag] + jnp.sum(grad * parts[lag], axis=0, keepdims=True)
                total = consts[stream : stream + 1, at] * grad
                total = total + consts[3 + stream : 4 + stream, at] * dcs[stream, b, pl.ds(1, size)]
                total = total + consts[6 + stream : 7 + stream, at] * dcs[stream, b, pl.ds(2, size)]
                du[pl.ds(b * size, size), out] = total.astype(BF)
                ends[stream, b, :, at] = total[size - 16 :]
            for lag in range(3):
                row = 3 * lag + stream
                sums[row : row + 1, at] = totals[lag]
        return carry

    lax.fori_loop(0, 8, streams, 0)
    edge.wait()

    inside = jnp.where(p.ch < 7, 1.0, 0.0)
    for stream in range(3):
        one = consts[3 + stream : 4 + stream, :] * inside
        two = consts[6 + stream : 7 + stream, :] * inside
        out = slice(stream * width, (stream + 1) * width)
        for b in range(2):
            row = 4 * stream + 2 * b
            near, far = edge_in[row : row + 1, :], edge_in[row + 1 : row + 2, :]
            ends[stream, b, 14:15] = ends[stream, b, 14:15] + two * near
            ends[stream, b, 15:16] = ends[stream, b, 15:16] + one * near + two * far
            du[(b + 1) * size - 16 : (b + 1) * size, out] = ends[stream, b].astype(BF)
    loads[16].start()
    scatter.second(1)
    scatter.second(2)
    scatter.second(3)
    scatter.near(0, outs[0], far_out)


def nt(a, b):
    return lax.dot_general(a, b, (((1,), (1,)), ((), ())), preferred_element_type=F32)


def tn(a, b):
    return lax.dot_general(a, b, (((0,), (0,)), ((), ())), preferred_element_type=F32)


GELU_ONE = math.sqrt(2.0 / math.pi)
GELU_THREE = GELU_ONE * 0.044715


class Planes:
    def __init__(self, place, column, acc, one_a, one_b, two_a, two_b, send, recv):
        self.p, self.column = place, column
        self.acc, self.one_a, self.one_b, self.two_a, self.two_b = acc, one_a, one_b, two_a, two_b
        self.send, self.recv = send, recv
        self.copies = {}
        cols = acc.shape[4]
        half = split_columns(cols, 0.5)
        self.low, self.high = pl.ds(0, half), pl.ds(half, cols - half)

    def go(self, n, slot, src, dst, device):
        self.copies[(n, slot)] = push(src, dst, self.send.at[n, slot], self.recv.at[n, slot], device)

    def done(self, n, *slots):
        for slot in slots:
            self.copies[(n, slot)].wait()

    def core(self, n, made):
        self.go(n, 0, made.at[:, :, 1 - self.p.core], self.acc.at[n], self.p.sibling)

    def sides(self, n, made):
        p, acc = self.p, self.acc.at[n]
        self.done(n, 0)

        def step(k, carry):
            xx, yy = k // 2, lax.rem(k, 2)
            acc[xx, yy] = add_rows(acc[xx, yy], made[xx, yy, p.core])
            return carry

        lax.fori_loop(0, 4, step, 0)

    def turn(self, n):
        p, acc = self.p, self.acc.at[n]
        self.go(n, 1, acc.at[:, 1 - p.y, :, self.low], self.one_a.at[n], p.along_y)
        self.go(n, 2, acc.at[1 - p.x, :, :, self.high], self.one_b.at[n], p.along_x)

    def cross(self, n):
        p, acc = self.p, self.acc.at[n]
        low, high = self.low, self.high
        self.done(n, 1, 2)
        for k in range(2):
            acc[k, p.y, :, low] = add_rows(acc[k, p.y, :, low], self.one_a[n, k])
            acc[p.x, k, :, high] = add_rows(acc[p.x, k, :, high], self.one_b[n, k])
        self.go(n, 3, acc.at[1 - p.x, p.y, :, low], self.two_a.at[n], p.along_x)
        self.go(n, 4, acc.at[p.x, 1 - p.y, :, high], self.two_b.at[n], p.along_y)

    def last(self, n, zz):
        p, acc = self.p, self.acc.at[n]
        low, high = self.low, self.high
        self.done(n, 3, 4)
        self.column[zz, :, low] = add_rows(acc[p.x, p.y, :, low], self.two_a[n])
        self.column[zz, :, high] = add_rows(acc[p.x, p.y, :, high], self.two_b[n])

    @staticmethod
    def scratch(count, rows, cols):
        half = split_columns(cols, 0.5)
        return [
            pltpu.VMEM((count, 2, rows, half), BF),
            pltpu.VMEM((count, 2, rows, cols - half), BF),
            pltpu.VMEM((count, rows, half), BF),
            pltpu.VMEM((count, rows, cols - half), BF),
            pltpu.SemaphoreType.DMA((count + 1, 5)),
            pltpu.SemaphoreType.DMA((count + 1, 5)),
        ]


def feed_forward_kernel(loads, *refs):
    mixer, tokens, mask, cot, consts, w_out, w_up, early, column = refs[:9]
    result, grad_after, grad_mixer, grad_gain, grad_out, sum_column, sum_last, grad_up = refs[9:17]
    up, planes, late, total, unit, scale, normed, turned, da, pre, dact, act, dpre, kept_down, kept_up = refs[17:32]
    up_sem, plane_sems, out_sems, sum_acc, far_place = refs[32:37]
    far_sems, gather_sems, scatter_refs = refs[37], refs[38:41], refs[41:47]
    p = Place()
    greet([p.along_x, p.along_y, p.along_z[0], p.sibling])
    loads[8].wait()
    gather = Gather(p, [column], [late], 0.5, *gather_sems, places=LATE, by_place=(0,))
    gather.source = {(0, 3): far_place}
    far = push(column.at[p.others[1]], far_place, far_sems.at[0], far_sems.at[1], p.along_z[0])
    gather.start_x([1, 2])
    gather.start_y([1, 2])
    sums = Planes(p, sum_column, sum_acc, *scatter_refs)
    weights = [pltpu.make_async_copy(w_up, up, up_sem)]
    weights += [pltpu.make_async_copy(early.at[n], planes.at[n], plane_sems.at[n]) for n in EARLY]
    for load in weights:
        load.start()
    gain = consts[11:12, :]
    loads[0].wait()
    loads[5].wait()
    total[...] = mm(mixer[...], w_out[...])
    loads[1].wait()
    loads[2].wait()
    loads[3].wait()

    def norm(i, carry):
        rows = pl.ds(pl.multiple_of(i * 32, 32), 32)
        zero = tokens[rows].astype(F32) * mask[rows, 0:1]
        value = zero + total[rows]
        total[rows] = value
        centre = value - jnp.mean(value, axis=1, keepdims=True)
        inverse = lax.rsqrt(jnp.mean(centre * centre, axis=1, keepdims=True) + EPS)
        one = centre * inverse
        unit[rows] = one
        scale[rows] = jnp.broadcast_to(inverse, (32, 128))
        normed[rows] = (one * gain).astype(BF)
        return carry

    lax.fori_loop(0, 16, norm, 0)
    turned[...] = normed[...].T
    wait_all(weights)
    writes = [None] * 4
    for n in range(4):
        zz = gather.place(n)
        cols = pl.ds(pl.multiple_of(zz * 1024, 1024), 1024)
        slot = n % 2
        made = kept_down.at[slot]
        pre[...] = mm(normed[...], up[:, cols])
        if n == 0:
            gather.pass_sides(1)
            far.wait()
            gather.start_x([3])
            gather.start_y([3])
            plane = planes.at[0]
        else:
            gather.arrived(n)
            plane = late.at[n - 1]
        if n > 0:
            sums.sides(n - 1, kept_down.at[1 - slot])
            sums.turn(n - 1)
        dact[...] = nt(cot[...], plane[...].reshape(1024, 1024))

        def gelu(i, carry):
            rows = pl.ds(pl.multiple_of(i * 16, 16), 16)
            x = pre[rows]
            square = x * x
            t = jnp.tanh(x * (GELU_ONE + GELU_THREE * square))
            half = 0.5 + 0.5 * t
            value = x * half
            act[rows] = value.astype(BF)
            slope = half + value * (1.0 - t) * (GELU_ONE + 3.0 * GELU_THREE * square)
            dpre[rows] = (dact[rows] * slope).astype(BF)
            return carry

        lax.fori_loop(0, 32, gelu, 0)
        if n > 1:
            wait_all(writes[n - 2])
        made[...] = tn(act[...], cot[...]).astype(BF).reshape(2, 2, 2, 128, 1024)
        sums.core(n, made)
        total[...] += mm(act[...], plane[...].reshape(1024, 1024))
        if n > 1:
            sums.cross(n - 2)
        if n < 2:
            gather.pass_sides(n + 2)
        back = nt(dpre[...], up[:, cols])
        da[...] = back if n == 0 else da[...] + back
        if n < 3:
            gather.pass_last(n + 1)
        kept_up[slot] = mm(turned[...], dpre[...]).astype(BF)
        writes[n] = [pltpu.make_async_copy(kept_up.at[slot], grad_up.at[:, cols], out_sems.at[n])]
        for copy in writes[n]:
            copy.start()
    sums.sides(3, kept_down.at[1])
    sum_last[0] = sum_acc[3]
    sums.last(0, gather.place(0))

    def finish(i, gain_sum):
        rows = pl.ds(pl.multiple_of(i * 32, 32), 32)
        result[rows] = total[rows].astype(BF)
        one = unit[rows]
        back = da[rows]
        e = back * gain
        inner = e - jnp.mean(e, axis=1, keepdims=True) - one * jnp.mean(e * one, axis=1, keepdims=True)
        after = cot[rows].astype(F32) + scale[rows, 0:1] * inner
        grad_after[rows] = after
        normed[rows] = after.astype(BF)
        return gain_sum + jnp.sum(back * one, axis=0, keepdims=True)

    grad_gain[...] = lax.fori_loop(0, 16, finish, jnp.zeros((1, 1024), F32))
    loads[9].start()
    loads[10].start()
    grad_mixer[...] = nt(normed[...], w_out[...]).astype(BF)
    loads[11].start()
    sums.cross(2)
    sums.last(1, gather.place(1))
    grad_out[...] = tn(mixer[...], normed[...]).astype(BF)
    for n in (2, 3):
        wait_all(writes[n])
    gather.finish()
    sums.last(2, gather.place(2))
    sum_column[gather.place(3)] = sum_acc[3, 0, 0]


def feed_forward_call(mixer, tokens, mask, cot, consts, w_out, w_up, early, column):
    rows, width = mixer.shape
    hidden = w_up.shape[1]
    wide = (rows, width)
    square = (width, width)
    part = column.shape[1:]
    operands = (mixer, tokens, mask, cot, consts, w_out, w_up, early, column)
    fetch = (0, 1, 2, 3, 5, 8)
    store = (0, 1, 2)
    outs = [
        jax.ShapeDtypeStruct(wide, BF),
        jax.ShapeDtypeStruct(wide, F32),
        jax.ShapeDtypeStruct(wide, BF),
        jax.ShapeDtypeStruct((1, width), F32),
        jax.ShapeDtypeStruct(square, BF),
        jax.ShapeDtypeStruct((4,) + part, BF),
        jax.ShapeDtypeStruct((1, 2, 2) + part, BF),
        jax.ShapeDtypeStruct((width, hidden), BF),
        ]
    return pl.pallas_call(
        fetching(feed_forward_kernel, fetch, [len(operands) + i for i in store]),
        out_shape=outs,
        in_specs=fetch_specs(operands[:6], fetch) + [ANYWHERE] * 3,
        out_specs=fetch_specs(outs[:7], store) + [ANYWHERE],
        scratch_shapes=[
            pltpu.VMEM((width, hidden), BF),
            pltpu.VMEM((len(EARLY), 2, 2, 2) + part, BF),
            pltpu.VMEM((len(LATE), 2, 2, 2) + part, BF),
            pltpu.VMEM(wide, F32),
            pltpu.VMEM(wide, F32),
            pltpu.VMEM((rows, 128), F32),
            pltpu.VMEM(wide, BF),
            pltpu.VMEM((width, rows), BF),
            pltpu.VMEM(wide, F32),
            pltpu.VMEM(wide, F32),
            pltpu.VMEM(wide, F32),
            pltpu.VMEM(wide, BF),
            pltpu.VMEM(wide, BF),
            pltpu.VMEM((2, 2, 2, 2) + part, BF),
            pltpu.VMEM((2,) + square, BF),
            pltpu.SemaphoreType.DMA,
            pltpu.SemaphoreType.DMA((len(EARLY),)),
            pltpu.SemaphoreType.DMA((4,)),
            pltpu.VMEM((4, 2, 2) + part, BF),
            pltpu.VMEM(part, BF),
            pltpu.SemaphoreType.DMA((2,)),
        ]
        + Gather.scratch(1)
        + Planes.scratch(3, *part)
        + fetch_scratch(operands, fetch, outs, store),
        compiler_params=pltpu.CompilerParams(collective_id=5, has_side_effects=True, vmem_limit_bytes=VMEM_LIMIT),
    )(*operands)


def exchange_sems():
    pieces = [pltpu.SemaphoreType.DMA((8, 2))] * 2 + [pltpu.SemaphoreType.DMA((2,))]
    return pieces + [pltpu.SemaphoreType.DMA((7, 2))] * 2 + [pltpu.SemaphoreType.DMA((2,))]


def forward_call(lengths, tokens, halo, consts, filt, tables, down_shard, columns, w_in, size):
    rows = 2 * size
    block = (8, size, 256)
    piece = (8, 2, size, 128)
    operands = (lengths, tokens, halo, consts, filt) + tables + (down_shard,) + tuple(columns)
    whole = [jax.ShapeDtypeStruct((4, 2, 2, 2) + one.shape[1:], BF) for one in columns]
    whole.append(jax.ShapeDtypeStruct((len(EARLY), 2, 2, 2) + down_shard.shape, BF))
    fetch = (1, 4, 10, 11, 12)
    store = (0, 1, 3)
    outs = [
        jax.ShapeDtypeStruct((rows, 1024), BF),
        jax.ShapeDtypeStruct((rows + 32, 3072), BF),
        jax.ShapeDtypeStruct((rows, 1024), BF),
        jax.ShapeDtypeStruct(block, BF),
        jax.ShapeDtypeStruct(block, BF),
        jax.ShapeDtypeStruct((rows, 128), F32),
        jax.ShapeDtypeStruct((4,) + down_shard.shape, BF),
    ]
    first = len(operands) + 1
    out = pl.pallas_call(
        fetching(functools.partial(forward_kernel, size), fetch, [first + i for i in store]),
        out_shape=outs + whole,
        in_specs=[pl.BlockSpec(memory_space=pltpu.SMEM)] + fetch_specs(operands, fetch)[1:] + [ANYWHERE],
        out_specs=fetch_specs(outs, store) + [ANYWHERE] * 3,
        scratch_shapes=[
            pltpu.VMEM(w_in.shape, BF),
            pltpu.VMEM((8, 2 * size, 256), F32),
            pltpu.VMEM((8, 2, size, 128), F32),
            pltpu.VMEM(block, BF),
            pltpu.VMEM(block, BF),
            pltpu.VMEM(piece, F32),
            pltpu.VMEM(piece, F32),
            pltpu.VMEM((3, size + 16, 128), F32),
            pltpu.VMEM((32, 128), F32),
            pltpu.VMEM(columns[0].shape[1:], BF),
            pltpu.VMEM(columns[1].shape[1:], BF),
        ]
        + exchange_sems()
        + [pltpu.SemaphoreType.DMA, pltpu.SemaphoreType.DMA((2, 2))]
        + Columns.scratch(1)
        + Gather.scratch(3)
        + fetch_scratch(operands, fetch, outs, store),
        compiler_params=pltpu.CompilerParams(collective_id=1, has_side_effects=True, vmem_limit_bytes=VMEM_LIMIT),
    )(*operands, w_in)
    return out[:7], [one.reshape(-1, one.shape[-1]) for one in out[7:9]], out[9]


def backward_call(u, consts, mask, grad_mixer, convolved, kept, filt, tables, grads, plane, size):
    rows = 2 * size
    block = (8, size, 256)
    piece = (8, 2, size, 128)
    operands = (u, consts, mask, grad_mixer, convolved, kept, filt) + tables
    count = len(grads)
    shapes = [grads[0].shape[1:]] + [(one.shape[0] // 32, one.shape[1]) for one in grads[1:]]
    views = [grads[0]] + [one.reshape((4, 2, 2, 2) + shape) for one, shape in zip(grads[1:], shapes[1:])]
    fetch = (0, 2, 3, 4, 5, 6, 12, 13)
    store = (0, 1)
    outs = [
        jax.ShapeDtypeStruct((rows, 3072), BF),
        jax.ShapeDtypeStruct((8, size, 128), F32),
        jax.ShapeDtypeStruct((16, 1024), F32),
    ]
    (up_rows, up_cols), out_kind = shapes[1], shapes[2]
    kinds = [shapes[0] + ("", False)] + [(up_rows, up_cols // 2, "load", True)] * 2 + [out_kind + ("load", True)]
    operands = operands + (views[0], plane)
    out = pl.pallas_call(
        fetching(functools.partial(backward_kernel, size, count), fetch, [len(operands) + count - 1 + i for i in store]),
        out_shape=outs
        + [jax.ShapeDtypeStruct(shapes[0], F32)]
        + [jax.ShapeDtypeStruct((4,) + shape, BF) for shape in shapes[1:]]
        + [jax.ShapeDtypeStruct(shapes[0], BF)],
        in_specs=fetch_specs(operands, fetch) + [ANYWHERE] * (count - 1),
        out_specs=fetch_specs(outs, store) + [VM] * (1 + count),
        scratch_shapes=[
            pltpu.VMEM((8, 2 * size, 256), F32),
            pltpu.VMEM((8, 2 * size, 256), F32),
            pltpu.VMEM((8, 2, size, 128), F32),
            pltpu.VMEM((8, 2, size, 128), F32),
            pltpu.VMEM(block, BF),
            pltpu.VMEM(block, BF),
            pltpu.VMEM(block, BF),
            pltpu.VMEM(piece, F32),
            pltpu.VMEM(piece, F32),
            pltpu.VMEM(piece, F32),
            pltpu.VMEM((3, 2, size + 8, 128), F32),
            pltpu.VMEM((16, 1024), F32),
            pltpu.VMEM((16, 1024), F32),
            pltpu.VMEM((3, 2, 16, 1024), F32),
            pltpu.VMEM((3, size + 16, 128), F32),
        ]
        + exchange_sems()
        + [pltpu.SemaphoreType.DMA((2,))]
        + Planes.scratch(1, *shapes[0])
        + Scatter.scratch(kinds, SHARE_BACK)
        + fetch_scratch(operands, fetch, outs, store),
        compiler_params=pltpu.CompilerParams(collective_id=2, has_side_effects=True, vmem_limit_bytes=VMEM_LIMIT),
    )(*operands, *views[1:])
    return out[:3], out[3:]


def add_rows(target, other):
    return (target.astype(F32) + other.astype(F32)).astype(BF)


class Scatter:
    SLOTS = 11

    def __init__(self, place, grads, outs, columns, share, refs):
        self.p, self.grads, self.outs, self.columns, self.share = place, grads, outs, columns, share
        count = len(grads)
        self.bufs = []
        at = 0
        for one, column in zip(grads, columns):
            names = Scatter.names(self.kind(one), column is not None)
            self.bufs.append(dict(zip(names, refs[at : at + len(names)])))
            at += len(names)
        self.send, self.recv, self.local = refs[at : at + 3]
        self.copies = {}

    @staticmethod
    def kind(grad):
        if not isinstance(grad, tuple):
            return ""
        return "load" if len(grad) == 3 else "made"

    @staticmethod
    def names(whole, stops):
        before = ("acc", "one_a", "one_b", "two_a", "two_b") if whole else ()
        if whole == "load":
            before += ("own",)
        return before + (() if stops else ("three", "four"))

    def go(self, i, slot, src, dst, device):
        copy = push(src, dst, self.send.at[i, slot], self.recv.at[i, slot], device)
        self.copies[(i, slot)] = copy

    def done(self, i, *slots):
        for slot in slots:
            self.copies[(i, slot)].wait()

    def part(self, i, zz, core):
        ref, first, cols = self.grads[i]
        if cols == ref.shape[5]:
            return ref.at[zz, :, :, core]
        return ref.at[zz, :, :, core, :, pl.ds(first, cols)]

    def load(self, i, zz):
        own = self.bufs[i]["own"]
        copy = pltpu.make_async_copy(self.part(i, zz, self.p.core), own.at[zz % 2], self.local.at[i, zz])
        copy.start()
        self.copies[(i, "own", zz)] = copy

    def start(self, i):
        if self.kind(self.grads[i]) == "made":
            self.go(i, 0, self.grads[i][0].at[:, :, :, 1 - self.p.core], self.bufs[i]["acc"], self.p.sibling)
            return
        for zz in range(4):
            self.go(i, zz, self.part(i, zz, 1 - self.p.core), self.bufs[i]["acc"].at[zz], self.p.sibling)
        self.load(i, 0)
        self.load(i, 1)

    def halves(self, i):
        cols = self.grads[i][2]
        part = split_columns(cols, self.share)
        return pl.ds(0, part), pl.ds(part, cols - part)

    def core(self, i):
        p, acc = self.p, self.bufs[i]["acc"]
        if self.kind(self.grads[i]) == "made":
            made = self.grads[i][0]
            self.done(i, 0)

            def add(n, carry):
                zz, xx, yy = n // 4, lax.rem(n // 2, 2), lax.rem(n, 2)
                acc[zz, xx, yy] = add_rows(acc[zz, xx, yy], made[zz, xx, yy, p.core])
                return carry

            lax.fori_loop(0, 16, add, 0)
        else:
            self.add_loaded(i)
        low, high = self.halves(i)
        self.go(i, 4, acc.at[:, :, 1 - p.y, :, low], self.bufs[i]["one_a"], p.along_y)
        self.go(i, 5, acc.at[:, 1 - p.x, :, :, high], self.bufs[i]["one_b"], p.along_x)

    def add_loaded(self, i):
        acc, own = self.bufs[i]["acc"], self.bufs[i]["own"]
        for zz in range(4):
            self.copies[(i, "own", zz)].wait()
            self.done(i, zz)

            def step(n, carry, zz=zz):
                xx, yy = n // 2, lax.rem(n, 2)
                acc[zz, xx, yy] = add_rows(acc[zz, xx, yy], own[zz % 2, xx, yy])
                return carry

            lax.fori_loop(0, 4, step, 0)
            if zz < 2:
                self.load(i, zz + 2)

    def first(self, i):
        p, acc = self.p, self.bufs[i]["acc"]
        one_a, one_b = self.bufs[i]["one_a"], self.bufs[i]["one_b"]
        low, high = self.halves(i)
        self.done(i, 4, 5)

        def step(n, carry):
            zz, w = n // 2, lax.rem(n, 2)
            acc[zz, w, p.y, :, low] = add_rows(acc[zz, w, p.y, :, low], one_a[zz, w])
            acc[zz, p.x, w, :, high] = add_rows(acc[zz, p.x, w, :, high], one_b[zz, w])
            return carry

        lax.fori_loop(0, 8, step, 0)
        self.go(i, 6, acc.at[:, 1 - p.x, p.y, :, low], self.bufs[i]["two_a"], p.along_x)
        self.go(i, 7, acc.at[:, p.x, 1 - p.y, :, high], self.bufs[i]["two_b"], p.along_y)

    def second(self, i):
        p, acc = self.p, self.bufs[i]["acc"]
        two_a, two_b = self.bufs[i]["two_a"], self.bufs[i]["two_b"]
        low, high = self.halves(i)
        self.done(i, 6, 7)
        column = self.columns[i]

        first, cols = (0, 0) if column is None else self.grads[i][1:3]

        def step(zz, carry):
            here = acc.at[zz, p.x, p.y] if column is None else column.at[zz, :, pl.ds(first, cols)]
            here[:, low] = add_rows(acc[zz, p.x, p.y, :, low], two_a[zz])
            here[:, high] = add_rows(acc[zz, p.x, p.y, :, high], two_b[zz])
            return carry

        lax.fori_loop(0, 4, step, 0)
        if column is None:
            self.turn(i)

    def sums(self, i, zz):
        if isinstance(self.grads[i], tuple):
            return self.bufs[i]["acc"].at[zz, self.p.x, self.p.y]
        return self.grads[i].at[zz]

    def turn(self, i):
        p, three = self.p, self.bufs[i]["three"]
        self.go(i, 8, self.sums(i, p.others[2]), three.at[0], p.along_z[0])
        self.go(i, 9, self.sums(i, p.others[0]), three.at[1], p.along_z[0])

    def third(self, i):
        p, three = self.p, self.bufs[i]["three"]
        self.done(i, 8, 9)
        far = self.sums(i, p.others[1])
        three[0] = add_rows(far[...], three[0])
        self.go(i, 10, three.at[0], self.bufs[i]["four"], p.along_z[1])

    def near(self, i, mine, far):
        three = self.bufs[i]["three"]
        self.done(i, 8, 9)
        far[...] = add_rows(self.sums(i, self.p.others[1])[...], three[0])
        mine[...] = self.sums(i, self.p.z)[...].astype(F32) + three[1].astype(F32)

    def last(self, i):
        three, four = self.bufs[i]["three"], self.bufs[i]["four"]
        self.done(i, 10)
        total = self.sums(i, self.p.z)[...].astype(F32) + three[1].astype(F32) + four[...].astype(F32)
        if isinstance(self.grads[i], tuple):
            first, cols = self.grads[i][1:3]
            self.outs[i][:, first : first + cols] = total
        else:
            self.outs[i][...] = total

    @classmethod
    def scratch(cls, kinds, share):
        count = len(kinds)
        bufs = []
        for rows, cols, whole, stops in kinds:
            part = split_columns(cols, share)
            shapes = {
                "own": (2, 2, 2, rows, cols),
                "acc": (4, 2, 2, rows, cols),
                "one_a": (4, 2, rows, part),
                "one_b": (4, 2, rows, cols - part),
                "two_a": (4, rows, part),
                "two_b": (4, rows, cols - part),
                "three": (2, rows, cols),
                "four": (rows, cols),
            }
            bufs += [pltpu.VMEM(shapes[name], BF) for name in cls.names(whole, stops)]
        return bufs + [
            pltpu.SemaphoreType.DMA((count, cls.SLOTS)),
            pltpu.SemaphoreType.DMA((count, cls.SLOTS)),
            pltpu.SemaphoreType.DMA((count, 4)),
        ]


def small_sums(p, vec, sec, fst, gathered, send, recv):
    rows, more = vec.shape[0], fst.shape[0]
    copies = []
    for d in range(7):
        lane = pl.multiple_of(p.ch_ahead[d] * 128, 128)
        pairs = (
            (vec.at[:, pl.ds(lane, 128)], gathered.at[p.ch, pl.ds(0, rows)]),
            (fst, gathered.at[p.ch, pl.ds(rows, more)]),
        )
        for n, (src, dst) in enumerate(pairs):
            copies.append(push(src, dst, send.at[2 * d + n], recv.at[2 * d + n], {"ch": p.ch_ahead[d]}))
    gathered[p.ch, :rows] = vec[:, pl.ds(pl.multiple_of(p.ch * 128, 128), 128)]
    gathered[p.ch, rows:] = fst[...]
    return copies


def join_sums(p, sec, gathered, joined, send, recv):
    rows = gathered.shape[1]
    total = gathered[0]
    for n in range(1, 8):
        total = total + gathered[n]
    joined[p.seq, :rows] = total
    joined[p.seq, rows:] = sec[...]
    return [
        push(joined.at[p.seq], joined.at[p.seq], send.at[14 + d], recv.at[14 + d], {"seq": p.seq_ahead[d]})
        for d in range(3)
    ]


def tail_kernel(size, loads, *refs):
    normed, du, tokens, mask, consts, grad_after, sums, gain_two = refs[:8]
    dh, hidden, table, first, second, shift, speed = refs[8:15]
    columns = list(refs[15:17])
    down_mine, down_far = refs[17:19]
    w_in = refs[19]
    grad_input, out, small_out = refs[20:23]
    outs = list(refs[23:25])
    down_out = refs[25]
    weight, turned, made, da, vec, sec, fst, gathered, joined, first_wide, down_last, packed = refs[26:38]
    weight_sem, small_send, small_recv, down_sems = refs[38:42]
    width = 1024
    p = Place()
    load = pltpu.make_async_copy(w_in, weight, weight_sem)
    load.start()
    greet([{"ch": one} for one in p.ch_ahead] + [{"seq": one} for one in p.seq_ahead])
    grads = [(made.at[n], n * width, width, None) for n in range(3)] + columns
    scatter = Scatter(p, grads, [out] * 3 + outs, [None] * 5, 0.5, refs[42:])
    loads[15].wait()
    loads[16].wait()
    for n in (3, 4):
        scatter.turn(n)
    loads[18].wait()
    down = push(down_far, down_last, down_sems.at[0], down_sems.at[1], p.along_z[1])
    loads[0].wait()
    turned[...] = normed[...].T
    loads[1].wait()

    def part(stream):
        made[stream] = mm(turned[...], du[:, stream * width : (stream + 1) * width]).astype(BF).reshape(made.shape[1:])
        scatter.start(stream)

    def back(stream):
        at = slice(stream * width, (stream + 1) * width)
        one = nt(du[:, at], weight[:, at])
        da[...] = one if stream == 0 else da[...] + one

    part(0)
    part(1)
    scatter.core(0)
    part(2)
    scatter.core(1)
    scatter.core(2)

    length = 8 * size
    lane = (lax.broadcasted_iota(jnp.int32, (1, 128), 1) + p.ch * 128).astype(F32)
    rate = SLOW_RATE + (FAST_RATE - SLOW_RATE) * lane / 1023.0
    emb, filt_width = first_wide.shape
    first_wide[...] = jnp.zeros_like(first_wide)
    first_wide[: first.shape[0]] = first[...]
    sec[...] = jnp.zeros_like(sec)
    fst[...] = jnp.zeros_like(fst)

    def high(a, b, dims):
        return lax.dot_general(a, b, ((dims), ((), ())), precision=HIGH, preferred_element_type=F32)

    def step(j, carry):
        rows = pl.ds(pl.multiple_of(j * size, size), size)
        place = (lax.broadcasted_iota(jnp.int32, (size, 1), 0) + j * size).astype(F32) / (length - 1)
        draw = dh[j] * jnp.exp(-place * rate)
        sec[...] += high(hidden[rows], draw, ((0,), (0,)))
        inner = high(table[rows], first_wide[...], ((1,), (0,))) + shift[...]
        q = high(draw, second[...], ((1,), (1,))) * jnp.cos(speed[...] * inner)
        scaled = q * speed[...]
        fst[:emb, :filt_width] += high(table[rows], scaled, ((0,), (0,)))
        fst[emb : emb + 1, :filt_width] += jnp.sum(scaled, axis=0, keepdims=True)
        fst[emb + 1 : emb + 2, :filt_width] += jnp.sum(q * inner, axis=0, keepdims=True)
        return carry

    for i in (8, 9, 10):
        loads[i].wait()
    load.wait()
    back(0)
    back(1)
    back(2)
    scatter.first(0)
    lax.fori_loop(0, 4, step, 0)
    scatter.first(1)
    for n in (3, 4):
        scatter.third(n)
    scatter.first(2)
    for i in (2, 3, 5):
        loads[i].wait()
    gain = consts[10:11, :]

    def norm(i, total):
        rows = pl.ds(pl.multiple_of(i * 32, 32), 32)
        one, inverse = norm_rows(tokens[rows].astype(F32) * mask[rows, 0:1], gain)
        grad = da[rows]
        e = grad * gain
        inner = e - jnp.mean(e, axis=1, keepdims=True) - one * jnp.mean(e * one, axis=1, keepdims=True)
        grad_input[rows] = ((grad_after[rows] + inverse * inner) * mask[rows, 0:1]).astype(BF)
        return total + jnp.sum(grad * one, axis=0, keepdims=True)

    gain_one = lax.fori_loop(0, normed.shape[0] // 32, norm, jnp.zeros((1, width), F32))
    loads[20].start()
    vec[...] = jnp.zeros_like(vec)
    vec[:10] = sums[:10]
    vec[10:11] = gain_one
    vec[11:12] = gain_two[...]
    scatter.second(0)
    scatter.second(1)
    lax.fori_loop(4, 8, step, 0)
    packed[...] = fst[:24] + pltpu.roll(fst[24:], 64, 1)
    small = small_sums(p, vec, sec, packed, gathered, small_send, small_recv)
    scatter.second(2)
    scatter.third(0)
    scatter.third(1)
    wait_all(small)
    small = join_sums(p, sec, gathered, joined, small_send, small_recv)
    scatter.third(2)
    for n in (3, 4):
        scatter.last(n)
    scatter.last(0)
    scatter.last(1)
    down.wait()
    loads[17].wait()
    down_out[...] = down_mine[...] + down_last[...].astype(F32)
    scatter.last(2)
    wait_all(small)
    total = joined[0]
    for n in range(1, 4):
        total = total + joined[n]
    small_out[:40] = total[:40]
    small_out[40:64] = pltpu.roll(total[16:40], 64, 1)
    small_out[64:] = total[40:]


def tail_call(operands, columns, down, w_in, size):
    rows, width = operands[0].shape
    emb, filt_width = operands[10].shape[1], operands[11].shape[1]
    part = w_in.shape[0] // 32
    small = 16 + 24
    kinds = [(part, width, "made", False)] * 3 + [one.shape[1:] + ("", False) for one in columns]
    operands = tuple(operands) + tuple(columns) + tuple(down)
    fetch = (0, 1, 2, 3, 5, 8, 9, 10, 15, 16, 17, 18)
    return pl.pallas_call(
        fetching(functools.partial(tail_kernel, size), fetch, [len(operands) + 1]),
        out_shape=[
            jax.ShapeDtypeStruct((rows, width), BF),
            jax.ShapeDtypeStruct((part, 3 * width), F32),
            jax.ShapeDtypeStruct((small + 24 + filt_width, 128), F32),
        ]
        + [jax.ShapeDtypeStruct(one.shape[1:], F32) for one in columns]
        + [jax.ShapeDtypeStruct(down[0].shape, F32)],
        in_specs=fetch_specs(operands, fetch) + [ANYWHERE],
        out_specs=[ANYWHERE] + [VM] * 5,
        scratch_shapes=[
            pltpu.VMEM(w_in.shape, BF),
            pltpu.VMEM((width, rows), BF),
            pltpu.VMEM((3, 4, 2, 2, 2, part, width), BF),
            pltpu.VMEM((rows, width), F32),
            pltpu.VMEM((16, width), F32),
            pltpu.VMEM((filt_width, 128), F32),
            pltpu.VMEM((48, 128), F32),
            pltpu.VMEM((8, small, 128), F32),
            pltpu.VMEM((4, small + filt_width, 128), F32),
            pltpu.VMEM((emb, filt_width), F32),
            pltpu.VMEM(down[1].shape, BF),
            pltpu.VMEM((24, 128), F32),
            pltpu.SemaphoreType.DMA,
            pltpu.SemaphoreType.DMA((17,)),
            pltpu.SemaphoreType.DMA((17,)),
            pltpu.SemaphoreType.DMA((2,)),
        ]
        + Scatter.scratch(kinds, 0.5)
        + fetch_scratch(operands, fetch, [jax.ShapeDtypeStruct((rows, width), BF)], (0,)),
        compiler_params=pltpu.CompilerParams(collective_id=3, has_side_effects=True, vmem_limit_bytes=VMEM_LIMIT),
    )(*operands, w_in)


def general_body(
    tokens,
    lengths,
    in_weight,
    out_weight,
    up_weight,
    down_weight,
    gain_one,
    gain_two,
    conv_taps,
    skip_gain,
    filter_first,
    filter_bias,
    frequency,
    filter_second,
    cotangent,
):
    ch_count = lax.axis_size("ch")
    ch_place = lax.axis_index("ch")
    size = tokens.shape[1]
    buckets = tokens.shape[2]
    width = tokens.shape[3]
    chans = skip_gain.shape[0]
    length = size * ch_count
    rows = size * buckets
    dims = (ch_count, size, buckets, chans)
    tables = tuple(jnp.asarray(one) for one in block_tables(size))

    def gather(shard):
        return lax.all_gather(shard, ("ch", "seq"), axis=0, tiled=True)

    full_in = gather(in_weight)
    full_gain_one = gather(gain_one).astype(F32)
    full_gain_two = gather(gain_two).astype(F32)
    full_out = gather(out_weight)
    full_up = gather(up_weight)
    full_down = gather(down_weight)

    local = ch_place * size + jnp.arange(size, dtype=jnp.int32)
    mask = (local[None, :] < lengths[0][:, None]).astype(F32).reshape(rows, 1)
    before = ch_place * size - 2 + jnp.arange(2, dtype=jnp.int32)
    mask_before = (before[None, :] < lengths[0][:, None]).astype(F32).reshape(2 * buckets, 1)
    chain = [(i, i + 1) for i in range(ch_count - 1)]
    halo = lax.ppermute(tokens[0, size - 2 :], "ch", chain)
    x_zero = jnp.swapaxes(tokens[0], 0, 1).reshape(rows, width).astype(F32) * mask
    x_before = jnp.swapaxes(halo, 0, 1).reshape(2 * buckets, width).astype(F32) * mask_before

    taps_full = lax.all_gather(conv_taps.reshape(9, chans), "ch", axis=1, tiled=True).reshape(3, 3, width)
    skip_full = lax.all_gather(skip_gain.reshape(1, chans), "ch", axis=1, tiled=True)

    table = positions_table(length, filter_first.shape[0])
    hidden = filter_hidden(filter_first, filter_bias, frequency, table)
    decay = decay_table(length, ch_place * chans, chans, width)
    filt = jnp.dot(hidden, filter_second, precision=HIGH) * decay
    filt_blocks = jnp.tile(filt.reshape(ch_count, size, chans), (1, 1, buckets))

    normed_one = layer_norm(x_zero, full_gain_one).astype(BF)
    normed_before = layer_norm(x_before, full_gain_one).astype(BF)
    streams = jnp.dot(normed_one, full_in, preferred_element_type=F32).astype(BF)
    streams_before = jnp.dot(normed_before, full_in, preferred_element_type=F32).astype(BF)
    lag = jnp.concatenate(
        [streams_before.reshape(buckets, 2, 3, width), streams.reshape(buckets, size, 3, width)], axis=1
    ).astype(F32)
    lag_zero, lag_one, lag_two = lag[:, 2:], lag[:, 1:-1], lag[:, :-2]
    conv = taps_full[0] * lag_zero + taps_full[1] * lag_one + taps_full[2] * lag_two
    gate = conv[:, :, 0].reshape(rows, width)
    key_part = conv[:, :, 1].reshape(rows, width)
    value_part = conv[:, :, 2].reshape(rows, width)
    mixed = key_part * value_part

    convolved, kept = conv_forward(mixed.astype(BF), filt_blocks, tables, dims)
    long_part = convolved.astype(F32) + skip_full * mixed
    mixer = (gate * long_part * mask).astype(BF)
    after_mix = x_zero + jnp.dot(mixer, full_out, preferred_element_type=F32)
    normed_two = layer_norm(after_mix, full_gain_two).astype(BF)
    inner_act = jnp.dot(normed_two, full_up, preferred_element_type=F32)
    active = jax.nn.gelu(inner_act).astype(BF)
    result = (after_mix + jnp.dot(active, full_down, preferred_element_type=F32)).astype(BF)
    result = jnp.swapaxes(result.reshape(buckets, size, width), 0, 1).reshape(1, size, buckets, width)

    grad_result = jnp.swapaxes(cotangent[0], 0, 1).reshape(rows, width)
    grad_active = jnp.dot(grad_result, full_down.T, preferred_element_type=F32)
    _, gelu_pull = jax.vjp(jax.nn.gelu, inner_act)
    grad_inner = gelu_pull(grad_active)[0].astype(BF)
    grad_down = jnp.dot(active.T, grad_result, preferred_element_type=F32)
    grad_up = jnp.dot(normed_two.T, grad_inner, preferred_element_type=F32)
    grad_normed_two = jnp.dot(grad_inner, full_up.T, preferred_element_type=F32)
    _, norm_two_pull = jax.vjp(layer_norm, after_mix, full_gain_two)
    grad_after_part, grad_gain_two = norm_two_pull(grad_normed_two)
    grad_after = grad_result.astype(F32) + grad_after_part
    grad_mix = grad_after.astype(BF)
    grad_out = jnp.dot(mixer.T, grad_mix, preferred_element_type=F32)
    grad_mixer = jnp.dot(grad_mix, full_out.T, preferred_element_type=F32).astype(BF)
    grad_masked = grad_mixer.astype(F32) * mask
    grad_gate = grad_masked * long_part
    grad_long = grad_masked * gate
    grad_skip = jnp.sum(grad_long * mixed, axis=0)
    grad_convolved, grad_filt = conv_backward(grad_long.astype(BF), kept, filt_blocks, tables, dims)
    grad_mixed = grad_convolved.astype(F32) + skip_full * grad_long
    grad_conv = jnp.stack([grad_gate, grad_mixed * value_part, grad_mixed * key_part], axis=1)
    grad_conv = grad_conv.reshape(buckets, size, 3, width)
    grad_taps = jnp.stack(
        [
            jnp.sum(grad_conv * lag_zero, axis=(0, 1)),
            jnp.sum(grad_conv * lag_one, axis=(0, 1)),
            jnp.sum(grad_conv * lag_two, axis=(0, 1)),
        ],
        axis=0,
    )
    next_rows = lax.ppermute(grad_conv[:, :2], "ch", [(j, i) for i, j in chain])
    ahead = jnp.concatenate([grad_conv, next_rows], axis=1)
    grad_streams = taps_full[0] * ahead[:, :-2] + taps_full[1] * ahead[:, 1:-1] + taps_full[2] * ahead[:, 2:]
    grad_projected = grad_streams.astype(BF).reshape(rows, 3 * width)
    grad_in = jnp.dot(normed_one.T, grad_projected, preferred_element_type=F32)
    grad_normed_one = jnp.dot(grad_projected, full_in.T, preferred_element_type=F32)
    _, norm_one_pull = jax.vjp(layer_norm, x_zero, full_gain_one)
    grad_zero_part, grad_gain_one = norm_one_pull(grad_normed_one)
    grad_input = ((grad_after + grad_zero_part) * mask).astype(BF)
    grad_input = jnp.swapaxes(grad_input.reshape(buckets, size, width), 0, 1).reshape(1, size, buckets, width)

    grad_filt = jnp.sum(grad_filt.reshape(length, buckets, chans), axis=1)
    grad_raw = grad_filt * decay
    grad_second = jnp.dot(hidden.T, grad_raw, precision=HIGH)
    grad_hidden = jnp.dot(grad_raw, filter_second.T, precision=HIGH)

    def hidden_of(first_layer, first_shift, freq_values):
        return filter_hidden(first_layer, first_shift, freq_values, table)

    _, hidden_pull = jax.vjp(hidden_of, filter_first, filter_bias, frequency)
    grad_first, grad_bias, grad_freq = hidden_pull(grad_hidden)

    sum_in, sum_out, sum_up, sum_down, sum_gain_one, sum_gain_two = (
        lax.psum_scatter(one, ("ch", "seq"), scatter_dimension=0, tiled=True)
        for one in (grad_in, grad_out, grad_up, grad_down, grad_gain_one, grad_gain_two)
    )
    sum_second = lax.psum(grad_second, "seq")
    all_taps, all_skip, sum_first, sum_bias, sum_freq = lax.psum(
        (grad_taps, grad_skip, grad_first, grad_bias, grad_freq), ("ch", "seq")
    )
    sum_taps = lax.dynamic_slice_in_dim(all_taps, ch_place * chans, chans, 2)
    sum_skip = lax.dynamic_slice_in_dim(all_skip, ch_place * chans, chans, 0)
    return (
        result,
        grad_input,
        sum_in,
        sum_out,
        sum_up,
        sum_down,
        sum_gain_one,
        sum_gain_two,
        sum_taps,
        sum_skip,
        sum_first,
        sum_bias,
        sum_freq,
        sum_second,
    )


def by_position(values, size):
    parts = values.reshape(2, size, values.shape[1])
    bucket = lax.broadcasted_iota(jnp.int32, (size, 2, values.shape[1]), 1)
    return jnp.where(bucket == 0, parts[0][:, None, :], parts[1][:, None, :])[None]


def filter_table(length, features):
    steps = np.arange(length).astype(np.float32)
    scaled = steps / np.float32(length - 1)
    bands = (features - 1) // 2
    freqs = np.float32(0.0001) + np.float32(bands - 1 - 0.0001) * np.arange(bands).astype(np.float32) / np.float32(bands - 1)
    angles = freqs[None, :] * (np.float32(2.0 * math.pi) * steps / np.float32(length))[:, None]
    table = np.concatenate([scaled[:, None], np.cos(angles), -np.sin(angles)], axis=1)
    return np.pad(table, ((0, 0), (0, -features % 8)))


def slice_body(
    tokens,
    lengths,
    in_weight,
    out_weight,
    up_weight,
    down_weight,
    gain_one,
    gain_two,
    conv_taps,
    skip_gain,
    filter_first,
    filter_bias,
    frequency,
    filter_second,
    cotangent,
):
    seq_place = lax.axis_index("seq")
    size = tokens.shape[1]
    buckets = tokens.shape[2]
    width = tokens.shape[3]
    chans = skip_gain.shape[0]
    length = size * 8
    rows = size * buckets
    part = gain_one.shape[0]
    emb, filt_width = filter_first.shape
    tables = tuple(jnp.asarray(one) for one in block_tables(size))

    by_bucket = jnp.swapaxes(tokens[0], 0, 1)
    flat = by_bucket.reshape(rows, width)
    wide_table = jnp.asarray(filter_table(length, emb))
    pads = wide_table.shape[1] - emb
    (consts, halo, hidden, filt), full_in, columns = start_call(
        conv_taps,
        skip_gain[None],
        jnp.stack([gain_one, gain_two]),
        by_bucket,
        wide_table,
        filter_first,
        filter_second,
        filter_bias[None],
        frequency[None],
        (in_weight, out_weight, up_weight),
        size,
    )
    (normed_one, streams, mixer, kept, convolved, wide_mask, column_down), (full_out, full_up), early = forward_call(
        lengths, flat, halo, consts, filt, tables, down_weight, columns, full_in, size
    )
    grad_result = jnp.swapaxes(cotangent[0], 0, 1).reshape(rows, width)
    result, grad_after, grad_mixer, grad_gain_two, grad_out, sum_column, sum_last, grad_up = feed_forward_call(
        mixer, flat, wide_mask, grad_result, consts, full_out, full_up, early, column_down
    )
    result = by_position(result, size)

    (grad_projected, grad_filt, sums), (down_mine, *late, down_far) = backward_call(
        streams, consts, wide_mask, grad_mixer, convolved, kept, filt, tables, (sum_column, grad_up, grad_out), sum_last, size
    )
    grad_input, sum_in, small, sum_up, sum_out, sum_down = tail_call(
        (normed_one, grad_projected, flat, wide_mask, consts, grad_after, sums, grad_gain_two)
        + (grad_filt, hidden, wide_table, filter_first, filter_second, filter_bias[None], frequency[None]),
        late,
        (down_mine, down_far),
        full_in,
        size,
    )
    grad_input = by_position(grad_input, size)
    after = 16 + emb + pads
    gain_sums = lax.dynamic_slice_in_dim(small[10:12], seq_place * part, part, 1)
    return (
        result,
        grad_input,
        sum_in,
        sum_out,
        sum_up,
        sum_down,
        gain_sums[0],
        gain_sums[1],
        small[:9].reshape(3, 3, chans),
        small[9],
        small[16 : 16 + emb, :filt_width],
        small[after, :filt_width],
        small[after + 1, :filt_width],
        small[64:],
    )


def solution(mesh):
    placed = (
        P("seq", "ch", None, None),
        P("seq", None),
        P(("ch", "seq"), None),
        P(("ch", "seq"), None),
        P(("ch", "seq"), None),
        P(("ch", "seq"), None),
        P(("ch", "seq")),
        P(("ch", "seq")),
        P(None, None, "ch"),
        P("ch"),
        P(),
        P(),
        P(),
        P(None, "ch"),
        P("seq", "ch", None, None),
    )
    custom = dict(mesh.shape) == {"ch": 8, "seq": 4}
    return jax.shard_map(
        slice_body if custom else general_body,
        mesh=mesh,
        in_specs=placed,
        out_specs=(
            P("seq", "ch", None, None),
            P("seq", "ch", None, None),
            P(("ch", "seq"), None),
            P(("ch", "seq"), None),
            P(("ch", "seq"), None),
            P(("ch", "seq"), None),
            P(("ch", "seq")),
            P(("ch", "seq")),
            P(None, None, "ch"),
            P("ch"),
            P(),
            P(),
            P(),
            P(None, "ch"),
        ),
        check_vma=False,
    )
```

```python
import functools
import math

import jax
import jax.numpy as jnp
import numpy as np
from jax import lax
from jax.experimental import pallas as pl
from jax.experimental.pallas import tpu as pltpu
from jax.sharding import PartitionSpec as P

EPS = 1e-05
SLOW_RATE = math.log(100.0) / 1.5
FAST_RATE = math.log(100.0) / 0.3
HIGH = lax.Precision.HIGHEST
BF = jnp.bfloat16
F32 = jnp.float32
MESH = pl.DeviceIdType.MESH
VMEM_LIMIT = 62 << 20
OWN = 256
SHARE = 0.85
SHARE_BACK = 0.69
EARLY, LATE = range(0, 1), range(1, 4)


def layer_norm(values, gain):
    centre = values - jnp.mean(values, axis=-1, keepdims=True)
    spread = jnp.mean(centre * centre, axis=-1, keepdims=True)
    return centre * lax.rsqrt(spread + EPS) * gain


def positions_table(length, features):
    steps = jnp.arange(length).astype(jnp.float32)
    scaled = steps / (length - 1)
    bands = (features - 1) // 2
    freqs = 0.0001 + (bands - 1 - 0.0001) * jnp.arange(bands).astype(jnp.float32) / (bands - 1)
    angles = freqs[None, :] * (2.0 * math.pi * steps / length)[:, None]
    return jnp.concatenate([scaled[:, None], jnp.cos(angles), -jnp.sin(angles)], axis=1)


def decay_table(length, chan_start, count, width):
    scaled = jnp.arange(length).astype(jnp.float32) / (length - 1)
    chans = (chan_start + jnp.arange(count)).astype(jnp.float32)
    rates = SLOW_RATE + (FAST_RATE - SLOW_RATE) * chans / (width - 1)
    return jnp.exp(-scaled[:, None] * rates[None, :])


def filter_hidden(filter_first, filter_bias, frequency, table):
    inner = jnp.dot(table, filter_first, precision=HIGH) + filter_bias
    return jnp.sin(frequency * inner)


def block_tables(size):
    k = np.arange(size)[:, None]
    t = np.arange(size)[None, :]
    angle = 2.0 * np.pi * ((k * t) % (2 * size)) / (2 * size)
    real = np.cos(angle)
    imag = -np.sin(angle)
    imag[0] = np.where(np.arange(size) % 2 == 0, 1.0, -1.0)
    full = np.concatenate([real, imag], axis=0).astype(np.float32)
    high = full.astype(jnp.bfloat16)
    low = (full - high.astype(np.float32)).astype(jnp.bfloat16)
    weight = np.full((size, 1), 1.0 / size, np.float32)
    weight[0] = 0.5 / size
    sign = np.where(np.arange(size) % 2 == 0, 1.0, -1.0).astype(np.float32)[:, None]
    lanes = np.zeros((size, 128), np.float32)
    lanes[:, 0:1] = weight
    lanes[:, 1:2] = sign
    lanes[:, 2] = 1.0
    lanes[0, 2] = 0.0
    return high, low, high.T.copy(), low.T.copy(), lanes


def split_high(values):
    high = values.astype(BF)
    return high, (values - high.astype(F32)).astype(BF)


def mm(a, b):
    return jnp.dot(a, b, preferred_element_type=F32)


def spectra(fh, fl, source, target, blocks, piece=slice(None)):
    def step(i, carry):
        block = source[i, :, piece]
        target[i, :, piece] = mm(fh[...], block) + mm(fl[...], block)
        return carry

    lax.fori_loop(0, blocks, step, 0)


def filter_spectra(fh, fl, lanes, h_ref, abc, blocks, size):
    weight = lanes[:, 0:1]
    sign = lanes[:, 1:2]

    def step(j, carry):
        prev_re, prev_im = carry
        high, low = split_high(h_ref[j])
        now = mm(fh[...], high) + mm(fl[...], high) + mm(fh[...], low)
        now_re = now[:size]
        now_im = now[size:]
        abc[j, 0] = (now_re + sign * prev_re) * weight
        abc[j, 1] = (now_im + sign * prev_im) * weight
        return now_re, now_im

    zero = jnp.zeros((size, h_ref.shape[2]), F32)
    lax.fori_loop(0, blocks, step, (zero, zero))


def row_chunks(size, body):
    def step(i, carry):
        body(pl.multiple_of(i * 8, 8))
        return carry

    lax.fori_loop(0, size // 8, step, 0)


def load_filter(abc, lanes, here, blocks):
    keep = lanes[here, 2:3]
    a = [abc[j, 0, here] for j in range(blocks)]
    raw = [abc[j, 1, here] for j in range(blocks)]
    b = [one * keep for one in raw]
    c = [jnp.where(keep > 0.5, one, two) for one, two in zip(a, raw)]
    return a, b, c


def products_forward(xs, abc, lanes, out, blocks, size, pieces=None):
    width = abc.shape[3]
    for n in range(xs.shape[2] // width) if pieces is None else pieces:
        piece = slice(n * width, (n + 1) * width)

        def body(row, piece=piece):
            here, there = pl.ds(row, 8), pl.ds(size + row, 8)
            re = [xs[i, here, piece] for i in range(blocks)]
            im = [xs[i, there, piece] for i in range(blocks)]
            a, b, c = load_filter(abc, lanes, here, blocks)
            for m in range(blocks):
                sum_re = re[0] * a[m] - im[0] * b[m]
                sum_im = re[0] * b[m] + im[0] * c[m]
                for i in range(1, m + 1):
                    sum_re = sum_re + (re[i] * a[m - i] - im[i] * b[m - i])
                    sum_im = sum_im + (re[i] * b[m - i] + im[i] * c[m - i])
                out[m, here, piece] = sum_re
                out[m, there, piece] = sum_im

        row_chunks(size, body)


def products_backward(xs, ds, abc, gh, lanes, blocks, size, pieces=None):
    width = abc.shape[3]
    count = xs.shape[2] // width
    for n in range(count) if pieces is None else pieces:
        piece = slice(n * width, (n + 1) * width)

        def body(row, n=n, piece=piece):
            here, there = pl.ds(row, 8), pl.ds(size + row, 8)
            d_re = [ds[i, here, piece] for i in range(blocks)]
            d_im = [ds[i, there, piece] for i in range(blocks)]
            a, b, c = load_filter(abc, lanes, here, blocks)
            for i in range(blocks):
                sum_re = d_re[i] * a[0] + d_im[i] * b[0]
                sum_im = d_im[i] * c[0] - d_re[i] * b[0]
                for m in range(i + 1, blocks):
                    sum_re = sum_re + (d_re[m] * a[m - i] + d_im[m] * b[m - i])
                    sum_im = sum_im + (d_im[m] * c[m - i] - d_re[m] * b[m - i])
                ds[i, here, piece] = sum_re
                ds[i, there, piece] = sum_im
            x_re = [xs[i, here, piece] for i in range(blocks)]
            x_im = [xs[i, there, piece] for i in range(blocks)]
            weight = lanes[here, 0:1]
            sign = lanes[here, 1:2]
            keep = lanes[here, 2:3] > 0.5
            later_re = None
            later_im = None
            for j in range(blocks - 1, -1, -1):
                rr = d_re[j] * x_re[0]
                ii = d_im[j] * x_im[0]
                cross = d_im[j] * x_re[0] - d_re[j] * x_im[0]
                for i in range(1, blocks - j):
                    rr = rr + d_re[i + j] * x_re[i]
                    ii = ii + d_im[i + j] * x_im[i]
                    cross = cross + (d_im[i + j] * x_re[i] - d_re[i + j] * x_im[i])
                g_re = jnp.where(keep, rr + ii, rr) * weight
                g_im = jnp.where(keep, cross, ii) * weight
                if n:
                    g_re = g_re + gh[j, 0, here]
                    g_im = g_im + gh[j, 1, here]
                if n == count - 1 and later_re is not None:
                    gh[j, 0, here] = g_re + sign * later_re
                    gh[j, 1, here] = g_im + sign * later_im
                else:
                    gh[j, 0, here] = g_re
                    gh[j, 1, here] = g_im
                later_re, later_im = g_re, g_im

        row_chunks(size, body)


def inverse_of(th, tl, values):
    high, low = split_high(values)
    return mm(th[...], high) + mm(tl[...], high) + mm(th[...], low)


def inverse_blocks(th, tl, source, target, blocks, piece=slice(None)):
    def step(m, carry):
        target[m, :, piece] = inverse_of(th, tl, source[m, :, piece]).astype(target.dtype)
        return carry

    lax.fori_loop(0, blocks, step, 0)


def filter_gradient(th, tl, gh, out, blocks, size):
    def step(j, carry):
        re_high, re_low = split_high(gh[j, 0])
        im_high, im_low = split_high(gh[j, 1])
        left, right = th[:, :size], th[:, size:]
        total = mm(left, re_high) + mm(right, im_high) + mm(left, re_low) + mm(right, im_low)
        total = total + mm(tl[:, :size], re_high) + mm(tl[:, size:], im_high)
        out[j] = total
        return carry

    lax.fori_loop(0, blocks, step, 0)


def conv_forward_kernel(dims, x_ref, h_ref, fh, fl, th, tl, lanes, out, xs, abc):
    blocks, size, buckets, chans = dims
    filter_spectra(fh, fl, lanes, h_ref, abc, blocks, size)
    spectra(fh, fl, x_ref, xs, blocks)
    products_forward(xs, abc, lanes, xs, blocks, size)
    inverse_blocks(th, tl, xs, out, blocks)


def conv_backward_kernel(dims, d_ref, x_ref, h_ref, fh, fl, th, tl, lanes, out, dh_ref, xs, ds, abc, gh):
    blocks, size, buckets, chans = dims
    filter_spectra(fh, fl, lanes, h_ref, abc, blocks, size)
    spectra(fh, fl, x_ref, xs, blocks)
    spectra(fh, fl, d_ref, ds, blocks)
    products_backward(xs, ds, abc, gh, lanes, blocks, size)
    inverse_blocks(th, tl, ds, out, blocks)
    filter_gradient(th, tl, gh, dh_ref, blocks, size)


VM = pl.BlockSpec(memory_space=pltpu.VMEM)
ANYWHERE = pl.BlockSpec(memory_space=pl.ANY)


def conv_call(kernel, dims, operands, kinds, spectra_count):
    blocks, size, buckets, chans = dims
    cols = buckets * chans
    scratch = [pltpu.VMEM((blocks, 2 * size, cols), F32)] * spectra_count
    return pl.pallas_call(
        functools.partial(kernel, dims),
        out_shape=[jax.ShapeDtypeStruct((blocks, size, cols), kind) for kind in kinds],
        in_specs=[VM] * len(operands),
        out_specs=[VM] * len(kinds),
        scratch_shapes=scratch + [pltpu.VMEM((blocks, 2, size, cols), F32)] * spectra_count,
        compiler_params=pltpu.CompilerParams(vmem_limit_bytes=VMEM_LIMIT),
    )(*operands)


def rows_to_blocks(rows, dims):
    blocks, size, buckets, chans = dims
    moved = lax.all_to_all(rows.reshape(buckets, size, blocks, chans), "ch", split_axis=2, concat_axis=0)
    return jnp.transpose(moved, (0, 2, 1, 3)).reshape(blocks, size, buckets * chans)


def blocks_to_rows(values, dims):
    blocks, size, buckets, chans = dims
    moved = lax.all_to_all(values.reshape(blocks, size, buckets, chans), "ch", split_axis=0, concat_axis=0)
    return jnp.transpose(moved, (2, 1, 0, 3)).reshape(buckets * size, blocks * chans)


def conv_forward(rows, filt, tables, dims):
    kept = rows_to_blocks(rows, dims)
    (out,) = conv_call(conv_forward_kernel, dims, (kept, filt) + tables, (BF,), 1)
    return blocks_to_rows(out, dims), kept


def conv_backward(rows, kept, filt, tables, dims):
    moved = rows_to_blocks(rows, dims)
    out, dfilt = conv_call(conv_backward_kernel, dims, (moved, kept, filt) + tables, (BF, F32), 2)
    return blocks_to_rows(out, dims), dfilt


class Place:
    def __init__(self):
        self.ch = lax.axis_index("ch")
        self.seq = lax.axis_index("seq")
        self.z, self.x = self.ch // 2, lax.rem(self.ch, 2)
        self.y, self.core = self.seq // 2, lax.rem(self.seq, 2)
        self.sibling = {"seq": self.y * 2 + (1 - self.core)}
        self.along_y = {"seq": (1 - self.y) * 2 + self.core}
        self.along_x = {"ch": self.z * 2 + (1 - self.x)}
        self.others = [self.z + 1 - 2 * lax.rem(self.z, 2), lax.rem(self.z + 2, 4), 3 - self.z]
        self.along_z = [{"ch": one * 2 + self.x} for one in self.others]
        self.ch_ahead = [lax.rem(self.ch + d, 8) for d in range(1, 8)]
        self.seq_ahead = [lax.rem(self.seq + d, 4) for d in range(1, 4)]


def greet(ids):
    barrier = pltpu.get_barrier_semaphore()
    for one in ids:
        pl.semaphore_signal(barrier, inc=1, device_id=one, device_id_type=MESH)
    pl.semaphore_wait(barrier, len(ids))


def wait_all(copies):
    for copy in copies:
        copy.wait()


def fetching(kernel, fetch, store=()):
    def wrapped(*refs):
        moved = tuple(fetch) + tuple(store)
        count = len(moved)
        refs, places, sems = list(refs[: -2 * count]), refs[-2 * count : -count], refs[-count:]
        moves = {}
        for n, i in enumerate(moved):
            ends = (refs[i], places[n]) if n < len(fetch) else (places[n], refs[i])
            moves[i] = pltpu.make_async_copy(*ends, sems[n])
            if n < len(fetch):
                moves[i].start()
            refs[i] = places[n]
        kernel(moves, *refs)
        for i in store:
            moves[i].wait()

    return wrapped


def fetch_scratch(operands, fetch, outs=(), store=()):
    arrays = [operands[i] for i in fetch] + [outs[i] for i in store]
    return [pltpu.VMEM(one.shape, one.dtype) for one in arrays] + [pltpu.SemaphoreType.DMA] * len(arrays)


def fetch_specs(operands, fetch):
    return [ANYWHERE if i in fetch else VM for i in range(len(operands))]


def push(src, dst, send, recv, device):
    copy = pltpu.make_async_remote_copy(
        src_ref=src, dst_ref=dst, send_sem=send, recv_sem=recv, device_id=device, device_id_type=MESH
    )
    copy.start()
    return copy


def split_columns(cols, share):
    return int(cols * share / 128 + 0.5) * 128


class Columns:
    SLOTS = 3

    def __init__(self, place, shards, columns, send, recv, local):
        self.p, self.shards, self.columns = place, shards, columns
        self.send, self.recv, self.local = send, recv, local
        self.copies = {}

    def go(self, i, slot, src, dst, device):
        self.copies[(i, slot)] = push(src, dst, self.send.at[i, slot], self.recv.at[i, slot], device)

    def start(self):
        p = self.p
        for i, shard in enumerate(self.shards):
            mine = self.columns[i].at[p.z]
            self.go(i, 1, shard, mine, p.along_z[1])
            self.go(i, 0, shard, mine, p.along_z[0])
            copy = pltpu.make_async_copy(shard, mine, self.local.at[i])
            copy.start()
            self.copies[(i, 3)] = copy

    def pass_far(self):
        p = self.p
        for i in range(len(self.shards)):
            self.copies[(i, 1)].wait_recv()
            here = self.columns[i].at[p.others[1]]
            self.go(i, 2, here, here, p.along_z[0])

    def finish(self):
        for (i, slot), copy in self.copies.items():
            if slot == 1:
                copy.wait_send()
            else:
                copy.wait()

    @classmethod
    def scratch(cls, count):
        return [
            pltpu.SemaphoreType.DMA((count, cls.SLOTS)),
            pltpu.SemaphoreType.DMA((count, cls.SLOTS)),
            pltpu.SemaphoreType.DMA((count,)),
        ]


class Gather:
    SLOTS = 32

    def __init__(self, place, columns, fulls, share, send, recv, local, places=range(4), by_place=()):
        self.source = {}
        self.p, self.columns, self.fulls, self.share = place, columns, fulls, share
        self.places, self.by_place = places, by_place
        self.send, self.recv, self.local = send, recv, local
        self.copies = {}
        self.seen = set()

    def go(self, i, slot, src, dst, device):
        self.copies[(i, slot)] = push(src, dst, self.send.at[i, slot], self.recv.at[i, slot], device)

    def place(self, n):
        return self.p.z if n == 0 else self.p.others[n - 1]

    def arrays(self, n):
        return [i for i in range(len(self.fulls)) if i not in self.by_place or n in self.places]

    def plane(self, i, n):
        if i in self.by_place:
            return self.fulls[i].at[n - self.places[0]]
        return self.fulls[i].at[self.place(n)]

    def ends(self, i, n):
        p, zz = self.p, self.place(n)
        src = self.source[i, n] if (i, n) in self.source else self.columns[i].at[zz]
        return src, self.plane(i, n).at[p.x, p.y, p.core]

    def start_y(self, places=range(4), arrays=None):
        for n in places:
            for i in self.arrays(n) if arrays is None else arrays:
                src, dst = self.ends(i, n)
                self.go(i, 4 + n, src, dst, self.p.along_y)
                self.go(i, 16 + n, src, dst, self.p.sibling)
                copy = pltpu.make_async_copy(src, dst, self.local.at[i, n])
                copy.start()
                self.copies[(i, 32 + n)] = copy

    def start_x(self, places=range(4), arrays=None):
        for n in places:
            for i in self.arrays(n) if arrays is None else arrays:
                src, dst = self.ends(i, n)
                self.go(i, n, src, dst, self.p.along_x)

    def pass_sides(self, n):
        p = self.p
        for i in self.arrays(n):
            full = self.plane(i, n)
            cols = full.shape[4]
            part = split_columns(cols, self.share)
            self.copies[(i, n)].wait_recv()
            whole = full.at[1 - p.x, p.y, p.core]
            some = full.at[1 - p.x, p.y, p.core, :, pl.ds(0, part)]
            self.go(i, 8 + n, some, some, p.along_y)
            self.go(i, 20 + n, whole, whole, p.sibling)
            self.copies[(i, 4 + n)].wait_recv()
            whole = full.at[p.x, 1 - p.y, p.core]
            some = full.at[p.x, 1 - p.y, p.core, :, pl.ds(part, cols - part)]
            self.go(i, 12 + n, some, some, p.along_x)
            self.go(i, 24 + n, whole, whole, p.sibling)

    def pass_last(self, n):
        p = self.p
        for i in self.arrays(n):
            self.copies[(i, 8 + n)].wait_recv()
            self.copies[(i, 12 + n)].wait_recv()
            whole = self.plane(i, n).at[1 - p.x, 1 - p.y, p.core]
            self.go(i, 28 + n, whole, whole, p.sibling)

    def arrived(self, n):
        for i in range(len(self.fulls)):
            for slot in (16, 20, 24, 28):
                self.copies[(i, slot + n)].wait_recv()
            self.copies.pop((i, 32 + n)).wait()
            self.seen.add((i, n))

    def finish(self):
        for (i, slot), copy in self.copies.items():
            if slot >= 32:
                copy.wait()
            else:
                copy.wait_send()
                if slot >= 16 and (i, slot % 4) not in self.seen:
                    copy.wait_recv()

    @classmethod
    def scratch(cls, count):
        return [
            pltpu.SemaphoreType.DMA((count, cls.SLOTS)),
            pltpu.SemaphoreType.DMA((count, cls.SLOTS)),
            pltpu.SemaphoreType.DMA((count, 4)),
        ]


def everyone(p):
    ids = []
    for d in range(8):
        for e in range(4):
            if d or e:
                ids.append({"ch": lax.rem(p.ch + d, 8), "seq": lax.rem(p.seq + e, 4)})
    return ids


def make_filter(p, table, first, second, shift, speed, hidden, filt, size, start, stop):
    length = 8 * size
    lane = (lax.broadcasted_iota(jnp.int32, (1, 128), 1) + p.ch * 128).astype(F32)
    rate = SLOW_RATE + (FAST_RATE - SLOW_RATE) * lane / 1023.0

    def step(j, carry):
        rows = pl.ds(pl.multiple_of(j * size, size), size)
        inner = jnp.dot(table[rows], first[...], precision=HIGH, preferred_element_type=F32) + shift[...]
        wave = jnp.sin(speed[...] * inner)
        hidden[rows] = wave
        place = (lax.broadcasted_iota(jnp.int32, (size, 1), 0) + j * size).astype(F32) / (length - 1)
        filt[j] = jnp.dot(wave, second[...], precision=HIGH, preferred_element_type=F32) * jnp.exp(-place * rate)
        return carry

    lax.fori_loop(start, stop, step, 0)


def start_kernel(size, *refs):
    taps, skip, gain_one, gain_two, tokens, table, first, second, shift, speed = refs[:10]
    refs = refs[1:]
    shards = refs[9:12]
    consts, halo, hidden, filt = refs[12:16]
    full = refs[16]
    columns = list(refs[17:19])
    pack, packs, send, recv, halo_sems, column_in, first_wide = refs[19:26]
    column_sems, later_sems, gather_sems = refs[26:29], refs[29:32], refs[32:35]
    p = Place()
    ids = everyone(p)
    greet(ids)
    column = Columns(p, shards[:1], [column_in], *column_sems)
    later = Columns(p, shards[1:], columns, *later_sems)
    gather = Gather(p, [column_in], [full], 0.5, *gather_sems)
    column.start()
    pack[...] = jnp.zeros_like(pack)
    part = gain_one.shape[1]
    pack[10:11, :part] = gain_one[...].astype(F32)
    pack[11:12, :part] = gain_two[...].astype(F32)
    moved = pltpu.roll(pack[8:16], p.seq * part, 1)
    pack[8:16] = moved
    for n in range(9):
        pack[n : n + 1] = taps[n // 3, n % 3 : n % 3 + 1]
    pack[9:10] = skip[...]
    column.copies[(0, 3)].wait()
    gather.start_x([0])
    gather.start_y([0])
    copies = [push(pack, packs.at[p.ch, p.seq], send.at[n], recv.at[n], one) for n, one in enumerate(ids)]
    copies.append(push(tokens.at[:, pl.ds(size - 16, 16)], halo, halo_sems.at[0], halo_sems.at[1], {"ch": lax.rem(p.ch + 1, 8)}))
    packs[p.ch, p.seq] = pack[...]
    column.copies[(0, 0)].wait_recv()
    gather.start_x([1])
    gather.start_y([1])
    column.pass_far()
    gather.start_x([2])
    gather.start_y([2])
    gather.pass_sides(0)
    first_wide[...] = jnp.zeros_like(first_wide)
    first_wide[: first.shape[0]] = first[...]

    def filter_part(start):
        make_filter(p, table, first_wide, second, shift, speed, hidden, filt, size, start, start + 2)

    filter_part(0)
    filter_part(2)
    column.copies[(0, 2)].wait_recv()
    gather.start_x([3])
    gather.start_y([3])
    later.start()
    gather.pass_sides(1)
    gather.pass_sides(2)
    filter_part(4)
    gather.pass_sides(3)
    gather.pass_last(0)
    gather.pass_last(1)
    filter_part(6)
    gather.pass_last(2)
    gather.pass_last(3)
    wait_all(copies)
    row = lax.broadcasted_iota(jnp.int32, (16, 128), 0)
    for c in range(8):
        one = packs[c, 0]
        total = one + packs[c, 1] + packs[c, 2] + packs[c, 3]
        consts[:, c * 128 : (c + 1) * 128] = jnp.where(row < 10, one, total)
    gather.finish()
    for slot in (0, 1, 2):
        column.copies[(0, slot)].wait_send()
    for i in range(2):
        for slot in (0, 1, 3):
            later.copies[(i, slot)].wait()


def start_call(taps, skip, gain_one, gain_two, tokens, table, first, second, shift, speed, shards, size):
    rows, cols = shards[0].shape
    filt_width = second.shape[0]
    out = pl.pallas_call(
        functools.partial(start_kernel, size),
        out_shape=[
            jax.ShapeDtypeStruct((16, 1024), F32),
            jax.ShapeDtypeStruct((2, 16, 1024), BF),
            jax.ShapeDtypeStruct((8 * size, filt_width), F32),
            jax.ShapeDtypeStruct((8, size, 128), F32),
            jax.ShapeDtypeStruct((4, 2, 2, 2, rows, cols), BF),
            jax.ShapeDtypeStruct((4,) + shards[1].shape, BF),
            jax.ShapeDtypeStruct((4,) + shards[2].shape, BF),
        ],
        in_specs=[VM] * 13,
        out_specs=[VM] * 4 + [ANYWHERE] + [VM] * 2,
        scratch_shapes=[
            pltpu.VMEM((16, 128), F32),
            pltpu.VMEM((8, 4, 16, 128), F32),
            pltpu.SemaphoreType.DMA((31,)),
            pltpu.SemaphoreType.DMA((31,)),
            pltpu.SemaphoreType.DMA((2,)),
            pltpu.VMEM((4, rows, cols), BF),
            pltpu.VMEM((table.shape[1], filt_width), F32),
        ]
        + Columns.scratch(1)
        + Columns.scratch(2)
        + Gather.scratch(1),
        compiler_params=pltpu.CompilerParams(collective_id=4, has_side_effects=True, vmem_limit_bytes=VMEM_LIMIT),
    )(taps, skip, gain_one, gain_two, tokens, table, first, second, shift, speed, *shards)
    return out[:4], out[4].reshape(rows * 32, cols), out[5:]


def lagged(u, buf, b, stream, lane, size, width):
    at = pl.ds(pl.multiple_of(stream * width + lane, 128), 128)
    rows = size * 2
    buf[pl.ds(0, 16)] = u[pl.ds(rows + 16 * b, 16), at].astype(F32)
    buf[pl.ds(16, size)] = u[pl.ds(b * size, size), at].astype(F32)
    return buf[pl.ds(16, size)], buf[pl.ds(15, size)], buf[pl.ds(14, size)]


def short_conv(u, buf, consts, b, stream, lane, size, width):
    now, one, two = lagged(u, buf, b, stream, lane, size, width)
    at = pl.ds(lane, 128)
    return consts[stream : stream + 1, at] * now + consts[3 + stream : 4 + stream, at] * one + consts[
        6 + stream : 7 + stream, at
    ] * two


def make_pieces(p, make):
    for d in (1, 2, 3, 0):
        make(lax.rem(p.ch // 2 + d, 4))


def send_pieces(p, pieces, blocks_ref, b, send, recv, local, make=None):
    copies = []
    mine = p.ch // 2
    at = pl.ds(b * 128, 128)
    for d in (1, 2, 3, 0):
        pair = lax.rem(mine + d, 4)
        if make is not None:
            make(pair)
        for k in range(2):
            block = 2 * pair + k if d else (p.ch + 1 - 2 * lax.rem(p.ch, 2) if k == 0 else p.ch)
            far = lax.rem(block - p.ch + 8, 8)
            src, dst = pieces.at[block, :, at], blocks_ref.at[p.ch, :, at]
            if d == 0 and k == 1:
                copy = pltpu.make_async_copy(src, dst, local.at[b])
                copy.start()
                copies.append(copy)
            else:
                copies.append(push(src, dst, send.at[far, b], recv.at[far, b], {"ch": block}))
    return copies


def send_blocks(p, ys, blocks_ref, b, send, recv, local):
    at = pl.ds(b * 128, 128)
    copies = []
    for d in range(7):
        src, dst = ys.at[p.ch_ahead[d], :, at], blocks_ref.at[p.ch, :, at]
        copies.append(push(src, dst, send.at[d, b], recv.at[d, b], {"ch": p.ch_ahead[d]}))
    copy = pltpu.make_async_copy(ys.at[p.ch, :, at], blocks_ref.at[p.ch, :, at], local.at[b])
    copy.start()
    return copies + [copy]


def half(b):
    return slice(b * 128, (b + 1) * 128)


def fill_mask(p, lengths, mask, size, first):
    for b in range(2):
        place = lax.broadcasted_iota(jnp.int32, (size, 128), 0) + (p.ch * OWN + first)
        inside = jnp.where(place < lengths[0, b], 1.0, 0.0)
        mask[pl.ds(b * size, size)] = jnp.where(place < 0, 0.0, inside)


def norm_rows(values, gain):
    centre = values - jnp.mean(values, axis=1, keepdims=True)
    inverse = lax.rsqrt(jnp.mean(centre * centre, axis=1, keepdims=True) + EPS)
    return centre * inverse, inverse


def forward_kernel(size, loads, *refs):
    lengths, tokens, halo, consts, h_ref, fh, fl, th, tl, lanes, down_shard = refs[:11]
    columns = list(refs[11:13])
    w_in = refs[13]
    normed, u, mixer, kept, convolved, mask, column_down = refs[14:21]
    fulls = refs[21:24]
    weight, xs, abc, ys, pieces, gates, mixes, bufs, mask_before, far_out, far_up = refs[24:35]
    send, recv, local, send_back, recv_back, local_back = refs[35:41]
    weight_sems, far_sems, column_sems, gather_sems = refs[41], refs[42], refs[43:46], refs[46:]
    p = Place()
    width = 1024
    rows = 2 * size
    load = pltpu.make_async_copy(w_in, weight, weight_sems)
    load.start()
    greet([{"ch": one} for one in p.ch_ahead] + [p.sibling, p.along_y])
    gather = Gather(p, columns, fulls, SHARE, *gather_sems, places=EARLY, by_place=(2,))
    for i in (10, 11, 12):
        loads[i].wait()
    gather.source = {(2, 0): down_shard, (0, 3): far_out, (1, 3): far_up}
    fars = []
    for i, place in enumerate((far_out, far_up)):
        fars.append(push(columns[i].at[p.others[1]], place, far_sems.at[i, 0], far_sems.at[i, 1], p.along_z[0]))
    gather.start_x([0])
    gather.start_y([0])
    gather.start_y([1], arrays=(0, 1))
    loads[1].wait()
    fill_mask(p, lengths, mask, size, 0)
    fill_mask(p, lengths, mask_before, 16, -16)
    gain = consts[10:11, :]

    def norm(i, carry):
        here = pl.ds(pl.multiple_of(i * 32, 32), 32)
        one, _ = norm_rows(tokens[here].astype(F32) * mask[here, 0:1], gain)
        normed[here] = (one * gain).astype(BF)
        return carry

    lax.fori_loop(0, rows // 32, norm, 0)
    before = halo[...].reshape(32, width).astype(F32) * mask_before[:, 0:1]
    before = (norm_rows(before, gain)[0] * gain).astype(BF)
    load.wait()

    def make(pair):
        for stream in range(3):
            at = pl.ds(pl.multiple_of(stream * width + pair * 256, 256), 256)
            u[pl.ds(0, rows), at] = mm(normed[...], weight[:, at]).astype(BF)
            u[pl.ds(rows, 32), at] = mm(before, weight[:, at]).astype(BF)
        for k in range(2):
            block = 2 * pair + k
            lane = pl.multiple_of(block * 128, 128)
            for b in range(2):
                gates[block, b] = short_conv(u, bufs.at[0], consts, b, 0, lane, size, width)
                key = short_conv(u, bufs.at[1], consts, b, 1, lane, size, width)
                mix = key * short_conv(u, bufs.at[2], consts, b, 2, lane, size, width)
                mixes[block, b] = mix
                pieces[block, :, half(b)] = mix.astype(BF)

    arriving = [send_pieces(p, pieces, kept, 0, send, recv, local, make)]
    arriving.append(send_pieces(p, pieces, kept, 1, send, recv, local))
    gather.start_x([1], arrays=(0, 1))
    loads[4].wait()
    loads[14].start()
    loads[15].start()
    filter_spectra(fh, fl, lanes, h_ref, abc, 8, size)
    gather.pass_sides(0)
    gather.start_y([2], arrays=(0, 1))
    leaving = []
    for b in range(2):
        wait_all(arriving[b])
        if b == 1:
            loads[17].start()
        spectra(fh, fl, kept, xs, 8, half(b))
        products_forward(xs, abc, lanes, xs, 8, size, (b,))
        inverse_blocks(th, tl, xs, ys, 8, half(b))
        leaving.append(send_blocks(p, ys, convolved, b, send_back, recv_back, local_back))
        if b == 0:
            gather.start_x([2], arrays=(0, 1))
            gather.pass_sides(1)
            wait_all(fars)
            gather.start_y([3], arrays=(0, 1))
    gather.start_x([3], arrays=(0, 1))
    gather.pass_sides(2)
    gather.pass_last(0)
    for b in range(2):
        rows = slice(b * size, (b + 1) * size)
        wait_all(leaving[b])
        for c in range(8):
            at = half(c)
            long_part = convolved[c, :, half(b)].astype(F32) + consts[9:10, at] * mixes[c, b]
            mixer[rows, at] = (gates[c, b] * long_part * mask[rows]).astype(BF)
        if b == 1:
            column = Columns(p, [down_shard], [column_down], *column_sems)
            column.start()
    gather.pass_sides(3)
    for n in range(1, 4):
        gather.pass_last(n)
    gather.finish()
    for slot in (0, 1, 3):
        column.copies[(0, slot)].wait()


def backward_kernel(size, count, loads, *refs):
    u, consts, mask, grad_mixer, convolved, kept, h_ref, fh, fl, th, tl, lanes = refs[:12]
    grads, plane = list(refs[12 : 13 + count]), refs[13]
    del grads[1]
    refs = refs[1:]
    du, dh_ref, sums = refs[12 + count : 15 + count]
    outs, far_out = refs[15 + count : 15 + 2 * count], refs[15 + 2 * count]
    rest = refs[16 + 2 * count :]
    xs, ds, abc, gh, pieces, arrived, returned, keys, values, dlongs, dcs, edge_out, edge_in, ends, bufs = rest[:15]
    send, recv, local, send_back, recv_back, local_back, edge_sems = rest[15:22]
    p = Place()
    width = 1024
    greet([{"ch": one} for one in p.ch_ahead] + [p.sibling, p.along_y])
    for i in (0, 2, 3):
        loads[i].wait()
    up_cols = grads[1].shape[5]
    whole = [grads[0], (grads[1], 0, up_cols // 2), (grads[1], up_cols // 2, up_cols // 2), (grads[2], 0, grads[2].shape[5])]
    stops = [None, outs[1], outs[1], outs[2]]
    scatter = Scatter(p, whole, [outs[0]] + [None] * 3, stops, SHARE_BACK, rest[28:])
    planes = Planes(p, grads[0], plane, *rest[22:28])
    loads[13].wait()
    planes.turn(0)
    scatter.start(1)
    scatter.start(2)
    scatter.start(3)
    sums[...] = jnp.zeros_like(sums)

    def grad_parts(block, b, rows, skip):
        at = pl.ds(pl.multiple_of(block * 128, 128), 128)
        take = max(rows, 16)
        masked = grad_mixer[pl.ds(b * size, take), at].astype(F32)[:rows] * mask[pl.ds(b * size, rows)]
        conv = convolved[block, :take, b * 128 : (b + 1) * 128].astype(F32)[:rows]
        return masked, conv + skip * (keys[block, b, :rows] * values[block, b, :rows])

    def make(pair):
        for k in range(2):
            make_block(2 * pair + k)

    def make_block(block):
        lane = pl.multiple_of(block * 128, 128)
        at = pl.ds(lane, 128)
        total = jnp.zeros((1, 128), F32)
        for b in range(2):
            rows = pl.ds(b * size, size)
            gate = short_conv(u, bufs.at[0], consts, b, 0, lane, size, width)
            key = short_conv(u, bufs.at[1], consts, b, 1, lane, size, width)
            value = short_conv(u, bufs.at[2], consts, b, 2, lane, size, width)
            keys[block, b] = key
            values[block, b] = value
            dlong = grad_mixer[rows, at].astype(F32) * mask[rows] * gate
            dlongs[block, b] = dlong
            pieces[block, :, b * 128 : (b + 1) * 128] = dlong.astype(BF)
            total = total + jnp.sum(dlong * (key * value), axis=0, keepdims=True)
        sums[9:10, at] = total

    arriving = [send_pieces(p, pieces, arrived, 0, send, recv, local, make)]
    arriving.append(send_pieces(p, pieces, arrived, 1, send, recv, local))
    scatter.core(1)
    loads[6].wait()
    filter_spectra(fh, fl, lanes, h_ref, abc, 8, size)
    loads[5].wait()
    spectra(fh, fl, kept, xs, 8)
    leaving = []
    for b in range(2):
        wait_all(arriving[b])
        spectra(fh, fl, arrived, ds, 8, half(b))
        products_backward(xs, ds, abc, gh, lanes, 8, size, (b,))
        inverse_blocks(th, tl, ds, pieces, 8, half(b))
        leaving.append(send_blocks(p, pieces, returned, b, send_back, recv_back, local_back))
        if b == 0:
            scatter.core(2)
            scatter.core(3)
            planes.cross(0)
    scatter.first(1)
    filter_gradient(th, tl, gh, dh_ref, 8, size)
    loads[17].start()
    loads[12].wait()
    planes.last(0, p.others[2])
    scatter.turn(0)
    loads[4].wait()
    wait_all(leaving[0])
    wait_all(leaving[1])

    def edges(c, carry):
        at = pl.ds(pl.multiple_of(c * 128, 128), 128)
        skip = consts[9:10, at]
        for b in range(2):
            masked, long_part = grad_parts(c, b, 8, skip)
            back = returned[c, :16, b * 128 : (b + 1) * 128].astype(F32)[:8]
            dmixed = back + skip * dlongs[c, b, :8]
            dmixed = dmixed[:2]
            edge_out[2 * b : 2 * b + 2, at] = (masked * long_part)[:2]
            edge_out[4 + 2 * b : 6 + 2 * b, at] = dmixed * values[c, b, :8][:2]
            edge_out[8 + 2 * b : 10 + 2 * b, at] = dmixed * keys[c, b, :8][:2]
        return carry

    lax.fori_loop(0, 8, edges, 0)
    edge = push(edge_out, edge_in, edge_sems.at[0], edge_sems.at[1], {"ch": lax.rem(p.ch + 7, 8)})
    scatter.first(2)
    scatter.first(3)

    def streams(c, carry):
        lane = pl.multiple_of(c * 128, 128)
        at = pl.ds(lane, 128)
        skip = consts[9:10, at]
        for b in range(2):
            masked, long_part = grad_parts(c, b, size, skip)
            dmixed = returned[c, :, b * 128 : (b + 1) * 128].astype(F32) + skip * dlongs[c, b]
            dcs[0, b, pl.ds(0, size)] = masked * long_part
            dcs[1, b, pl.ds(0, size)] = dmixed * values[c, b]
            dcs[2, b, pl.ds(0, size)] = dmixed * keys[c, b]
        for stream in range(3):
            out = pl.ds(pl.multiple_of(stream * width + lane, 128), 128)
            totals = [jnp.zeros((1, 128), F32)] * 3
            for b in range(2):
                dcs[stream, b, pl.ds(size, 8)] = jnp.zeros((8, 128), F32)
                parts = lagged(u, bufs.at[stream], b, stream, lane, size, width)
                grad = dcs[stream, b, pl.ds(0, size)]
                for lag in range(3):
                    totals[lag] = totals[lag] + jnp.sum(grad * parts[lag], axis=0, keepdims=True)
                total = consts[stream : stream + 1, at] * grad
                total = total + consts[3 + stream : 4 + stream, at] * dcs[stream, b, pl.ds(1, size)]
                total = total + consts[6 + stream : 7 + stream, at] * dcs[stream, b, pl.ds(2, size)]
                du[pl.ds(b * size, size), out] = total.astype(BF)
                ends[stream, b, :, at] = total[size - 16 :]
            for lag in range(3):
                row = 3 * lag + stream
                sums[row : row + 1, at] = totals[lag]
        return carry

    lax.fori_loop(0, 8, streams, 0)
    edge.wait()

    inside = jnp.where(p.ch < 7, 1.0, 0.0)
    for stream in range(3):
        one = consts[3 + stream : 4 + stream, :] * inside
        two = consts[6 + stream : 7 + stream, :] * inside
        out = slice(stream * width, (stream + 1) * width)
        for b in range(2):
            row = 4 * stream + 2 * b
            near, far = edge_in[row : row + 1, :], edge_in[row + 1 : row + 2, :]
            ends[stream, b, 14:15] = ends[stream, b, 14:15] + two * near
            ends[stream, b, 15:16] = ends[stream, b, 15:16] + one * near + two * far
            du[(b + 1) * size - 16 : (b + 1) * size, out] = ends[stream, b].astype(BF)
    loads[16].start()
    scatter.second(1)
    scatter.second(2)
    scatter.second(3)
    scatter.near(0, outs[0], far_out)


def nt(a, b):
    return lax.dot_general(a, b, (((1,), (1,)), ((), ())), preferred_element_type=F32)


def tn(a, b):
    return lax.dot_general(a, b, (((0,), (0,)), ((), ())), preferred_element_type=F32)


GELU_ONE = math.sqrt(2.0 / math.pi)
GELU_THREE = GELU_ONE * 0.044715


class Planes:
    def __init__(self, place, column, acc, one_a, one_b, two_a, two_b, send, recv):
        self.p, self.column = place, column
        self.acc, self.one_a, self.one_b, self.two_a, self.two_b = acc, one_a, one_b, two_a, two_b
        self.send, self.recv = send, recv
        self.copies = {}
        cols = acc.shape[4]
        half = split_columns(cols, 0.5)
        self.low, self.high = pl.ds(0, half), pl.ds(half, cols - half)

    def go(self, n, slot, src, dst, device):
        self.copies[(n, slot)] = push(src, dst, self.send.at[n, slot], self.recv.at[n, slot], device)

    def done(self, n, *slots):
        for slot in slots:
            self.copies[(n, slot)].wait()

    def core(self, n, made):
        self.go(n, 0, made.at[:, :, 1 - self.p.core], self.acc.at[n], self.p.sibling)

    def sides(self, n, made):
        p, acc = self.p, self.acc.at[n]
        self.done(n, 0)

        def step(k, carry):
            xx, yy = k // 2, lax.rem(k, 2)
            acc[xx, yy] = add_rows(acc[xx, yy], made[xx, yy, p.core])
            return carry

        lax.fori_loop(0, 4, step, 0)

    def turn(self, n):
        p, acc = self.p, self.acc.at[n]
        self.go(n, 1, acc.at[:, 1 - p.y, :, self.low], self.one_a.at[n], p.along_y)
        self.go(n, 2, acc.at[1 - p.x, :, :, self.high], self.one_b.at[n], p.along_x)

    def cross(self, n):
        p, acc = self.p, self.acc.at[n]
        low, high = self.low, self.high
        self.done(n, 1, 2)
        for k in range(2):
            acc[k, p.y, :, low] = add_rows(acc[k, p.y, :, low], self.one_a[n, k])
            acc[p.x, k, :, high] = add_rows(acc[p.x, k, :, high], self.one_b[n, k])
        self.go(n, 3, acc.at[1 - p.x, p.y, :, low], self.two_a.at[n], p.along_x)
        self.go(n, 4, acc.at[p.x, 1 - p.y, :, high], self.two_b.at[n], p.along_y)

    def last(self, n, zz):
        p, acc = self.p, self.acc.at[n]
        low, high = self.low, self.high
        self.done(n, 3, 4)
        self.column[zz, :, low] = add_rows(acc[p.x, p.y, :, low], self.two_a[n])
        self.column[zz, :, high] = add_rows(acc[p.x, p.y, :, high], self.two_b[n])

    @staticmethod
    def scratch(count, rows, cols):
        half = split_columns(cols, 0.5)
        return [
            pltpu.VMEM((count, 2, rows, half), BF),
            pltpu.VMEM((count, 2, rows, cols - half), BF),
            pltpu.VMEM((count, rows, half), BF),
            pltpu.VMEM((count, rows, cols - half), BF),
            pltpu.SemaphoreType.DMA((count + 1, 5)),
            pltpu.SemaphoreType.DMA((count + 1, 5)),
        ]


def feed_forward_kernel(loads, *refs):
    mixer, tokens, mask, cot, consts, w_out, w_up, early, column = refs[:9]
    result, grad_after, grad_mixer, grad_gain, grad_out, sum_column, sum_last, grad_up = refs[9:17]
    up, planes, late, total, unit, scale, normed, turned, da, pre, dact, act, dpre, kept_down, kept_up = refs[17:32]
    up_sem, plane_sems, out_sems, sum_acc, far_place = refs[32:37]
    far_sems, gather_sems, scatter_refs = refs[37], refs[38:41], refs[41:47]
    p = Place()
    greet([p.along_x, p.along_y, p.along_z[0], p.sibling])
    loads[8].wait()
    gather = Gather(p, [column], [late], 0.5, *gather_sems, places=LATE, by_place=(0,))
    gather.source = {(0, 3): far_place}
    far = push(column.at[p.others[1]], far_place, far_sems.at[0], far_sems.at[1], p.along_z[0])
    gather.start_x([1, 2])
    gather.start_y([1, 2])
    sums = Planes(p, sum_column, sum_acc, *scatter_refs)
    weights = [pltpu.make_async_copy(w_up, up, up_sem)]
    weights += [pltpu.make_async_copy(early.at[n], planes.at[n], plane_sems.at[n]) for n in EARLY]
    for load in weights:
        load.start()
    gain = consts[11:12, :]
    loads[0].wait()
    loads[5].wait()
    total[...] = mm(mixer[...], w_out[...])
    loads[1].wait()
    loads[2].wait()
    loads[3].wait()

    def norm(i, carry):
        rows = pl.ds(pl.multiple_of(i * 32, 32), 32)
        zero = tokens[rows].astype(F32) * mask[rows, 0:1]
        value = zero + total[rows]
        total[rows] = value
        centre = value - jnp.mean(value, axis=1, keepdims=True)
        inverse = lax.rsqrt(jnp.mean(centre * centre, axis=1, keepdims=True) + EPS)
        one = centre * inverse
        unit[rows] = one
        scale[rows] = jnp.broadcast_to(inverse, (32, 128))
        normed[rows] = (one * gain).astype(BF)
        return carry

    lax.fori_loop(0, 16, norm, 0)
    turned[...] = normed[...].T
    wait_all(weights)
    writes = [None] * 4
    for n in range(4):
        zz = gather.place(n)
        cols = pl.ds(pl.multiple_of(zz * 1024, 1024), 1024)
        slot = n % 2
        made = kept_down.at[slot]
        pre[...] = mm(normed[...], up[:, cols])
        if n == 0:
            gather.pass_sides(1)
            far.wait()
            gather.start_x([3])
            gather.start_y([3])
            plane = planes.at[0]
        else:
            gather.arrived(n)
            plane = late.at[n - 1]
        if n > 0:
            sums.sides(n - 1, kept_down.at[1 - slot])
            sums.turn(n - 1)
        dact[...] = nt(cot[...], plane[...].reshape(1024, 1024))

        def gelu(i, carry):
            rows = pl.ds(pl.multiple_of(i * 16, 16), 16)
            x = pre[rows]
            square = x * x
            t = jnp.tanh(x * (GELU_ONE + GELU_THREE * square))
            half = 0.5 + 0.5 * t
            value = x * half
            act[rows] = value.astype(BF)
            slope = half + value * (1.0 - t) * (GELU_ONE + 3.0 * GELU_THREE * square)
            dpre[rows] = (dact[rows] * slope).astype(BF)
            return carry

        lax.fori_loop(0, 32, gelu, 0)
        if n > 1:
            wait_all(writes[n - 2])
        made[...] = tn(act[...], cot[...]).astype(BF).reshape(2, 2, 2, 128, 1024)
        sums.core(n, made)
        total[...] += mm(act[...], plane[...].reshape(1024, 1024))
        if n > 1:
            sums.cross(n - 2)
        if n < 2:
            gather.pass_sides(n + 2)
        back = nt(dpre[...], up[:, cols])
        da[...] = back if n == 0 else da[...] + back
        if n < 3:
            gather.pass_last(n + 1)
        kept_up[slot] = mm(turned[...], dpre[...]).astype(BF)
        writes[n] = [pltpu.make_async_copy(kept_up.at[slot], grad_up.at[:, cols], out_sems.at[n])]
        for copy in writes[n]:
            copy.start()
    sums.sides(3, kept_down.at[1])
    sum_last[0] = sum_acc[3]
    sums.last(0, gather.place(0))

    def finish(i, gain_sum):
        rows = pl.ds(pl.multiple_of(i * 32, 32), 32)
        result[rows] = total[rows].astype(BF)
        one = unit[rows]
        back = da[rows]
        e = back * gain
        inner = e - jnp.mean(e, axis=1, keepdims=True) - one * jnp.mean(e * one, axis=1, keepdims=True)
        after = cot[rows].astype(F32) + scale[rows, 0:1] * inner
        grad_after[rows] = after
        normed[rows] = after.astype(BF)
        return gain_sum + jnp.sum(back * one, axis=0, keepdims=True)

    grad_gain[...] = lax.fori_loop(0, 16, finish, jnp.zeros((1, 1024), F32))
    loads[9].start()
    loads[10].start()
    grad_mixer[...] = nt(normed[...], w_out[...]).astype(BF)
    loads[11].start()
    sums.cross(2)
    sums.last(1, gather.place(1))
    grad_out[...] = tn(mixer[...], normed[...]).astype(BF)
    for n in (2, 3):
        wait_all(writes[n])
    gather.finish()
    sums.last(2, gather.place(2))
    sum_column[gather.place(3)] = sum_acc[3, 0, 0]


def feed_forward_call(mixer, tokens, mask, cot, consts, w_out, w_up, early, column):
    rows, width = mixer.shape
    hidden = w_up.shape[1]
    wide = (rows, width)
    square = (width, width)
    part = column.shape[1:]
    operands = (mixer, tokens, mask, cot, consts, w_out, w_up, early, column)
    fetch = (0, 1, 2, 3, 5, 8)
    store = (0, 1, 2)
    outs = [
        jax.ShapeDtypeStruct(wide, BF),
        jax.ShapeDtypeStruct(wide, F32),
        jax.ShapeDtypeStruct(wide, BF),
        jax.ShapeDtypeStruct((1, width), F32),
        jax.ShapeDtypeStruct(square, BF),
        jax.ShapeDtypeStruct((4,) + part, BF),
        jax.ShapeDtypeStruct((1, 2, 2) + part, BF),
        jax.ShapeDtypeStruct((width, hidden), BF),
        ]
    return pl.pallas_call(
        fetching(feed_forward_kernel, fetch, [len(operands) + i for i in store]),
        out_shape=outs,
        in_specs=fetch_specs(operands[:6], fetch) + [ANYWHERE] * 3,
        out_specs=fetch_specs(outs[:7], store) + [ANYWHERE],
        scratch_shapes=[
            pltpu.VMEM((width, hidden), BF),
            pltpu.VMEM((len(EARLY), 2, 2, 2) + part, BF),
            pltpu.VMEM((len(LATE), 2, 2, 2) + part, BF),
            pltpu.VMEM(wide, F32),
            pltpu.VMEM(wide, F32),
            pltpu.VMEM((rows, 128), F32),
            pltpu.VMEM(wide, BF),
            pltpu.VMEM((width, rows), BF),
            pltpu.VMEM(wide, F32),
            pltpu.VMEM(wide, F32),
            pltpu.VMEM(wide, F32),
            pltpu.VMEM(wide, BF),
            pltpu.VMEM(wide, BF),
            pltpu.VMEM((2, 2, 2, 2) + part, BF),
            pltpu.VMEM((2,) + square, BF),
            pltpu.SemaphoreType.DMA,
            pltpu.SemaphoreType.DMA((len(EARLY),)),
            pltpu.SemaphoreType.DMA((4,)),
            pltpu.VMEM((4, 2, 2) + part, BF),
            pltpu.VMEM(part, BF),
            pltpu.SemaphoreType.DMA((2,)),
        ]
        + Gather.scratch(1)
        + Planes.scratch(3, *part)
        + fetch_scratch(operands, fetch, outs, store),
        compiler_params=pltpu.CompilerParams(collective_id=5, has_side_effects=True, vmem_limit_bytes=VMEM_LIMIT),
    )(*operands)


def exchange_sems():
    pieces = [pltpu.SemaphoreType.DMA((8, 2))] * 2 + [pltpu.SemaphoreType.DMA((2,))]
    return pieces + [pltpu.SemaphoreType.DMA((7, 2))] * 2 + [pltpu.SemaphoreType.DMA((2,))]


def forward_call(lengths, tokens, halo, consts, filt, tables, down_shard, columns, w_in, size):
    rows = 2 * size
    block = (8, size, 256)
    piece = (8, 2, size, 128)
    operands = (lengths, tokens, halo, consts, filt) + tables + (down_shard,) + tuple(columns)
    whole = [jax.ShapeDtypeStruct((4, 2, 2, 2) + one.shape[1:], BF) for one in columns]
    whole.append(jax.ShapeDtypeStruct((len(EARLY), 2, 2, 2) + down_shard.shape, BF))
    fetch = (1, 4, 10, 11, 12)
    store = (0, 1, 3)
    outs = [
        jax.ShapeDtypeStruct((rows, 1024), BF),
        jax.ShapeDtypeStruct((rows + 32, 3072), BF),
        jax.ShapeDtypeStruct((rows, 1024), BF),
        jax.ShapeDtypeStruct(block, BF),
        jax.ShapeDtypeStruct(block, BF),
        jax.ShapeDtypeStruct((rows, 128), F32),
        jax.ShapeDtypeStruct((4,) + down_shard.shape, BF),
    ]
    first = len(operands) + 1
    out = pl.pallas_call(
        fetching(functools.partial(forward_kernel, size), fetch, [first + i for i in store]),
        out_shape=outs + whole,
        in_specs=[pl.BlockSpec(memory_space=pltpu.SMEM)] + fetch_specs(operands, fetch)[1:] + [ANYWHERE],
        out_specs=fetch_specs(outs, store) + [ANYWHERE] * 3,
        scratch_shapes=[
            pltpu.VMEM(w_in.shape, BF),
            pltpu.VMEM((8, 2 * size, 256), F32),
            pltpu.VMEM((8, 2, size, 128), F32),
            pltpu.VMEM(block, BF),
            pltpu.VMEM(block, BF),
            pltpu.VMEM(piece, F32),
            pltpu.VMEM(piece, F32),
            pltpu.VMEM((3, size + 16, 128), F32),
            pltpu.VMEM((32, 128), F32),
            pltpu.VMEM(columns[0].shape[1:], BF),
            pltpu.VMEM(columns[1].shape[1:], BF),
        ]
        + exchange_sems()
        + [pltpu.SemaphoreType.DMA, pltpu.SemaphoreType.DMA((2, 2))]
        + Columns.scratch(1)
        + Gather.scratch(3)
        + fetch_scratch(operands, fetch, outs, store),
        compiler_params=pltpu.CompilerParams(collective_id=1, has_side_effects=True, vmem_limit_bytes=VMEM_LIMIT),
    )(*operands, w_in)
    return out[:7], [one.reshape(-1, one.shape[-1]) for one in out[7:9]], out[9]


def backward_call(u, consts, mask, grad_mixer, convolved, kept, filt, tables, grads, plane, size):
    rows = 2 * size
    block = (8, size, 256)
    piece = (8, 2, size, 128)
    operands = (u, consts, mask, grad_mixer, convolved, kept, filt) + tables
    count = len(grads)
    shapes = [grads[0].shape[1:]] + [(one.shape[0] // 32, one.shape[1]) for one in grads[1:]]
    views = [grads[0]] + [one.reshape((4, 2, 2, 2) + shape) for one, shape in zip(grads[1:], shapes[1:])]
    fetch = (0, 2, 3, 4, 5, 6, 12, 13)
    store = (0, 1)
    outs = [
        jax.ShapeDtypeStruct((rows, 3072), BF),
        jax.ShapeDtypeStruct((8, size, 128), F32),
        jax.ShapeDtypeStruct((16, 1024), F32),
    ]
    (up_rows, up_cols), out_kind = shapes[1], shapes[2]
    kinds = [shapes[0] + ("", False)] + [(up_rows, up_cols // 2, "load", True)] * 2 + [out_kind + ("load", True)]
    operands = operands + (views[0], plane)
    out = pl.pallas_call(
        fetching(functools.partial(backward_kernel, size, count), fetch, [len(operands) + count - 1 + i for i in store]),
        out_shape=outs
        + [jax.ShapeDtypeStruct(shapes[0], F32)]
        + [jax.ShapeDtypeStruct((4,) + shape, BF) for shape in shapes[1:]]
        + [jax.ShapeDtypeStruct(shapes[0], BF)],
        in_specs=fetch_specs(operands, fetch) + [ANYWHERE] * (count - 1),
        out_specs=fetch_specs(outs, store) + [VM] * (1 + count),
        scratch_shapes=[
            pltpu.VMEM((8, 2 * size, 256), F32),
            pltpu.VMEM((8, 2 * size, 256), F32),
            pltpu.VMEM((8, 2, size, 128), F32),
            pltpu.VMEM((8, 2, size, 128), F32),
            pltpu.VMEM(block, BF),
            pltpu.VMEM(block, BF),
            pltpu.VMEM(block, BF),
            pltpu.VMEM(piece, F32),
            pltpu.VMEM(piece, F32),
            pltpu.VMEM(piece, F32),
            pltpu.VMEM((3, 2, size + 8, 128), F32),
            pltpu.VMEM((16, 1024), F32),
            pltpu.VMEM((16, 1024), F32),
            pltpu.VMEM((3, 2, 16, 1024), F32),
            pltpu.VMEM((3, size + 16, 128), F32),
        ]
        + exchange_sems()
        + [pltpu.SemaphoreType.DMA((2,))]
        + Planes.scratch(1, *shapes[0])
        + Scatter.scratch(kinds, SHARE_BACK)
        + fetch_scratch(operands, fetch, outs, store),
        compiler_params=pltpu.CompilerParams(collective_id=2, has_side_effects=True, vmem_limit_bytes=VMEM_LIMIT),
    )(*operands, *views[1:])
    return out[:3], out[3:]


def add_rows(target, other):
    return (target.astype(F32) + other.astype(F32)).astype(BF)


class Scatter:
    SLOTS = 11

    def __init__(self, place, grads, outs, columns, share, refs):
        self.p, self.grads, self.outs, self.columns, self.share = place, grads, outs, columns, share
        count = len(grads)
        self.bufs = []
        at = 0
        for one, column in zip(grads, columns):
            names = Scatter.names(self.kind(one), column is not None)
            self.bufs.append(dict(zip(names, refs[at : at + len(names)])))
            at += len(names)
        self.send, self.recv, self.local = refs[at : at + 3]
        self.copies = {}

    @staticmethod
    def kind(grad):
        if not isinstance(grad, tuple):
            return ""
        return "load" if len(grad) == 3 else "made"

    @staticmethod
    def names(whole, stops):
        before = ("acc", "one_a", "one_b", "two_a", "two_b") if whole else ()
        if whole == "load":
            before += ("own",)
        return before + (() if stops else ("three", "four"))

    def go(self, i, slot, src, dst, device):
        copy = push(src, dst, self.send.at[i, slot], self.recv.at[i, slot], device)
        self.copies[(i, slot)] = copy

    def done(self, i, *slots):
        for slot in slots:
            self.copies[(i, slot)].wait()

    def part(self, i, zz, core):
        ref, first, cols = self.grads[i]
        if cols == ref.shape[5]:
            return ref.at[zz, :, :, core]
        return ref.at[zz, :, :, core, :, pl.ds(first, cols)]

    def load(self, i, zz):
        own = self.bufs[i]["own"]
        copy = pltpu.make_async_copy(self.part(i, zz, self.p.core), own.at[zz % 2], self.local.at[i, zz])
        copy.start()
        self.copies[(i, "own", zz)] = copy

    def start(self, i):
        if self.kind(self.grads[i]) == "made":
            self.go(i, 0, self.grads[i][0].at[:, :, :, 1 - self.p.core], self.bufs[i]["acc"], self.p.sibling)
            return
        for zz in range(4):
            self.go(i, zz, self.part(i, zz, 1 - self.p.core), self.bufs[i]["acc"].at[zz], self.p.sibling)
        self.load(i, 0)
        self.load(i, 1)

    def halves(self, i):
        cols = self.grads[i][2]
        part = split_columns(cols, self.share)
        return pl.ds(0, part), pl.ds(part, cols - part)

    def core(self, i):
        p, acc = self.p, self.bufs[i]["acc"]
        if self.kind(self.grads[i]) == "made":
            made = self.grads[i][0]
            self.done(i, 0)

            def add(n, carry):
                zz, xx, yy = n // 4, lax.rem(n // 2, 2), lax.rem(n, 2)
                acc[zz, xx, yy] = add_rows(acc[zz, xx, yy], made[zz, xx, yy, p.core])
                return carry

            lax.fori_loop(0, 16, add, 0)
        else:
            self.add_loaded(i)
        low, high = self.halves(i)
        self.go(i, 4, acc.at[:, :, 1 - p.y, :, low], self.bufs[i]["one_a"], p.along_y)
        self.go(i, 5, acc.at[:, 1 - p.x, :, :, high], self.bufs[i]["one_b"], p.along_x)

    def add_loaded(self, i):
        acc, own = self.bufs[i]["acc"], self.bufs[i]["own"]
        for zz in range(4):
            self.copies[(i, "own", zz)].wait()
            self.done(i, zz)

            def step(n, carry, zz=zz):
                xx, yy = n // 2, lax.rem(n, 2)
                acc[zz, xx, yy] = add_rows(acc[zz, xx, yy], own[zz % 2, xx, yy])
                return carry

            lax.fori_loop(0, 4, step, 0)
            if zz < 2:
                self.load(i, zz + 2)

    def first(self, i):
        p, acc = self.p, self.bufs[i]["acc"]
        one_a, one_b = self.bufs[i]["one_a"], self.bufs[i]["one_b"]
        low, high = self.halves(i)
        self.done(i, 4, 5)

        def step(n, carry):
            zz, w = n // 2, lax.rem(n, 2)
            acc[zz, w, p.y, :, low] = add_rows(acc[zz, w, p.y, :, low], one_a[zz, w])
            acc[zz, p.x, w, :, high] = add_rows(acc[zz, p.x, w, :, high], one_b[zz, w])
            return carry

        lax.fori_loop(0, 8, step, 0)
        self.go(i, 6, acc.at[:, 1 - p.x, p.y, :, low], self.bufs[i]["two_a"], p.along_x)
        self.go(i, 7, acc.at[:, p.x, 1 - p.y, :, high], self.bufs[i]["two_b"], p.along_y)

    def second(self, i):
        p, acc = self.p, self.bufs[i]["acc"]
        two_a, two_b = self.bufs[i]["two_a"], self.bufs[i]["two_b"]
        low, high = self.halves(i)
        self.done(i, 6, 7)
        column = self.columns[i]

        first, cols = (0, 0) if column is None else self.grads[i][1:3]

        def step(zz, carry):
            here = acc.at[zz, p.x, p.y] if column is None else column.at[zz, :, pl.ds(first, cols)]
            here[:, low] = add_rows(acc[zz, p.x, p.y, :, low], two_a[zz])
            here[:, high] = add_rows(acc[zz, p.x, p.y, :, high], two_b[zz])
            return carry

        lax.fori_loop(0, 4, step, 0)
        if column is None:
            self.turn(i)

    def sums(self, i, zz):
        if isinstance(self.grads[i], tuple):
            return self.bufs[i]["acc"].at[zz, self.p.x, self.p.y]
        return self.grads[i].at[zz]

    def turn(self, i):
        p, three = self.p, self.bufs[i]["three"]
        self.go(i, 8, self.sums(i, p.others[2]), three.at[0], p.along_z[0])
        self.go(i, 9, self.sums(i, p.others[0]), three.at[1], p.along_z[0])

    def third(self, i):
        p, three = self.p, self.bufs[i]["three"]
        self.done(i, 8, 9)
        far = self.sums(i, p.others[1])
        three[0] = add_rows(far[...], three[0])
        self.go(i, 10, three.at[0], self.bufs[i]["four"], p.along_z[1])

    def near(self, i, mine, far):
        three = self.bufs[i]["three"]
        self.done(i, 8, 9)
        far[...] = add_rows(self.sums(i, self.p.others[1])[...], three[0])
        mine[...] = self.sums(i, self.p.z)[...].astype(F32) + three[1].astype(F32)

    def last(self, i):
        three, four = self.bufs[i]["three"], self.bufs[i]["four"]
        self.done(i, 10)
        total = self.sums(i, self.p.z)[...].astype(F32) + three[1].astype(F32) + four[...].astype(F32)
        if isinstance(self.grads[i], tuple):
            first, cols = self.grads[i][1:3]
            self.outs[i][:, first : first + cols] = total
        else:
            self.outs[i][...] = total

    @classmethod
    def scratch(cls, kinds, share):
        count = len(kinds)
        bufs = []
        for rows, cols, whole, stops in kinds:
            part = split_columns(cols, share)
            shapes = {
                "own": (2, 2, 2, rows, cols),
                "acc": (4, 2, 2, rows, cols),
                "one_a": (4, 2, rows, part),
                "one_b": (4, 2, rows, cols - part),
                "two_a": (4, rows, part),
                "two_b": (4, rows, cols - part),
                "three": (2, rows, cols),
                "four": (rows, cols),
            }
            bufs += [pltpu.VMEM(shapes[name], BF) for name in cls.names(whole, stops)]
        return bufs + [
            pltpu.SemaphoreType.DMA((count, cls.SLOTS)),
            pltpu.SemaphoreType.DMA((count, cls.SLOTS)),
            pltpu.SemaphoreType.DMA((count, 4)),
        ]


def small_sums(p, vec, sec, fst, gathered, send, recv):
    rows, more = vec.shape[0], fst.shape[0]
    copies = []
    for d in range(7):
        lane = pl.multiple_of(p.ch_ahead[d] * 128, 128)
        pairs = (
            (vec.at[:, pl.ds(lane, 128)], gathered.at[p.ch, pl.ds(0, rows)]),
            (fst, gathered.at[p.ch, pl.ds(rows, more)]),
        )
        for n, (src, dst) in enumerate(pairs):
            copies.append(push(src, dst, send.at[2 * d + n], recv.at[2 * d + n], {"ch": p.ch_ahead[d]}))
    gathered[p.ch, :rows] = vec[:, pl.ds(pl.multiple_of(p.ch * 128, 128), 128)]
    gathered[p.ch, rows:] = fst[...]
    return copies


def join_sums(p, sec, gathered, joined, send, recv):
    rows = gathered.shape[1]
    total = gathered[0]
    for n in range(1, 8):
        total = total + gathered[n]
    joined[p.seq, :rows] = total
    joined[p.seq, rows:] = sec[...]
    return [
        push(joined.at[p.seq], joined.at[p.seq], send.at[14 + d], recv.at[14 + d], {"seq": p.seq_ahead[d]})
        for d in range(3)
    ]


def tail_kernel(size, loads, *refs):
    normed, du, tokens, mask, consts, grad_after, sums, gain_two = refs[:8]
    dh, hidden, table, first, second, shift, speed = refs[8:15]
    columns = list(refs[15:17])
    down_mine, down_far = refs[17:19]
    w_in = refs[19]
    grad_input, out, small_out = refs[20:23]
    outs = list(refs[23:25])
    down_out = refs[25]
    weight, turned, made, da, vec, sec, fst, gathered, joined, first_wide, down_last, packed = refs[26:38]
    weight_sem, small_send, small_recv, down_sems = refs[38:42]
    width = 1024
    p = Place()
    load = pltpu.make_async_copy(w_in, weight, weight_sem)
    load.start()
    greet([{"ch": one} for one in p.ch_ahead] + [{"seq": one} for one in p.seq_ahead])
    grads = [(made.at[n], n * width, width, None) for n in range(3)] + columns
    scatter = Scatter(p, grads, [out] * 3 + outs, [None] * 5, 0.5, refs[42:])
    loads[15].wait()
    loads[16].wait()
    for n in (3, 4):
        scatter.turn(n)
    loads[18].wait()
    down = push(down_far, down_last, down_sems.at[0], down_sems.at[1], p.along_z[1])
    loads[0].wait()
    turned[...] = normed[...].T
    loads[1].wait()

    def part(stream):
        made[stream] = mm(turned[...], du[:, stream * width : (stream + 1) * width]).astype(BF).reshape(made.shape[1:])
        scatter.start(stream)

    def back(stream):
        at = slice(stream * width, (stream + 1) * width)
        one = nt(du[:, at], weight[:, at])
        da[...] = one if stream == 0 else da[...] + one

    part(0)
    part(1)
    scatter.core(0)
    part(2)
    scatter.core(1)
    scatter.core(2)

    length = 8 * size
    lane = (lax.broadcasted_iota(jnp.int32, (1, 128), 1) + p.ch * 128).astype(F32)
    rate = SLOW_RATE + (FAST_RATE - SLOW_RATE) * lane / 1023.0
    emb, filt_width = first_wide.shape
    first_wide[...] = jnp.zeros_like(first_wide)
    first_wide[: first.shape[0]] = first[...]
    sec[...] = jnp.zeros_like(sec)
    fst[...] = jnp.zeros_like(fst)

    def high(a, b, dims):
        return lax.dot_general(a, b, ((dims), ((), ())), precision=HIGH, preferred_element_type=F32)

    def step(j, carry):
        rows = pl.ds(pl.multiple_of(j * size, size), size)
        place = (lax.broadcasted_iota(jnp.int32, (size, 1), 0) + j * size).astype(F32) / (length - 1)
        draw = dh[j] * jnp.exp(-place * rate)
        sec[...] += high(hidden[rows], draw, ((0,), (0,)))
        inner = high(table[rows], first_wide[...], ((1,), (0,))) + shift[...]
        q = high(draw, second[...], ((1,), (1,))) * jnp.cos(speed[...] * inner)
        scaled = q * speed[...]
        fst[:emb, :filt_width] += high(table[rows], scaled, ((0,), (0,)))
        fst[emb : emb + 1, :filt_width] += jnp.sum(scaled, axis=0, keepdims=True)
        fst[emb + 1 : emb + 2, :filt_width] += jnp.sum(q * inner, axis=0, keepdims=True)
        return carry

    for i in (8, 9, 10):
        loads[i].wait()
    load.wait()
    back(0)
    back(1)
    back(2)
    scatter.first(0)
    lax.fori_loop(0, 4, step, 0)
    scatter.first(1)
    for n in (3, 4):
        scatter.third(n)
    scatter.first(2)
    for i in (2, 3, 5):
        loads[i].wait()
    gain = consts[10:11, :]

    def norm(i, total):
        rows = pl.ds(pl.multiple_of(i * 32, 32), 32)
        one, inverse = norm_rows(tokens[rows].astype(F32) * mask[rows, 0:1], gain)
        grad = da[rows]
        e = grad * gain
        inner = e - jnp.mean(e, axis=1, keepdims=True) - one * jnp.mean(e * one, axis=1, keepdims=True)
        grad_input[rows] = ((grad_after[rows] + inverse * inner) * mask[rows, 0:1]).astype(BF)
        return total + jnp.sum(grad * one, axis=0, keepdims=True)

    gain_one = lax.fori_loop(0, normed.shape[0] // 32, norm, jnp.zeros((1, width), F32))
    loads[20].start()
    vec[...] = jnp.zeros_like(vec)
    vec[:10] = sums[:10]
    vec[10:11] = gain_one
    vec[11:12] = gain_two[...]
    scatter.second(0)
    scatter.second(1)
    lax.fori_loop(4, 8, step, 0)
    packed[...] = fst[:24] + pltpu.roll(fst[24:], 64, 1)
    small = small_sums(p, vec, sec, packed, gathered, small_send, small_recv)
    scatter.second(2)
    scatter.third(0)
    scatter.third(1)
    wait_all(small)
    small = join_sums(p, sec, gathered, joined, small_send, small_recv)
    scatter.third(2)
    for n in (3, 4):
        scatter.last(n)
    scatter.last(0)
    scatter.last(1)
    down.wait()
    loads[17].wait()
    down_out[...] = down_mine[...] + down_last[...].astype(F32)
    scatter.last(2)
    wait_all(small)
    total = joined[0]
    for n in range(1, 4):
        total = total + joined[n]
    small_out[:40] = total[:40]
    small_out[40:64] = pltpu.roll(total[16:40], 64, 1)
    small_out[64:] = total[40:]


def tail_call(operands, columns, down, w_in, size):
    rows, width = operands[0].shape
    emb, filt_width = operands[10].shape[1], operands[11].shape[1]
    part = w_in.shape[0] // 32
    small = 16 + 24
    kinds = [(part, width, "made", False)] * 3 + [one.shape[1:] + ("", False) for one in columns]
    operands = tuple(operands) + tuple(columns) + tuple(down)
    fetch = (0, 1, 2, 3, 5, 8, 9, 10, 15, 16, 17, 18)
    return pl.pallas_call(
        fetching(functools.partial(tail_kernel, size), fetch, [len(operands) + 1]),
        out_shape=[
            jax.ShapeDtypeStruct((rows, width), BF),
            jax.ShapeDtypeStruct((part, 3 * width), F32),
            jax.ShapeDtypeStruct((small + 24 + filt_width, 128), F32),
        ]
        + [jax.ShapeDtypeStruct(one.shape[1:], F32) for one in columns]
        + [jax.ShapeDtypeStruct(down[0].shape, F32)],
        in_specs=fetch_specs(operands, fetch) + [ANYWHERE],
        out_specs=[ANYWHERE] + [VM] * 5,
        scratch_shapes=[
            pltpu.VMEM(w_in.shape, BF),
            pltpu.VMEM((width, rows), BF),
            pltpu.VMEM((3, 4, 2, 2, 2, part, width), BF),
            pltpu.VMEM((rows, width), F32),
            pltpu.VMEM((16, width), F32),
            pltpu.VMEM((filt_width, 128), F32),
            pltpu.VMEM((48, 128), F32),
            pltpu.VMEM((8, small, 128), F32),
            pltpu.VMEM((4, small + filt_width, 128), F32),
            pltpu.VMEM((emb, filt_width), F32),
            pltpu.VMEM(down[1].shape, BF),
            pltpu.VMEM((24, 128), F32),
            pltpu.SemaphoreType.DMA,
            pltpu.SemaphoreType.DMA((17,)),
            pltpu.SemaphoreType.DMA((17,)),
            pltpu.SemaphoreType.DMA((2,)),
        ]
        + Scatter.scratch(kinds, 0.5)
        + fetch_scratch(operands, fetch, [jax.ShapeDtypeStruct((rows, width), BF)], (0,)),
        compiler_params=pltpu.CompilerParams(collective_id=3, has_side_effects=True, vmem_limit_bytes=VMEM_LIMIT),
    )(*operands, w_in)


def general_body(
    tokens,
    lengths,
    in_weight,
    out_weight,
    up_weight,
    down_weight,
    gain_one,
    gain_two,
    conv_taps,
    skip_gain,
    filter_first,
    filter_bias,
    frequency,
    filter_second,
    cotangent,
):
    ch_count = lax.axis_size("ch")
    ch_place = lax.axis_index("ch")
    size = tokens.shape[1]
    buckets = tokens.shape[2]
    width = tokens.shape[3]
    chans = skip_gain.shape[0]
    length = size * ch_count
    rows = size * buckets
    dims = (ch_count, size, buckets, chans)
    tables = tuple(jnp.asarray(one) for one in block_tables(size))

    def gather(shard):
        return lax.all_gather(shard, ("ch", "seq"), axis=0, tiled=True)

    full_in = gather(in_weight)
    full_gain_one = gather(gain_one).astype(F32)
    full_gain_two = gather(gain_two).astype(F32)
    full_out = gather(out_weight)
    full_up = gather(up_weight)
    full_down = gather(down_weight)

    local = ch_place * size + jnp.arange(size, dtype=jnp.int32)
    mask = (local[None, :] < lengths[0][:, None]).astype(F32).reshape(rows, 1)
    before = ch_place * size - 2 + jnp.arange(2, dtype=jnp.int32)
    mask_before = (before[None, :] < lengths[0][:, None]).astype(F32).reshape(2 * buckets, 1)
    chain = [(i, i + 1) for i in range(ch_count - 1)]
    halo = lax.ppermute(tokens[0, size - 2 :], "ch", chain)
    x_zero = jnp.swapaxes(tokens[0], 0, 1).reshape(rows, width).astype(F32) * mask
    x_before = jnp.swapaxes(halo, 0, 1).reshape(2 * buckets, width).astype(F32) * mask_before

    taps_full = lax.all_gather(conv_taps.reshape(9, chans), "ch", axis=1, tiled=True).reshape(3, 3, width)
    skip_full = lax.all_gather(skip_gain.reshape(1, chans), "ch", axis=1, tiled=True)

    table = positions_table(length, filter_first.shape[0])
    hidden = filter_hidden(filter_first, filter_bias, frequency, table)
    decay = decay_table(length, ch_place * chans, chans, width)
    filt = jnp.dot(hidden, filter_second, precision=HIGH) * decay
    filt_blocks = jnp.tile(filt.reshape(ch_count, size, chans), (1, 1, buckets))

    normed_one = layer_norm(x_zero, full_gain_one).astype(BF)
    normed_before = layer_norm(x_before, full_gain_one).astype(BF)
    streams = jnp.dot(normed_one, full_in, preferred_element_type=F32).astype(BF)
    streams_before = jnp.dot(normed_before, full_in, preferred_element_type=F32).astype(BF)
    lag = jnp.concatenate(
        [streams_before.reshape(buckets, 2, 3, width), streams.reshape(buckets, size, 3, width)], axis=1
    ).astype(F32)
    lag_zero, lag_one, lag_two = lag[:, 2:], lag[:, 1:-1], lag[:, :-2]
    conv = taps_full[0] * lag_zero + taps_full[1] * lag_one + taps_full[2] * lag_two
    gate = conv[:, :, 0].reshape(rows, width)
    key_part = conv[:, :, 1].reshape(rows, width)
    value_part = conv[:, :, 2].reshape(rows, width)
    mixed = key_part * value_part

    convolved, kept = conv_forward(mixed.astype(BF), filt_blocks, tables, dims)
    long_part = convolved.astype(F32) + skip_full * mixed
    mixer = (gate * long_part * mask).astype(BF)
    after_mix = x_zero + jnp.dot(mixer, full_out, preferred_element_type=F32)
    normed_two = layer_norm(after_mix, full_gain_two).astype(BF)
    inner_act = jnp.dot(normed_two, full_up, preferred_element_type=F32)
    active = jax.nn.gelu(inner_act).astype(BF)
    result = (after_mix + jnp.dot(active, full_down, preferred_element_type=F32)).astype(BF)
    result = jnp.swapaxes(result.reshape(buckets, size, width), 0, 1).reshape(1, size, buckets, width)

    grad_result = jnp.swapaxes(cotangent[0], 0, 1).reshape(rows, width)
    grad_active = jnp.dot(grad_result, full_down.T, preferred_element_type=F32)
    _, gelu_pull = jax.vjp(jax.nn.gelu, inner_act)
    grad_inner = gelu_pull(grad_active)[0].astype(BF)
    grad_down = jnp.dot(active.T, grad_result, preferred_element_type=F32)
    grad_up = jnp.dot(normed_two.T, grad_inner, preferred_element_type=F32)
    grad_normed_two = jnp.dot(grad_inner, full_up.T, preferred_element_type=F32)
    _, norm_two_pull = jax.vjp(layer_norm, after_mix, full_gain_two)
    grad_after_part, grad_gain_two = norm_two_pull(grad_normed_two)
    grad_after = grad_result.astype(F32) + grad_after_part
    grad_mix = grad_after.astype(BF)
    grad_out = jnp.dot(mixer.T, grad_mix, preferred_element_type=F32)
    grad_mixer = jnp.dot(grad_mix, full_out.T, preferred_element_type=F32).astype(BF)
    grad_masked = grad_mixer.astype(F32) * mask
    grad_gate = grad_masked * long_part
    grad_long = grad_masked * gate
    grad_skip = jnp.sum(grad_long * mixed, axis=0)
    grad_convolved, grad_filt = conv_backward(grad_long.astype(BF), kept, filt_blocks, tables, dims)
    grad_mixed = grad_convolved.astype(F32) + skip_full * grad_long
    grad_conv = jnp.stack([grad_gate, grad_mixed * value_part, grad_mixed * key_part], axis=1)
    grad_conv = grad_conv.reshape(buckets, size, 3, width)
    grad_taps = jnp.stack(
        [
            jnp.sum(grad_conv * lag_zero, axis=(0, 1)),
            jnp.sum(grad_conv * lag_one, axis=(0, 1)),
            jnp.sum(grad_conv * lag_two, axis=(0, 1)),
        ],
        axis=0,
    )
    next_rows = lax.ppermute(grad_conv[:, :2], "ch", [(j, i) for i, j in chain])
    ahead = jnp.concatenate([grad_conv, next_rows], axis=1)
    grad_streams = taps_full[0] * ahead[:, :-2] + taps_full[1] * ahead[:, 1:-1] + taps_full[2] * ahead[:, 2:]
    grad_projected = grad_streams.astype(BF).reshape(rows, 3 * width)
    grad_in = jnp.dot(normed_one.T, grad_projected, preferred_element_type=F32)
    grad_normed_one = jnp.dot(grad_projected, full_in.T, preferred_element_type=F32)
    _, norm_one_pull = jax.vjp(layer_norm, x_zero, full_gain_one)
    grad_zero_part, grad_gain_one = norm_one_pull(grad_normed_one)
    grad_input = ((grad_after + grad_zero_part) * mask).astype(BF)
    grad_input = jnp.swapaxes(grad_input.reshape(buckets, size, width), 0, 1).reshape(1, size, buckets, width)

    grad_filt = jnp.sum(grad_filt.reshape(length, buckets, chans), axis=1)
    grad_raw = grad_filt * decay
    grad_second = jnp.dot(hidden.T, grad_raw, precision=HIGH)
    grad_hidden = jnp.dot(grad_raw, filter_second.T, precision=HIGH)

    def hidden_of(first_layer, first_shift, freq_values):
        return filter_hidden(first_layer, first_shift, freq_values, table)

    _, hidden_pull = jax.vjp(hidden_of, filter_first, filter_bias, frequency)
    grad_first, grad_bias, grad_freq = hidden_pull(grad_hidden)

    sum_in, sum_out, sum_up, sum_down, sum_gain_one, sum_gain_two = (
        lax.psum_scatter(one, ("ch", "seq"), scatter_dimension=0, tiled=True)
        for one in (grad_in, grad_out, grad_up, grad_down, grad_gain_one, grad_gain_two)
    )
    sum_second = lax.psum(grad_second, "seq")
    all_taps, all_skip, sum_first, sum_bias, sum_freq = lax.psum(
        (grad_taps, grad_skip, grad_first, grad_bias, grad_freq), ("ch", "seq")
    )
    sum_taps = lax.dynamic_slice_in_dim(all_taps, ch_place * chans, chans, 2)
    sum_skip = lax.dynamic_slice_in_dim(all_skip, ch_place * chans, chans, 0)
    return (
        result,
        grad_input,
        sum_in,
        sum_out,
        sum_up,
        sum_down,
        sum_gain_one,
        sum_gain_two,
        sum_taps,
        sum_skip,
        sum_first,
        sum_bias,
        sum_freq,
        sum_second,
    )


def by_position(values, size):
    parts = values.reshape(2, size, values.shape[1])
    bucket = lax.broadcasted_iota(jnp.int32, (size, 2, values.shape[1]), 1)
    return jnp.where(bucket == 0, parts[0][:, None, :], parts[1][:, None, :])[None]


def filter_table(length, features):
    steps = np.arange(length).astype(np.float32)
    scaled = steps / np.float32(length - 1)
    bands = (features - 1) // 2
    freqs = np.float32(0.0001) + np.float32(bands - 1 - 0.0001) * np.arange(bands).astype(np.float32) / np.float32(bands - 1)
    angles = freqs[None, :] * (np.float32(2.0 * math.pi) * steps / np.float32(length))[:, None]
    table = np.concatenate([scaled[:, None], np.cos(angles), -np.sin(angles)], axis=1)
    return np.pad(table, ((0, 0), (0, -features % 8)))


def slice_body(
    tokens,
    lengths,
    in_weight,
    out_weight,
    up_weight,
    down_weight,
    gain_one,
    gain_two,
    conv_taps,
    skip_gain,
    filter_first,
    filter_bias,
    frequency,
    filter_second,
    cotangent,
):
    seq_place = lax.axis_index("seq")
    size = tokens.shape[1]
    buckets = tokens.shape[2]
    width = tokens.shape[3]
    chans = skip_gain.shape[0]
    length = size * 8
    rows = size * buckets
    part = gain_one.shape[0]
    emb, filt_width = filter_first.shape
    tables = tuple(jnp.asarray(one) for one in block_tables(size))

    by_bucket = jnp.swapaxes(tokens[0], 0, 1)
    flat = by_bucket.reshape(rows, width)
    wide_table = jnp.asarray(filter_table(length, emb))
    pads = wide_table.shape[1] - emb
    (consts, halo, hidden, filt), full_in, columns = start_call(
        conv_taps,
        skip_gain[None],
        gain_one[None],
        gain_two[None],
        by_bucket,
        wide_table,
        filter_first,
        filter_second,
        filter_bias[None],
        frequency[None],
        (in_weight, out_weight, up_weight),
        size,
    )
    (normed_one, streams, mixer, kept, convolved, wide_mask, column_down), (full_out, full_up), early = forward_call(
        lengths, flat, halo, consts, filt, tables, down_weight, columns, full_in, size
    )
    grad_result = jnp.swapaxes(cotangent[0], 0, 1).reshape(rows, width)
    result, grad_after, grad_mixer, grad_gain_two, grad_out, sum_column, sum_last, grad_up = feed_forward_call(
        mixer, flat, wide_mask, grad_result, consts, full_out, full_up, early, column_down
    )
    result = by_position(result, size)

    (grad_projected, grad_filt, sums), (down_mine, *late, down_far) = backward_call(
        streams, consts, wide_mask, grad_mixer, convolved, kept, filt, tables, (sum_column, grad_up, grad_out), sum_last, size
    )
    grad_input, sum_in, small, sum_up, sum_out, sum_down = tail_call(
        (normed_one, grad_projected, flat, wide_mask, consts, grad_after, sums, grad_gain_two)
        + (grad_filt, hidden, wide_table, filter_first, filter_second, filter_bias[None], frequency[None]),
        late,
        (down_mine, down_far),
        full_in,
        size,
    )
    grad_input = by_position(grad_input, size)
    after = 16 + emb + pads
    gain_sums = lax.dynamic_slice_in_dim(small[10:12], seq_place * part, part, 1)
    return (
        result,
        grad_input,
        sum_in,
        sum_out,
        sum_up,
        sum_down,
        gain_sums[0],
        gain_sums[1],
        small[:9].reshape(3, 3, chans),
        small[9],
        small[16 : 16 + emb, :filt_width],
        small[after, :filt_width],
        small[after + 1, :filt_width],
        small[64:],
    )


def solution(mesh):
    placed = (
        P("seq", "ch", None, None),
        P("seq", None),
        P(("ch", "seq"), None),
        P(("ch", "seq"), None),
        P(("ch", "seq"), None),
        P(("ch", "seq"), None),
        P(("ch", "seq")),
        P(("ch", "seq")),
        P(None, None, "ch"),
        P("ch"),
        P(),
        P(),
        P(),
        P(None, "ch"),
        P("seq", "ch", None, None),
    )
    custom = dict(mesh.shape) == {"ch": 8, "seq": 4}
    return jax.shard_map(
        slice_body if custom else general_body,
        mesh=mesh,
        in_specs=placed,
        out_specs=(
            P("seq", "ch", None, None),
            P("seq", "ch", None, None),
            P(("ch", "seq"), None),
            P(("ch", "seq"), None),
            P(("ch", "seq"), None),
            P(("ch", "seq"), None),
            P(("ch", "seq")),
            P(("ch", "seq")),
            P(None, None, "ch"),
            P("ch"),
            P(),
            P(),
            P(),
            P(None, "ch"),
        ),
        check_vma=False,
    )
```
